32 devices in a mesh: band: 16 (over z, y, x), disp: 2 (over core).
Axes of the slice: x: 2, y: 2, z: 4, core: 2. Of those that a mesh axis runs over, the one named last changes fastest.
Arguments:
- feat_left: bfloat16 [16, 96, 256], P('band', None, 'disp'), may hold values from -19 to 19
- feat_right: bfloat16 [16, 96, 256], P('band', None, 'disp'), may hold values from -19 to 19
- limit: int32 [16, 256], P('band', 'disp'), may hold values from 24 to 96
- indices: int32 [3, 16, 256], P(None, 'band', 'disp'), may hold values from 0 to 95
- hidden_start: bfloat16 [16, 256, 128], P('band', 'disp'), may hold values from -1 to 1
- vol_kernel: bfloat16 [3, 3, 3, 8, 8], replicated, may hold values from -0.4375 to 0.4375
- group_gain: float32 [8], replicated, may hold values from 0.5 to 2
- hid_kernel: bfloat16 [3, 3, 128, 384], replicated, may hold values from -0.1875 to 0.1875
- in_kernel: bfloat16 [3, 3, 9, 384], replicated, may hold values from -0.625 to 0.625
- head_weight: bfloat16 [128, 1], replicated, may hold values from -0.5 to 0.5
Outputs:
- disparity: float32 [16, 256], P('band', 'disp')
- hidden: bfloat16 [16, 256, 128], P('band', 'disp')
The draws below stay inside these ranges and needn't reach their ends.
All inputs are finite; a program needn't handle non-finite values.
Results may differ from the reference program's by a relative error of at most 0.007.
Values may be sent and summed in bfloat16 or wider, within the bound.
No kernel may reach another device: no remote copies, remote signals or barrier semaphores. Data moves between devices by JAX's collectives and lax.ppermute only.
A program may use at most 128 MiB of HBM per device.

```python
import math
import jax
import jax.numpy as jnp
from jax import lax

ROWS_DEV = 1
FEAT_CH = 96
GROUPS = 8
DISPS = 96
HID_CH = 128
ITERS = 3
HEIGHT = 16
WIDTH = 256


def feature_pair(key):
    left = jnp.clip(jax.random.normal(jax.random.fold_in(key, 11), (HEIGHT, FEAT_CH, WIDTH), jnp.float32), -6.0, 6.0)
    right = jnp.clip(jax.random.normal(jax.random.fold_in(key, 12), (HEIGHT, FEAT_CH, WIDTH), jnp.float32), -6.0, 6.0)
    return (left, right)


def draw_feat_left(key, part):
    return feature_pair(key)[0].astype(jnp.bfloat16)


def draw_feat_right(key, part):
    return feature_pair(key)[1].astype(jnp.bfloat16)


def touch_ends(array, stream_key, least, high):
    longest = array.shape.index(max(array.shape))
    spots = []
    for shift in (0, 1):
        where = [jax.random.randint(jax.random.fold_in(stream_key, axis), (), 0, length) for axis, length in enumerate(array.shape)]
        where[longest] = (where[longest] + shift) % array.shape[longest]
        spots.append(tuple(where))
    return array.at[spots[0]].set(least).at[spots[1]].set(high)


def steps_of(rng, shape, shards, least, largest):
    factor_of, own = 1.0, jax.random.fold_in(rng, 6)
    for axis_at, parts in shards:
        steps = jnp.exp(jax.random.uniform(jax.random.fold_in(own, axis_at), (parts,), jnp.float32, least / len(shards), largest / len(shards)))
        factor_of = factor_of * jnp.repeat(steps, shape[axis_at] // parts).reshape([-1 if axis == axis_at else 1 for axis in range(len(shape))])
    return factor_of


def gaussian(rng, dims, spread, reach, kind=jnp.bfloat16):
    drawn = spread * jax.random.normal(rng, dims, jnp.float32)
    return jnp.clip(drawn, min=-reach, max=reach).astype(kind)


def setup_inputs(seed: int = 0) -> dict:
    key_list = jax.random.split(jax.random.key(seed), 11)
    return {
        "feat_left": draw_feat_left(jax.random.fold_in(key_list[10], 71), 0),
        "feat_right": draw_feat_right(jax.random.fold_in(key_list[10], 71), 0),
        "limit": touch_ends(jax.random.randint(key_list[2], (HEIGHT, WIDTH), DISPS // 4, DISPS + 1), jax.random.fold_in(key_list[2], 1), DISPS // 4, DISPS).astype(jnp.int32),
        "indices": touch_ends(jax.random.randint(key_list[3], (ITERS, HEIGHT, WIDTH), 0, DISPS), jax.random.fold_in(key_list[3], 1), 0, DISPS - 1).astype(jnp.int32),
        "hidden_start": jnp.clip(jax.random.uniform(key_list[4], (HEIGHT, WIDTH, HID_CH), jnp.float32, -1.0, 1.0) * steps_of(key_list[4], (HEIGHT, WIDTH, HID_CH), ((0, 16), (1, 2)), -0.4, 0.0), -1.0, 1.0).astype(jnp.bfloat16),
        "vol_kernel": gaussian(key_list[5], (3, 3, 3, GROUPS, GROUPS), (27 * GROUPS) ** -0.5, 0.4375),
        "group_gain": jnp.clip(jnp.exp(jax.random.uniform(key_list[6], (GROUPS,), jnp.float32, math.log(0.5), math.log(2.0))), 0.5, 2.0),
        "hid_kernel": gaussian(key_list[7], (3, 3, HID_CH, 3 * HID_CH), (9 * HID_CH) ** -0.5, 0.1875),
        "in_kernel": gaussian(key_list[8], (3, 3, GROUPS + 1, 3 * HID_CH), (9 * (GROUPS + 1)) ** -0.5, 0.625),
        "head_weight": gaussian(key_list[9], (HID_CH, 1), HID_CH ** -0.5, 0.5),
    }


pixel_unit = 8.0
feature_scale = 0.25
floor_logit = -1e30


def correlate(left, right):
    row_count, channels, col_count = left.shape
    per_group = channels // GROUPS
    padded = jnp.pad(right, ((0, 0), (0, 0), (DISPS, 0)))

    def one_disp(offset):
        shifted = lax.dynamic_slice_in_dim(padded, (DISPS - offset).astype(jnp.int32), col_count, 2)
        products = left.astype(jnp.float32) * shifted.astype(jnp.float32)
        return products.reshape(row_count, GROUPS, per_group, col_count).sum(2) / per_group

    volume = lax.map(one_disp, jnp.arange(DISPS, dtype=jnp.int32))
    return volume.astype(jnp.bfloat16)


def conv_plane(values, kernel):
    result = lax.conv_general_dilated(values[None], kernel, (1, 1), ((1, 1), (1, 1)),
                                      dimension_numbers=("NHWC", "HWIO", "NHWC"),
                                      preferred_element_type=jnp.float32)
    return result[0]


def reference(feat_left, feat_right, limit, indices, hidden_start, vol_kernel, group_gain, hid_kernel, in_kernel, head_weight):
    left_pad = jnp.pad(feat_left, ((1, 1), (0, 0), (0, 0)))
    right_pad = jnp.pad(feat_right, ((1, 1), (0, 0), (0, 0)))
    levels = jnp.arange(DISPS, dtype=jnp.int32)[:, None, None]

    def band_block(band_index):
        first_row = band_index * ROWS_DEV
        left_rows = lax.dynamic_slice_in_dim(left_pad, first_row, ROWS_DEV + 2, 0)
        right_rows = lax.dynamic_slice_in_dim(right_pad, first_row, ROWS_DEV + 2, 0)
        raw_volume = correlate(left_rows, right_rows).transpose(0, 1, 3, 2)
        conv_out = lax.conv_general_dilated(raw_volume[None], vol_kernel, (1, 1, 1), ((1, 1), (0, 0), (1, 1)),
                                            dimension_numbers=("NDHWC", "DHWIO", "NDHWC"),
                                            preferred_element_type=jnp.float32)[0]
        volume = (raw_volume[:, 1:-1].astype(jnp.float32) + jnp.maximum(conv_out, 0.0)).astype(jnp.bfloat16)
        logits = jnp.sum(volume.astype(jnp.float32) * group_gain, axis=-1)
        limit_rows = lax.dynamic_slice_in_dim(limit, first_row, ROWS_DEV, 0)
        valid = levels < limit_rows[None]
        masked = jnp.where(valid, logits, floor_logit)
        row_top = jnp.max(masked, axis=0)
        weights = jnp.where(valid, jnp.exp(masked - row_top), 0.0)
        moment = jnp.sum(weights * levels.astype(jnp.float32), axis=0)
        initial = moment / jnp.sum(weights, axis=0) / pixel_unit
        index_rows = lax.dynamic_slice_in_dim(indices, first_row, ROWS_DEV, 1)
        lookups = []
        for iteration in range(ITERS):
            where_at = jnp.broadcast_to(index_rows[iteration][None, :, :, None], (1,) + volume.shape[1:])
            lookups.append(jnp.take_along_axis(volume, where_at, axis=0)[0])
        return initial, jnp.stack(lookups)

    initial, lookups = lax.map(band_block, jnp.arange(HEIGHT // ROWS_DEV, dtype=jnp.int32))
    disparity = initial.reshape(HEIGHT, WIDTH)
    lookups = lookups.transpose(1, 0, 2, 3, 4).reshape(ITERS, HEIGHT, WIDTH, GROUPS)
    hidden = hidden_start
    for iteration in range(ITERS):
        inputs = jnp.concatenate([lookups[iteration].astype(jnp.float32), (feature_scale * disparity)[..., None]], -1).astype(jnp.bfloat16)
        in_conv = conv_plane(inputs, in_kernel)
        hid_conv = conv_plane(hidden, hid_kernel[:, :, :, :2 * HID_CH])
        update = jax.nn.sigmoid(hid_conv[..., :HID_CH] + in_conv[..., :HID_CH])
        reset_gate = jax.nn.sigmoid(hid_conv[..., HID_CH:] + in_conv[..., HID_CH:2 * HID_CH])
        reset_hidden = (reset_gate * hidden.astype(jnp.float32)).astype(jnp.bfloat16)
        candidate = jnp.tanh(conv_plane(reset_hidden, hid_kernel[:, :, :, 2 * HID_CH:]) + in_conv[..., 2 * HID_CH:])
        hidden = ((1.0 - update) * hidden.astype(jnp.float32) + update * candidate).astype(jnp.bfloat16)
        change = jnp.dot(hidden.reshape(-1, HID_CH), head_weight, preferred_element_type=jnp.float32)
        disparity = disparity + change.reshape(HEIGHT, WIDTH)
    return disparity, hidden
```

```python
import jax
import jax.numpy as jnp
from jax import lax
from jax.experimental import pallas as pl
from jax.experimental.pallas import tpu as pltpu
from jax.sharding import PartitionSpec as P

GROUPS = 8
DISPS = 96
FEAT_CH = 96
HID_CH = 128
ITERS = 3
TILE = 128
REACH = 2 * ITERS
EDGE = 8
SPAN = TILE + 2 * EDGE
ROWS = 2 * REACH + 1
PACK = 32
BLOCK = 8
SLAB = (BLOCK + 2) * GROUPS
OUT_SLAB = BLOCK * GROUPS

pixel_unit = 8.0
feature_scale = 0.25
floor_logit = -1e30

f32 = jnp.float32
bf16 = jnp.bfloat16


def dot(a, b):
    return jnp.dot(a, b, preferred_element_type=f32)


def dot_nt(a, b):
    return lax.dot_general(a, b, (((1,), (1,)), ((), ())), preferred_element_type=f32)


def copy_all(copies):
    for copy in copies:
        copy.start()
    for copy in copies:
        copy.wait()


def volume_kernel(
    place, gain, left_all, right_all, limit, indices, taps, out, left, right, wide, extra, logit, sems
):
    band, disp, bands, disps = place[0], place[1], place[2], place[3]
    columns = (jnp.maximum(disp - 1, 0), disp, jnp.minimum(disp + 1, disps - 1))
    copies = []
    for b in range(3):
        row = jnp.clip(band + b - 1, 0, bands - 1)
        for s in range(3):
            where = row * disps + columns[s]
            copies.append(
                pltpu.make_async_copy(left_all.at[where], left.at[b, s], sems.at[0, b, s])
            )
            copies.append(
                pltpu.make_async_copy(right_all.at[where], right.at[b, s], sems.at[1, b, s])
            )
    for copy in copies:
        copy.start()

    lane = lax.broadcasted_iota(jnp.int32, (TILE, TILE), 1)
    sub = lax.broadcasted_iota(jnp.int32, (TILE, TILE), 0)
    flip = jnp.where(lane + sub == TILE - 1, 1.0, 0.0).astype(bf16)
    has_left = (disp > 0).astype(f32)
    has_right = (disp < disps - 1).astype(f32)
    per_group = FEAT_CH // GROUPS
    channel = lax.broadcasted_iota(jnp.int32, (TILE, FEAT_CH), 1)
    group_masks = [
        (channel >= g * per_group) & (channel < (g + 1) * per_group) for g in range(GROUPS)
    ]
    lane96 = lax.broadcasted_iota(jnp.int32, (FEAT_CH, TILE), 1)
    zero_slab = jnp.zeros((GROUPS, TILE), f32)
    for b in range(3):
        for at in (0, (DISPS + 1) * GROUPS):
            wide[b, pl.ds(at, GROUPS), :] = zero_slab
            extra[b, pl.ds(at, GROUPS), :] = zero_slab
    for copy in copies:
        copy.wait()

    for b in range(3):
        row = band + b - 1
        row_ok = ((row >= 0) & (row < bands)).astype(f32)
        own = left[b, 1].astype(f32) * row_ok
        own_t = own.T
        side = jnp.where(
            lane96 < EDGE,
            left[b, 2].astype(f32) * (has_right * row_ok),
            jnp.where(lane96 >= TILE - EDGE, left[b, 0].astype(f32) * (has_left * row_ok), 0.0),
        )
        side_t = side.T
        flipped = []
        for s, factor in ((2, has_right), (1, None), (0, has_left)):
            part = dot(right[b, s], flip)
            flipped.append(part if factor is None else part * factor)
        line = jnp.concatenate(flipped, axis=1)
        windows = [
            line[:, 2 * TILE - 32 - 32 * k : 3 * TILE - 32 - 32 * k].astype(bf16)
            for k in range(-1, 5)
        ]
        sheared = [[] for _ in range(GROUPS)]
        for k in range(4):
            rows = own_t[32 * k : 32 * k + 32]
            lhs = jnp.concatenate(
                [jnp.where(m[:32], rows, 0.0) for m in group_masks], axis=0
            ).astype(bf16)
            product = dot(lhs, windows[k + 1])
            for g in range(GROUPS):
                sheared[g].append(
                    pltpu.roll(
                        product[32 * g : 32 * g + 32], TILE - 31, 1, stride=1, stride_axis=0
                    )
                )
        after = side_t[:EDGE]
        before = side_t[TILE - EDGE :]
        lhs_after = jnp.concatenate(
            [jnp.where(m[:EDGE], after, 0.0) for m in group_masks], axis=0
        ).astype(bf16)
        lhs_before = jnp.concatenate(
            [jnp.where(m[:EDGE], before, 0.0) for m in group_masks], axis=0
        ).astype(bf16)
        product_after = dot(lhs_after, windows[5])
        product_before = dot(lhs_before, windows[0])
        gap = jnp.zeros((TILE - 2 * EDGE, TILE), f32)
        for g in range(GROUPS):
            part = jnp.concatenate(sheared[g], axis=0).T * (1.0 / per_group)
            wide[b, pl.ds(GROUPS + g, DISPS, stride=GROUPS), :] = part[:DISPS]
            rows_after = pltpu.roll(
                product_after[EDGE * g : EDGE * g + EDGE], TILE - 31, 1, stride=1, stride_axis=0
            )
            rows_before = pltpu.roll(
                product_before[EDGE * g : EDGE * g + EDGE],
                TILE - 31 + 32 - EDGE,
                1,
                stride=1,
                stride_axis=0,
            )
            part = jnp.concatenate([rows_after, gap, rows_before], axis=0).T * (1.0 / per_group)
            extra[b, pl.ds(GROUPS + g, DISPS, stride=GROUPS), :] = part[:DISPS]

    lane8 = lax.broadcasted_iota(jnp.int32, (OUT_SLAB, TILE), 1)
    group_at = lax.broadcasted_iota(jnp.int32, (GROUPS, TILE), 0)
    gains = jnp.zeros((GROUPS, TILE), f32)
    for g in range(GROUPS):
        gains = jnp.where(group_at == g, gain[g], gains)
    wanted = [jnp.broadcast_to(indices[t : t + 1, :], (GROUPS, TILE)) for t in range(ITERS)]
    found = [jnp.zeros((GROUPS, TILE), f32) for _ in range(ITERS)]
    for q in range(DISPS // BLOCK):
        at = q * OUT_SLAB
        slabs = []
        for b in range(3):
            slabs.append(
                jnp.concatenate(
                    [wide[b, at : at + SLAB, :], extra[b, at : at + SLAB, :]], axis=1
                ).astype(bf16)
            )
        product = dot(taps[...], jnp.concatenate(slabs, axis=0))
        first, middle, last = (
            product[:OUT_SLAB],
            product[OUT_SLAB : 2 * OUT_SLAB],
            product[2 * OUT_SLAB :],
        )
        conv = (
            middle[:, :TILE]
            + jnp.where(
                lane8 == 0,
                pltpu.roll(first[:, TILE:], 1, 1),
                pltpu.roll(first[:, :TILE], 1, 1),
            )
            + jnp.where(
                lane8 == TILE - 1,
                pltpu.roll(last[:, TILE:], TILE - 1, 1),
                pltpu.roll(last[:, :TILE], TILE - 1, 1),
            )
        )
        raw = wide[1, at + GROUPS : at + GROUPS + OUT_SLAB, :].astype(bf16).astype(f32)
        volume = (raw + jnp.maximum(conv, 0.0)).astype(bf16).astype(f32)
        volume = volume.reshape(BLOCK, GROUPS, TILE)
        logit[q * BLOCK : (q + 1) * BLOCK, :] = jnp.sum(volume * gains[None], axis=1)
        for d in range(BLOCK):
            for t in range(ITERS):
                found[t] = found[t] + jnp.where(wanted[t] == q * BLOCK + d, volume[d], 0.0)

    level = lax.broadcasted_iota(jnp.int32, (DISPS, TILE), 0)
    valid = level < limit[...]
    masked = jnp.where(valid, logit[...], floor_logit)
    top = jnp.max(masked, axis=0, keepdims=True)
    weights = jnp.where(valid, jnp.exp(masked - top), 0.0)
    moment = jnp.sum(weights * level.astype(f32), axis=0, keepdims=True)
    start = moment / jnp.sum(weights, axis=0, keepdims=True) / pixel_unit
    high = start.astype(bf16).astype(f32)
    low = (start - high).astype(bf16).astype(f32)
    ends = jnp.where(
        group_at == 0,
        jnp.broadcast_to(high, (GROUPS, TILE)),
        jnp.where(group_at == 1, jnp.broadcast_to(low, (GROUPS, TILE)), 0.0),
    )
    out[...] = jnp.concatenate(found + [ends], axis=0).astype(bf16)


def refine_kernel(
    place,
    packed_all,
    hidden_all,
    hid_weight,
    in_weight,
    head,
    disparity_out,
    hidden_out,
    packed,
    tiles,
    sides,
    weight,
    lookups,
    taps,
    reset_taps,
    gate,
    inputs,
    level,
    sems,
):
    band, disp, bands, disps = place[0], place[1], place[2], place[3]
    held = packed.shape[1]
    first = jnp.clip(band - REACH, 0, bands - held)
    before, after = jnp.maximum(disp - 1, 0), jnp.minimum(disp + 1, disps - 1)
    rows = pl.ds(first, held)
    hidden_copies = [
        pltpu.make_async_copy(hidden_all.at[rows, disp], tiles, sems.at[0]),
        pltpu.make_async_copy(
            hidden_all.at[rows, before, pl.ds(TILE - 16, 16)], sides.at[0], sems.at[1]
        ),
        pltpu.make_async_copy(
            hidden_all.at[rows, after, pl.ds(0, 16)], sides.at[1], sems.at[2]
        ),
    ]
    packed_copies = [
        pltpu.make_async_copy(packed_all.at[rows, column], packed.at[s], sems.at[3 + s])
        for s, column in enumerate((before, disp, after))
    ]
    weight_copies = [
        pltpu.make_async_copy(hid_weight, weight.at[pl.ds(0, 9 * HID_CH)], sems.at[6]),
        pltpu.make_async_copy(in_weight, weight.at[pl.ds(9 * HID_CH, HID_CH)], sems.at[7]),
    ]
    for copy in packed_copies + hidden_copies + weight_copies:
        copy.start()

    has_left = (disp > 0).astype(f32)
    has_right = (disp < disps - 1).astype(f32)
    held_at, row_ok = [], []
    for r in range(ROWS):
        row = band - REACH + r
        held_at.append(jnp.clip(row, 0, bands - 1) - first)
        row_ok.append(((row >= 0) & (row < bands)).astype(f32))
    column = lax.broadcasted_iota(jnp.int32, (SPAN, HID_CH), 0)
    column_ok = jnp.where(
        column < EDGE, has_left, jnp.where(column >= TILE + EDGE, has_right, 1.0)
    )
    lane = lax.broadcasted_iota(jnp.int32, (SPAN, HID_CH), 1)
    lane_tap = lane - 9 * GROUPS
    at_sub = lax.broadcasted_iota(jnp.int32, (SPAN, 2 * TILE), 0)
    at_lane = lax.broadcasted_iota(jnp.int32, (SPAN, 2 * TILE), 1)
    spread = jnp.where(
        ((at_sub >= EDGE) & (at_lane == at_sub - EDGE))
        | ((at_sub < EDGE) & (at_lane == at_sub - EDGE + 2 * TILE)),
        1.0,
        0.0,
    ).astype(bf16)
    lane_pack = lax.broadcasted_iota(jnp.int32, (PACK, TILE), 1)

    for copy in packed_copies:
        copy.wait()

    shifted = []
    for r in range(ROWS):
        centre = packed[1, held_at[r]].astype(f32) * row_ok[r]
        halo = jnp.where(
            lane_pack < TILE // 2,
            packed[2, held_at[r]].astype(f32) * (row_ok[r] * has_right),
            packed[0, held_at[r]].astype(f32) * (row_ok[r] * has_left),
        )
        both = jnp.concatenate([centre, halo], axis=1)
        shifted.append((pltpu.roll(both, 1, 1), both, pltpu.roll(both, 2 * TILE - 1, 1)))
    fill = jnp.zeros((HID_CH - 9 * GROUPS, 2 * TILE), f32)
    base = 0
    look_at = []
    for t in range(ITERS):
        low, high = 1 + 2 * t, ROWS - 2 - 2 * t
        look_at.append((base, low))
        for r in range(low, high + 1):
            pieces = []
            for a in range(3):
                for b in range(3):
                    pieces.append(shifted[r + a - 1][b][t * GROUPS : (t + 1) * GROUPS])
            line = jnp.concatenate(pieces + [fill], axis=0).astype(bf16)
            lookups[base + r - low] = dot_nt(spread, line)
        base += high - low + 1
    for r in range(ROWS):
        ends = shifted[r][1][3 * GROUPS : 4 * GROUPS]
        wide_high = jnp.broadcast_to(ends[0:1], (HID_CH, 2 * TILE)).astype(bf16)
        wide_low = jnp.broadcast_to(ends[1:2], (HID_CH, 2 * TILE)).astype(bf16)
        level[r * SPAN : (r + 1) * SPAN, :] = dot_nt(spread, wide_high) + dot_nt(spread, wide_low)

    for copy in hidden_copies + weight_copies:
        copy.wait()

    def keep(target, at, values):
        length = values.shape[0]
        target[at : at + length, 0:HID_CH] = pltpu.roll(values, 1, 0).astype(bf16)
        target[at : at + length, HID_CH : 2 * HID_CH] = values.astype(bf16)
        target[at : at + length, 2 * HID_CH :] = pltpu.roll(values, length - 1, 0).astype(bf16)

    for r in range(ROWS):
        values = jnp.concatenate(
            [
                sides[0, held_at[r]].astype(f32)[16 - EDGE :],
                tiles[held_at[r]].astype(f32),
                sides[1, held_at[r]].astype(f32)[:EDGE],
            ],
            axis=0,
        )
        keep(taps, r * SPAN, values * (column_ok * row_ok[r]))

    def chunks(low, high, most):
        count = high - low + 1
        parts = -(-count // most)
        out = []
        for i in range(parts):
            size = count // parts + (1 if i < count % parts else 0)
            out.append((low, size))
            low += size
        return out

    for t in range(ITERS):
        low, high = 1 + 2 * t, ROWS - 2 - 2 * t
        spread_level = {}
        for r in range(low - 1, high + 2):
            value = level[r * SPAN : (r + 1) * SPAN, :] * feature_scale
            which = lane_tap % 3
            spread_level[r] = jnp.where(
                which == 0,
                pltpu.roll(value, 1, 0),
                jnp.where(which == 1, value, pltpu.roll(value, SPAN - 1, 0)),
            )
        for r in range(low, high + 1):
            base, from_row = look_at[t]
            value = lookups[base + r - from_row]
            for a in range(3):
                value = jnp.where(
                    (lane_tap >= 3 * a) & (lane_tap < 3 * a + 3), spread_level[r + a - 1], value
                )
            inputs[r * SPAN : (r + 1) * SPAN, :] = value.astype(bf16)

        for r, count in chunks(low, high, 4):
            at, length = r * SPAN, count * SPAN
            lhs = jnp.concatenate(
                [taps[at + (a - 1) * SPAN : at + (a - 1) * SPAN + length, :] for a in range(3)]
                + [inputs[at : at + length, :]],
                axis=1,
            )
            both = dot(lhs, weight[:, : 2 * HID_CH])
            both = 0.5 * jnp.tanh(0.5 * both) + 0.5
            hidden = taps[at : at + length, HID_CH : 2 * HID_CH].astype(f32)
            gate[at : at + length, :] = both[:, :HID_CH]
            keep(reset_taps, at, both[:, HID_CH:] * hidden)
        for r, count in chunks(low + 1, high - 1, 4):
            at, length = r * SPAN, count * SPAN
            lhs = jnp.concatenate(
                [
                    reset_taps[at + (a - 1) * SPAN : at + (a - 1) * SPAN + length, :]
                    for a in range(3)
                ]
                + [inputs[at : at + length, :]],
                axis=1,
            )
            candidate = jnp.tanh(dot(lhs, weight[:, 2 * HID_CH :]))
            update = gate[at : at + length, :]
            hidden = taps[at : at + length, HID_CH : 2 * HID_CH].astype(f32)
            hidden = (1.0 - update) * hidden + update * candidate
            mask = jnp.concatenate([column_ok * row_ok[r + i] for i in range(count)], axis=0)
            hidden = (hidden * mask).astype(bf16)
            level[at : at + length, :] += dot(hidden, head[...])
            if t < ITERS - 1:
                keep(taps, at, hidden.astype(f32))
            else:
                hidden_out[0] = hidden.astype(f32)[EDGE : EDGE + TILE].astype(bf16)
    at = REACH * SPAN + EDGE
    disparity_out[...] = level[at : at + TILE, :].T[0:1]


def local(
    feat_left,
    feat_right,
    limit,
    indices,
    hidden_start,
    vol_kernel,
    group_gain,
    hid_kernel,
    in_kernel,
    head_weight,
):
    bands, disps = lax.axis_size("band"), lax.axis_size("disp")
    axes = ("band", "disp")
    place = jnp.stack(
        [lax.axis_index("band"), lax.axis_index("disp"), jnp.int32(bands), jnp.int32(disps)]
    ).astype(jnp.int32)
    left_all = lax.all_gather(feat_left[0], axes)
    right_all = lax.all_gather(feat_right[0], axes)
    hidden_all = lax.all_gather(hidden_start[0], axes).reshape(bands, disps, TILE, HID_CH)

    shift = jnp.arange(BLOCK + 2)[None, :] - jnp.arange(BLOCK)[:, None]
    pick = (shift[:, :, None] == jnp.arange(3)).astype(bf16)
    taps = jnp.einsum("dxa,abeio->edobxi", pick, vol_kernel, preferred_element_type=f32)
    taps = taps.astype(bf16).reshape(3 * OUT_SLAB, 3 * SLAB)
    in_weight = jnp.concatenate(
        [
            in_kernel[:, :, :GROUPS].reshape(9 * GROUPS, 3 * HID_CH),
            in_kernel[:, :, GROUPS].reshape(9, 3 * HID_CH),
            jnp.zeros((HID_CH - 9 * (GROUPS + 1), 3 * HID_CH), bf16),
        ],
        axis=0,
    )
    head = jnp.broadcast_to(head_weight, (HID_CH, HID_CH))

    smem = pl.BlockSpec(memory_space=pltpu.SMEM)
    vmem = pl.BlockSpec(memory_space=pltpu.VMEM)
    anywhere = pl.BlockSpec(memory_space=pl.ANY)
    padded = (DISPS + 2) * GROUPS
    packed = pl.pallas_call(
        volume_kernel,
        out_shape=jax.ShapeDtypeStruct((PACK, TILE), bf16),
        in_specs=[smem, smem, anywhere, anywhere, vmem, vmem, vmem],
        out_specs=vmem,
        scratch_shapes=[
            pltpu.VMEM((3, 3, FEAT_CH, TILE), bf16),
            pltpu.VMEM((3, 3, FEAT_CH, TILE), bf16),
            pltpu.VMEM((3, padded, TILE), f32),
            pltpu.VMEM((3, padded, TILE), f32),
            pltpu.VMEM((DISPS, TILE), f32),
            pltpu.SemaphoreType.DMA((2, 3, 3)),
        ],
        compiler_params=pltpu.CompilerParams(vmem_limit_bytes=32 * 2**20),
    )(place, group_gain, left_all, right_all, limit, indices[:, 0], taps)

    packed_all = lax.all_gather(packed, axes).reshape(bands, disps, PACK, TILE)
    held = min(ROWS, bands)
    area = ROWS * SPAN
    looked = sum(ROWS - 2 - 4 * t for t in range(ITERS))
    disparity, hidden = pl.pallas_call(
        refine_kernel,
        out_shape=(
            jax.ShapeDtypeStruct((1, TILE), f32),
            jax.ShapeDtypeStruct((1, TILE, HID_CH), bf16),
        ),
        in_specs=[smem, anywhere, anywhere, anywhere, anywhere, vmem],
        out_specs=(vmem, vmem),
        scratch_shapes=[
            pltpu.VMEM((3, held, PACK, TILE), bf16),
            pltpu.VMEM((held, TILE, HID_CH), bf16),
            pltpu.VMEM((2, held, 16, HID_CH), bf16),
            pltpu.VMEM((10 * HID_CH, 3 * HID_CH), bf16),
            pltpu.VMEM((looked, SPAN, HID_CH), f32),
            pltpu.VMEM((area, 3 * HID_CH), bf16),
            pltpu.VMEM((area, 3 * HID_CH), bf16),
            pltpu.VMEM((area, HID_CH), f32),
            pltpu.VMEM((area, HID_CH), bf16),
            pltpu.VMEM((area, HID_CH), f32),
            pltpu.SemaphoreType.DMA((8,)),
        ],
        compiler_params=pltpu.CompilerParams(vmem_limit_bytes=40 * 2**20),
    )(place, packed_all, hidden_all, hid_kernel.reshape(9 * HID_CH, 3 * HID_CH), in_weight, head)
    return (disparity, hidden)


def solution(mesh):
    in_specs = (
        P("band", None, "disp"),
        P("band", None, "disp"),
        P("band", "disp"),
        P(None, "band", "disp"),
        P("band", "disp", None),
        P(),
        P(),
        P(),
        P(),
        P(),
    )
    out_specs = (P("band", "disp"), P("band", "disp", None))
    return jax.shard_map(local, mesh=mesh, in_specs=in_specs, out_specs=out_specs, check_vma=False)
```

```python
import jax
import jax.numpy as jnp
from jax import lax
from jax.experimental import pallas as pl
from jax.experimental.pallas import tpu as pltpu
from jax.sharding import PartitionSpec as P

GROUPS = 8
DISPS = 96
FEAT_CH = 96
HID_CH = 128
ITERS = 3
TILE = 128
REACH = 2 * ITERS
EDGE = 8
SPAN = TILE + 2 * EDGE
ROWS = 2 * REACH + 1
PACK = 32
BLOCK = 8
SLAB = (BLOCK + 2) * GROUPS
OUT_SLAB = BLOCK * GROUPS

pixel_unit = 8.0
feature_scale = 0.25
floor_logit = -1e30

f32 = jnp.float32
bf16 = jnp.bfloat16


def dot(a, b):
    return jnp.dot(a, b, preferred_element_type=f32)


def dot_nt(a, b):
    return lax.dot_general(a, b, (((1,), (1,)), ((), ())), preferred_element_type=f32)


def copy_all(copies):
    for copy in copies:
        copy.start()
    for copy in copies:
        copy.wait()


def volume_kernel(
    place, gain, own, across, odd_own, odd_across, even_own, even_across, limit, indices, taps,
    out, wide, extra, logit,
):
    band, disp, bands, disps = place[0], place[1], place[2], place[3]
    is_even = band % 2 == 0

    def features(b, s, half):
        rows = slice(half * FEAT_CH, (half + 1) * FEAT_CH)
        pick = 0 if s == 0 else across.shape[0] - 1
        if b == 1:
            return (own[rows] if s == 1 else across[pick, rows]).astype(f32)
        odd = odd_own[rows] if s == 1 else odd_across[pick, rows]
        even = even_own[rows] if s == 1 else even_across[pick, rows]
        odd, even = odd.astype(f32), even.astype(f32)
        return jnp.where(is_even, even, odd) if b == 0 else jnp.where(is_even, odd, even)

    lane = lax.broadcasted_iota(jnp.int32, (TILE, TILE), 1)
    sub = lax.broadcasted_iota(jnp.int32, (TILE, TILE), 0)
    flip = jnp.where(lane + sub == TILE - 1, 1.0, 0.0).astype(bf16)
    has_left = (disp > 0).astype(f32)
    has_right = (disp < disps - 1).astype(f32)
    per_group = FEAT_CH // GROUPS
    channel = lax.broadcasted_iota(jnp.int32, (TILE, FEAT_CH), 1)
    group_masks = [
        (channel >= g * per_group) & (channel < (g + 1) * per_group) for g in range(GROUPS)
    ]
    lane96 = lax.broadcasted_iota(jnp.int32, (FEAT_CH, TILE), 1)
    zero_slab = jnp.zeros((GROUPS, TILE), f32)
    for b in range(3):
        for at in (0, (DISPS + 1) * GROUPS):
            wide[b, pl.ds(at, GROUPS), :] = zero_slab
            extra[b, pl.ds(at, GROUPS), :] = zero_slab

    for b in range(3):
        row = band + b - 1
        row_ok = ((row >= 0) & (row < bands)).astype(f32)
        own_t = (features(b, 1, 0) * row_ok).T
        side = jnp.where(
            lane96 < EDGE,
            features(b, 2, 0) * (has_right * row_ok),
            jnp.where(lane96 >= TILE - EDGE, features(b, 0, 0) * (has_left * row_ok), 0.0),
        )
        side_t = side.T
        flipped = []
        for s, factor in ((2, has_right), (1, None), (0, has_left)):
            part = dot(features(b, s, 1).astype(bf16), flip)
            flipped.append(part if factor is None else part * factor)
        line = jnp.concatenate(flipped, axis=1)
        windows = [
            line[:, 2 * TILE - 32 - 32 * k : 3 * TILE - 32 - 32 * k].astype(bf16)
            for k in range(-1, 5)
        ]
        sheared = [[] for _ in range(GROUPS)]
        for k in range(4):
            rows = own_t[32 * k : 32 * k + 32]
            lhs = jnp.concatenate(
                [jnp.where(m[:32], rows, 0.0) for m in group_masks], axis=0
            ).astype(bf16)
            product = dot(lhs, windows[k + 1])
            for g in range(GROUPS):
                sheared[g].append(
                    pltpu.roll(
                        product[32 * g : 32 * g + 32], TILE - 31, 1, stride=1, stride_axis=0
                    )
                )
        after = side_t[:EDGE]
        before = side_t[TILE - EDGE :]
        lhs_after = jnp.concatenate(
            [jnp.where(m[:EDGE], after, 0.0) for m in group_masks], axis=0
        ).astype(bf16)
        lhs_before = jnp.concatenate(
            [jnp.where(m[:EDGE], before, 0.0) for m in group_masks], axis=0
        ).astype(bf16)
        product_after = dot(lhs_after, windows[5])
        product_before = dot(lhs_before, windows[0])
        gap = jnp.zeros((TILE - 2 * EDGE, TILE), f32)
        for g in range(GROUPS):
            part = jnp.concatenate(sheared[g], axis=0).T * (1.0 / per_group)
            wide[b, pl.ds(GROUPS + g, DISPS, stride=GROUPS), :] = part[:DISPS]
            rows_after = pltpu.roll(
                product_after[EDGE * g : EDGE * g + EDGE], TILE - 31, 1, stride=1, stride_axis=0
            )
            rows_before = pltpu.roll(
                product_before[EDGE * g : EDGE * g + EDGE],
                TILE - 31 + 32 - EDGE,
                1,
                stride=1,
                stride_axis=0,
            )
            part = jnp.concatenate([rows_after, gap, rows_before], axis=0).T * (1.0 / per_group)
            extra[b, pl.ds(GROUPS + g, DISPS, stride=GROUPS), :] = part[:DISPS]

    lane8 = lax.broadcasted_iota(jnp.int32, (OUT_SLAB, TILE), 1)
    group_at = lax.broadcasted_iota(jnp.int32, (GROUPS, TILE), 0)
    gains = jnp.zeros((GROUPS, TILE), f32)
    for g in range(GROUPS):
        gains = jnp.where(group_at == g, gain[g], gains)
    wanted = [jnp.broadcast_to(indices[t : t + 1, :], (GROUPS, TILE)) for t in range(ITERS)]
    found = [jnp.zeros((GROUPS, TILE), f32) for _ in range(ITERS)]
    for q in range(DISPS // BLOCK):
        at = q * OUT_SLAB
        slabs = []
        for b in range(3):
            slabs.append(
                jnp.concatenate(
                    [wide[b, at : at + SLAB, :], extra[b, at : at + SLAB, :]], axis=1
                ).astype(bf16)
            )
        product = dot(taps[...], jnp.concatenate(slabs, axis=0))
        first, middle, last = (
            product[:OUT_SLAB],
            product[OUT_SLAB : 2 * OUT_SLAB],
            product[2 * OUT_SLAB :],
        )
        conv = (
            middle[:, :TILE]
            + jnp.where(
                lane8 == 0,
                pltpu.roll(first[:, TILE:], 1, 1),
                pltpu.roll(first[:, :TILE], 1, 1),
            )
            + jnp.where(
                lane8 == TILE - 1,
                pltpu.roll(last[:, TILE:], TILE - 1, 1),
                pltpu.roll(last[:, :TILE], TILE - 1, 1),
            )
        )
        raw = wide[1, at + GROUPS : at + GROUPS + OUT_SLAB, :].astype(bf16).astype(f32)
        volume = (raw + jnp.maximum(conv, 0.0)).astype(bf16).astype(f32)
        volume = volume.reshape(BLOCK, GROUPS, TILE)
        logit[q * BLOCK : (q + 1) * BLOCK, :] = jnp.sum(volume * gains[None], axis=1)
        for d in range(BLOCK):
            for t in range(ITERS):
                found[t] = found[t] + jnp.where(wanted[t] == q * BLOCK + d, volume[d], 0.0)

    level = lax.broadcasted_iota(jnp.int32, (DISPS, TILE), 0)
    valid = level < limit[...]
    masked = jnp.where(valid, logit[...], floor_logit)
    top = jnp.max(masked, axis=0, keepdims=True)
    weights = jnp.where(valid, jnp.exp(masked - top), 0.0)
    moment = jnp.sum(weights * level.astype(f32), axis=0, keepdims=True)
    start = moment / jnp.sum(weights, axis=0, keepdims=True) / pixel_unit
    high = start.astype(bf16).astype(f32)
    low = (start - high).astype(bf16).astype(f32)
    ends = jnp.where(
        group_at == 0,
        jnp.broadcast_to(high, (GROUPS, TILE)),
        jnp.where(group_at == 1, jnp.broadcast_to(low, (GROUPS, TILE)), 0.0),
    )
    packed = jnp.concatenate(found + [ends], axis=0).astype(bf16)
    for i in range(out.shape[0]):
        out[i] = packed


def refine_kernel(
    place,
    packed_all,
    hidden_all,
    hid_weight,
    in_weight,
    head,
    disparity_out,
    hidden_out,
    packed,
    tiles,
    sides,
    weight,
    lookups,
    taps,
    reset_taps,
    gate,
    inputs,
    level,
    sems,
):
    band, disp, bands, disps = place[0], place[1], place[2], place[3]
    held = packed.shape[1]
    first = jnp.clip(band - REACH, 0, bands - held)
    before, after = jnp.maximum(disp - 1, 0), jnp.minimum(disp + 1, disps - 1)
    rows = pl.ds(first, held)
    hidden_copies = [
        pltpu.make_async_copy(hidden_all.at[rows, pl.ds(0, TILE)], tiles, sems.at[0]),
        pltpu.make_async_copy(hidden_all.at[rows, pl.ds(TILE, 16)], sides.at[0], sems.at[1]),
        pltpu.make_async_copy(
            hidden_all.at[rows, pl.ds(hidden_all.shape[1] - 16, 16)], sides.at[1], sems.at[2]
        ),
    ]
    packed_copies = [
        pltpu.make_async_copy(packed_all.at[rows, column], packed.at[s], sems.at[3 + s])
        for s, column in enumerate((before, disp, after))
    ]
    weight_copies = [
        pltpu.make_async_copy(hid_weight, weight.at[pl.ds(0, 9 * HID_CH)], sems.at[6]),
        pltpu.make_async_copy(in_weight, weight.at[pl.ds(9 * HID_CH, HID_CH)], sems.at[7]),
    ]
    for copy in packed_copies + hidden_copies + weight_copies:
        copy.start()

    has_left = (disp > 0).astype(f32)
    has_right = (disp < disps - 1).astype(f32)
    held_at, row_ok = [], []
    for r in range(ROWS):
        row = band - REACH + r
        held_at.append(jnp.clip(row, 0, bands - 1) - first)
        row_ok.append(((row >= 0) & (row < bands)).astype(f32))
    column = lax.broadcasted_iota(jnp.int32, (SPAN, HID_CH), 0)
    column_ok = jnp.where(
        column < EDGE, has_left, jnp.where(column >= TILE + EDGE, has_right, 1.0)
    )
    lane = lax.broadcasted_iota(jnp.int32, (SPAN, HID_CH), 1)
    lane_tap = lane - 9 * GROUPS
    at_sub = lax.broadcasted_iota(jnp.int32, (SPAN, 2 * TILE), 0)
    at_lane = lax.broadcasted_iota(jnp.int32, (SPAN, 2 * TILE), 1)
    spread = jnp.where(
        ((at_sub >= EDGE) & (at_lane == at_sub - EDGE))
        | ((at_sub < EDGE) & (at_lane == at_sub - EDGE + 2 * TILE)),
        1.0,
        0.0,
    ).astype(bf16)
    lane_pack = lax.broadcasted_iota(jnp.int32, (PACK, TILE), 1)

    for copy in packed_copies:
        copy.wait()

    shifted = []
    for r in range(ROWS):
        centre = packed[1, held_at[r]].astype(f32) * row_ok[r]
        halo = jnp.where(
            lane_pack < TILE // 2,
            packed[2, held_at[r]].astype(f32) * (row_ok[r] * has_right),
            packed[0, held_at[r]].astype(f32) * (row_ok[r] * has_left),
        )
        both = jnp.concatenate([centre, halo], axis=1)
        shifted.append((pltpu.roll(both, 1, 1), both, pltpu.roll(both, 2 * TILE - 1, 1)))
    fill = jnp.zeros((HID_CH - 9 * GROUPS, 2 * TILE), f32)
    base = 0
    look_at = []
    for t in range(ITERS):
        low, high = 1 + 2 * t, ROWS - 2 - 2 * t
        look_at.append((base, low))
        for r in range(low, high + 1):
            pieces = []
            for a in range(3):
                for b in range(3):
                    pieces.append(shifted[r + a - 1][b][t * GROUPS : (t + 1) * GROUPS])
            line = jnp.concatenate(pieces + [fill], axis=0).astype(bf16)
            lookups[base + r - low] = dot_nt(spread, line)
        base += high - low + 1
    for r in range(ROWS):
        ends = shifted[r][1][3 * GROUPS : 4 * GROUPS]
        wide_high = jnp.broadcast_to(ends[0:1], (HID_CH, 2 * TILE)).astype(bf16)
        wide_low = jnp.broadcast_to(ends[1:2], (HID_CH, 2 * TILE)).astype(bf16)
        level[r * SPAN : (r + 1) * SPAN, :] = dot_nt(spread, wide_high) + dot_nt(spread, wide_low)

    for copy in hidden_copies + weight_copies:
        copy.wait()

    def keep(target, at, values):
        length = values.shape[0]
        target[at : at + length, 0:HID_CH] = pltpu.roll(values, 1, 0).astype(bf16)
        target[at : at + length, HID_CH : 2 * HID_CH] = values.astype(bf16)
        target[at : at + length, 2 * HID_CH :] = pltpu.roll(values, length - 1, 0).astype(bf16)

    for r in range(ROWS):
        values = jnp.concatenate(
            [
                sides[0, held_at[r]].astype(f32)[16 - EDGE :],
                tiles[held_at[r]].astype(f32),
                sides[1, held_at[r]].astype(f32)[:EDGE],
            ],
            axis=0,
        )
        keep(taps, r * SPAN, values * (column_ok * row_ok[r]))

    def chunks(low, high, most):
        count = high - low + 1
        parts = -(-count // most)
        out = []
        for i in range(parts):
            size = count // parts + (1 if i < count % parts else 0)
            out.append((low, size))
            low += size
        return out

    for t in range(ITERS):
        low, high = 1 + 2 * t, ROWS - 2 - 2 * t
        spread_level = {}
        for r in range(low - 1, high + 2):
            value = level[r * SPAN : (r + 1) * SPAN, :] * feature_scale
            which = lane_tap % 3
            spread_level[r] = jnp.where(
                which == 0,
                pltpu.roll(value, 1, 0),
                jnp.where(which == 1, value, pltpu.roll(value, SPAN - 1, 0)),
            )
        for r in range(low, high + 1):
            base, from_row = look_at[t]
            value = lookups[base + r - from_row]
            for a in range(3):
                value = jnp.where(
                    (lane_tap >= 3 * a) & (lane_tap < 3 * a + 3), spread_level[r + a - 1], value
                )
            inputs[r * SPAN : (r + 1) * SPAN, :] = value.astype(bf16)

        for r, count in chunks(low, high, 4):
            at, length = r * SPAN, count * SPAN
            lhs = jnp.concatenate(
                [taps[at + (a - 1) * SPAN : at + (a - 1) * SPAN + length, :] for a in range(3)]
                + [inputs[at : at + length, :]],
                axis=1,
            )
            both = dot(lhs, weight[:, : 2 * HID_CH])
            both = 0.5 * jnp.tanh(0.5 * both) + 0.5
            hidden = taps[at : at + length, HID_CH : 2 * HID_CH].astype(f32)
            gate[at : at + length, :] = both[:, :HID_CH]
            keep(reset_taps, at, both[:, HID_CH:] * hidden)
        for r, count in chunks(low + 1, high - 1, 4):
            at, length = r * SPAN, count * SPAN
            lhs = jnp.concatenate(
                [
                    reset_taps[at + (a - 1) * SPAN : at + (a - 1) * SPAN + length, :]
                    for a in range(3)
                ]
                + [inputs[at : at + length, :]],
                axis=1,
            )
            candidate = jnp.tanh(dot(lhs, weight[:, 2 * HID_CH :]))
            update = gate[at : at + length, :]
            hidden = taps[at : at + length, HID_CH : 2 * HID_CH].astype(f32)
            hidden = (1.0 - update) * hidden + update * candidate
            mask = jnp.concatenate([column_ok * row_ok[r + i] for i in range(count)], axis=0)
            hidden = (hidden * mask).astype(bf16)
            level[at : at + length, :] += dot(hidden, head[...])
            if t < ITERS - 1:
                keep(taps, at, hidden.astype(f32))
            else:
                hidden_out[0] = hidden.astype(f32)[EDGE : EDGE + TILE].astype(bf16)
    at = REACH * SPAN + EDGE
    disparity_out[...] = level[at : at + TILE, :].T[0:1]


def to_sides(value, edges, shift):
    bands, disps = lax.axis_size("band"), lax.axis_size("disp")
    pairs = [(i, shift(i)) for i in range(bands) if 0 <= shift(i) < bands]

    def moved(step):
        return [
            (i * disps + d, j * disps + d + step)
            for i, j in pairs
            for d in range(disps)
            if 0 <= d + step < disps
        ]

    if disps == 2:
        perm = moved(1) + moved(-1)
        piece = value if edges is None else jnp.where(lax.axis_index("disp") == 0, *edges)
        return lax.ppermute(piece, ("band", "disp"), perm)[None]
    last, initial = (value, value) if edges is None else edges
    return jnp.stack(
        [
            lax.ppermute(last, ("band", "disp"), moved(1)),
            lax.ppermute(initial, ("band", "disp"), moved(-1)),
        ]
    )


def to_rows(value, shift):
    bands = lax.axis_size("band")
    return lax.ppermute(
        value, "band", [(i, shift(i)) for i in range(bands) if 0 <= shift(i) < bands]
    )


def same(i):
    return i


def odd_pair(i):
    return i ^ 1


def even_pair(i):
    return i - 1 if i % 2 == 0 else i + 1


def local(
    feat_left,
    feat_right,
    limit,
    indices,
    hidden_start,
    vol_kernel,
    group_gain,
    hid_kernel,
    in_kernel,
    head_weight,
):
    bands, disps = lax.axis_size("band"), lax.axis_size("disp")
    axes = ("band", "disp")
    place = jnp.stack(
        [lax.axis_index("band"), lax.axis_index("disp"), jnp.int32(bands), jnp.int32(disps)]
    ).astype(jnp.int32)
    hidden = hidden_start[0]
    hidden_side = to_sides(None, (hidden[TILE - 16 :], hidden[:16]), same)
    feats = jnp.concatenate([feat_left[0], feat_right[0]], axis=0)
    across = to_sides(feats, None, same)
    odd_own, odd_across = to_rows(feats, odd_pair), to_sides(feats, None, odd_pair)
    even_own, even_across = to_rows(feats, even_pair), to_sides(feats, None, even_pair)
    hidden_all = lax.all_gather(
        jnp.concatenate([hidden, hidden_side.reshape(-1, HID_CH)], axis=0), "band"
    )

    shift = jnp.arange(BLOCK + 2)[None, :] - jnp.arange(BLOCK)[:, None]
    pick = (shift[:, :, None] == jnp.arange(3)).astype(bf16)
    taps = jnp.einsum("dxa,abeio->edobxi", pick, vol_kernel, preferred_element_type=f32)
    taps = taps.astype(bf16).reshape(3 * OUT_SLAB, 3 * SLAB)
    in_weight = jnp.concatenate(
        [
            in_kernel[:, :, :GROUPS].reshape(9 * GROUPS, 3 * HID_CH),
            in_kernel[:, :, GROUPS].reshape(9, 3 * HID_CH),
            jnp.zeros((HID_CH - 9 * (GROUPS + 1), 3 * HID_CH), bf16),
        ],
        axis=0,
    )
    head = jnp.broadcast_to(head_weight, (HID_CH, HID_CH))

    smem = pl.BlockSpec(memory_space=pltpu.SMEM)
    vmem = pl.BlockSpec(memory_space=pltpu.VMEM)
    anywhere = pl.BlockSpec(memory_space=pl.ANY)
    padded = (DISPS + 2) * GROUPS
    packed = pl.pallas_call(
        volume_kernel,
        out_shape=jax.ShapeDtypeStruct((bands * disps, PACK, TILE), bf16),
        in_specs=[smem, smem] + [vmem] * 9,
        out_specs=vmem,
        scratch_shapes=[
            pltpu.VMEM((3, padded, TILE), f32),
            pltpu.VMEM((3, padded, TILE), f32),
            pltpu.VMEM((DISPS, TILE), f32),
        ],
        compiler_params=pltpu.CompilerParams(vmem_limit_bytes=32 * 2**20),
    )(
        place, group_gain, feats, across, odd_own, odd_across, even_own, even_across,
        limit, indices[:, 0], taps,
    )

    packed_all = lax.all_to_all(packed, axes, 0, 0, tiled=True)
    packed_all = packed_all.reshape(bands, disps, PACK, TILE)
    held = min(ROWS, bands)
    area = ROWS * SPAN
    looked = sum(ROWS - 2 - 4 * t for t in range(ITERS))
    disparity, hidden = pl.pallas_call(
        refine_kernel,
        out_shape=(
            jax.ShapeDtypeStruct((1, TILE), f32),
            jax.ShapeDtypeStruct((1, TILE, HID_CH), bf16),
        ),
        in_specs=[smem, anywhere, anywhere, anywhere, anywhere, vmem],
        out_specs=(vmem, vmem),
        scratch_shapes=[
            pltpu.VMEM((3, held, PACK, TILE), bf16),
            pltpu.VMEM((held, TILE, HID_CH), bf16),
            pltpu.VMEM((2, held, 16, HID_CH), bf16),
            pltpu.VMEM((10 * HID_CH, 3 * HID_CH), bf16),
            pltpu.VMEM((looked, SPAN, HID_CH), f32),
            pltpu.VMEM((area, 3 * HID_CH), bf16),
            pltpu.VMEM((area, 3 * HID_CH), bf16),
            pltpu.VMEM((area, HID_CH), f32),
            pltpu.VMEM((area, HID_CH), bf16),
            pltpu.VMEM((area, HID_CH), f32),
            pltpu.SemaphoreType.DMA((8,)),
        ],
        compiler_params=pltpu.CompilerParams(vmem_limit_bytes=40 * 2**20),
    )(place, packed_all, hidden_all, hid_kernel.reshape(9 * HID_CH, 3 * HID_CH), in_weight, head)
    return (disparity, hidden)


def solution(mesh):
    in_specs = (
        P("band", None, "disp"),
        P("band", None, "disp"),
        P("band", "disp"),
        P(None, "band", "disp"),
        P("band", "disp", None),
        P(),
        P(),
        P(),
        P(),
        P(),
    )
    out_specs = (P("band", "disp"), P("band", "disp", None))
    return jax.shard_map(local, mesh=mesh, in_specs=in_specs, out_specs=out_specs, check_vma=False)
```

```python
import jax
import jax.numpy as jnp
from jax import lax
from jax.experimental import pallas as pl
from jax.experimental.pallas import tpu as pltpu
from jax.sharding import PartitionSpec as P

GROUPS = 8
DISPS = 96
FEAT_CH = 96
HID_CH = 128
ITERS = 3
TILE = 128
REACH = 2 * ITERS
EDGE = 8
SPAN = TILE + 2 * EDGE
ROWS = 2 * REACH + 1
PACK = 32
BLOCK = 8
SLAB = (BLOCK + 2) * GROUPS
OUT_SLAB = BLOCK * GROUPS

pixel_unit = 8.0
feature_scale = 0.25
floor_logit = -1e30

f32 = jnp.float32
bf16 = jnp.bfloat16


def dot(a, b):
    return jnp.dot(a, b, preferred_element_type=f32)


def dot_nt(a, b):
    return lax.dot_general(a, b, (((1,), (1,)), ((), ())), preferred_element_type=f32)


def copy_all(copies):
    for copy in copies:
        copy.start()
    for copy in copies:
        copy.wait()


def toeplitz(vol_kernel):
    size = 27 * GROUPS
    flat = vol_kernel[...].astype(f32).reshape(size, GROUPS)
    flat = jnp.concatenate([flat, jnp.zeros((size, TILE - GROUPS), f32)], axis=1).T[:GROUPS]
    row = lax.broadcasted_iota(jnp.int32, (9 * GROUPS, size), 0) >> 3
    tap = lax.broadcasted_iota(jnp.int32, (9 * GROUPS, size), 1) >> 3
    tap_a = (tap >= 9).astype(jnp.int32) + (tap >= 18).astype(jnp.int32)
    within = tap - 9 * tap_a
    tap_b = (within >= 3).astype(jnp.int32) + (within >= 6).astype(jnp.int32)
    tap_e = within - 3 * tap_b
    pairs = jnp.where(
        row == 3 * tap_a + tap_e, jnp.concatenate([flat] * 9, axis=0), 0.0
    ).astype(bf16)
    from_row = lax.broadcasted_iota(jnp.int32, (size, 3 * SLAB), 0)
    to = lax.broadcasted_iota(jnp.int32, (size, 3 * SLAB), 1)
    from_tap = from_row >> 3
    from_in = from_tap - 9 * ((from_tap >= 9).astype(jnp.int32) + (from_tap >= 18).astype(jnp.int32))
    from_b = (from_in >= 3).astype(jnp.int32) + (from_in >= 6).astype(jnp.int32)
    to_b = (to >= SLAB).astype(jnp.int32) + (to >= 2 * SLAB).astype(jnp.int32)
    repeat = jnp.where((from_b == to_b) & ((from_row & 7) == (to & 7)), 1.0, 0.0).astype(bf16)
    spread = dot(pairs, repeat)
    to = lax.broadcasted_iota(jnp.int32, (GROUPS, 3 * SLAB), 1)
    to_b = (to >= SLAB).astype(jnp.int32) + (to >= 2 * SLAB).astype(jnp.int32)
    to_d = (to - SLAB * to_b) >> 3
    rows = []
    for e in range(3):
        for d in range(BLOCK):
            value = jnp.zeros((GROUPS, 3 * SLAB), f32)
            for a in range(3):
                at = (3 * a + e) * GROUPS
                value = jnp.where(to_d == d + a, spread[at : at + GROUPS], value)
            rows.append(value)
    return jnp.concatenate(rows, axis=0).astype(bf16)


def volume_kernel(
    place, gain, own, across, odd_own, odd_across, even_own, even_across, limit, indices, vol_kernel,
    out, wide, extra, logit,
):
    band, disp, bands, disps = place[0], place[1], place[2], place[3]
    is_even = band % 2 == 0

    def features(b, s, half):
        rows = slice(half * FEAT_CH, (half + 1) * FEAT_CH)
        pick = 0 if s == 0 else across.shape[0] - 1
        if b == 1:
            return (own[rows] if s == 1 else across[pick, rows]).astype(f32)
        odd = odd_own[rows] if s == 1 else odd_across[pick, rows]
        even = even_own[rows] if s == 1 else even_across[pick, rows]
        odd, even = odd.astype(f32), even.astype(f32)
        return jnp.where(is_even, even, odd) if b == 0 else jnp.where(is_even, odd, even)

    lane = lax.broadcasted_iota(jnp.int32, (TILE, TILE), 1)
    sub = lax.broadcasted_iota(jnp.int32, (TILE, TILE), 0)
    flip = jnp.where(lane + sub == TILE - 1, 1.0, 0.0).astype(bf16)
    has_left = (disp > 0).astype(f32)
    has_right = (disp < disps - 1).astype(f32)
    per_group = FEAT_CH // GROUPS
    channel = lax.broadcasted_iota(jnp.int32, (TILE, FEAT_CH), 1)
    group_masks = [
        (channel >= g * per_group) & (channel < (g + 1) * per_group) for g in range(GROUPS)
    ]
    lane96 = lax.broadcasted_iota(jnp.int32, (FEAT_CH, TILE), 1)
    zero_slab = jnp.zeros((GROUPS, TILE), f32)
    for b in range(3):
        for at in (0, (DISPS + 1) * GROUPS):
            wide[b, pl.ds(at, GROUPS), :] = zero_slab
            extra[b, pl.ds(at, GROUPS), :] = zero_slab

    for b in range(3):
        row = band + b - 1
        row_ok = ((row >= 0) & (row < bands)).astype(f32)
        own_t = (features(b, 1, 0) * row_ok).T
        side = jnp.where(
            lane96 < EDGE,
            features(b, 2, 0) * (has_right * row_ok),
            jnp.where(lane96 >= TILE - EDGE, features(b, 0, 0) * (has_left * row_ok), 0.0),
        )
        side_t = side.T
        flipped = []
        for s, factor in ((2, has_right), (1, None), (0, has_left)):
            part = dot(features(b, s, 1).astype(bf16), flip)
            flipped.append(part if factor is None else part * factor)
        line = jnp.concatenate(flipped, axis=1)
        windows = [
            line[:, 2 * TILE - 32 - 32 * k : 3 * TILE - 32 - 32 * k].astype(bf16)
            for k in range(-1, 5)
        ]
        sheared = [[] for _ in range(GROUPS)]
        for k in range(4):
            rows = own_t[32 * k : 32 * k + 32]
            lhs = jnp.concatenate(
                [jnp.where(m[:32], rows, 0.0) for m in group_masks], axis=0
            ).astype(bf16)
            product = dot(lhs, windows[k + 1])
            for g in range(GROUPS):
                sheared[g].append(
                    pltpu.roll(
                        product[32 * g : 32 * g + 32], TILE - 31, 1, stride=1, stride_axis=0
                    )
                )
        after = side_t[:EDGE]
        before = side_t[TILE - EDGE :]
        lhs_after = jnp.concatenate(
            [jnp.where(m[:EDGE], after, 0.0) for m in group_masks], axis=0
        ).astype(bf16)
        lhs_before = jnp.concatenate(
            [jnp.where(m[:EDGE], before, 0.0) for m in group_masks], axis=0
        ).astype(bf16)
        product_after = dot(lhs_after, windows[5])
        product_before = dot(lhs_before, windows[0])
        gap = jnp.zeros((TILE - 2 * EDGE, TILE), f32)
        for g in range(GROUPS):
            part = jnp.concatenate(sheared[g], axis=0).T * (1.0 / per_group)
            wide[b, pl.ds(GROUPS + g, DISPS, stride=GROUPS), :] = part[:DISPS]
            rows_after = pltpu.roll(
                product_after[EDGE * g : EDGE * g + EDGE], TILE - 31, 1, stride=1, stride_axis=0
            )
            rows_before = pltpu.roll(
                product_before[EDGE * g : EDGE * g + EDGE],
                TILE - 31 + 32 - EDGE,
                1,
                stride=1,
                stride_axis=0,
            )
            part = jnp.concatenate([rows_after, gap, rows_before], axis=0).T * (1.0 / per_group)
            extra[b, pl.ds(GROUPS + g, DISPS, stride=GROUPS), :] = part[:DISPS]

    taps = toeplitz(vol_kernel)
    lane8 = lax.broadcasted_iota(jnp.int32, (OUT_SLAB, TILE), 1)
    group_at = lax.broadcasted_iota(jnp.int32, (GROUPS, TILE), 0)
    gains = jnp.zeros((GROUPS, TILE), f32)
    for g in range(GROUPS):
        gains = jnp.where(group_at == g, gain[g], gains)
    wanted = [jnp.broadcast_to(indices[t : t + 1, :], (GROUPS, TILE)) for t in range(ITERS)]
    found = [jnp.zeros((GROUPS, TILE), f32) for _ in range(ITERS)]
    for q in range(DISPS // BLOCK):
        at = q * OUT_SLAB
        slabs = []
        for b in range(3):
            slabs.append(
                jnp.concatenate(
                    [wide[b, at : at + SLAB, :], extra[b, at : at + SLAB, :]], axis=1
                ).astype(bf16)
            )
        product = dot(taps, jnp.concatenate(slabs, axis=0))
        first, middle, last = (
            product[:OUT_SLAB],
            product[OUT_SLAB : 2 * OUT_SLAB],
            product[2 * OUT_SLAB :],
        )
        conv = (
            middle[:, :TILE]
            + jnp.where(
                lane8 == 0,
                pltpu.roll(first[:, TILE:], 1, 1),
                pltpu.roll(first[:, :TILE], 1, 1),
            )
            + jnp.where(
                lane8 == TILE - 1,
                pltpu.roll(last[:, TILE:], TILE - 1, 1),
                pltpu.roll(last[:, :TILE], TILE - 1, 1),
            )
        )
        raw = wide[1, at + GROUPS : at + GROUPS + OUT_SLAB, :].astype(bf16).astype(f32)
        volume = (raw + jnp.maximum(conv, 0.0)).astype(bf16).astype(f32)
        volume = volume.reshape(BLOCK, GROUPS, TILE)
        logit[q * BLOCK : (q + 1) * BLOCK, :] = jnp.sum(volume * gains[None], axis=1)
        for d in range(BLOCK):
            for t in range(ITERS):
                found[t] = found[t] + jnp.where(wanted[t] == q * BLOCK + d, volume[d], 0.0)

    level = lax.broadcasted_iota(jnp.int32, (DISPS, TILE), 0)
    valid = level < limit[...]
    masked = jnp.where(valid, logit[...], floor_logit)
    top = jnp.max(masked, axis=0, keepdims=True)
    weights = jnp.where(valid, jnp.exp(masked - top), 0.0)
    moment = jnp.sum(weights * level.astype(f32), axis=0, keepdims=True)
    start = moment / jnp.sum(weights, axis=0, keepdims=True) / pixel_unit
    high = start.astype(bf16).astype(f32)
    low = (start - high).astype(bf16).astype(f32)
    ends = jnp.where(
        group_at == 0,
        jnp.broadcast_to(high, (GROUPS, TILE)),
        jnp.where(group_at == 1, jnp.broadcast_to(low, (GROUPS, TILE)), 0.0),
    )
    packed = jnp.concatenate(found + [ends], axis=0).astype(bf16)
    for i in range(out.shape[0]):
        out[i] = packed


def refine_kernel(
    place,
    packed_all,
    hidden_all,
    hid_weight,
    in_weight,
    head,
    disparity_out,
    hidden_out,
    packed,
    tiles,
    sides,
    weight,
    lookups,
    taps,
    reset_taps,
    gate,
    inputs,
    level,
    sems,
):
    band, disp, bands, disps = place[0], place[1], place[2], place[3]
    held = packed.shape[1]
    first = jnp.clip(band - REACH, 0, bands - held)
    before, after = jnp.maximum(disp - 1, 0), jnp.minimum(disp + 1, disps - 1)
    rows = pl.ds(first, held)
    hidden_copies = [
        pltpu.make_async_copy(hidden_all.at[rows, pl.ds(0, TILE)], tiles, sems.at[0]),
        pltpu.make_async_copy(hidden_all.at[rows, pl.ds(TILE, 16)], sides.at[0], sems.at[1]),
        pltpu.make_async_copy(
            hidden_all.at[rows, pl.ds(hidden_all.shape[1] - 16, 16)], sides.at[1], sems.at[2]
        ),
    ]
    packed_copies = [
        pltpu.make_async_copy(packed_all.at[rows, column], packed.at[s], sems.at[3 + s])
        for s, column in enumerate((before, disp, after))
    ]
    weight_copies = [
        pltpu.make_async_copy(hid_weight, weight.at[pl.ds(0, 9 * HID_CH)], sems.at[6]),
        pltpu.make_async_copy(in_weight, weight.at[pl.ds(9 * HID_CH, HID_CH)], sems.at[7]),
    ]
    for copy in packed_copies + hidden_copies + weight_copies:
        copy.start()

    has_left = (disp > 0).astype(f32)
    has_right = (disp < disps - 1).astype(f32)
    held_at, row_ok = [], []
    for r in range(ROWS):
        row = band - REACH + r
        held_at.append(jnp.clip(row, 0, bands - 1) - first)
        row_ok.append(((row >= 0) & (row < bands)).astype(f32))
    column = lax.broadcasted_iota(jnp.int32, (SPAN, HID_CH), 0)
    column_ok = jnp.where(
        column < EDGE, has_left, jnp.where(column >= TILE + EDGE, has_right, 1.0)
    )
    lane = lax.broadcasted_iota(jnp.int32, (SPAN, HID_CH), 1)
    lane_tap = lane - 9 * GROUPS
    at_sub = lax.broadcasted_iota(jnp.int32, (SPAN, 2 * TILE), 0)
    at_lane = lax.broadcasted_iota(jnp.int32, (SPAN, 2 * TILE), 1)
    spread = jnp.where(
        ((at_sub >= EDGE) & (at_lane == at_sub - EDGE))
        | ((at_sub < EDGE) & (at_lane == at_sub - EDGE + 2 * TILE)),
        1.0,
        0.0,
    ).astype(bf16)
    lane_pack = lax.broadcasted_iota(jnp.int32, (PACK, TILE), 1)

    for copy in packed_copies:
        copy.wait()

    shifted = []
    for r in range(ROWS):
        centre = packed[1, held_at[r]].astype(f32) * row_ok[r]
        halo = jnp.where(
            lane_pack < TILE // 2,
            packed[2, held_at[r]].astype(f32) * (row_ok[r] * has_right),
            packed[0, held_at[r]].astype(f32) * (row_ok[r] * has_left),
        )
        both = jnp.concatenate([centre, halo], axis=1)
        shifted.append((pltpu.roll(both, 1, 1), both, pltpu.roll(both, 2 * TILE - 1, 1)))
    fill = jnp.zeros((HID_CH - 9 * GROUPS, 2 * TILE), f32)
    base = 0
    look_at = []
    for t in range(ITERS):
        low, high = 1 + 2 * t, ROWS - 2 - 2 * t
        look_at.append((base, low))
        for r in range(low, high + 1):
            pieces = []
            for a in range(3):
                for b in range(3):
                    pieces.append(shifted[r + a - 1][b][t * GROUPS : (t + 1) * GROUPS])
            line = jnp.concatenate(pieces + [fill], axis=0).astype(bf16)
            lookups[base + r - low] = dot_nt(spread, line)
        base += high - low + 1
    for r in range(ROWS):
        ends = shifted[r][1][3 * GROUPS : 4 * GROUPS]
        wide_high = jnp.broadcast_to(ends[0:1], (HID_CH, 2 * TILE)).astype(bf16)
        wide_low = jnp.broadcast_to(ends[1:2], (HID_CH, 2 * TILE)).astype(bf16)
        level[r * SPAN : (r + 1) * SPAN, :] = dot_nt(spread, wide_high) + dot_nt(spread, wide_low)

    for copy in hidden_copies + weight_copies:
        copy.wait()

    def keep(target, at, values):
        length = values.shape[0]
        target[at : at + length, 0:HID_CH] = pltpu.roll(values, 1, 0).astype(bf16)
        target[at : at + length, HID_CH : 2 * HID_CH] = values.astype(bf16)
        target[at : at + length, 2 * HID_CH :] = pltpu.roll(values, length - 1, 0).astype(bf16)

    for r in range(ROWS):
        values = jnp.concatenate(
            [
                sides[0, held_at[r]].astype(f32)[16 - EDGE :],
                tiles[held_at[r]].astype(f32),
                sides[1, held_at[r]].astype(f32)[:EDGE],
            ],
            axis=0,
        )
        keep(taps, r * SPAN, values * (column_ok * row_ok[r]))

    def chunks(low, high, most):
        count = high - low + 1
        parts = -(-count // most)
        out = []
        for i in range(parts):
            size = count // parts + (1 if i < count % parts else 0)
            out.append((low, size))
            low += size
        return out

    for t in range(ITERS):
        low, high = 1 + 2 * t, ROWS - 2 - 2 * t
        spread_level = {}
        for r in range(low - 1, high + 2):
            value = level[r * SPAN : (r + 1) * SPAN, :] * feature_scale
            which = lane_tap % 3
            spread_level[r] = jnp.where(
                which == 0,
                pltpu.roll(value, 1, 0),
                jnp.where(which == 1, value, pltpu.roll(value, SPAN - 1, 0)),
            )
        for r in range(low, high + 1):
            base, from_row = look_at[t]
            value = lookups[base + r - from_row]
            for a in range(3):
                value = jnp.where(
                    (lane_tap >= 3 * a) & (lane_tap < 3 * a + 3), spread_level[r + a - 1], value
                )
            inputs[r * SPAN : (r + 1) * SPAN, :] = value.astype(bf16)

        for r, count in chunks(low, high, 4):
            at, length = r * SPAN, count * SPAN
            lhs = jnp.concatenate(
                [taps[at + (a - 1) * SPAN : at + (a - 1) * SPAN + length, :] for a in range(3)]
                + [inputs[at : at + length, :]],
                axis=1,
            )
            both = dot(lhs, weight[:, : 2 * HID_CH])
            both = 0.5 * jnp.tanh(0.5 * both) + 0.5
            hidden = taps[at : at + length, HID_CH : 2 * HID_CH].astype(f32)
            gate[at : at + length, :] = both[:, :HID_CH]
            keep(reset_taps, at, both[:, HID_CH:] * hidden)
        for r, count in chunks(low + 1, high - 1, 4):
            at, length = r * SPAN, count * SPAN
            lhs = jnp.concatenate(
                [
                    reset_taps[at + (a - 1) * SPAN : at + (a - 1) * SPAN + length, :]
                    for a in range(3)
                ]
                + [inputs[at : at + length, :]],
                axis=1,
            )
            candidate = jnp.tanh(dot(lhs, weight[:, 2 * HID_CH :]))
            update = gate[at : at + length, :]
            hidden = taps[at : at + length, HID_CH : 2 * HID_CH].astype(f32)
            hidden = (1.0 - update) * hidden + update * candidate
            mask = jnp.concatenate([column_ok * row_ok[r + i] for i in range(count)], axis=0)
            hidden = (hidden * mask).astype(bf16)
            level[at : at + length, :] += dot(hidden, head[...])
            if t < ITERS - 1:
                keep(taps, at, hidden.astype(f32))
            else:
                hidden_out[0] = hidden.astype(f32)[EDGE : EDGE + TILE].astype(bf16)
    at = REACH * SPAN + EDGE
    disparity_out[...] = level[at : at + TILE, :].T[0:1]


def to_sides(value, edges, shift):
    bands, disps = lax.axis_size("band"), lax.axis_size("disp")
    pairs = [(i, shift(i)) for i in range(bands) if 0 <= shift(i) < bands]

    def moved(step):
        return [
            (i * disps + d, j * disps + d + step)
            for i, j in pairs
            for d in range(disps)
            if 0 <= d + step < disps
        ]

    if disps == 2:
        perm = moved(1) + moved(-1)
        piece = value if edges is None else jnp.where(lax.axis_index("disp") == 0, *edges)
        return lax.ppermute(piece, ("band", "disp"), perm)[None]
    last, initial = (value, value) if edges is None else edges
    return jnp.stack(
        [
            lax.ppermute(last, ("band", "disp"), moved(1)),
            lax.ppermute(initial, ("band", "disp"), moved(-1)),
        ]
    )


def to_rows(value, shift):
    bands = lax.axis_size("band")
    return lax.ppermute(
        value, "band", [(i, shift(i)) for i in range(bands) if 0 <= shift(i) < bands]
    )


def same(i):
    return i


def odd_pair(i):
    return i ^ 1


def even_pair(i):
    return i - 1 if i % 2 == 0 else i + 1


def local(
    feat_left,
    feat_right,
    limit,
    indices,
    hidden_start,
    vol_kernel,
    group_gain,
    hid_kernel,
    in_kernel,
    head_weight,
):
    bands, disps = lax.axis_size("band"), lax.axis_size("disp")
    axes = ("band", "disp")
    place = jnp.stack(
        [lax.axis_index("band"), lax.axis_index("disp"), jnp.int32(bands), jnp.int32(disps)]
    ).astype(jnp.int32)
    hidden = hidden_start[0]
    hidden_side = to_sides(None, (hidden[TILE - 16 :], hidden[:16]), same)
    feats = jnp.concatenate([feat_left[0], feat_right[0]], axis=0)
    across = to_sides(feats, None, same)
    odd_own, odd_across = to_rows(feats, odd_pair), to_sides(feats, None, odd_pair)
    even_own, even_across = to_rows(feats, even_pair), to_sides(feats, None, even_pair)
    hidden_wide = jnp.concatenate([hidden, hidden_side.reshape(-1, HID_CH)], axis=0)
    hidden_all = lax.all_to_all(
        jnp.broadcast_to(hidden_wide, (bands,) + hidden_wide.shape), "band", 0, 0, tiled=True
    )

    in_weight = jnp.concatenate(
        [
            in_kernel[:, :, :GROUPS].reshape(9 * GROUPS, 3 * HID_CH),
            in_kernel[:, :, GROUPS].reshape(9, 3 * HID_CH),
            jnp.zeros((HID_CH - 9 * (GROUPS + 1), 3 * HID_CH), bf16),
        ],
        axis=0,
    )
    head = jnp.broadcast_to(head_weight, (HID_CH, HID_CH))

    smem = pl.BlockSpec(memory_space=pltpu.SMEM)
    vmem = pl.BlockSpec(memory_space=pltpu.VMEM)
    anywhere = pl.BlockSpec(memory_space=pl.ANY)
    padded = (DISPS + 2) * GROUPS
    packed = pl.pallas_call(
        volume_kernel,
        out_shape=jax.ShapeDtypeStruct((bands * disps, PACK, TILE), bf16),
        in_specs=[smem, smem] + [vmem] * 9,
        out_specs=vmem,
        scratch_shapes=[
            pltpu.VMEM((3, padded, TILE), f32),
            pltpu.VMEM((3, padded, TILE), f32),
            pltpu.VMEM((DISPS, TILE), f32),
        ],
        compiler_params=pltpu.CompilerParams(vmem_limit_bytes=32 * 2**20),
    )(
        place, group_gain, feats, across, odd_own, odd_across, even_own, even_across,
        limit, indices[:, 0], vol_kernel.reshape(27, GROUPS, GROUPS),
    )

    packed_all = lax.all_to_all(packed, axes, 0, 0, tiled=True)
    packed_all = packed_all.reshape(bands, disps, PACK, TILE)
    held = min(ROWS, bands)
    area = ROWS * SPAN
    looked = sum(ROWS - 2 - 4 * t for t in range(ITERS))
    disparity, hidden = pl.pallas_call(
        refine_kernel,
        out_shape=(
            jax.ShapeDtypeStruct((1, TILE), f32),
            jax.ShapeDtypeStruct((1, TILE, HID_CH), bf16),
        ),
        in_specs=[smem, anywhere, anywhere, anywhere, anywhere, vmem],
        out_specs=(vmem, vmem),
        scratch_shapes=[
            pltpu.VMEM((3, held, PACK, TILE), bf16),
            pltpu.VMEM((held, TILE, HID_CH), bf16),
            pltpu.VMEM((2, held, 16, HID_CH), bf16),
            pltpu.VMEM((10 * HID_CH, 3 * HID_CH), bf16),
            pltpu.VMEM((looked, SPAN, HID_CH), f32),
            pltpu.VMEM((area, 3 * HID_CH), bf16),
            pltpu.VMEM((area, 3 * HID_CH), bf16),
            pltpu.VMEM((area, HID_CH), f32),
            pltpu.VMEM((area, HID_CH), bf16),
            pltpu.VMEM((area, HID_CH), f32),
            pltpu.SemaphoreType.DMA((8,)),
        ],
        compiler_params=pltpu.CompilerParams(vmem_limit_bytes=40 * 2**20),
    )(place, packed_all, hidden_all, hid_kernel.reshape(9 * HID_CH, 3 * HID_CH), in_weight, head)
    return (disparity, hidden)


def solution(mesh):
    in_specs = (
        P("band", None, "disp"),
        P("band", None, "disp"),
        P("band", "disp"),
        P(None, "band", "disp"),
        P("band", "disp", None),
        P(),
        P(),
        P(),
        P(),
        P(),
    )
    out_specs = (P("band", "disp"), P("band", "disp", None))
    return jax.shard_map(local, mesh=mesh, in_specs=in_specs, out_specs=out_specs, check_vma=False)
```

```python
import jax
import jax.numpy as jnp
from jax import lax
from jax.experimental import pallas as pl
from jax.experimental.pallas import tpu as pltpu
from jax.sharding import PartitionSpec as P

GROUPS = 8
DISPS = 96
FEAT_CH = 96
HID_CH = 128
ITERS = 3
TILE = 128
REACH = 2 * ITERS
EDGE = 8
SPAN = TILE + 2 * EDGE
ROWS = 2 * REACH + 1
PACK = 32
BLOCK = 8
SLAB = (BLOCK + 2) * GROUPS
OUT_SLAB = BLOCK * GROUPS

pixel_unit = 8.0
feature_scale = 0.25
floor_logit = -1e30

f32 = jnp.float32
bf16 = jnp.bfloat16


def dot(a, b):
    return jnp.dot(a, b, preferred_element_type=f32)


def dot_nt(a, b):
    return lax.dot_general(a, b, (((1,), (1,)), ((), ())), preferred_element_type=f32)


def copy_all(copies):
    for copy in copies:
        copy.start()
    for copy in copies:
        copy.wait()


def toeplitz(vol_kernel):
    size = 27 * GROUPS
    flat = vol_kernel[...].astype(f32).reshape(size, GROUPS)
    flat = jnp.concatenate([flat, jnp.zeros((size, TILE - GROUPS), f32)], axis=1).T[:GROUPS]
    row = lax.broadcasted_iota(jnp.int32, (9 * GROUPS, size), 0) >> 3
    tap = lax.broadcasted_iota(jnp.int32, (9 * GROUPS, size), 1) >> 3
    tap_a = (tap >= 9).astype(jnp.int32) + (tap >= 18).astype(jnp.int32)
    within = tap - 9 * tap_a
    tap_b = (within >= 3).astype(jnp.int32) + (within >= 6).astype(jnp.int32)
    tap_e = within - 3 * tap_b
    pairs = jnp.where(
        row == 3 * tap_a + tap_e, jnp.concatenate([flat] * 9, axis=0), 0.0
    ).astype(bf16)
    from_row = lax.broadcasted_iota(jnp.int32, (size, 3 * SLAB), 0)
    to = lax.broadcasted_iota(jnp.int32, (size, 3 * SLAB), 1)
    from_tap = from_row >> 3
    from_in = from_tap - 9 * ((from_tap >= 9).astype(jnp.int32) + (from_tap >= 18).astype(jnp.int32))
    from_b = (from_in >= 3).astype(jnp.int32) + (from_in >= 6).astype(jnp.int32)
    to_b = (to >= SLAB).astype(jnp.int32) + (to >= 2 * SLAB).astype(jnp.int32)
    repeat = jnp.where((from_b == to_b) & ((from_row & 7) == (to & 7)), 1.0, 0.0).astype(bf16)
    spread = dot(pairs, repeat)
    to = lax.broadcasted_iota(jnp.int32, (GROUPS, 3 * SLAB), 1)
    to_b = (to >= SLAB).astype(jnp.int32) + (to >= 2 * SLAB).astype(jnp.int32)
    to_d = (to - SLAB * to_b) >> 3
    rows = []
    for e in range(3):
        for d in range(BLOCK):
            value = jnp.zeros((GROUPS, 3 * SLAB), f32)
            for a in range(3):
                at = (3 * a + e) * GROUPS
                value = jnp.where(to_d == d + a, spread[at : at + GROUPS], value)
            rows.append(value)
    return jnp.concatenate(rows, axis=0).astype(bf16)


def volume_kernel(
    place, gain, own, across, odd_own, odd_across, even_own, even_across, limit, indices, vol_kernel,
    out, wide, extra, logit,
):
    band, disp, bands, disps = place[0], place[1], place[2], place[3]
    is_even = band % 2 == 0

    def features(b, s, half):
        rows = slice(half * FEAT_CH, (half + 1) * FEAT_CH)
        pick = 0 if s == 0 else across.shape[0] - 1
        if b == 1:
            return (own[rows] if s == 1 else across[pick, rows]).astype(f32)
        odd = odd_own[rows] if s == 1 else odd_across[pick, rows]
        even = even_own[rows] if s == 1 else even_across[pick, rows]
        odd, even = odd.astype(f32), even.astype(f32)
        return jnp.where(is_even, even, odd) if b == 0 else jnp.where(is_even, odd, even)

    lane = lax.broadcasted_iota(jnp.int32, (TILE, TILE), 1)
    sub = lax.broadcasted_iota(jnp.int32, (TILE, TILE), 0)
    flip = jnp.where(lane + sub == TILE - 1, 1.0, 0.0).astype(bf16)
    has_left = (disp > 0).astype(f32)
    has_right = (disp < disps - 1).astype(f32)
    per_group = FEAT_CH // GROUPS
    channel = lax.broadcasted_iota(jnp.int32, (TILE, FEAT_CH), 1)
    group_masks = [
        (channel >= g * per_group) & (channel < (g + 1) * per_group) for g in range(GROUPS)
    ]
    lane96 = lax.broadcasted_iota(jnp.int32, (FEAT_CH, TILE), 1)
    zero_slab = jnp.zeros((GROUPS, TILE), f32)
    for b in range(3):
        for at in (0, (DISPS + 1) * GROUPS):
            wide[b, pl.ds(at, GROUPS), :] = zero_slab
            extra[b, pl.ds(at, GROUPS), :] = zero_slab

    for b in range(3):
        row = band + b - 1
        row_ok = ((row >= 0) & (row < bands)).astype(f32)
        own_t = (features(b, 1, 0) * row_ok).T
        side = jnp.where(
            lane96 < EDGE,
            features(b, 2, 0) * (has_right * row_ok),
            jnp.where(lane96 >= TILE - EDGE, features(b, 0, 0) * (has_left * row_ok), 0.0),
        )
        side_t = side.T
        flipped = []
        for s, factor in ((2, has_right), (1, None), (0, has_left)):
            part = dot(features(b, s, 1).astype(bf16), flip)
            flipped.append(part if factor is None else part * factor)
        line = jnp.concatenate(flipped, axis=1)
        windows = [
            line[:, 2 * TILE - 32 - 32 * k : 3 * TILE - 32 - 32 * k].astype(bf16)
            for k in range(-1, 5)
        ]
        sheared = [[] for _ in range(GROUPS)]
        for k in range(4):
            rows = own_t[32 * k : 32 * k + 32]
            lhs = jnp.concatenate(
                [jnp.where(m[:32], rows, 0.0) for m in group_masks], axis=0
            ).astype(bf16)
            product = dot(lhs, windows[k + 1])
            for g in range(GROUPS):
                sheared[g].append(
                    pltpu.roll(
                        product[32 * g : 32 * g + 32], TILE - 31, 1, stride=1, stride_axis=0
                    )
                )
        after = side_t[:EDGE]
        before = side_t[TILE - EDGE :]
        lhs_after = jnp.concatenate(
            [jnp.where(m[:EDGE], after, 0.0) for m in group_masks], axis=0
        ).astype(bf16)
        lhs_before = jnp.concatenate(
            [jnp.where(m[:EDGE], before, 0.0) for m in group_masks], axis=0
        ).astype(bf16)
        product_after = dot(lhs_after, windows[5])
        product_before = dot(lhs_before, windows[0])
        gap = jnp.zeros((TILE - 2 * EDGE, TILE), f32)
        for g in range(GROUPS):
            part = jnp.concatenate(sheared[g], axis=0).T * (1.0 / per_group)
            wide[b, pl.ds(GROUPS + g, DISPS, stride=GROUPS), :] = part[:DISPS]
            rows_after = pltpu.roll(
                product_after[EDGE * g : EDGE * g + EDGE], TILE - 31, 1, stride=1, stride_axis=0
            )
            rows_before = pltpu.roll(
                product_before[EDGE * g : EDGE * g + EDGE],
                TILE - 31 + 32 - EDGE,
                1,
                stride=1,
                stride_axis=0,
            )
            part = jnp.concatenate([rows_after, gap, rows_before], axis=0).T * (1.0 / per_group)
            extra[b, pl.ds(GROUPS + g, DISPS, stride=GROUPS), :] = part[:DISPS]

    taps = toeplitz(vol_kernel)
    lane8 = lax.broadcasted_iota(jnp.int32, (OUT_SLAB, TILE), 1)
    group_at = lax.broadcasted_iota(jnp.int32, (GROUPS, TILE), 0)
    gains = jnp.zeros((GROUPS, TILE), f32)
    for g in range(GROUPS):
        gains = jnp.where(group_at == g, gain[g], gains)
    wanted = [jnp.broadcast_to(indices[t : t + 1, :], (GROUPS, TILE)) for t in range(ITERS)]
    found = [jnp.zeros((GROUPS, TILE), f32) for _ in range(ITERS)]
    for q in range(DISPS // BLOCK):
        at = q * OUT_SLAB
        slabs = []
        for b in range(3):
            slabs.append(
                jnp.concatenate(
                    [wide[b, at : at + SLAB, :], extra[b, at : at + SLAB, :]], axis=1
                ).astype(bf16)
            )
        product = dot(taps, jnp.concatenate(slabs, axis=0))
        first, middle, last = (
            product[:OUT_SLAB],
            product[OUT_SLAB : 2 * OUT_SLAB],
            product[2 * OUT_SLAB :],
        )
        conv = (
            middle[:, :TILE]
            + jnp.where(
                lane8 == 0,
                pltpu.roll(first[:, TILE:], 1, 1),
                pltpu.roll(first[:, :TILE], 1, 1),
            )
            + jnp.where(
                lane8 == TILE - 1,
                pltpu.roll(last[:, TILE:], TILE - 1, 1),
                pltpu.roll(last[:, :TILE], TILE - 1, 1),
            )
        )
        raw = wide[1, at + GROUPS : at + GROUPS + OUT_SLAB, :].astype(bf16).astype(f32)
        volume = (raw + jnp.maximum(conv, 0.0)).astype(bf16).astype(f32)
        volume = volume.reshape(BLOCK, GROUPS, TILE)
        logit[q * BLOCK : (q + 1) * BLOCK, :] = jnp.sum(volume * gains[None], axis=1)
        for d in range(BLOCK):
            for t in range(ITERS):
                found[t] = found[t] + jnp.where(wanted[t] == q * BLOCK + d, volume[d], 0.0)

    level = lax.broadcasted_iota(jnp.int32, (DISPS, TILE), 0)
    valid = level < limit[...]
    masked = jnp.where(valid, logit[...], floor_logit)
    top = jnp.max(masked, axis=0, keepdims=True)
    weights = jnp.where(valid, jnp.exp(masked - top), 0.0)
    moment = jnp.sum(weights * level.astype(f32), axis=0, keepdims=True)
    start = moment / jnp.sum(weights, axis=0, keepdims=True) / pixel_unit
    high = start.astype(bf16).astype(f32)
    low = (start - high).astype(bf16).astype(f32)
    ends = jnp.where(
        group_at == 0,
        jnp.broadcast_to(high, (GROUPS, TILE)),
        jnp.where(group_at == 1, jnp.broadcast_to(low, (GROUPS, TILE)), 0.0),
    )
    packed = jnp.concatenate(found + [ends], axis=0).astype(bf16)
    for i in range(out.shape[0]):
        out[i] = packed


def refine_kernel(
    place,
    packed_all,
    packed_side,
    hidden_all,
    hidden_side,
    hid_weight,
    in_weight,
    head,
    disparity_out,
    hidden_out,
    packed,
    tiles,
    sides,
    weight,
    lookups,
    taps,
    reset_taps,
    gate,
    inputs,
    level,
    sems,
):
    band, disp, bands, disps = place[0], place[1], place[2], place[3]
    held = packed.shape[1]
    first = jnp.clip(band - REACH, 0, bands - held)
    rows = pl.ds(first, held)
    last = hidden_side.shape[0] - 1
    hidden_copies = [
        pltpu.make_async_copy(hidden_all.at[rows], tiles, sems.at[0]),
        pltpu.make_async_copy(
            hidden_side.at[0, rows, pl.ds(TILE - 16, 16)], sides.at[0], sems.at[1]
        ),
        pltpu.make_async_copy(hidden_side.at[last, rows, pl.ds(0, 16)], sides.at[1], sems.at[2]),
    ]
    packed_copies = [
        pltpu.make_async_copy(packed_side.at[0, rows], packed.at[0], sems.at[3]),
        pltpu.make_async_copy(packed_all.at[rows], packed.at[1], sems.at[4]),
        pltpu.make_async_copy(packed_side.at[last, rows], packed.at[2], sems.at[5]),
    ]
    weight_copies = [
        pltpu.make_async_copy(hid_weight, weight.at[pl.ds(0, 9 * HID_CH)], sems.at[6]),
        pltpu.make_async_copy(in_weight, weight.at[pl.ds(9 * HID_CH, HID_CH)], sems.at[7]),
    ]
    for copy in packed_copies + hidden_copies + weight_copies:
        copy.start()

    has_left = (disp > 0).astype(f32)
    has_right = (disp < disps - 1).astype(f32)
    held_at, row_ok = [], []
    for r in range(ROWS):
        row = band - REACH + r
        held_at.append(jnp.clip(row, 0, bands - 1) - first)
        row_ok.append(((row >= 0) & (row < bands)).astype(f32))
    column = lax.broadcasted_iota(jnp.int32, (SPAN, HID_CH), 0)
    column_ok = jnp.where(
        column < EDGE, has_left, jnp.where(column >= TILE + EDGE, has_right, 1.0)
    )
    lane = lax.broadcasted_iota(jnp.int32, (SPAN, HID_CH), 1)
    lane_tap = lane - 9 * GROUPS
    at_sub = lax.broadcasted_iota(jnp.int32, (SPAN, 2 * TILE), 0)
    at_lane = lax.broadcasted_iota(jnp.int32, (SPAN, 2 * TILE), 1)
    spread = jnp.where(
        ((at_sub >= EDGE) & (at_lane == at_sub - EDGE))
        | ((at_sub < EDGE) & (at_lane == at_sub - EDGE + 2 * TILE)),
        1.0,
        0.0,
    ).astype(bf16)
    lane_pack = lax.broadcasted_iota(jnp.int32, (PACK, TILE), 1)

    for copy in packed_copies:
        copy.wait()

    shifted = []
    for r in range(ROWS):
        centre = packed[1, held_at[r]].astype(f32) * row_ok[r]
        halo = jnp.where(
            lane_pack < TILE // 2,
            packed[2, held_at[r]].astype(f32) * (row_ok[r] * has_right),
            packed[0, held_at[r]].astype(f32) * (row_ok[r] * has_left),
        )
        both = jnp.concatenate([centre, halo], axis=1)
        shifted.append((pltpu.roll(both, 1, 1), both, pltpu.roll(both, 2 * TILE - 1, 1)))
    fill = jnp.zeros((HID_CH - 9 * GROUPS, 2 * TILE), f32)
    base = 0
    look_at = []
    for t in range(ITERS):
        low, high = 1 + 2 * t, ROWS - 2 - 2 * t
        look_at.append((base, low))
        for r in range(low, high + 1):
            pieces = []
            for a in range(3):
                for b in range(3):
                    pieces.append(shifted[r + a - 1][b][t * GROUPS : (t + 1) * GROUPS])
            line = jnp.concatenate(pieces + [fill], axis=0).astype(bf16)
            lookups[base + r - low] = dot_nt(spread, line)
        base += high - low + 1
    for r in range(ROWS):
        ends = shifted[r][1][3 * GROUPS : 4 * GROUPS]
        wide_high = jnp.broadcast_to(ends[0:1], (HID_CH, 2 * TILE)).astype(bf16)
        wide_low = jnp.broadcast_to(ends[1:2], (HID_CH, 2 * TILE)).astype(bf16)
        level[r * SPAN : (r + 1) * SPAN, :] = dot_nt(spread, wide_high) + dot_nt(spread, wide_low)

    for copy in hidden_copies + weight_copies:
        copy.wait()

    def keep(target, at, values):
        length = values.shape[0]
        target[at : at + length, 0:HID_CH] = pltpu.roll(values, 1, 0).astype(bf16)
        target[at : at + length, HID_CH : 2 * HID_CH] = values.astype(bf16)
        target[at : at + length, 2 * HID_CH :] = pltpu.roll(values, length - 1, 0).astype(bf16)

    for r in range(ROWS):
        values = jnp.concatenate(
            [
                sides[0, held_at[r]].astype(f32)[16 - EDGE :],
                tiles[held_at[r]].astype(f32),
                sides[1, held_at[r]].astype(f32)[:EDGE],
            ],
            axis=0,
        )
        keep(taps, r * SPAN, values * (column_ok * row_ok[r]))

    def chunks(low, high, most):
        count = high - low + 1
        parts = -(-count // most)
        out = []
        for i in range(parts):
            size = count // parts + (1 if i < count % parts else 0)
            out.append((low, size))
            low += size
        return out

    for t in range(ITERS):
        low, high = 1 + 2 * t, ROWS - 2 - 2 * t
        spread_level = {}
        for r in range(low - 1, high + 2):
            value = level[r * SPAN : (r + 1) * SPAN, :] * feature_scale
            which = lane_tap % 3
            spread_level[r] = jnp.where(
                which == 0,
                pltpu.roll(value, 1, 0),
                jnp.where(which == 1, value, pltpu.roll(value, SPAN - 1, 0)),
            )
        for r in range(low, high + 1):
            base, from_row = look_at[t]
            value = lookups[base + r - from_row]
            for a in range(3):
                value = jnp.where(
                    (lane_tap >= 3 * a) & (lane_tap < 3 * a + 3), spread_level[r + a - 1], value
                )
            inputs[r * SPAN : (r + 1) * SPAN, :] = value.astype(bf16)

        for r, count in chunks(low, high, 4):
            at, length = r * SPAN, count * SPAN
            lhs = jnp.concatenate(
                [taps[at + (a - 1) * SPAN : at + (a - 1) * SPAN + length, :] for a in range(3)]
                + [inputs[at : at + length, :]],
                axis=1,
            )
            both = dot(lhs, weight[:, : 2 * HID_CH])
            both = 0.5 * jnp.tanh(0.5 * both) + 0.5
            hidden = taps[at : at + length, HID_CH : 2 * HID_CH].astype(f32)
            gate[at : at + length, :] = both[:, :HID_CH]
            keep(reset_taps, at, both[:, HID_CH:] * hidden)
        for r, count in chunks(low + 1, high - 1, 4):
            at, length = r * SPAN, count * SPAN
            lhs = jnp.concatenate(
                [
                    reset_taps[at + (a - 1) * SPAN : at + (a - 1) * SPAN + length, :]
                    for a in range(3)
                ]
                + [inputs[at : at + length, :]],
                axis=1,
            )
            candidate = jnp.tanh(dot(lhs, weight[:, 2 * HID_CH :]))
            update = gate[at : at + length, :]
            hidden = taps[at : at + length, HID_CH : 2 * HID_CH].astype(f32)
            hidden = (1.0 - update) * hidden + update * candidate
            mask = jnp.concatenate([column_ok * row_ok[r + i] for i in range(count)], axis=0)
            hidden = (hidden * mask).astype(bf16)
            level[at : at + length, :] += dot(hidden, head[...])
            if t < ITERS - 1:
                keep(taps, at, hidden.astype(f32))
            else:
                hidden_out[0] = hidden.astype(f32)[EDGE : EDGE + TILE].astype(bf16)
    at = REACH * SPAN + EDGE
    disparity_out[...] = level[at : at + TILE, :].T[0:1]


def to_sides(value):
    disps = lax.axis_size("disp")
    right = [(d, d + 1) for d in range(disps - 1)]
    left = [(d + 1, d) for d in range(disps - 1)]
    if disps == 2:
        return lax.ppermute(value, "disp", right + left)[None]
    return jnp.stack([lax.ppermute(value, "disp", right), lax.ppermute(value, "disp", left)])


def to_rows(value, shift):
    bands = lax.axis_size("band")
    return lax.ppermute(
        value, "band", [(i, shift(i)) for i in range(bands) if 0 <= shift(i) < bands]
    )


def odd_pair(i):
    return i ^ 1


def even_pair(i):
    return i - 1 if i % 2 == 0 else i + 1


def local(
    feat_left,
    feat_right,
    limit,
    indices,
    hidden_start,
    vol_kernel,
    group_gain,
    hid_kernel,
    in_kernel,
    head_weight,
):
    bands, disps = lax.axis_size("band"), lax.axis_size("disp")
    place = jnp.stack(
        [lax.axis_index("band"), lax.axis_index("disp"), jnp.int32(bands), jnp.int32(disps)]
    ).astype(jnp.int32)
    hidden_all = lax.all_to_all(
        jnp.broadcast_to(hidden_start, (bands, TILE, HID_CH)), "band", 0, 0, tiled=True
    )
    hidden_side = to_sides(hidden_all)
    feats = jnp.concatenate([feat_left[0], feat_right[0]], axis=0)
    odd_own, even_own = to_rows(feats, odd_pair), to_rows(feats, even_pair)
    across, odd_across, even_across = to_sides(feats), to_sides(odd_own), to_sides(even_own)

    in_weight = jnp.concatenate(
        [
            in_kernel[:, :, :GROUPS].reshape(9 * GROUPS, 3 * HID_CH),
            in_kernel[:, :, GROUPS].reshape(9, 3 * HID_CH),
            jnp.zeros((HID_CH - 9 * (GROUPS + 1), 3 * HID_CH), bf16),
        ],
        axis=0,
    )
    head = jnp.broadcast_to(head_weight, (HID_CH, HID_CH))

    smem = pl.BlockSpec(memory_space=pltpu.SMEM)
    vmem = pl.BlockSpec(memory_space=pltpu.VMEM)
    anywhere = pl.BlockSpec(memory_space=pl.ANY)
    padded = (DISPS + 2) * GROUPS
    packed = pl.pallas_call(
        volume_kernel,
        out_shape=jax.ShapeDtypeStruct((bands, PACK, TILE), bf16),
        in_specs=[smem, smem] + [vmem] * 9,
        out_specs=vmem,
        scratch_shapes=[
            pltpu.VMEM((3, padded, TILE), f32),
            pltpu.VMEM((3, padded, TILE), f32),
            pltpu.VMEM((DISPS, TILE), f32),
        ],
        compiler_params=pltpu.CompilerParams(vmem_limit_bytes=32 * 2**20),
    )(
        place, group_gain, feats, across, odd_own, odd_across, even_own, even_across,
        limit, indices[:, 0], vol_kernel.reshape(27, GROUPS, GROUPS),
    )

    packed, hidden_all = lax.optimization_barrier((packed, hidden_all))
    packed_all = lax.all_to_all(packed, "band", 0, 0, tiled=True)
    packed_side = to_sides(packed_all)
    held = min(ROWS, bands)
    area = ROWS * SPAN
    looked = sum(ROWS - 2 - 4 * t for t in range(ITERS))
    disparity, hidden = pl.pallas_call(
        refine_kernel,
        out_shape=(
            jax.ShapeDtypeStruct((1, TILE), f32),
            jax.ShapeDtypeStruct((1, TILE, HID_CH), bf16),
        ),
        in_specs=[smem] + [anywhere] * 6 + [vmem],
        out_specs=(vmem, vmem),
        scratch_shapes=[
            pltpu.VMEM((3, held, PACK, TILE), bf16),
            pltpu.VMEM((held, TILE, HID_CH), bf16),
            pltpu.VMEM((2, held, 16, HID_CH), bf16),
            pltpu.VMEM((10 * HID_CH, 3 * HID_CH), bf16),
            pltpu.VMEM((looked, SPAN, HID_CH), f32),
            pltpu.VMEM((area, 3 * HID_CH), bf16),
            pltpu.VMEM((area, 3 * HID_CH), bf16),
            pltpu.VMEM((area, HID_CH), f32),
            pltpu.VMEM((area, HID_CH), bf16),
            pltpu.VMEM((area, HID_CH), f32),
            pltpu.SemaphoreType.DMA((8,)),
        ],
        compiler_params=pltpu.CompilerParams(vmem_limit_bytes=40 * 2**20),
    )(
        place, packed_all, packed_side, hidden_all, hidden_side,
        hid_kernel.reshape(9 * HID_CH, 3 * HID_CH), in_weight, head,
    )
    return (disparity, hidden)


def solution(mesh):
    in_specs = (
        P("band", None, "disp"),
        P("band", None, "disp"),
        P("band", "disp"),
        P(None, "band", "disp"),
        P("band", "disp", None),
        P(),
        P(),
        P(),
        P(),
        P(),
    )
    out_specs = (P("band", "disp"), P("band", "disp", None))
    return jax.shard_map(local, mesh=mesh, in_specs=in_specs, out_specs=out_specs, check_vma=False)
```

```python
import jax
import jax.numpy as jnp
from jax import lax
from jax.experimental import pallas as pl
from jax.experimental.pallas import tpu as pltpu
from jax.sharding import PartitionSpec as P

GROUPS = 8
DISPS = 96
FEAT_CH = 96
HID_CH = 128
ITERS = 3
TILE = 128
REACH = 2 * ITERS
EDGE = 8
SPAN = TILE + 2 * EDGE
ROWS = 2 * REACH + 1
PACK = 32
BLOCK = 8
SLAB = (BLOCK + 2) * GROUPS
OUT_SLAB = BLOCK * GROUPS

pixel_unit = 8.0
feature_scale = 0.25
floor_logit = -1e30

f32 = jnp.float32
bf16 = jnp.bfloat16


def dot(a, b):
    return jnp.dot(a, b, preferred_element_type=f32)


def dot_nt(a, b):
    return lax.dot_general(a, b, (((1,), (1,)), ((), ())), preferred_element_type=f32)


def copy_all(copies):
    for copy in copies:
        copy.start()
    for copy in copies:
        copy.wait()


def toeplitz(vol_kernel):
    size = 27 * GROUPS
    flat = vol_kernel[...].astype(f32).reshape(size, GROUPS)
    flat = jnp.concatenate([flat, jnp.zeros((size, TILE - GROUPS), f32)], axis=1).T[:GROUPS]
    row = lax.broadcasted_iota(jnp.int32, (9 * GROUPS, size), 0) >> 3
    tap = lax.broadcasted_iota(jnp.int32, (9 * GROUPS, size), 1) >> 3
    tap_a = (tap >= 9).astype(jnp.int32) + (tap >= 18).astype(jnp.int32)
    within = tap - 9 * tap_a
    tap_b = (within >= 3).astype(jnp.int32) + (within >= 6).astype(jnp.int32)
    tap_e = within - 3 * tap_b
    pairs = jnp.where(
        row == 3 * tap_a + tap_e, jnp.concatenate([flat] * 9, axis=0), 0.0
    ).astype(bf16)
    from_row = lax.broadcasted_iota(jnp.int32, (size, 3 * SLAB), 0)
    to = lax.broadcasted_iota(jnp.int32, (size, 3 * SLAB), 1)
    from_tap = from_row >> 3
    from_in = from_tap - 9 * ((from_tap >= 9).astype(jnp.int32) + (from_tap >= 18).astype(jnp.int32))
    from_b = (from_in >= 3).astype(jnp.int32) + (from_in >= 6).astype(jnp.int32)
    to_b = (to >= SLAB).astype(jnp.int32) + (to >= 2 * SLAB).astype(jnp.int32)
    repeat = jnp.where((from_b == to_b) & ((from_row & 7) == (to & 7)), 1.0, 0.0).astype(bf16)
    spread = dot(pairs, repeat)
    to = lax.broadcasted_iota(jnp.int32, (GROUPS, 3 * SLAB), 1)
    to_b = (to >= SLAB).astype(jnp.int32) + (to >= 2 * SLAB).astype(jnp.int32)
    to_d = (to - SLAB * to_b) >> 3
    rows = []
    for e in range(3):
        for d in range(BLOCK):
            value = jnp.zeros((GROUPS, 3 * SLAB), f32)
            for a in range(3):
                at = (3 * a + e) * GROUPS
                value = jnp.where(to_d == d + a, spread[at : at + GROUPS], value)
            rows.append(value)
    return jnp.concatenate(rows, axis=0).astype(bf16)


def volume_kernel(
    place, gain, own, across, odd_own, odd_across, even_own, even_across, limit, indices, vol_kernel,
    out, wide, extra, logit,
):
    band, disp, bands, disps = place[0], place[1], place[2], place[3]
    is_even = band % 2 == 0

    def features(b, s, half):
        rows = slice(half * FEAT_CH, (half + 1) * FEAT_CH)
        pick = 0 if s == 0 else across.shape[0] - 1
        if b == 1:
            return (own[rows] if s == 1 else across[pick, rows]).astype(f32)
        odd = odd_own[rows] if s == 1 else odd_across[pick, rows]
        even = even_own[rows] if s == 1 else even_across[pick, rows]
        odd, even = odd.astype(f32), even.astype(f32)
        return jnp.where(is_even, even, odd) if b == 0 else jnp.where(is_even, odd, even)

    lane = lax.broadcasted_iota(jnp.int32, (TILE, TILE), 1)
    sub = lax.broadcasted_iota(jnp.int32, (TILE, TILE), 0)
    flip = jnp.where(lane + sub == TILE - 1, 1.0, 0.0).astype(bf16)
    has_left = (disp > 0).astype(f32)
    has_right = (disp < disps - 1).astype(f32)
    per_group = FEAT_CH // GROUPS
    channel = lax.broadcasted_iota(jnp.int32, (TILE, FEAT_CH), 1)
    group_masks = [
        (channel >= g * per_group) & (channel < (g + 1) * per_group) for g in range(GROUPS)
    ]
    lane96 = lax.broadcasted_iota(jnp.int32, (FEAT_CH, TILE), 1)
    zero_slab = jnp.zeros((GROUPS, TILE), f32)
    for b in range(3):
        for at in (0, (DISPS + 1) * GROUPS):
            wide[b, pl.ds(at, GROUPS), :] = zero_slab
            extra[b, pl.ds(at, GROUPS), :] = zero_slab

    for b in range(3):
        row = band + b - 1
        row_ok = ((row >= 0) & (row < bands)).astype(f32)
        own_t = (features(b, 1, 0) * row_ok).T
        side = jnp.where(
            lane96 < EDGE,
            features(b, 2, 0) * (has_right * row_ok),
            jnp.where(lane96 >= TILE - EDGE, features(b, 0, 0) * (has_left * row_ok), 0.0),
        )
        side_t = side.T
        flipped = []
        for s, factor in ((2, has_right), (1, None), (0, has_left)):
            part = dot(features(b, s, 1).astype(bf16), flip)
            flipped.append(part if factor is None else part * factor)
        line = jnp.concatenate(flipped, axis=1)
        windows = [
            line[:, 2 * TILE - 32 - 32 * k : 3 * TILE - 32 - 32 * k].astype(bf16)
            for k in range(-1, 5)
        ]
        sheared = [[] for _ in range(GROUPS)]
        for k in range(4):
            rows = own_t[32 * k : 32 * k + 32]
            lhs = jnp.concatenate(
                [jnp.where(m[:32], rows, 0.0) for m in group_masks], axis=0
            ).astype(bf16)
            product = dot(lhs, windows[k + 1])
            for g in range(GROUPS):
                sheared[g].append(
                    pltpu.roll(
                        product[32 * g : 32 * g + 32], TILE - 31, 1, stride=1, stride_axis=0
                    )
                )
        after = side_t[:EDGE]
        before = side_t[TILE - EDGE :]
        lhs_after = jnp.concatenate(
            [jnp.where(m[:EDGE], after, 0.0) for m in group_masks], axis=0
        ).astype(bf16)
        lhs_before = jnp.concatenate(
            [jnp.where(m[:EDGE], before, 0.0) for m in group_masks], axis=0
        ).astype(bf16)
        product_after = dot(lhs_after, windows[5])
        product_before = dot(lhs_before, windows[0])
        sides = []
        for g in range(GROUPS):
            part = jnp.concatenate(sheared[g], axis=0).T * (1.0 / per_group)
            wide[b, pl.ds(GROUPS + g, DISPS, stride=GROUPS), :] = part[:DISPS]
            sides.append(
                pltpu.roll(
                    product_after[EDGE * g : EDGE * g + EDGE], TILE - 31, 1, stride=1, stride_axis=0
                )
            )
            sides.append(
                pltpu.roll(
                    product_before[EDGE * g : EDGE * g + EDGE],
                    TILE - 31 + 32 - EDGE,
                    1,
                    stride=1,
                    stride_axis=0,
                )
            )
        part = jnp.concatenate(sides, axis=0).T[:DISPS] * (1.0 / per_group)
        for g in range(GROUPS):
            extra[b, pl.ds(GROUPS + g, DISPS, stride=GROUPS), :] = (
                part if g == 0 else pltpu.roll(part, TILE - 2 * EDGE * g, 1)
            )

    taps = toeplitz(vol_kernel)
    lane8 = lax.broadcasted_iota(jnp.int32, (OUT_SLAB, TILE), 1)
    group_at = lax.broadcasted_iota(jnp.int32, (GROUPS, TILE), 0)
    gains = jnp.zeros((GROUPS, TILE), f32)
    for g in range(GROUPS):
        gains = jnp.where(group_at == g, gain[g], gains)
    wanted = [jnp.broadcast_to(indices[t : t + 1, :], (GROUPS, TILE)) for t in range(ITERS)]
    found = [jnp.zeros((GROUPS, TILE), f32) for _ in range(ITERS)]
    for q in range(DISPS // BLOCK):
        at = q * OUT_SLAB
        slabs = []
        for b in range(3):
            slabs.append(
                jnp.concatenate(
                    [wide[b, at : at + SLAB, :], extra[b, at : at + SLAB, :]], axis=1
                ).astype(bf16)
            )
        product = dot(taps, jnp.concatenate(slabs, axis=0))
        first, middle, last = (
            product[:OUT_SLAB],
            product[OUT_SLAB : 2 * OUT_SLAB],
            product[2 * OUT_SLAB :],
        )
        conv = (
            middle[:, :TILE]
            + jnp.where(
                lane8 == 0,
                pltpu.roll(first[:, TILE:], TILE - 2 * EDGE + 1, 1),
                pltpu.roll(first[:, :TILE], 1, 1),
            )
            + jnp.where(
                lane8 == TILE - 1,
                pltpu.roll(last[:, TILE:], TILE - 1, 1),
                pltpu.roll(last[:, :TILE], TILE - 1, 1),
            )
        )
        raw = wide[1, at + GROUPS : at + GROUPS + OUT_SLAB, :].astype(bf16).astype(f32)
        volume = (raw + jnp.maximum(conv, 0.0)).astype(bf16).astype(f32)
        volume = volume.reshape(BLOCK, GROUPS, TILE)
        logit[q * BLOCK : (q + 1) * BLOCK, :] = jnp.sum(volume * gains[None], axis=1)
        for d in range(BLOCK):
            for t in range(ITERS):
                found[t] = found[t] + jnp.where(wanted[t] == q * BLOCK + d, volume[d], 0.0)

    level = lax.broadcasted_iota(jnp.int32, (DISPS, TILE), 0)
    valid = level < limit[...]
    masked = jnp.where(valid, logit[...], floor_logit)
    top = jnp.max(masked, axis=0, keepdims=True)
    weights = jnp.where(valid, jnp.exp(masked - top), 0.0)
    moment = jnp.sum(weights * level.astype(f32), axis=0, keepdims=True)
    start = moment / jnp.sum(weights, axis=0, keepdims=True) / pixel_unit
    high = start.astype(bf16).astype(f32)
    low = (start - high).astype(bf16).astype(f32)
    ends = jnp.where(
        group_at == 0,
        jnp.broadcast_to(high, (GROUPS, TILE)),
        jnp.where(group_at == 1, jnp.broadcast_to(low, (GROUPS, TILE)), 0.0),
    )
    packed = jnp.concatenate(found + [ends], axis=0).astype(bf16)
    for i in range(out.shape[0]):
        out[i] = packed


def refine_kernel(
    place,
    packed_all,
    packed_side,
    hidden_all,
    hidden_side,
    hid_weight,
    in_weight,
    head,
    disparity_out,
    hidden_out,
    line,
    weight,
    lookups,
    taps,
    reset_taps,
    gate,
    inputs,
    level,
    sems,
):
    band, disp, bands, disps = place[0], place[1], place[2], place[3]
    weight_copies = [
        pltpu.make_async_copy(hid_weight, weight.at[pl.ds(0, 9 * HID_CH)], sems.at[0]),
        pltpu.make_async_copy(in_weight, weight.at[pl.ds(9 * HID_CH, HID_CH)], sems.at[1]),
    ]
    for copy in weight_copies:
        copy.start()

    has_left = (disp > 0).astype(f32)
    has_right = (disp < disps - 1).astype(f32)
    held_at, row_ok = [], []
    for r in range(ROWS):
        row = band - REACH + r
        held_at.append(jnp.clip(row, 0, bands - 1))
        row_ok.append(((row >= 0) & (row < bands)).astype(f32))
    column = lax.broadcasted_iota(jnp.int32, (SPAN, HID_CH), 0)
    column_ok = jnp.where(
        column < EDGE, has_left, jnp.where(column >= TILE + EDGE, has_right, 1.0)
    )
    lane = lax.broadcasted_iota(jnp.int32, (SPAN, HID_CH), 1)
    lane_tap = lane - 9 * GROUPS
    at_sub = lax.broadcasted_iota(jnp.int32, (SPAN, 2 * TILE), 0)
    at_lane = lax.broadcasted_iota(jnp.int32, (SPAN, 2 * TILE), 1)
    spread = jnp.where(
        ((at_sub >= EDGE) & (at_lane == at_sub - EDGE))
        | ((at_sub < EDGE) & (at_lane == at_sub - EDGE + 2 * TILE)),
        1.0,
        0.0,
    ).astype(bf16)
    lane_pack = lax.broadcasted_iota(jnp.int32, (PACK, TILE), 1)

    last = packed_side.shape[0] - 1
    shifted = []
    for r in range(ROWS):
        centre = packed_all[held_at[r]].astype(f32) * row_ok[r]
        halo = jnp.where(
            lane_pack < TILE // 2,
            packed_side[last, held_at[r]].astype(f32) * (row_ok[r] * has_right),
            packed_side[0, held_at[r]].astype(f32) * (row_ok[r] * has_left),
        )
        both = jnp.concatenate([centre, halo], axis=1)
        shifted.append((pltpu.roll(both, 1, 1), both, pltpu.roll(both, 2 * TILE - 1, 1)))
    fill = jnp.zeros((HID_CH - 9 * GROUPS, 2 * TILE), f32)
    base = 0
    look_at = []
    for t in range(ITERS):
        low, high = 1 + 2 * t, ROWS - 2 - 2 * t
        look_at.append((base, low))
        for r in range(low, high + 1):
            pieces = []
            for a in range(3):
                for b in range(3):
                    pieces.append(shifted[r + a - 1][b][t * GROUPS : (t + 1) * GROUPS])
            taken = jnp.concatenate(pieces + [fill], axis=0).astype(bf16)
            lookups[base + r - low] = dot_nt(spread, taken)
        base += high - low + 1
    high = [shifted[r][1][3 * GROUPS : 3 * GROUPS + 1] for r in range(ROWS)]
    low = [shifted[r][1][3 * GROUPS + 1 : 3 * GROUPS + 2] for r in range(ROWS)]
    ends = jnp.concatenate(high + low + [jnp.zeros((HID_CH - 2 * ROWS, 2 * TILE), f32)], axis=0)
    ends = dot_nt(spread, ends.astype(bf16))
    for r in range(ROWS):
        level[r * SPAN : (r + 1) * SPAN, :] = jnp.broadcast_to(
            ends[:, r : r + 1] + ends[:, ROWS + r : ROWS + r + 1], (SPAN, HID_CH)
        )

    def keep(target, at, values):
        length = values.shape[0]
        start = EDGE + at
        line[start : start + length, :] = values
        target[at : at + length, 0:HID_CH] = line[start - 1 : start - 1 + length, :].astype(bf16)
        target[at : at + length, HID_CH : 2 * HID_CH] = values.astype(bf16)
        target[at : at + length, 2 * HID_CH :] = line[start + 1 : start + 1 + length, :].astype(
            bf16
        )

    line[...] = jnp.zeros_like(line)
    for r in range(ROWS):
        values = jnp.concatenate(
            [
                hidden_side[0, held_at[r], TILE - 16 :, :].astype(f32)[16 - EDGE :],
                hidden_all[held_at[r]].astype(f32),
                hidden_side[last, held_at[r], :16, :].astype(f32)[:EDGE],
            ],
            axis=0,
        )
        keep(taps, r * SPAN, values * (column_ok * row_ok[r]))

    for copy in weight_copies:
        copy.wait()

    def chunks(low, high, most):
        count = high - low + 1
        parts = -(-count // most)
        out = []
        for i in range(parts):
            size = count // parts + (1 if i < count % parts else 0)
            out.append((low, size))
            low += size
        return out

    for t in range(ITERS):
        low, high = 1 + 2 * t, ROWS - 2 - 2 * t
        spread_level = {}
        for r in range(low - 1, high + 2):
            value = level[r * SPAN : (r + 1) * SPAN, :] * feature_scale
            which = lane_tap % 3
            spread_level[r] = jnp.where(
                which == 0,
                pltpu.roll(value, 1, 0),
                jnp.where(which == 1, value, pltpu.roll(value, SPAN - 1, 0)),
            )
        for r in range(low, high + 1):
            base, from_row = look_at[t]
            value = lookups[base + r - from_row]
            for a in range(3):
                value = jnp.where(
                    (lane_tap >= 3 * a) & (lane_tap < 3 * a + 3), spread_level[r + a - 1], value
                )
            inputs[r * SPAN : (r + 1) * SPAN, :] = value.astype(bf16)

        for r, count in chunks(low, high, 4):
            at, length = r * SPAN, count * SPAN
            lhs = jnp.concatenate(
                [taps[at + (a - 1) * SPAN : at + (a - 1) * SPAN + length, :] for a in range(3)]
                + [inputs[at : at + length, :]],
                axis=1,
            )
            both = dot(lhs, weight[:, : 2 * HID_CH])
            both = 0.5 * jnp.tanh(0.5 * both) + 0.5
            hidden = taps[at : at + length, HID_CH : 2 * HID_CH].astype(f32)
            gate[at : at + length, :] = both[:, :HID_CH]
            keep(reset_taps, at, both[:, HID_CH:] * hidden)
        for r, count in chunks(low + 1, high - 1, 4):
            at, length = r * SPAN, count * SPAN
            lhs = jnp.concatenate(
                [
                    reset_taps[at + (a - 1) * SPAN : at + (a - 1) * SPAN + length, :]
                    for a in range(3)
                ]
                + [inputs[at : at + length, :]],
                axis=1,
            )
            candidate = jnp.tanh(dot(lhs, weight[:, 2 * HID_CH :]))
            update = gate[at : at + length, :]
            hidden = taps[at : at + length, HID_CH : 2 * HID_CH].astype(f32)
            hidden = (1.0 - update) * hidden + update * candidate
            mask = jnp.concatenate([column_ok * row_ok[r + i] for i in range(count)], axis=0)
            hidden = (hidden * mask).astype(bf16)
            level[at : at + length, :] += dot(hidden, head[...])
            if t < ITERS - 1:
                keep(taps, at, hidden.astype(f32))
            else:
                hidden_out[0] = hidden.astype(f32)[EDGE : EDGE + TILE].astype(bf16)
    at = REACH * SPAN + EDGE
    disparity_out[...] = level[at : at + TILE, :].T[0:1]


def to_sides(value):
    disps = lax.axis_size("disp")
    right = [(d, d + 1) for d in range(disps - 1)]
    left = [(d + 1, d) for d in range(disps - 1)]
    if disps == 2:
        return lax.ppermute(value, "disp", right + left)[None]
    return jnp.stack([lax.ppermute(value, "disp", right), lax.ppermute(value, "disp", left)])


def to_rows(value, shift):
    bands = lax.axis_size("band")
    return lax.ppermute(
        value, "band", [(i, shift(i)) for i in range(bands) if 0 <= shift(i) < bands]
    )


def odd_pair(i):
    return i ^ 1


def even_pair(i):
    return i - 1 if i % 2 == 0 else i + 1


def local(
    feat_left,
    feat_right,
    limit,
    indices,
    hidden_start,
    vol_kernel,
    group_gain,
    hid_kernel,
    in_kernel,
    head_weight,
):
    bands, disps = lax.axis_size("band"), lax.axis_size("disp")
    place = jnp.stack(
        [lax.axis_index("band"), lax.axis_index("disp"), jnp.int32(bands), jnp.int32(disps)]
    ).astype(jnp.int32)
    feats = jnp.concatenate([feat_left[0], feat_right[0]], axis=0)
    odd_own, even_own = to_rows(feats, odd_pair), to_rows(feats, even_pair)
    odd_own, even_own, hidden = lax.optimization_barrier((odd_own, even_own, hidden_start))
    across, odd_across, even_across = to_sides(feats), to_sides(odd_own), to_sides(even_own)
    hidden_all = lax.all_to_all(
        jnp.broadcast_to(hidden, (bands, TILE, HID_CH)), "band", 0, 0, tiled=True
    )
    hidden_side = to_sides(hidden_all)

    in_weight = jnp.concatenate(
        [
            in_kernel[:, :, :GROUPS].reshape(9 * GROUPS, 3 * HID_CH),
            in_kernel[:, :, GROUPS].reshape(9, 3 * HID_CH),
            jnp.zeros((HID_CH - 9 * (GROUPS + 1), 3 * HID_CH), bf16),
        ],
        axis=0,
    )
    head = jnp.broadcast_to(head_weight, (HID_CH, HID_CH))

    smem = pl.BlockSpec(memory_space=pltpu.SMEM)
    vmem = pl.BlockSpec(memory_space=pltpu.VMEM)
    anywhere = pl.BlockSpec(memory_space=pl.ANY)
    padded = (DISPS + 2) * GROUPS
    packed = pl.pallas_call(
        volume_kernel,
        out_shape=jax.ShapeDtypeStruct((bands, PACK, TILE), bf16),
        in_specs=[smem, smem] + [vmem] * 9,
        out_specs=vmem,
        scratch_shapes=[
            pltpu.VMEM((3, padded, TILE), f32),
            pltpu.VMEM((3, padded, TILE), f32),
            pltpu.VMEM((DISPS, TILE), f32),
        ],
        compiler_params=pltpu.CompilerParams(vmem_limit_bytes=32 * 2**20),
    )(
        place, group_gain, feats, across, odd_own, odd_across, even_own, even_across,
        limit, indices[:, 0], vol_kernel.reshape(27, GROUPS, GROUPS),
    )

    packed, hidden_all = lax.optimization_barrier((packed, hidden_all))
    packed_all = lax.all_to_all(packed, "band", 0, 0, tiled=True)
    packed_side = to_sides(packed_all)
    area = ROWS * SPAN
    looked = sum(ROWS - 2 - 4 * t for t in range(ITERS))
    disparity, hidden = pl.pallas_call(
        refine_kernel,
        out_shape=(
            jax.ShapeDtypeStruct((1, TILE), f32),
            jax.ShapeDtypeStruct((1, TILE, HID_CH), bf16),
        ),
        in_specs=[smem] + [vmem] * 4 + [anywhere] * 2 + [vmem],
        out_specs=(vmem, vmem),
        scratch_shapes=[
            pltpu.VMEM((area + 2 * EDGE, HID_CH), f32),
            pltpu.VMEM((10 * HID_CH, 3 * HID_CH), bf16),
            pltpu.VMEM((looked, SPAN, HID_CH), f32),
            pltpu.VMEM((area, 3 * HID_CH), bf16),
            pltpu.VMEM((area, 3 * HID_CH), bf16),
            pltpu.VMEM((area, HID_CH), f32),
            pltpu.VMEM((area, HID_CH), bf16),
            pltpu.VMEM((area, HID_CH), f32),
            pltpu.SemaphoreType.DMA((2,)),
        ],
        compiler_params=pltpu.CompilerParams(vmem_limit_bytes=40 * 2**20),
    )(
        place, packed_all, packed_side, hidden_all, hidden_side,
        hid_kernel.reshape(9 * HID_CH, 3 * HID_CH), in_weight, head,
    )
    return (disparity, hidden)


def solution(mesh):
    in_specs = (
        P("band", None, "disp"),
        P("band", None, "disp"),
        P("band", "disp"),
        P(None, "band", "disp"),
        P("band", "disp", None),
        P(),
        P(),
        P(),
        P(),
        P(),
    )
    out_specs = (P("band", "disp"), P("band", "disp", None))
    return jax.shard_map(local, mesh=mesh, in_specs=in_specs, out_specs=out_specs, check_vma=False)
```

```python
import jax
import jax.numpy as jnp
from jax import lax
from jax.experimental import pallas as pl
from jax.experimental.pallas import tpu as pltpu
from jax.sharding import PartitionSpec as P

GROUPS = 8
DISPS = 96
FEAT_CH = 96
HID_CH = 128
ITERS = 3
TILE = 128
REACH = 2 * ITERS
EDGE = 8
SPAN = TILE + 2 * EDGE
ROWS = 2 * REACH + 1
PACK = 32
BLOCK = 8
SLAB = (BLOCK + 2) * GROUPS
OUT_SLAB = BLOCK * GROUPS

pixel_unit = 8.0
feature_scale = 0.25
floor_logit = -1e30

f32 = jnp.float32
bf16 = jnp.bfloat16


def dot(a, b):
    return jnp.dot(a, b, preferred_element_type=f32)


def dot_nt(a, b):
    return lax.dot_general(a, b, (((1,), (1,)), ((), ())), preferred_element_type=f32)


def copy_all(copies):
    for copy in copies:
        copy.start()
    for copy in copies:
        copy.wait()


def toeplitz(vol_kernel):
    size = 27 * GROUPS
    flat = vol_kernel[...].astype(f32).reshape(size, GROUPS)
    flat = jnp.concatenate([flat, jnp.zeros((size, TILE - GROUPS), f32)], axis=1).T[:GROUPS]
    row = lax.broadcasted_iota(jnp.int32, (9 * GROUPS, size), 0) >> 3
    tap = lax.broadcasted_iota(jnp.int32, (9 * GROUPS, size), 1) >> 3
    tap_a = (tap >= 9).astype(jnp.int32) + (tap >= 18).astype(jnp.int32)
    within = tap - 9 * tap_a
    tap_b = (within >= 3).astype(jnp.int32) + (within >= 6).astype(jnp.int32)
    tap_e = within - 3 * tap_b
    pairs = jnp.where(
        row == 3 * tap_a + tap_e, jnp.concatenate([flat] * 9, axis=0), 0.0
    ).astype(bf16)
    from_row = lax.broadcasted_iota(jnp.int32, (size, 3 * SLAB), 0)
    to = lax.broadcasted_iota(jnp.int32, (size, 3 * SLAB), 1)
    from_tap = from_row >> 3
    from_in = from_tap - 9 * ((from_tap >= 9).astype(jnp.int32) + (from_tap >= 18).astype(jnp.int32))
    from_b = (from_in >= 3).astype(jnp.int32) + (from_in >= 6).astype(jnp.int32)
    to_b = (to >= SLAB).astype(jnp.int32) + (to >= 2 * SLAB).astype(jnp.int32)
    repeat = jnp.where((from_b == to_b) & ((from_row & 7) == (to & 7)), 1.0, 0.0).astype(bf16)
    spread = dot(pairs, repeat)
    to = lax.broadcasted_iota(jnp.int32, (GROUPS, 3 * SLAB), 1)
    to_b = (to >= SLAB).astype(jnp.int32) + (to >= 2 * SLAB).astype(jnp.int32)
    to_d = (to - SLAB * to_b) >> 3
    rows = []
    for e in range(3):
        for d in range(BLOCK):
            value = jnp.zeros((GROUPS, 3 * SLAB), f32)
            for a in range(3):
                at = (3 * a + e) * GROUPS
                value = jnp.where(to_d == d + a, spread[at : at + GROUPS], value)
            rows.append(value)
    return jnp.concatenate(rows, axis=0).astype(bf16)


def volume_kernel(
    place, gain, own, across, odd_own, odd_across, even_own, even_across, limit, indices, vol_kernel,
    out, wide, extra, logit,
):
    band, disp, bands, disps = place[0], place[1], place[2], place[3]
    is_even = band % 2 == 0

    def features(b, s, half):
        rows = slice(half * FEAT_CH, (half + 1) * FEAT_CH)
        pick = 0 if s == 0 else across.shape[0] - 1
        if b == 1:
            return (own[rows] if s == 1 else across[pick, rows]).astype(f32)
        odd = odd_own[rows] if s == 1 else odd_across[pick, rows]
        even = even_own[rows] if s == 1 else even_across[pick, rows]
        odd, even = odd.astype(f32), even.astype(f32)
        return jnp.where(is_even, even, odd) if b == 0 else jnp.where(is_even, odd, even)

    lane = lax.broadcasted_iota(jnp.int32, (TILE, TILE), 1)
    sub = lax.broadcasted_iota(jnp.int32, (TILE, TILE), 0)
    flip = jnp.where(lane + sub == TILE - 1, 1.0, 0.0).astype(bf16)
    has_left = (disp > 0).astype(f32)
    has_right = (disp < disps - 1).astype(f32)
    per_group = FEAT_CH // GROUPS
    channel = lax.broadcasted_iota(jnp.int32, (TILE, FEAT_CH), 1)
    group_masks = [
        (channel >= g * per_group) & (channel < (g + 1) * per_group) for g in range(GROUPS)
    ]
    lane96 = lax.broadcasted_iota(jnp.int32, (FEAT_CH, TILE), 1)
    zero_slab = jnp.zeros((GROUPS, TILE), f32)
    for b in range(3):
        for at in (0, (DISPS + 1) * GROUPS):
            wide[b, pl.ds(at, GROUPS), :] = zero_slab
            extra[b, pl.ds(at, GROUPS), :] = zero_slab

    for b in range(3):
        row = band + b - 1
        row_ok = ((row >= 0) & (row < bands)).astype(f32)
        own_t = (features(b, 1, 0) * row_ok).T
        side = jnp.where(
            lane96 < EDGE,
            features(b, 2, 0) * (has_right * row_ok),
            jnp.where(lane96 >= TILE - EDGE, features(b, 0, 0) * (has_left * row_ok), 0.0),
        )
        side_t = side.T
        flipped = []
        for s, factor in ((2, has_right), (1, None), (0, has_left)):
            part = dot(features(b, s, 1).astype(bf16), flip)
            flipped.append(part if factor is None else part * factor)
        line = jnp.concatenate(flipped, axis=1)
        windows = [
            line[:, 2 * TILE - 32 - 32 * k : 3 * TILE - 32 - 32 * k].astype(bf16)
            for k in range(-1, 5)
        ]
        sheared = [[] for _ in range(GROUPS)]
        for k in range(4):
            rows = own_t[32 * k : 32 * k + 32]
            lhs = jnp.concatenate(
                [jnp.where(m[:32], rows, 0.0) for m in group_masks], axis=0
            ).astype(bf16)
            product = dot(lhs, windows[k + 1])
            for g in range(GROUPS):
                sheared[g].append(
                    pltpu.roll(
                        product[32 * g : 32 * g + 32], TILE - 31, 1, stride=1, stride_axis=0
                    )
                )
        after = side_t[:EDGE]
        before = side_t[TILE - EDGE :]
        lhs_after = jnp.concatenate(
            [jnp.where(m[:EDGE], after, 0.0) for m in group_masks], axis=0
        ).astype(bf16)
        lhs_before = jnp.concatenate(
            [jnp.where(m[:EDGE], before, 0.0) for m in group_masks], axis=0
        ).astype(bf16)
        product_after = dot(lhs_after, windows[5])
        product_before = dot(lhs_before, windows[0])
        sides = []
        for g in range(GROUPS):
            part = jnp.concatenate(sheared[g], axis=0).T * (1.0 / per_group)
            wide[b, pl.ds(GROUPS + g, DISPS, stride=GROUPS), :] = part[:DISPS]
            sides.append(
                pltpu.roll(
                    product_after[EDGE * g : EDGE * g + EDGE], TILE - 31, 1, stride=1, stride_axis=0
                )
            )
            sides.append(
                pltpu.roll(
                    product_before[EDGE * g : EDGE * g + EDGE],
                    TILE - 31 + 32 - EDGE,
                    1,
                    stride=1,
                    stride_axis=0,
                )
            )
        part = jnp.concatenate(sides, axis=0).T[:DISPS] * (1.0 / per_group)
        for g in range(GROUPS):
            extra[b, pl.ds(GROUPS + g, DISPS, stride=GROUPS), :] = (
                part if g == 0 else pltpu.roll(part, TILE - 2 * EDGE * g, 1)
            )

    taps = toeplitz(vol_kernel)
    lane8 = lax.broadcasted_iota(jnp.int32, (OUT_SLAB, TILE), 1)
    group_at = lax.broadcasted_iota(jnp.int32, (GROUPS, TILE), 0)
    gains = jnp.zeros((GROUPS, TILE), f32)
    for g in range(GROUPS):
        gains = jnp.where(group_at == g, gain[g], gains)
    wanted = [jnp.broadcast_to(indices[t : t + 1, :], (GROUPS, TILE)) for t in range(ITERS)]
    found = [jnp.zeros((GROUPS, TILE), f32) for _ in range(ITERS)]
    for q in range(DISPS // BLOCK):
        at = q * OUT_SLAB
        slabs = []
        for b in range(3):
            slabs.append(
                jnp.concatenate(
                    [wide[b, at : at + SLAB, :], extra[b, at : at + SLAB, :]], axis=1
                ).astype(bf16)
            )
        product = dot(taps, jnp.concatenate(slabs, axis=0))
        first, middle, last = (
            product[:OUT_SLAB],
            product[OUT_SLAB : 2 * OUT_SLAB],
            product[2 * OUT_SLAB :],
        )
        conv = (
            middle[:, :TILE]
            + jnp.where(
                lane8 == 0,
                pltpu.roll(first[:, TILE:], TILE - 2 * EDGE + 1, 1),
                pltpu.roll(first[:, :TILE], 1, 1),
            )
            + jnp.where(
                lane8 == TILE - 1,
                pltpu.roll(last[:, TILE:], TILE - 1, 1),
                pltpu.roll(last[:, :TILE], TILE - 1, 1),
            )
        )
        raw = wide[1, at + GROUPS : at + GROUPS + OUT_SLAB, :].astype(bf16).astype(f32)
        volume = (raw + jnp.maximum(conv, 0.0)).astype(bf16).astype(f32)
        volume = volume.reshape(BLOCK, GROUPS, TILE)
        logit[q * BLOCK : (q + 1) * BLOCK, :] = jnp.sum(volume * gains[None], axis=1)
        for d in range(BLOCK):
            for t in range(ITERS):
                found[t] = found[t] + jnp.where(wanted[t] == q * BLOCK + d, volume[d], 0.0)

    level = lax.broadcasted_iota(jnp.int32, (DISPS, TILE), 0)
    valid = level < limit[...]
    masked = jnp.where(valid, logit[...], floor_logit)
    top = jnp.max(masked, axis=0, keepdims=True)
    weights = jnp.where(valid, jnp.exp(masked - top), 0.0)
    moment = jnp.sum(weights * level.astype(f32), axis=0, keepdims=True)
    start = moment / jnp.sum(weights, axis=0, keepdims=True) / pixel_unit
    high = start.astype(bf16).astype(f32)
    low = (start - high).astype(bf16).astype(f32)
    ends = jnp.where(
        group_at == 0,
        jnp.broadcast_to(high, (GROUPS, TILE)),
        jnp.where(group_at == 1, jnp.broadcast_to(low, (GROUPS, TILE)), 0.0),
    )
    packed = jnp.concatenate(found + [ends], axis=0).astype(bf16)
    for i in range(out.shape[0]):
        out[i] = packed


def spot(place, r):
    band, bands = place[0], place[2]
    row = band - REACH + r
    return jnp.clip(row, 0, bands - 1), ((row >= 0) & (row < bands)).astype(f32)


def column_inside(place):
    column = lax.broadcasted_iota(jnp.int32, (SPAN, HID_CH), 0)
    has_left = (place[1] > 0).astype(f32)
    has_right = (place[1] < place[3] - 1).astype(f32)
    return jnp.where(column < EDGE, has_left, jnp.where(column >= TILE + EDGE, has_right, 1.0))


def keep(line, target, at, values):
    length = values.shape[0]
    start = EDGE + at
    line[start : start + length, :] = values
    target[at : at + length, 0:HID_CH] = line[start - 1 : start - 1 + length, :].astype(bf16)
    target[at : at + length, HID_CH : 2 * HID_CH] = values.astype(bf16)
    target[at : at + length, 2 * HID_CH :] = line[start + 1 : start + 1 + length, :].astype(bf16)


def around(target, at, length):
    return [target[at + a * SPAN : at + a * SPAN + length, :] for a in (-1, 0, 1)]


def chunks(low, high, most):
    count = high - low + 1
    parts = -(-count // most)
    out = []
    for i in range(parts):
        size = count // parts + (1 if i < count % parts else 0)
        out.append((low, size))
        low += size
    return out


def first_conv_kernel(
    place, hidden_all, hidden_side, hid_weight, hidden_out, conv_out, line, taps
):
    last = hidden_side.shape[0] - 1
    column_ok = column_inside(place)
    line[...] = jnp.zeros_like(line)
    for r in range(ROWS):
        held, row_ok = spot(place, r)
        values = jnp.concatenate(
            [
                hidden_side[0, held, TILE - 16 :, :].astype(f32)[16 - EDGE :],
                hidden_all[held].astype(f32),
                hidden_side[last, held, :16, :].astype(f32)[:EDGE],
            ],
            axis=0,
        )
        values = values * (column_ok * row_ok)
        keep(line, taps, r * SPAN, values)
        hidden_out[r * SPAN : (r + 1) * SPAN, :] = values.astype(bf16)
    for r, count in chunks(1, ROWS - 2, 4):
        at, length = r * SPAN, count * SPAN
        lhs = jnp.concatenate(around(taps, at, length), axis=1)
        conv_out[at - SPAN : at - SPAN + length, :] = dot(lhs, hid_weight[:, : 2 * HID_CH])


def refine_kernel(
    place,
    packed_all,
    packed_side,
    hidden_first,
    conv_first,
    hid_weight,
    in_weight,
    disparity_out,
    hidden_out,
    line,
    weight,
    lookups,
    taps,
    reset_taps,
    gate,
    inputs,
    level,
    sems,
):
    weight_copies = [
        pltpu.make_async_copy(hid_weight, weight.at[pl.ds(0, 9 * HID_CH)], sems.at[0]),
        pltpu.make_async_copy(
            in_weight.at[pl.ds(0, HID_CH)], weight.at[pl.ds(9 * HID_CH, HID_CH)], sems.at[1]
        ),
    ]
    for copy in weight_copies:
        copy.start()

    column_ok = column_inside(place)
    has_left, has_right = column_ok[0:1, 0:1], column_ok[SPAN - 1 :, 0:1]
    lane_tap = lax.broadcasted_iota(jnp.int32, (SPAN, HID_CH), 1) - 9 * GROUPS
    at_sub = lax.broadcasted_iota(jnp.int32, (SPAN, 2 * TILE), 0)
    at_lane = lax.broadcasted_iota(jnp.int32, (SPAN, 2 * TILE), 1)
    spread = jnp.where(
        ((at_sub >= EDGE) & (at_lane == at_sub - EDGE))
        | ((at_sub < EDGE) & (at_lane == at_sub - EDGE + 2 * TILE)),
        1.0,
        0.0,
    ).astype(bf16)
    lane_pack = lax.broadcasted_iota(jnp.int32, (PACK, TILE), 1)

    last = packed_side.shape[0] - 1
    shifted = []
    for r in range(ROWS):
        held, row_ok = spot(place, r)
        centre = packed_all[held].astype(f32) * row_ok
        halo = jnp.where(
            lane_pack < TILE // 2,
            packed_side[last, held].astype(f32) * (has_right * row_ok),
            packed_side[0, held].astype(f32) * (has_left * row_ok),
        )
        both = jnp.concatenate([centre, halo], axis=1)
        shifted.append((pltpu.roll(both, 1, 1), both, pltpu.roll(both, 2 * TILE - 1, 1)))
    fill = jnp.zeros((HID_CH - 9 * GROUPS, 2 * TILE), f32)
    base = 0
    look_at = []
    for t in range(ITERS):
        low, high = 1 + 2 * t, ROWS - 2 - 2 * t
        look_at.append((base, low))
        for r in range(low, high + 1):
            pieces = []
            for a in range(3):
                for b in range(3):
                    pieces.append(shifted[r + a - 1][b][t * GROUPS : (t + 1) * GROUPS])
            taken = jnp.concatenate(pieces + [fill], axis=0).astype(bf16)
            lookups[base + r - low] = dot_nt(spread, taken)
        base += high - low + 1
    high = [shifted[r][1][3 * GROUPS : 3 * GROUPS + 1] for r in range(ROWS)]
    low = [shifted[r][1][3 * GROUPS + 1 : 3 * GROUPS + 2] for r in range(ROWS)]
    ends = jnp.concatenate(high + low + [jnp.zeros((HID_CH - 2 * ROWS, 2 * TILE), f32)], axis=0)
    ends = dot_nt(spread, ends.astype(bf16))
    blank = jnp.zeros((EDGE, HID_CH), f32)
    level[:EDGE, :] = blank
    level[EDGE + ROWS * SPAN :, :] = blank
    for r in range(ROWS):
        level[EDGE + r * SPAN : EDGE + (r + 1) * SPAN, :] = jnp.broadcast_to(
            ends[:, r : r + 1] + ends[:, ROWS + r : ROWS + r + 1], (SPAN, HID_CH)
        )
    line[...] = jnp.zeros_like(line)
    head = jnp.broadcast_to(in_weight[HID_CH : HID_CH + 16, :HID_CH][0:1], (HID_CH, HID_CH))
    for copy in weight_copies:
        copy.wait()

    for t in range(ITERS):
        low, high = 1 + 2 * t, ROWS - 2 - 2 * t
        which = lane_tap % 3
        spread_level = {}
        for r in range(low - 1, high + 2):
            at = EDGE + r * SPAN
            spread_level[r] = feature_scale * jnp.where(
                which == 0,
                level[at - 1 : at - 1 + SPAN, :],
                jnp.where(which == 1, level[at : at + SPAN, :], level[at + 1 : at + 1 + SPAN, :]),
            )
        for r in range(low, high + 1):
            base, from_row = look_at[t]
            value = lookups[base + r - from_row]
            for a in range(3):
                value = jnp.where(
                    (lane_tap >= 3 * a) & (lane_tap < 3 * a + 3), spread_level[r + a - 1], value
                )
            inputs[r * SPAN : (r + 1) * SPAN, :] = value.astype(bf16)

        for r, count in chunks(low, high, 4):
            at, length = r * SPAN, count * SPAN
            if t == 0:
                both = conv_first[at - SPAN : at - SPAN + length, :] + dot(
                    inputs[at : at + length, :], weight[9 * HID_CH :, : 2 * HID_CH]
                )
                hidden = hidden_first[at : at + length, :].astype(f32)
            else:
                lhs = around(taps, at, length) + [inputs[at : at + length, :]]
                both = dot(jnp.concatenate(lhs, axis=1), weight[:, : 2 * HID_CH])
                hidden = taps[at : at + length, HID_CH : 2 * HID_CH].astype(f32)
            both = 0.5 * jnp.tanh(0.5 * both) + 0.5
            gate[at : at + length, :] = both[:, :HID_CH]
            keep(line, reset_taps, at, both[:, HID_CH:] * hidden)
        for r, count in chunks(low + 1, high - 1, 4):
            at, length = r * SPAN, count * SPAN
            lhs = around(reset_taps, at, length) + [inputs[at : at + length, :]]
            candidate = jnp.tanh(dot(jnp.concatenate(lhs, axis=1), weight[:, 2 * HID_CH :]))
            update = gate[at : at + length, :]
            if t == 0:
                hidden = hidden_first[at : at + length, :].astype(f32)
            else:
                hidden = taps[at : at + length, HID_CH : 2 * HID_CH].astype(f32)
            hidden = (1.0 - update) * hidden + update * candidate
            mask = [column_ok * spot(place, r + i)[1] for i in range(count)]
            hidden = (hidden * jnp.concatenate(mask, axis=0)).astype(bf16)
            level[EDGE + at : EDGE + at + length, :] += dot_nt(hidden, head)
            if t < ITERS - 1:
                keep(line, taps, at, hidden.astype(f32))
            else:
                hidden_out[0] = hidden.astype(f32)[EDGE : EDGE + TILE].astype(bf16)
    at = EDGE + REACH * SPAN + EDGE
    disparity_out[...] = level[at : at + TILE, :].T[0:1]


def to_sides(value):
    disps = lax.axis_size("disp")
    right = [(d, d + 1) for d in range(disps - 1)]
    left = [(d + 1, d) for d in range(disps - 1)]
    if disps == 2:
        return lax.ppermute(value, "disp", right + left)[None]
    return jnp.stack([lax.ppermute(value, "disp", right), lax.ppermute(value, "disp", left)])


def to_rows(value, shift):
    bands = lax.axis_size("band")
    return lax.ppermute(
        value, "band", [(i, shift(i)) for i in range(bands) if 0 <= shift(i) < bands]
    )


def odd_pair(i):
    return i ^ 1


def even_pair(i):
    return i - 1 if i % 2 == 0 else i + 1


def local(
    feat_left,
    feat_right,
    limit,
    indices,
    hidden_start,
    vol_kernel,
    group_gain,
    hid_kernel,
    in_kernel,
    head_weight,
):
    bands, disps = lax.axis_size("band"), lax.axis_size("disp")
    place = jnp.stack(
        [lax.axis_index("band"), lax.axis_index("disp"), jnp.int32(bands), jnp.int32(disps)]
    ).astype(jnp.int32)
    feats = jnp.concatenate([feat_left[0], feat_right[0]], axis=0)
    odd_own, even_own = to_rows(feats, odd_pair), to_rows(feats, even_pair)
    across, hidden = lax.optimization_barrier((to_sides(feats), hidden_start))
    odd_across, even_across = to_sides(odd_own), to_sides(even_own)
    hidden_all = lax.all_to_all(
        jnp.broadcast_to(hidden, (bands, TILE, HID_CH)), "band", 0, 0, tiled=True
    )

    in_weight = jnp.concatenate(
        [
            in_kernel[:, :, :GROUPS].reshape(9 * GROUPS, 3 * HID_CH),
            in_kernel[:, :, GROUPS].reshape(9, 3 * HID_CH),
            jnp.zeros((HID_CH - 9 * (GROUPS + 1), 3 * HID_CH), bf16),
            jnp.pad(head_weight.reshape(1, HID_CH), ((0, 15), (0, 2 * HID_CH))),
        ],
        axis=0,
    )

    smem = pl.BlockSpec(memory_space=pltpu.SMEM)
    vmem = pl.BlockSpec(memory_space=pltpu.VMEM)
    anywhere = pl.BlockSpec(memory_space=pl.ANY)
    padded = (DISPS + 2) * GROUPS
    packed = pl.pallas_call(
        volume_kernel,
        out_shape=jax.ShapeDtypeStruct((bands, PACK, TILE), bf16),
        in_specs=[smem, smem] + [vmem] * 9,
        out_specs=vmem,
        scratch_shapes=[
            pltpu.VMEM((3, padded, TILE), f32),
            pltpu.VMEM((3, padded, TILE), f32),
            pltpu.VMEM((DISPS, TILE), f32),
        ],
        compiler_params=pltpu.CompilerParams(vmem_limit_bytes=24 * 2**20),
        cost_estimate=pl.CostEstimate(
            flops=6 * 10**9, bytes_accessed=16 * 2**20, transcendentals=DISPS * TILE
        ),
    )(
        place, group_gain, feats, across, odd_own, odd_across, even_own, even_across,
        limit, indices[:, 0], vol_kernel.reshape(27, GROUPS, GROUPS),
    )

    packed, hidden_all = lax.optimization_barrier((packed, hidden_all))
    packed_all = lax.all_to_all(packed, "band", 0, 0, tiled=True)
    hidden_side = to_sides(hidden_all)
    packed_side = to_sides(packed_all)
    area = ROWS * SPAN
    looked = sum(ROWS - 2 - 4 * t for t in range(ITERS))
    hid_weight = hid_kernel.reshape(9 * HID_CH, 3 * HID_CH)
    hidden_first, conv_first = pl.pallas_call(
        first_conv_kernel,
        out_shape=(
            jax.ShapeDtypeStruct((area, HID_CH), bf16),
            jax.ShapeDtypeStruct((area - 2 * SPAN, 2 * HID_CH), f32),
        ),
        in_specs=[smem] + [vmem] * 3,
        out_specs=(vmem, vmem),
        scratch_shapes=[
            pltpu.VMEM((area + 2 * EDGE, HID_CH), f32),
            pltpu.VMEM((area, 3 * HID_CH), bf16),
        ],
        compiler_params=pltpu.CompilerParams(vmem_limit_bytes=24 * 2**20),
        cost_estimate=pl.CostEstimate(
            flops=2 * 11 * SPAN * 9 * HID_CH * 2 * HID_CH, bytes_accessed=6 * 2**20, transcendentals=0
        ),
    )(place, hidden_all, hidden_side, hid_weight)
    disparity, hidden = pl.pallas_call(
        refine_kernel,
        out_shape=(
            jax.ShapeDtypeStruct((1, TILE), f32),
            jax.ShapeDtypeStruct((1, TILE, HID_CH), bf16),
        ),
        in_specs=[smem] + [vmem] * 4 + [anywhere, vmem],
        out_specs=(vmem, vmem),
        scratch_shapes=[
            pltpu.VMEM((area + 2 * EDGE, HID_CH), f32),
            pltpu.VMEM((10 * HID_CH, 3 * HID_CH), bf16),
            pltpu.VMEM((looked, SPAN, HID_CH), f32),
            pltpu.VMEM((area, 3 * HID_CH), bf16),
            pltpu.VMEM((area, 3 * HID_CH), bf16),
            pltpu.VMEM((area, HID_CH), f32),
            pltpu.VMEM((area, HID_CH), bf16),
            pltpu.VMEM((area + 2 * EDGE, HID_CH), f32),
            pltpu.SemaphoreType.DMA((2,)),
        ],
        compiler_params=pltpu.CompilerParams(vmem_limit_bytes=32 * 2**20),
    )(place, packed_all, packed_side, hidden_first, conv_first, hid_weight, in_weight)
    return (disparity, hidden)


def solution(mesh):
    in_specs = (
        P("band", None, "disp"),
        P("band", None, "disp"),
        P("band", "disp"),
        P(None, "band", "disp"),
        P("band", "disp", None),
        P(),
        P(),
        P(),
        P(),
        P(),
    )
    out_specs = (P("band", "disp"), P("band", "disp", None))
    return jax.shard_map(local, mesh=mesh, in_specs=in_specs, out_specs=out_specs, check_vma=False)
```

```python
import jax
import jax.numpy as jnp
from jax import lax
from jax.experimental import pallas as pl
from jax.experimental.pallas import tpu as pltpu
from jax.sharding import PartitionSpec as P

GROUPS = 8
DISPS = 96
FEAT_CH = 96
HID_CH = 128
ITERS = 3
TILE = 128
REACH = 2 * ITERS
EDGE = 8
SPAN = TILE + 2 * EDGE
ROWS = 2 * REACH + 1
PACK = 32
BLOCK = 8
SLAB = (BLOCK + 2) * GROUPS
OUT_SLAB = BLOCK * GROUPS

pixel_unit = 8.0
feature_scale = 0.25
floor_logit = -1e30

f32 = jnp.float32
bf16 = jnp.bfloat16


def dot(a, b):
    return jnp.dot(a, b, preferred_element_type=f32)


def dot_nt(a, b):
    return lax.dot_general(a, b, (((1,), (1,)), ((), ())), preferred_element_type=f32)


def copy_all(copies):
    for copy in copies:
        copy.start()
    for copy in copies:
        copy.wait()


def toeplitz_kernel(vol_kernel, out):
    size = 27 * GROUPS
    flat = vol_kernel[...].astype(f32).reshape(size, GROUPS)
    flat = jnp.concatenate([flat, jnp.zeros((size, TILE - GROUPS), f32)], axis=1).T[:GROUPS]
    row = lax.broadcasted_iota(jnp.int32, (9 * GROUPS, size), 0) >> 3
    tap = lax.broadcasted_iota(jnp.int32, (9 * GROUPS, size), 1) >> 3
    tap_a = (tap >= 9).astype(jnp.int32) + (tap >= 18).astype(jnp.int32)
    within = tap - 9 * tap_a
    tap_b = (within >= 3).astype(jnp.int32) + (within >= 6).astype(jnp.int32)
    tap_e = within - 3 * tap_b
    pairs = jnp.where(
        row == 3 * tap_a + tap_e, jnp.concatenate([flat] * 9, axis=0), 0.0
    ).astype(bf16)
    from_row = lax.broadcasted_iota(jnp.int32, (size, 3 * SLAB), 0)
    to = lax.broadcasted_iota(jnp.int32, (size, 3 * SLAB), 1)
    from_tap = from_row >> 3
    from_in = from_tap - 9 * ((from_tap >= 9).astype(jnp.int32) + (from_tap >= 18).astype(jnp.int32))
    from_b = (from_in >= 3).astype(jnp.int32) + (from_in >= 6).astype(jnp.int32)
    to_b = (to >= SLAB).astype(jnp.int32) + (to >= 2 * SLAB).astype(jnp.int32)
    repeat = jnp.where((from_b == to_b) & ((from_row & 7) == (to & 7)), 1.0, 0.0).astype(bf16)
    spread = dot(pairs, repeat)
    to = lax.broadcasted_iota(jnp.int32, (GROUPS, 3 * SLAB), 1)
    to_b = (to >= SLAB).astype(jnp.int32) + (to >= 2 * SLAB).astype(jnp.int32)
    to_d = (to - SLAB * to_b) >> 3
    rows = []
    for e in range(3):
        for d in range(BLOCK):
            value = jnp.zeros((GROUPS, 3 * SLAB), f32)
            for a in range(3):
                at = (3 * a + e) * GROUPS
                value = jnp.where(to_d == d + a, spread[at : at + GROUPS], value)
            rows.append(value)
    out[...] = jnp.concatenate(rows, axis=0).astype(bf16)


def volume_kernel(
    place, gain, own, across, odd_own, odd_across, even_own, even_across, limit, indices, taps,
    out, wide, extra, logit,
):
    band, disp, bands, disps = place[0], place[1], place[2], place[3]
    is_even = band % 2 == 0

    def features(b, s, half):
        rows = slice(half * FEAT_CH, (half + 1) * FEAT_CH)
        pick = 0 if s == 0 else across.shape[0] - 1
        if b == 1:
            return (own[rows] if s == 1 else across[pick, rows]).astype(f32)
        odd = odd_own[rows] if s == 1 else odd_across[pick, rows]
        even = even_own[rows] if s == 1 else even_across[pick, rows]
        odd, even = odd.astype(f32), even.astype(f32)
        return jnp.where(is_even, even, odd) if b == 0 else jnp.where(is_even, odd, even)

    lane = lax.broadcasted_iota(jnp.int32, (TILE, TILE), 1)
    sub = lax.broadcasted_iota(jnp.int32, (TILE, TILE), 0)
    flip = jnp.where(lane + sub == TILE - 1, 1.0, 0.0).astype(bf16)
    has_left = (disp > 0).astype(f32)
    has_right = (disp < disps - 1).astype(f32)
    per_group = FEAT_CH // GROUPS
    channel = lax.broadcasted_iota(jnp.int32, (TILE, FEAT_CH), 1)
    group_masks = [
        (channel >= g * per_group) & (channel < (g + 1) * per_group) for g in range(GROUPS)
    ]
    lane96 = lax.broadcasted_iota(jnp.int32, (FEAT_CH, TILE), 1)
    zero_slab = jnp.zeros((GROUPS, TILE), f32)
    for b in range(3):
        for at in (0, (DISPS + 1) * GROUPS):
            wide[b, pl.ds(at, GROUPS), :] = zero_slab
            extra[b, pl.ds(at, GROUPS), :] = zero_slab

    sources = [features(b, s, 1).astype(bf16) for b in range(3) for s in range(3)]
    reversed_all = dot(jnp.concatenate(sources, axis=0), flip)

    for b in range(3):
        row = band + b - 1
        row_ok = ((row >= 0) & (row < bands)).astype(f32)
        own_t = (features(b, 1, 0) * row_ok).T
        side = jnp.where(
            lane96 < EDGE,
            features(b, 2, 0) * (has_right * row_ok),
            jnp.where(lane96 >= TILE - EDGE, features(b, 0, 0) * (has_left * row_ok), 0.0),
        )
        side_t = side.T
        flipped = []
        for s, factor in ((2, has_right), (1, None), (0, has_left)):
            at = (3 * b + s) * FEAT_CH
            part = reversed_all[at : at + FEAT_CH]
            flipped.append(part if factor is None else part * factor)
        line = jnp.concatenate(flipped, axis=1)
        windows = [
            line[:, 2 * TILE - 32 - 32 * k : 3 * TILE - 32 - 32 * k].astype(bf16)
            for k in range(-1, 5)
        ]
        sheared = [[] for _ in range(GROUPS)]
        for k in range(4):
            rows = own_t[32 * k : 32 * k + 32]
            lhs = jnp.concatenate(
                [jnp.where(m[:32], rows, 0.0) for m in group_masks], axis=0
            ).astype(bf16)
            product = dot(lhs, windows[k + 1])
            for g in range(GROUPS):
                sheared[g].append(
                    pltpu.roll(
                        product[32 * g : 32 * g + 32], TILE - 31, 1, stride=1, stride_axis=0
                    )
                )
        after = side_t[:EDGE]
        before = side_t[TILE - EDGE :]
        lhs_after = jnp.concatenate(
            [jnp.where(m[:EDGE], after, 0.0) for m in group_masks], axis=0
        ).astype(bf16)
        lhs_before = jnp.concatenate(
            [jnp.where(m[:EDGE], before, 0.0) for m in group_masks], axis=0
        ).astype(bf16)
        product_after = dot(lhs_after, windows[5])
        product_before = dot(lhs_before, windows[0])
        sides = []
        for g in range(GROUPS):
            part = jnp.concatenate(sheared[g], axis=0).T * (1.0 / per_group)
            wide[b, pl.ds(GROUPS + g, DISPS, stride=GROUPS), :] = part[:DISPS]
            sides.append(
                pltpu.roll(
                    product_after[EDGE * g : EDGE * g + EDGE], TILE - 31, 1, stride=1, stride_axis=0
                )
            )
            sides.append(
                pltpu.roll(
                    product_before[EDGE * g : EDGE * g + EDGE],
                    TILE - 31 + 32 - EDGE,
                    1,
                    stride=1,
                    stride_axis=0,
                )
            )
        part = jnp.concatenate(sides, axis=0).T[:DISPS] * (1.0 / per_group)
        for g in range(GROUPS):
            extra[b, pl.ds(GROUPS + g, DISPS, stride=GROUPS), :] = (
                part if g == 0 else pltpu.roll(part, TILE - 2 * EDGE * g, 1)
            )

    lane8 = lax.broadcasted_iota(jnp.int32, (OUT_SLAB, TILE), 1)
    group_at = lax.broadcasted_iota(jnp.int32, (GROUPS, TILE), 0)
    gains = jnp.zeros((GROUPS, TILE), f32)
    for g in range(GROUPS):
        gains = jnp.where(group_at == g, gain[g], gains)
    wanted = [jnp.broadcast_to(indices[t : t + 1, :], (GROUPS, TILE)) for t in range(ITERS)]
    found = [jnp.zeros((GROUPS, TILE), f32) for _ in range(ITERS)]
    for q in range(DISPS // BLOCK):
        at = q * OUT_SLAB
        slabs = []
        for b in range(3):
            slabs.append(
                jnp.concatenate(
                    [wide[b, at : at + SLAB, :], extra[b, at : at + SLAB, :]], axis=1
                ).astype(bf16)
            )
        product = dot(taps[...], jnp.concatenate(slabs, axis=0))
        first, middle, last = (
            product[:OUT_SLAB],
            product[OUT_SLAB : 2 * OUT_SLAB],
            product[2 * OUT_SLAB :],
        )
        conv = (
            middle[:, :TILE]
            + jnp.where(
                lane8 == 0,
                pltpu.roll(first[:, TILE:], TILE - 2 * EDGE + 1, 1),
                pltpu.roll(first[:, :TILE], 1, 1),
            )
            + jnp.where(
                lane8 == TILE - 1,
                pltpu.roll(last[:, TILE:], TILE - 1, 1),
                pltpu.roll(last[:, :TILE], TILE - 1, 1),
            )
        )
        raw = wide[1, at + GROUPS : at + GROUPS + OUT_SLAB, :].astype(bf16).astype(f32)
        volume = (raw + jnp.maximum(conv, 0.0)).astype(bf16).astype(f32)
        volume = volume.reshape(BLOCK, GROUPS, TILE)
        logit[q * BLOCK : (q + 1) * BLOCK, :] = jnp.sum(volume * gains[None], axis=1)
        for d in range(BLOCK):
            for t in range(ITERS):
                found[t] = found[t] + jnp.where(wanted[t] == q * BLOCK + d, volume[d], 0.0)

    level = lax.broadcasted_iota(jnp.int32, (DISPS, TILE), 0)
    valid = level < limit[...]
    masked = jnp.where(valid, logit[...], floor_logit)
    top = jnp.max(masked, axis=0, keepdims=True)
    weights = jnp.where(valid, jnp.exp(masked - top), 0.0)
    moment = jnp.sum(weights * level.astype(f32), axis=0, keepdims=True)
    start = moment / jnp.sum(weights, axis=0, keepdims=True) / pixel_unit
    high = start.astype(bf16).astype(f32)
    low = (start - high).astype(bf16).astype(f32)
    ends = jnp.where(
        group_at == 0,
        jnp.broadcast_to(high, (GROUPS, TILE)),
        jnp.where(group_at == 1, jnp.broadcast_to(low, (GROUPS, TILE)), 0.0),
    )
    packed = jnp.concatenate(found + [ends], axis=0).astype(bf16)
    for i in range(out.shape[0]):
        out[i] = packed


def spot(place, r):
    band, bands = place[0], place[2]
    row = band - REACH + r
    return jnp.clip(row, 0, bands - 1), ((row >= 0) & (row < bands)).astype(f32)


def column_inside(place):
    column = lax.broadcasted_iota(jnp.int32, (SPAN, HID_CH), 0)
    has_left = (place[1] > 0).astype(f32)
    has_right = (place[1] < place[3] - 1).astype(f32)
    return jnp.where(column < EDGE, has_left, jnp.where(column >= TILE + EDGE, has_right, 1.0))


def keep(line, target, at, values):
    length = values.shape[0]
    start = EDGE + at
    line[start : start + length, :] = values
    target[at : at + length, 0:HID_CH] = line[start - 1 : start - 1 + length, :].astype(bf16)
    target[at : at + length, HID_CH : 2 * HID_CH] = values.astype(bf16)
    target[at : at + length, 2 * HID_CH :] = line[start + 1 : start + 1 + length, :].astype(bf16)


def around(target, at, length):
    return [target[at + a * SPAN : at + a * SPAN + length, :] for a in (-1, 0, 1)]


def chunks(low, high, most):
    count = high - low + 1
    parts = -(-count // most)
    out = []
    for i in range(parts):
        size = count // parts + (1 if i < count % parts else 0)
        out.append((low, size))
        low += size
    return out


def first_conv_kernel(
    place, hidden_all, hidden_side, hid_weight, hidden_out, conv_out, line, taps
):
    last = hidden_side.shape[0] - 1
    column_ok = column_inside(place)
    line[...] = jnp.zeros_like(line)
    for r in range(ROWS):
        held, row_ok = spot(place, r)
        values = jnp.concatenate(
            [
                hidden_side[0, held, TILE - 16 :, :].astype(f32)[16 - EDGE :],
                hidden_all[held].astype(f32),
                hidden_side[last, held, :16, :].astype(f32)[:EDGE],
            ],
            axis=0,
        )
        values = values * (column_ok * row_ok)
        keep(line, taps, r * SPAN, values)
        hidden_out[r * SPAN : (r + 1) * SPAN, :] = values.astype(bf16)
    for r, count in chunks(1, ROWS - 2, 4):
        at, length = r * SPAN, count * SPAN
        lhs = jnp.concatenate(around(taps, at, length), axis=1)
        conv_out[at - SPAN : at - SPAN + length, :] = dot(lhs, hid_weight[:, : 2 * HID_CH])


def refine_kernel(
    place,
    packed_all,
    packed_side,
    hidden_first,
    conv_first,
    hid_weight,
    in_weight,
    disparity_out,
    hidden_out,
    line,
    weight,
    looked,
    taps,
    reset_taps,
    gate,
    inputs,
    level,
    sems,
):
    weight_copies = [
        pltpu.make_async_copy(hid_weight, weight.at[pl.ds(0, 9 * HID_CH)], sems.at[0]),
        pltpu.make_async_copy(
            in_weight.at[pl.ds(0, 3 * HID_CH)], weight.at[pl.ds(9 * HID_CH, 3 * HID_CH)], sems.at[1]
        ),
    ]
    for copy in weight_copies:
        copy.start()

    column_ok = column_inside(place)
    has_left, has_right = column_ok[0:1, 0:1], column_ok[SPAN - 1 :, 0:1]
    lane = lax.broadcasted_iota(jnp.int32, (SPAN, HID_CH), 1)
    tap, channel = lane // PACK, lane % PACK
    at_sub = lax.broadcasted_iota(jnp.int32, (SPAN, 2 * TILE), 0)
    at_lane = lax.broadcasted_iota(jnp.int32, (SPAN, 2 * TILE), 1)
    spread = jnp.where(
        ((at_sub >= EDGE) & (at_lane == at_sub - EDGE))
        | ((at_sub < EDGE) & (at_lane == at_sub - EDGE + 2 * TILE)),
        1.0,
        0.0,
    ).astype(bf16)
    lane_pack = lax.broadcasted_iota(jnp.int32, (PACK, TILE), 1)

    last = packed_side.shape[0] - 1
    shifted = []
    for r in range(ROWS):
        held, row_ok = spot(place, r)
        centre = packed_all[held].astype(f32) * row_ok
        halo = jnp.where(
            lane_pack < TILE // 2,
            packed_side[last, held].astype(f32) * (has_right * row_ok),
            packed_side[0, held].astype(f32) * (has_left * row_ok),
        )
        both = jnp.concatenate([centre, halo], axis=1)
        shifted.append((pltpu.roll(both, 1, 1), both, pltpu.roll(both, 2 * TILE - 1, 1)))
    fill = jnp.zeros((PACK, 2 * TILE), f32)
    lines = [jnp.concatenate(shifted[r] + (fill,), axis=0).astype(bf16) for r in range(ROWS)]
    for r in range(0, ROWS, 2):
        pair = lines[r : r + 2]
        both = dot_nt(spread, jnp.concatenate(pair, axis=0))
        for i in range(len(pair)):
            looked[(r + i) * SPAN : (r + i + 1) * SPAN, :] = both[:, i * HID_CH : (i + 1) * HID_CH]
    sub = lax.broadcasted_iota(jnp.int32, (HID_CH, HID_CH), 0)
    ends = jnp.where((sub == PACK + 24) | (sub == PACK + 25), feature_scale, 0.0).astype(bf16)
    blank = jnp.zeros((EDGE, HID_CH), f32)
    level[:EDGE, :] = blank
    level[EDGE + ROWS * SPAN :, :] = blank
    level[EDGE : EDGE + ROWS * SPAN, :] = dot(looked[...].astype(bf16), ends)
    line[...] = jnp.zeros_like(line)
    head = in_weight[3 * HID_CH :, :HID_CH].astype(f32)[0:1] * feature_scale
    head = jnp.broadcast_to(head, (HID_CH, HID_CH)).astype(bf16)
    for copy in weight_copies:
        copy.wait()

    for t in range(ITERS):
        low, high = 1 + 2 * t, ROWS - 2 - 2 * t
        at_level = (channel == 3 * GROUPS) & (tap < 3)
        at_lookup = (channel >= t * GROUPS) & (channel < (t + 1) * GROUPS)
        for r in range(low - 1, high + 2):
            at = EDGE + r * SPAN
            value = jnp.where(
                tap == 0,
                level[at - 1 : at - 1 + SPAN, :],
                jnp.where(tap == 1, level[at : at + SPAN, :], level[at + 1 : at + 1 + SPAN, :]),
            )
            found = jnp.where(at_lookup, looked[r * SPAN : (r + 1) * SPAN, :], 0.0)
            inputs[r * SPAN : (r + 1) * SPAN, :] = jnp.where(at_level, value, found).astype(bf16)

        for r, count in chunks(low, high, 4):
            at, length = r * SPAN, count * SPAN
            if t == 0:
                both = conv_first[at - SPAN : at - SPAN + length, :] + dot(
                    jnp.concatenate(around(inputs, at, length), axis=1),
                    weight[9 * HID_CH :, : 2 * HID_CH],
                )
                hidden = hidden_first[at : at + length, :].astype(f32)
            else:
                lhs = around(taps, at, length) + around(inputs, at, length)
                both = dot(jnp.concatenate(lhs, axis=1), weight[:, : 2 * HID_CH])
                hidden = taps[at : at + length, HID_CH : 2 * HID_CH].astype(f32)
            both = 0.5 * jnp.tanh(0.5 * both) + 0.5
            gate[at : at + length, :] = both[:, :HID_CH]
            keep(line, reset_taps, at, both[:, HID_CH:] * hidden)
        for r, count in chunks(low + 1, high - 1, 4):
            at, length = r * SPAN, count * SPAN
            lhs = around(reset_taps, at, length) + around(inputs, at, length)
            candidate = jnp.tanh(dot(jnp.concatenate(lhs, axis=1), weight[:, 2 * HID_CH :]))
            update = gate[at : at + length, :]
            if t == 0:
                hidden = hidden_first[at : at + length, :].astype(f32)
            else:
                hidden = taps[at : at + length, HID_CH : 2 * HID_CH].astype(f32)
            hidden = (1.0 - update) * hidden + update * candidate
            mask = [column_ok * spot(place, r + i)[1] for i in range(count)]
            hidden = (hidden * jnp.concatenate(mask, axis=0)).astype(bf16)
            level[EDGE + at : EDGE + at + length, :] += dot_nt(hidden, head)
            if t < ITERS - 1:
                keep(line, taps, at, hidden.astype(f32))
            else:
                hidden_out[0] = hidden.astype(f32)[EDGE : EDGE + TILE].astype(bf16)
    at = EDGE + REACH * SPAN + EDGE
    disparity_out[...] = level[at : at + TILE, :].T[0:1] * (1.0 / feature_scale)


def to_sides(value):
    disps = lax.axis_size("disp")
    right = [(d, d + 1) for d in range(disps - 1)]
    left = [(d + 1, d) for d in range(disps - 1)]
    if disps == 2:
        return lax.ppermute(value, "disp", right + left)[None]
    return jnp.stack([lax.ppermute(value, "disp", right), lax.ppermute(value, "disp", left)])


def to_rows(value, shift):
    bands = lax.axis_size("band")
    return lax.ppermute(
        value, "band", [(i, shift(i)) for i in range(bands) if 0 <= shift(i) < bands]
    )


def odd_pair(i):
    return i ^ 1


def even_pair(i):
    return i - 1 if i % 2 == 0 else i + 1


def local(
    feat_left,
    feat_right,
    limit,
    indices,
    hidden_start,
    vol_kernel,
    group_gain,
    hid_kernel,
    in_kernel,
    head_weight,
):
    bands, disps = lax.axis_size("band"), lax.axis_size("disp")
    place = jnp.stack(
        [lax.axis_index("band"), lax.axis_index("disp"), jnp.int32(bands), jnp.int32(disps)]
    ).astype(jnp.int32)
    feats = jnp.concatenate([feat_left[0], feat_right[0]], axis=0)
    odd_own, even_own = to_rows(feats, odd_pair), to_rows(feats, even_pair)
    odd_own, even_own, hidden = lax.optimization_barrier((odd_own, even_own, hidden_start))
    across, odd_across, even_across = to_sides(feats), to_sides(odd_own), to_sides(even_own)
    hidden_all = lax.all_to_all(
        jnp.broadcast_to(hidden, (bands, TILE, HID_CH)), "band", 0, 0, tiled=True
    )

    lookup_rows, level_rows = in_kernel[:, :, :GROUPS], in_kernel[:, :, GROUPS:]
    in_weight = jnp.concatenate([lookup_rows] * ITERS + [level_rows], axis=2)
    in_weight = jnp.pad(in_weight, ((0, 0), (0, 1), (0, PACK - in_weight.shape[2]), (0, 0)))
    in_weight = jnp.concatenate(
        [
            in_weight.reshape(3 * HID_CH, 3 * HID_CH),
            jnp.pad(head_weight.reshape(1, HID_CH), ((0, 15), (0, 2 * HID_CH))),
        ],
        axis=0,
    )

    smem = pl.BlockSpec(memory_space=pltpu.SMEM)
    vmem = pl.BlockSpec(memory_space=pltpu.VMEM)
    anywhere = pl.BlockSpec(memory_space=pl.ANY)
    padded = (DISPS + 2) * GROUPS
    taps = pl.pallas_call(
        toeplitz_kernel,
        out_shape=jax.ShapeDtypeStruct((3 * OUT_SLAB, 3 * SLAB), bf16),
        in_specs=[vmem],
        out_specs=vmem,
        cost_estimate=pl.CostEstimate(flops=10**9, bytes_accessed=2**20, transcendentals=0),
    )(vol_kernel.reshape(27, GROUPS, GROUPS))
    packed = pl.pallas_call(
        volume_kernel,
        out_shape=jax.ShapeDtypeStruct((bands, PACK, TILE), bf16),
        in_specs=[smem, smem] + [vmem] * 9,
        out_specs=vmem,
        scratch_shapes=[
            pltpu.VMEM((3, padded, TILE), f32),
            pltpu.VMEM((3, padded, TILE), f32),
            pltpu.VMEM((DISPS, TILE), f32),
        ],
        compiler_params=pltpu.CompilerParams(vmem_limit_bytes=24 * 2**20),
        cost_estimate=pl.CostEstimate(
            flops=6 * 10**9, bytes_accessed=16 * 2**20, transcendentals=DISPS * TILE
        ),
    )(
        place, group_gain, feats, across, odd_own, odd_across, even_own, even_across,
        limit, indices[:, 0], taps,
    )

    packed, hidden_all = lax.optimization_barrier((packed, hidden_all))
    packed_all = lax.all_to_all(packed, "band", 0, 0, tiled=True)
    hidden_side = to_sides(hidden_all)
    area = ROWS * SPAN
    hid_weight = hid_kernel.reshape(9 * HID_CH, 3 * HID_CH)
    hidden_first, conv_first = pl.pallas_call(
        first_conv_kernel,
        out_shape=(
            jax.ShapeDtypeStruct((area, HID_CH), bf16),
            jax.ShapeDtypeStruct((area - 2 * SPAN, 2 * HID_CH), f32),
        ),
        in_specs=[smem] + [vmem] * 3,
        out_specs=(vmem, vmem),
        scratch_shapes=[
            pltpu.VMEM((area + 2 * EDGE, HID_CH), f32),
            pltpu.VMEM((area, 3 * HID_CH), bf16),
        ],
        compiler_params=pltpu.CompilerParams(vmem_limit_bytes=24 * 2**20),
        cost_estimate=pl.CostEstimate(
            flops=2 * 11 * SPAN * 9 * HID_CH * 2 * HID_CH, bytes_accessed=6 * 2**20, transcendentals=0
        ),
    )(place, hidden_all, hidden_side, hid_weight)
    packed_all, conv_first, in_weight = lax.optimization_barrier(
        (packed_all, conv_first, in_weight)
    )
    packed_side = to_sides(packed_all)
    disparity, hidden = pl.pallas_call(
        refine_kernel,
        out_shape=(
            jax.ShapeDtypeStruct((1, TILE), f32),
            jax.ShapeDtypeStruct((1, TILE, HID_CH), bf16),
        ),
        in_specs=[smem] + [vmem] * 4 + [anywhere, vmem],
        out_specs=(vmem, vmem),
        scratch_shapes=[
            pltpu.VMEM((area + 2 * EDGE, HID_CH), f32),
            pltpu.VMEM((12 * HID_CH, 3 * HID_CH), bf16),
            pltpu.VMEM((area, HID_CH), f32),
            pltpu.VMEM((area, 3 * HID_CH), bf16),
            pltpu.VMEM((area, 3 * HID_CH), bf16),
            pltpu.VMEM((area, HID_CH), f32),
            pltpu.VMEM((area, HID_CH), bf16),
            pltpu.VMEM((area + 2 * EDGE, HID_CH), f32),
            pltpu.SemaphoreType.DMA((2,)),
        ],
        compiler_params=pltpu.CompilerParams(vmem_limit_bytes=32 * 2**20),
    )(place, packed_all, packed_side, hidden_first, conv_first, hid_weight, in_weight)
    return (disparity, hidden)


def solution(mesh):
    in_specs = (
        P("band", None, "disp"),
        P("band", None, "disp"),
        P("band", "disp"),
        P(None, "band", "disp"),
        P("band", "disp", None),
        P(),
        P(),
        P(),
        P(),
        P(),
    )
    out_specs = (P("band", "disp"), P("band", "disp", None))
    return jax.shard_map(local, mesh=mesh, in_specs=in_specs, out_specs=out_specs, check_vma=False)
```

```python
import jax
import jax.numpy as jnp
from jax import lax
from jax.experimental import pallas as pl
from jax.experimental.pallas import tpu as pltpu
from jax.sharding import PartitionSpec as P

GROUPS = 8
DISPS = 96
FEAT_CH = 96
HID_CH = 128
ITERS = 3
TILE = 128
REACH = 2 * ITERS
EDGE = 8
SPAN = TILE + 2 * EDGE
ROWS = 2 * REACH + 1
PACK = 32
BLOCK = 8
SLAB = (BLOCK + 2) * GROUPS
OUT_SLAB = BLOCK * GROUPS

pixel_unit = 8.0
feature_scale = 0.25
floor_logit = -1e30

f32 = jnp.float32
bf16 = jnp.bfloat16


def dot(a, b):
    return jnp.dot(a, b, preferred_element_type=f32)


def dot_nt(a, b):
    return lax.dot_general(a, b, (((1,), (1,)), ((), ())), preferred_element_type=f32)


def copy_all(copies):
    for copy in copies:
        copy.start()
    for copy in copies:
        copy.wait()


def toeplitz(vol_kernel):
    size = 27 * GROUPS
    flat = vol_kernel[...].astype(f32).reshape(size, GROUPS)
    flat = jnp.concatenate([flat, jnp.zeros((size, TILE - GROUPS), f32)], axis=1).T[:GROUPS]
    row = lax.broadcasted_iota(jnp.int32, (9 * GROUPS, size), 0) >> 3
    tap = lax.broadcasted_iota(jnp.int32, (9 * GROUPS, size), 1) >> 3
    tap_a = (tap >= 9).astype(jnp.int32) + (tap >= 18).astype(jnp.int32)
    within = tap - 9 * tap_a
    tap_b = (within >= 3).astype(jnp.int32) + (within >= 6).astype(jnp.int32)
    tap_e = within - 3 * tap_b
    pairs = jnp.where(
        row == 3 * tap_a + tap_e, jnp.concatenate([flat] * 9, axis=0), 0.0
    ).astype(bf16)
    from_row = lax.broadcasted_iota(jnp.int32, (size, 3 * SLAB), 0)
    to = lax.broadcasted_iota(jnp.int32, (size, 3 * SLAB), 1)
    from_tap = from_row >> 3
    from_in = from_tap - 9 * ((from_tap >= 9).astype(jnp.int32) + (from_tap >= 18).astype(jnp.int32))
    from_b = (from_in >= 3).astype(jnp.int32) + (from_in >= 6).astype(jnp.int32)
    to_b = (to >= SLAB).astype(jnp.int32) + (to >= 2 * SLAB).astype(jnp.int32)
    repeat = jnp.where((from_b == to_b) & ((from_row & 7) == (to & 7)), 1.0, 0.0).astype(bf16)
    spread = dot(pairs, repeat)
    to = lax.broadcasted_iota(jnp.int32, (GROUPS, 3 * SLAB), 1)
    to_b = (to >= SLAB).astype(jnp.int32) + (to >= 2 * SLAB).astype(jnp.int32)
    to_d = (to - SLAB * to_b) >> 3
    rows = []
    for e in range(3):
        for d in range(BLOCK):
            value = jnp.zeros((GROUPS, 3 * SLAB), f32)
            for a in range(3):
                at = (3 * a + e) * GROUPS
                value = jnp.where(to_d == d + a, spread[at : at + GROUPS], value)
            rows.append(value)
    return jnp.concatenate(rows, axis=0).astype(bf16)


def correlate(lefts, rights, place, row_ok, wide, extra):
    has_left = (place[1] > 0).astype(f32)
    has_right = (place[1] < place[3] - 1).astype(f32)
    lane = lax.broadcasted_iota(jnp.int32, (TILE, TILE), 1)
    sub = lax.broadcasted_iota(jnp.int32, (TILE, TILE), 0)
    flip = jnp.where(lane + sub == TILE - 1, 1.0, 0.0).astype(bf16)
    per_group = FEAT_CH // GROUPS
    channel = lax.broadcasted_iota(jnp.int32, (32, FEAT_CH), 1)
    group_masks = [
        (channel >= g * per_group) & (channel < (g + 1) * per_group) for g in range(GROUPS)
    ]
    lane96 = lax.broadcasted_iota(jnp.int32, (FEAT_CH, TILE), 1)
    zero_slab = jnp.zeros((GROUPS, TILE), f32)
    for at in (0, (DISPS + 1) * GROUPS):
        wide[pl.ds(at, GROUPS), :] = zero_slab
        extra[pl.ds(at, GROUPS), :] = zero_slab

    own_t = (lefts[1] * row_ok).T
    side_t = jnp.where(
        lane96 < EDGE,
        lefts[2] * (has_right * row_ok),
        jnp.where(lane96 >= TILE - EDGE, lefts[0] * (has_left * row_ok), 0.0),
    ).T
    sources = jnp.concatenate([rights[2] * has_right, rights[1], rights[0] * has_left], axis=0)
    flipped = dot(sources.astype(bf16), flip)
    reverse = jnp.concatenate(
        [flipped[i * FEAT_CH : (i + 1) * FEAT_CH] for i in range(3)], axis=1
    )
    windows = [
        reverse[:, 2 * TILE - 32 - 32 * k : 3 * TILE - 32 - 32 * k].astype(bf16)
        for k in range(-1, 5)
    ]

    def by_group(rows):
        count = rows.shape[0]
        parts = [jnp.where(m[:count], rows, 0.0) for m in group_masks]
        return jnp.concatenate(parts, axis=0).astype(bf16)

    def shear(product, g, count, first):
        rows = product[count * g : count * g + count]
        return pltpu.roll(rows, TILE - 31 + first, 1, stride=1, stride_axis=0)

    products = [
        dot(by_group(own_t[32 * k : 32 * k + 32]), windows[k + 1]) for k in range(TILE // 32)
    ]
    after = dot(by_group(side_t[:EDGE]), windows[5])
    before = dot(by_group(side_t[TILE - EDGE :]), windows[0])
    sides = []
    for g in range(GROUPS):
        part = jnp.concatenate([shear(product, g, 32, 0) for product in products], axis=0)
        wide[pl.ds(GROUPS + g, DISPS, stride=GROUPS), :] = part.T[:DISPS] * (1.0 / per_group)
        sides += [shear(after, g, EDGE, 0), shear(before, g, EDGE, 32 - EDGE)]
    part = jnp.concatenate(sides, axis=0).T[:DISPS] * (1.0 / per_group)
    for g in range(GROUPS):
        extra[pl.ds(GROUPS + g, DISPS, stride=GROUPS), :] = (
            part if g == 0 else pltpu.roll(part, TILE - 2 * EDGE * g, 1)
        )


def own_row_kernel(place, own, across, vol_kernel, raw_out, taps_out, wide, extra):
    tiles = [across[0], own[...], across[across.shape[0] - 1]]
    tiles = [tile.astype(f32) for tile in tiles]
    correlate(
        [tile[:FEAT_CH] for tile in tiles], [tile[FEAT_CH:] for tile in tiles],
        place, 1.0, wide, extra,
    )
    raw_out[...] = jnp.concatenate([wide[...], extra[...]], axis=1).astype(bf16)
    taps_out[...] = toeplitz(vol_kernel)


def volume_kernel(
    place, gain, odd_own, odd_across, even_own, even_across, limit, indices, raw_own, taps_own,
    out, raw, taps, wide, extra, logit, sems,
):
    band, bands = place[0], place[2]
    is_even = band % 2 == 0
    copies = [
        pltpu.make_async_copy(raw_own, raw, sems.at[0]),
        pltpu.make_async_copy(taps_own, taps, sems.at[1]),
    ]
    for copy in copies:
        copy.start()

    last = odd_across.shape[0] - 1
    odd = [tile.astype(f32) for tile in (odd_across[0], odd_own[...], odd_across[last])]
    even = [tile.astype(f32) for tile in (even_across[0], even_own[...], even_across[last])]
    for b in range(2):
        row = band + 2 * b - 1
        row_ok = ((row >= 0) & (row < bands)).astype(f32)
        tiles = [
            jnp.where(is_even, y, x) if b == 0 else jnp.where(is_even, x, y)
            for x, y in zip(odd, even)
        ]
        correlate(
            [tile[:FEAT_CH] for tile in tiles], [tile[FEAT_CH:] for tile in tiles],
            place, row_ok, wide.at[b], extra.at[b],
        )
    for copy in copies:
        copy.wait()

    lane8 = lax.broadcasted_iota(jnp.int32, (OUT_SLAB, TILE), 1)
    group_at = lax.broadcasted_iota(jnp.int32, (GROUPS, TILE), 0)
    gains = jnp.zeros((GROUPS, TILE), f32)
    for g in range(GROUPS):
        gains = jnp.where(group_at == g, gain[g], gains)
    wanted = [jnp.broadcast_to(indices[t : t + 1, :], (GROUPS, TILE)) for t in range(ITERS)]
    found = [jnp.zeros((GROUPS, TILE), f32) for _ in range(ITERS)]
    for q in range(DISPS // BLOCK):
        at = q * OUT_SLAB
        slabs = [
            jnp.concatenate(
                [wide[b, at : at + SLAB, :], extra[b, at : at + SLAB, :]], axis=1
            ).astype(bf16)
            for b in range(2)
        ]
        slabs.insert(1, raw[at : at + SLAB, :])
        product = dot(taps[...], jnp.concatenate(slabs, axis=0))
        first, middle, last = (
            product[:OUT_SLAB],
            product[OUT_SLAB : 2 * OUT_SLAB],
            product[2 * OUT_SLAB :],
        )
        conv = (
            middle[:, :TILE]
            + jnp.where(
                lane8 == 0,
                pltpu.roll(first[:, TILE:], TILE - 2 * EDGE + 1, 1),
                pltpu.roll(first[:, :TILE], 1, 1),
            )
            + jnp.where(
                lane8 == TILE - 1,
                pltpu.roll(last[:, TILE:], TILE - 1, 1),
                pltpu.roll(last[:, :TILE], TILE - 1, 1),
            )
        )
        centre = slabs[1][:, :TILE].astype(f32)[GROUPS : GROUPS + OUT_SLAB]
        volume = (centre + jnp.maximum(conv, 0.0)).astype(bf16).astype(f32)
        volume = volume.reshape(BLOCK, GROUPS, TILE)
        logit[q * BLOCK : (q + 1) * BLOCK, :] = jnp.sum(volume * gains[None], axis=1)
        for d in range(BLOCK):
            for t in range(ITERS):
                found[t] = found[t] + jnp.where(wanted[t] == q * BLOCK + d, volume[d], 0.0)

    level = lax.broadcasted_iota(jnp.int32, (DISPS, TILE), 0)
    valid = level < limit[...]
    masked = jnp.where(valid, logit[...], floor_logit)
    top = jnp.max(masked, axis=0, keepdims=True)
    weights = jnp.where(valid, jnp.exp(masked - top), 0.0)
    moment = jnp.sum(weights * level.astype(f32), axis=0, keepdims=True)
    start = moment / jnp.sum(weights, axis=0, keepdims=True) / pixel_unit
    high = start.astype(bf16).astype(f32)
    low = (start - high).astype(bf16).astype(f32)
    ends = jnp.where(
        group_at == 0,
        jnp.broadcast_to(high, (GROUPS, TILE)),
        jnp.where(group_at == 1, jnp.broadcast_to(low, (GROUPS, TILE)), 0.0),
    )
    packed = jnp.concatenate(found + [ends], axis=0).astype(bf16)
    for i in range(out.shape[0]):
        out[i] = packed


def spot(place, r):
    band, bands = place[0], place[2]
    row = band - REACH + r
    return jnp.clip(row, 0, bands - 1), ((row >= 0) & (row < bands)).astype(f32)


def column_inside(place):
    column = lax.broadcasted_iota(jnp.int32, (SPAN, HID_CH), 0)
    has_left = (place[1] > 0).astype(f32)
    has_right = (place[1] < place[3] - 1).astype(f32)
    return jnp.where(column < EDGE, has_left, jnp.where(column >= TILE + EDGE, has_right, 1.0))


def keep(line, target, at, values):
    length = values.shape[0]
    start = EDGE + at
    line[start : start + length, :] = values
    target[at : at + length, 0:HID_CH] = line[start - 1 : start - 1 + length, :].astype(bf16)
    target[at : at + length, HID_CH : 2 * HID_CH] = values.astype(bf16)
    target[at : at + length, 2 * HID_CH :] = line[start + 1 : start + 1 + length, :].astype(bf16)


def around(target, at, length):
    return [target[at + a * SPAN : at + a * SPAN + length, :] for a in (-1, 0, 1)]


def chunks(low, high, most):
    count = high - low + 1
    parts = -(-count // most)
    out = []
    for i in range(parts):
        size = count // parts + (1 if i < count % parts else 0)
        out.append((low, size))
        low += size
    return out


def first_conv_kernel(place, hidden_all, hidden_side, hid_weight, out, line, taps, sides, sems):
    last = hidden_side.shape[0] - 1
    copies = [
        pltpu.make_async_copy(
            hidden_side.at[0, :, pl.ds(TILE - 16, 16)], sides.at[0], sems.at[0]
        ),
        pltpu.make_async_copy(hidden_side.at[last, :, pl.ds(0, 16)], sides.at[1], sems.at[1]),
    ]
    for copy in copies:
        copy.start()
    column_ok = column_inside(place)
    line[...] = jnp.zeros_like(line)
    for copy in copies:
        copy.wait()
    for r in range(ROWS):
        held, row_ok = spot(place, r)
        values = jnp.concatenate(
            [
                sides[0, held].astype(f32)[16 - EDGE :],
                hidden_all[held].astype(f32),
                sides[1, held].astype(f32)[:EDGE],
            ],
            axis=0,
        )
        values = values * (column_ok * row_ok)
        keep(line, taps, r * SPAN, values)
        if 1 <= r <= ROWS - 2:
            out[(r - 1) * SPAN : r * SPAN, 2 * HID_CH :] = values
    for r, count in chunks(1, ROWS - 2, 4):
        at, length = r * SPAN, count * SPAN
        lhs = jnp.concatenate(around(taps, at, length), axis=1)
        out[at - SPAN : at - SPAN + length, : 2 * HID_CH] = dot(
            lhs, hid_weight[:, : 2 * HID_CH]
        )


def refine_kernel(
    place,
    packed_all,
    packed_side,
    conv_first,
    hid_weight,
    in_weight,
    disparity_out,
    hidden_out,
    line,
    weight,
    looked,
    taps,
    reset_taps,
    gate,
    inputs,
    level,
    sems,
):
    weight_copies = [
        pltpu.make_async_copy(hid_weight, weight.at[pl.ds(0, 9 * HID_CH)], sems.at[0]),
        pltpu.make_async_copy(
            in_weight.at[pl.ds(0, HID_CH)], weight.at[pl.ds(9 * HID_CH, HID_CH)], sems.at[1]
        ),
    ]
    for copy in weight_copies:
        copy.start()

    column_ok = column_inside(place)
    has_left, has_right = column_ok[0:1, 0:1], column_ok[SPAN - 1 :, 0:1]
    tap = lax.broadcasted_iota(jnp.int32, (SPAN, HID_CH), 1) - 9 * GROUPS
    at_sub = lax.broadcasted_iota(jnp.int32, (SPAN, 2 * TILE), 0)
    at_lane = lax.broadcasted_iota(jnp.int32, (SPAN, 2 * TILE), 1)
    spread = jnp.where(
        ((at_sub >= EDGE) & (at_lane == at_sub - EDGE))
        | ((at_sub < EDGE) & (at_lane == at_sub - EDGE + 2 * TILE)),
        1.0,
        0.0,
    ).astype(bf16)
    lane_pack = lax.broadcasted_iota(jnp.int32, (PACK, TILE), 1)

    last = packed_side.shape[0] - 1
    shifted = []
    for r in range(ROWS):
        held, row_ok = spot(place, r)
        centre = packed_all[held].astype(f32) * row_ok
        halo = jnp.where(
            lane_pack < TILE // 2,
            packed_side[last, held].astype(f32) * (has_right * row_ok),
            packed_side[0, held].astype(f32) * (has_left * row_ok),
        )
        both = jnp.concatenate([centre, halo], axis=1)
        shifted.append((pltpu.roll(both, 1, 1), both, pltpu.roll(both, 2 * TILE - 1, 1)))
    levels = [
        [feature_scale * (x[3 * GROUPS : 3 * GROUPS + 1] + x[3 * GROUPS + 1 : 3 * GROUPS + 2])
         for x in shifted[r]]
        for r in range(ROWS)
    ]
    sub = lax.broadcasted_iota(jnp.int32, (16, 2 * TILE), 0)
    fill = jnp.zeros((HID_CH - 9 * GROUPS - 16, 2 * TILE), f32)

    def taken(t, r):
        pieces = []
        ends = jnp.zeros((16, 2 * TILE), f32)
        for a in range(3):
            for b in range(3):
                pieces.append(shifted[r + a - 1][b][t * GROUPS : (t + 1) * GROUPS])
                if t == 0:
                    ends = jnp.where(sub == 3 * a + b, levels[r + a - 1][b], ends)
        return jnp.concatenate(pieces + [ends, fill], axis=0).astype(bf16)

    wanted = [(t, r) for t in range(ITERS) for r in range(1 + 2 * t, ROWS - 1 - 2 * t)]
    for i in range(0, len(wanted), 2):
        pair = wanted[i : i + 2]
        both = dot_nt(spread, jnp.concatenate([taken(t, r) for t, r in pair], axis=0))
        for j, (t, r) in enumerate(pair):
            part = both[:, j * HID_CH : (j + 1) * HID_CH]
            if t == 0:
                inputs[r * SPAN : (r + 1) * SPAN, :] = part.astype(bf16)
            else:
                looked[t - 1, r * SPAN : (r + 1) * SPAN, :] = part
    blank = jnp.zeros((EDGE, HID_CH), f32)
    level[EDGE + 2 * SPAN - EDGE : EDGE + 2 * SPAN, :] = blank
    level[EDGE + (ROWS - 2) * SPAN : EDGE + (ROWS - 2) * SPAN + EDGE, :] = blank
    twice = jnp.concatenate([spread, spread], axis=1)
    for r in range(2, ROWS - 2, 2):
        pair = range(r, min(r + 2, ROWS - 2))
        ends = [
            jnp.concatenate(
                [
                    jnp.broadcast_to(shifted[i][1][at : at + 1], (HID_CH, 2 * TILE))
                    for at in (3 * GROUPS, 3 * GROUPS + 1)
                ],
                axis=1,
            )
            for i in pair
        ]
        both = dot_nt(twice, (feature_scale * jnp.concatenate(ends, axis=0)).astype(bf16))
        for j, i in enumerate(pair):
            level[EDGE + i * SPAN : EDGE + (i + 1) * SPAN, :] = both[
                :, j * HID_CH : (j + 1) * HID_CH
            ]
    line[...] = jnp.zeros_like(line)
    head = in_weight[HID_CH:, :HID_CH].astype(f32)[0:1] * feature_scale
    head = jnp.broadcast_to(head, (HID_CH, HID_CH)).astype(bf16)
    for copy in weight_copies:
        copy.wait()

    for t in range(ITERS):
        low, high = 1 + 2 * t, ROWS - 2 - 2 * t
        if t > 0:
            spread_level = {}
            for r in range(low - 1, high + 2):
                at = EDGE + r * SPAN
                spread_level[r] = jnp.where(
                    tap % 3 == 0,
                    level[at - 1 : at - 1 + SPAN, :],
                    jnp.where(
                        tap % 3 == 1, level[at : at + SPAN, :], level[at + 1 : at + 1 + SPAN, :]
                    ),
                )
            for r in range(low, high + 1):
                value = looked[t - 1, r * SPAN : (r + 1) * SPAN, :]
                for a in range(3):
                    value = jnp.where(
                        (tap >= 3 * a) & (tap < 3 * a + 3), spread_level[r + a - 1], value
                    )
                inputs[r * SPAN : (r + 1) * SPAN, :] = value.astype(bf16)

        def held(at, length):
            if t == 0:
                return conv_first[at - SPAN : at - SPAN + length, 2 * HID_CH :]
            return taps[at : at + length, HID_CH : 2 * HID_CH].astype(f32)

        for r, count in chunks(low, high, 4):
            at, length = r * SPAN, count * SPAN
            if t == 0:
                both = conv_first[at - SPAN : at - SPAN + length, : 2 * HID_CH] + dot(
                    inputs[at : at + length, :], weight[9 * HID_CH :, : 2 * HID_CH]
                )
            else:
                lhs = around(taps, at, length) + [inputs[at : at + length, :]]
                both = dot(jnp.concatenate(lhs, axis=1), weight[:, : 2 * HID_CH])
            skip, until = (SPAN if r == low else 0), (SPAN if r + count - 1 == high else 0)
            update = both[skip : length - until, :HID_CH]
            gate[at + skip : at + length - until, :] = 0.5 * jnp.tanh(0.5 * update) + 0.5
            reset = 0.5 * jnp.tanh(0.5 * both[:, HID_CH:]) + 0.5
            keep(line, reset_taps, at, reset * held(at, length))
        for r, count in chunks(low + 1, high - 1, 4):
            at, length = r * SPAN, count * SPAN
            lhs = around(reset_taps, at, length) + [inputs[at : at + length, :]]
            candidate = jnp.tanh(dot(jnp.concatenate(lhs, axis=1), weight[:, 2 * HID_CH :]))
            hidden = held(at, length)
            hidden = hidden + gate[at : at + length, :] * (candidate - hidden)
            mask = [column_ok * spot(place, r + i)[1] for i in range(count)]
            hidden = (hidden * jnp.concatenate(mask, axis=0)).astype(bf16)
            level[EDGE + at : EDGE + at + length, :] += dot_nt(hidden, head)
            if t < ITERS - 1:
                keep(line, taps, at, hidden.astype(f32))
            else:
                hidden_out[0] = hidden.astype(f32)[EDGE : EDGE + TILE].astype(bf16)
    at = EDGE + REACH * SPAN + EDGE
    disparity_out[...] = level[at : at + TILE, :].T[0:1] * (1.0 / feature_scale)


def to_sides(value):
    disps = lax.axis_size("disp")
    right = [(d, d + 1) for d in range(disps - 1)]
    left = [(d + 1, d) for d in range(disps - 1)]
    if disps == 2:
        return lax.ppermute(value, "disp", right + left)[None]
    return jnp.stack([lax.ppermute(value, "disp", right), lax.ppermute(value, "disp", left)])


def to_rows(value, shift):
    bands = lax.axis_size("band")
    return lax.ppermute(
        value, "band", [(i, shift(i)) for i in range(bands) if 0 <= shift(i) < bands]
    )


def odd_pair(i):
    return i ^ 1


def even_pair(i):
    return i - 1 if i % 2 == 0 else i + 1


def local(
    feat_left,
    feat_right,
    limit,
    indices,
    hidden_start,
    vol_kernel,
    group_gain,
    hid_kernel,
    in_kernel,
    head_weight,
):
    bands, disps = lax.axis_size("band"), lax.axis_size("disp")
    place = jnp.stack(
        [lax.axis_index("band"), lax.axis_index("disp"), jnp.int32(bands), jnp.int32(disps)]
    ).astype(jnp.int32)
    smem = pl.BlockSpec(memory_space=pltpu.SMEM)
    vmem = pl.BlockSpec(memory_space=pltpu.VMEM)
    hbm = pl.BlockSpec(memory_space=pltpu.HBM)
    anywhere = pl.BlockSpec(memory_space=pl.ANY)
    padded = (DISPS + 2) * GROUPS

    feats = jnp.concatenate([feat_left[0], feat_right[0]], axis=0)
    odd_own, even_own = to_rows(feats, odd_pair), to_rows(feats, even_pair)
    across = to_sides(feats)
    raw_own, taps = pl.pallas_call(
        own_row_kernel,
        out_shape=(
            jax.ShapeDtypeStruct((padded, 2 * TILE), bf16),
            jax.ShapeDtypeStruct((3 * OUT_SLAB, 3 * SLAB), bf16),
        ),
        in_specs=[smem, vmem, vmem, vmem],
        out_specs=(vmem, vmem),
        scratch_shapes=[pltpu.VMEM((padded, TILE), f32), pltpu.VMEM((padded, TILE), f32)],
        compiler_params=pltpu.CompilerParams(vmem_limit_bytes=16 * 2**20),
        cost_estimate=pl.CostEstimate(flops=2 * 10**9, bytes_accessed=4 * 2**20, transcendentals=0),
    )(place, feats, across, vol_kernel.reshape(27, GROUPS, GROUPS))
    hidden = jnp.broadcast_to(hidden_start, (bands, TILE, HID_CH))
    odd_own, even_own, hidden, raw_own, taps = lax.optimization_barrier(
        (odd_own, even_own, hidden, raw_own, taps)
    )
    odd_across, even_across = to_sides(odd_own), to_sides(even_own)
    hidden_all = lax.all_to_all(hidden, "band", 0, 0, tiled=True)

    in_weight = jnp.concatenate(
        [
            in_kernel[:, :, :GROUPS].reshape(9 * GROUPS, 3 * HID_CH),
            in_kernel[:, :, GROUPS].reshape(9, 3 * HID_CH),
            jnp.zeros((HID_CH - 9 * (GROUPS + 1), 3 * HID_CH), bf16),
            jnp.pad(head_weight.reshape(1, HID_CH), ((0, 15), (0, 2 * HID_CH))),
        ],
        axis=0,
    )

    packed = pl.pallas_call(
        volume_kernel,
        out_shape=jax.ShapeDtypeStruct((bands, PACK, TILE), bf16),
        in_specs=[smem, smem] + [vmem] * 6 + [hbm, hbm],
        out_specs=vmem,
        scratch_shapes=[
            pltpu.VMEM((padded, 2 * TILE), bf16),
            pltpu.VMEM((3 * OUT_SLAB, 3 * SLAB), bf16),
            pltpu.VMEM((2, padded, TILE), f32),
            pltpu.VMEM((2, padded, TILE), f32),
            pltpu.VMEM((DISPS, TILE), f32),
            pltpu.SemaphoreType.DMA((2,)),
        ],
        compiler_params=pltpu.CompilerParams(vmem_limit_bytes=24 * 2**20),
        cost_estimate=pl.CostEstimate(
            flops=5 * 10**9, bytes_accessed=16 * 2**20, transcendentals=DISPS * TILE
        ),
    )(
        place, group_gain, odd_own, odd_across, even_own, even_across,
        limit, indices[:, 0], raw_own, taps,
    )

    packed, hidden_all = lax.optimization_barrier((packed, hidden_all))
    packed_all = lax.all_to_all(packed, "band", 0, 0, tiled=True)
    hidden_side = to_sides(hidden_all)
    area = ROWS * SPAN
    hid_weight = hid_kernel.reshape(9 * HID_CH, 3 * HID_CH)
    conv_first = pl.pallas_call(
        first_conv_kernel,
        out_shape=jax.ShapeDtypeStruct((area - 2 * SPAN, 3 * HID_CH), f32),
        in_specs=[smem, vmem, hbm, vmem],
        out_specs=vmem,
        scratch_shapes=[
            pltpu.VMEM((area + 2 * EDGE, HID_CH), f32),
            pltpu.VMEM((area, 3 * HID_CH), bf16),
            pltpu.VMEM((2, bands, 16, HID_CH), bf16),
            pltpu.SemaphoreType.DMA((2,)),
        ],
        compiler_params=pltpu.CompilerParams(vmem_limit_bytes=24 * 2**20),
        cost_estimate=pl.CostEstimate(
            flops=2 * 11 * SPAN * 9 * HID_CH * 2 * HID_CH, bytes_accessed=6 * 2**20, transcendentals=0
        ),
    )(place, hidden_all, hidden_side, hid_weight)
    packed_all, conv_first, in_weight = lax.optimization_barrier(
        (packed_all, conv_first, in_weight)
    )
    packed_side = to_sides(packed_all)
    disparity, hidden = pl.pallas_call(
        refine_kernel,
        out_shape=(
            jax.ShapeDtypeStruct((1, TILE), f32),
            jax.ShapeDtypeStruct((1, TILE, HID_CH), bf16),
        ),
        in_specs=[smem] + [vmem] * 3 + [anywhere, vmem],
        out_specs=(vmem, vmem),
        scratch_shapes=[
            pltpu.VMEM((area + 2 * EDGE, HID_CH), f32),
            pltpu.VMEM((10 * HID_CH, 3 * HID_CH), bf16),
            pltpu.VMEM((ITERS - 1, area, HID_CH), f32),
            pltpu.VMEM((area, 3 * HID_CH), bf16),
            pltpu.VMEM((area, 3 * HID_CH), bf16),
            pltpu.VMEM((area, HID_CH), f32),
            pltpu.VMEM((area, HID_CH), bf16),
            pltpu.VMEM((area + 2 * EDGE, HID_CH), f32),
            pltpu.SemaphoreType.DMA((2,)),
        ],
        compiler_params=pltpu.CompilerParams(vmem_limit_bytes=32 * 2**20),
    )(place, packed_all, packed_side, conv_first, hid_weight, in_weight)
    return (disparity, hidden)


def solution(mesh):
    in_specs = (
        P("band", None, "disp"),
        P("band", None, "disp"),
        P("band", "disp"),
        P(None, "band", "disp"),
        P("band", "disp", None),
        P(),
        P(),
        P(),
        P(),
        P(),
    )
    out_specs = (P("band", "disp"), P("band", "disp", None))
    return jax.shard_map(local, mesh=mesh, in_specs=in_specs, out_specs=out_specs, check_vma=False)
```

```python
import jax
import jax.numpy as jnp
from jax import lax
from jax.experimental import pallas as pl
from jax.experimental.pallas import tpu as pltpu
from jax.sharding import PartitionSpec as P

GROUPS = 8
DISPS = 96
FEAT_CH = 96
HID_CH = 128
ITERS = 3
TILE = 128
REACH = 2 * ITERS
EDGE = 8
SPAN = TILE + 2 * EDGE
ROWS = 2 * REACH + 1
PACK = 32
BLOCK = 8
SLAB = (BLOCK + 2) * GROUPS
OUT_SLAB = BLOCK * GROUPS

pixel_unit = 8.0
feature_scale = 0.25
floor_logit = -1e30

f32 = jnp.float32
bf16 = jnp.bfloat16


def dot(a, b):
    return jnp.dot(a, b, preferred_element_type=f32)


def dot_nt(a, b):
    return lax.dot_general(a, b, (((1,), (1,)), ((), ())), preferred_element_type=f32)


def copy_all(copies):
    for copy in copies:
        copy.start()
    for copy in copies:
        copy.wait()


def toeplitz(vol_kernel):
    size = 27 * GROUPS
    flat = vol_kernel[...].astype(f32).reshape(size, GROUPS)
    flat = jnp.concatenate([flat, jnp.zeros((size, TILE - GROUPS), f32)], axis=1).T[:GROUPS]
    row = lax.broadcasted_iota(jnp.int32, (9 * GROUPS, size), 0) >> 3
    tap = lax.broadcasted_iota(jnp.int32, (9 * GROUPS, size), 1) >> 3
    tap_a = (tap >= 9).astype(jnp.int32) + (tap >= 18).astype(jnp.int32)
    within = tap - 9 * tap_a
    tap_b = (within >= 3).astype(jnp.int32) + (within >= 6).astype(jnp.int32)
    tap_e = within - 3 * tap_b
    pairs = jnp.where(
        row == 3 * tap_a + tap_e, jnp.concatenate([flat] * 9, axis=0), 0.0
    ).astype(bf16)
    from_row = lax.broadcasted_iota(jnp.int32, (size, 3 * SLAB), 0)
    to = lax.broadcasted_iota(jnp.int32, (size, 3 * SLAB), 1)
    from_tap = from_row >> 3
    from_in = from_tap - 9 * ((from_tap >= 9).astype(jnp.int32) + (from_tap >= 18).astype(jnp.int32))
    from_b = (from_in >= 3).astype(jnp.int32) + (from_in >= 6).astype(jnp.int32)
    to_b = (to >= SLAB).astype(jnp.int32) + (to >= 2 * SLAB).astype(jnp.int32)
    repeat = jnp.where((from_b == to_b) & ((from_row & 7) == (to & 7)), 1.0, 0.0).astype(bf16)
    spread = dot(pairs, repeat)
    to = lax.broadcasted_iota(jnp.int32, (GROUPS, 3 * SLAB), 1)
    to_b = (to >= SLAB).astype(jnp.int32) + (to >= 2 * SLAB).astype(jnp.int32)
    to_d = (to - SLAB * to_b) >> 3
    rows = []
    for e in range(3):
        for d in range(BLOCK):
            value = jnp.zeros((GROUPS, 3 * SLAB), f32)
            for a in range(3):
                at = (3 * a + e) * GROUPS
                value = jnp.where(to_d == d + a, spread[at : at + GROUPS], value)
            rows.append(value)
    return jnp.concatenate(rows, axis=0).astype(bf16)


def correlate(lefts, rights, place, row_ok, wide, extra):
    has_left = (place[1] > 0).astype(f32)
    has_right = (place[1] < place[3] - 1).astype(f32)
    lane = lax.broadcasted_iota(jnp.int32, (TILE, TILE), 1)
    sub = lax.broadcasted_iota(jnp.int32, (TILE, TILE), 0)
    flip = jnp.where(lane + sub == TILE - 1, 1.0, 0.0).astype(bf16)
    per_group = FEAT_CH // GROUPS
    channel = lax.broadcasted_iota(jnp.int32, (32, FEAT_CH), 1)
    group_masks = [
        (channel >= g * per_group) & (channel < (g + 1) * per_group) for g in range(GROUPS)
    ]
    lane96 = lax.broadcasted_iota(jnp.int32, (FEAT_CH, TILE), 1)
    zero_slab = jnp.zeros((GROUPS, TILE), f32)
    for at in (0, (DISPS + 1) * GROUPS):
        wide[pl.ds(at, GROUPS), :] = zero_slab
        extra[pl.ds(at, GROUPS), :] = zero_slab

    own_t = (lefts[1] * row_ok).T
    side_t = jnp.where(
        lane96 < EDGE,
        lefts[2] * (has_right * row_ok),
        jnp.where(lane96 >= TILE - EDGE, lefts[0] * (has_left * row_ok), 0.0),
    ).T
    sources = jnp.concatenate([rights[2] * has_right, rights[1], rights[0] * has_left], axis=0)
    flipped = dot(sources.astype(bf16), flip)
    reverse = jnp.concatenate(
        [flipped[i * FEAT_CH : (i + 1) * FEAT_CH] for i in range(3)], axis=1
    )
    windows = [
        reverse[:, 2 * TILE - 32 - 32 * k : 3 * TILE - 32 - 32 * k].astype(bf16)
        for k in range(-1, 5)
    ]

    def by_group(rows):
        count = rows.shape[0]
        parts = [jnp.where(m[:count], rows, 0.0) for m in group_masks]
        return jnp.concatenate(parts, axis=0).astype(bf16)

    def shear(product, g, count, first):
        rows = product[count * g : count * g + count]
        return pltpu.roll(rows, TILE - 31 + first, 1, stride=1, stride_axis=0)

    products = [
        dot(by_group(own_t[32 * k : 32 * k + 32]), windows[k + 1]) for k in range(TILE // 32)
    ]
    after = dot(by_group(side_t[:EDGE]), windows[5])
    before = dot(by_group(side_t[TILE - EDGE :]), windows[0])
    sides = []
    for g in range(GROUPS):
        part = jnp.concatenate([shear(product, g, 32, 0) for product in products], axis=0)
        wide[pl.ds(GROUPS + g, DISPS, stride=GROUPS), :] = part.T[:DISPS] * (1.0 / per_group)
        sides += [shear(after, g, EDGE, 0), shear(before, g, EDGE, 32 - EDGE)]
    part = jnp.concatenate(sides, axis=0).T[:DISPS] * (1.0 / per_group)
    for g in range(GROUPS):
        extra[pl.ds(GROUPS + g, DISPS, stride=GROUPS), :] = (
            part if g == 0 else pltpu.roll(part, TILE - 2 * EDGE * g, 1)
        )


def own_row_kernel(place, own, across, vol_kernel, raw_out, taps_out, wide, extra, kernel, sem):
    copy = pltpu.make_async_copy(vol_kernel, kernel, sem.at[0])
    copy.start()
    tiles = [across[0], own[...], across[across.shape[0] - 1]]
    tiles = [tile.astype(f32) for tile in tiles]
    correlate(
        [tile[:FEAT_CH] for tile in tiles], [tile[FEAT_CH:] for tile in tiles],
        place, 1.0, wide, extra,
    )
    raw_out[...] = jnp.concatenate([wide[...], extra[...]], axis=1).astype(bf16)
    copy.wait()
    taps_out[...] = toeplitz(kernel)


def volume_kernel(
    place, gain, odd_own, odd_across, even_own, even_across, limit, indices, raw_own, taps_own,
    out, raw, taps, wide, extra, logit, sems,
):
    band, bands = place[0], place[2]
    is_even = band % 2 == 0
    copies = [
        pltpu.make_async_copy(raw_own, raw, sems.at[0]),
        pltpu.make_async_copy(taps_own, taps, sems.at[1]),
    ]
    for copy in copies:
        copy.start()

    last = odd_across.shape[0] - 1
    odd = [tile.astype(f32) for tile in (odd_across[0], odd_own[...], odd_across[last])]
    even = [tile.astype(f32) for tile in (even_across[0], even_own[...], even_across[last])]
    for b in range(2):
        row = band + 2 * b - 1
        row_ok = ((row >= 0) & (row < bands)).astype(f32)
        tiles = [
            jnp.where(is_even, y, x) if b == 0 else jnp.where(is_even, x, y)
            for x, y in zip(odd, even)
        ]
        correlate(
            [tile[:FEAT_CH] for tile in tiles], [tile[FEAT_CH:] for tile in tiles],
            place, row_ok, wide.at[b], extra.at[b],
        )
    for copy in copies:
        copy.wait()

    lane8 = lax.broadcasted_iota(jnp.int32, (OUT_SLAB, TILE), 1)
    group_at = lax.broadcasted_iota(jnp.int32, (GROUPS, TILE), 0)
    gains = jnp.zeros((GROUPS, TILE), f32)
    for g in range(GROUPS):
        gains = jnp.where(group_at == g, gain[g], gains)
    wanted = [jnp.broadcast_to(indices[t : t + 1, :], (GROUPS, TILE)) for t in range(ITERS)]
    found = [jnp.zeros((GROUPS, TILE), f32) for _ in range(ITERS)]
    for q in range(DISPS // BLOCK):
        at = q * OUT_SLAB
        slabs = [
            jnp.concatenate(
                [wide[b, at : at + SLAB, :], extra[b, at : at + SLAB, :]], axis=1
            ).astype(bf16)
            for b in range(2)
        ]
        slabs.insert(1, raw[at : at + SLAB, :])
        product = dot(taps[...], jnp.concatenate(slabs, axis=0))
        first, middle, last = (
            product[:OUT_SLAB],
            product[OUT_SLAB : 2 * OUT_SLAB],
            product[2 * OUT_SLAB :],
        )
        conv = (
            middle[:, :TILE]
            + jnp.where(
                lane8 == 0,
                pltpu.roll(first[:, TILE:], TILE - 2 * EDGE + 1, 1),
                pltpu.roll(first[:, :TILE], 1, 1),
            )
            + jnp.where(
                lane8 == TILE - 1,
                pltpu.roll(last[:, TILE:], TILE - 1, 1),
                pltpu.roll(last[:, :TILE], TILE - 1, 1),
            )
        )
        centre = slabs[1][:, :TILE].astype(f32)[GROUPS : GROUPS + OUT_SLAB]
        volume = (centre + jnp.maximum(conv, 0.0)).astype(bf16).astype(f32)
        volume = volume.reshape(BLOCK, GROUPS, TILE)
        logit[q * BLOCK : (q + 1) * BLOCK, :] = jnp.sum(volume * gains[None], axis=1)
        for d in range(BLOCK):
            for t in range(ITERS):
                found[t] = found[t] + jnp.where(wanted[t] == q * BLOCK + d, volume[d], 0.0)

    level = lax.broadcasted_iota(jnp.int32, (DISPS, TILE), 0)
    valid = level < limit[...]
    masked = jnp.where(valid, logit[...], floor_logit)
    top = jnp.max(masked, axis=0, keepdims=True)
    weights = jnp.where(valid, jnp.exp(masked - top), 0.0)
    moment = jnp.sum(weights * level.astype(f32), axis=0, keepdims=True)
    start = moment / jnp.sum(weights, axis=0, keepdims=True) / pixel_unit
    high = start.astype(bf16).astype(f32)
    low = (start - high).astype(bf16).astype(f32)
    ends = jnp.where(
        group_at == 0,
        jnp.broadcast_to(high, (GROUPS, TILE)),
        jnp.where(group_at == 1, jnp.broadcast_to(low, (GROUPS, TILE)), 0.0),
    )
    packed = jnp.concatenate(found + [ends], axis=0).astype(bf16)
    for i in range(out.shape[0]):
        out[i] = packed


def spot(place, r):
    band, bands = place[0], place[2]
    row = band - REACH + r
    return jnp.clip(row, 0, bands - 1), ((row >= 0) & (row < bands)).astype(f32)


def column_inside(place):
    column = lax.broadcasted_iota(jnp.int32, (SPAN, HID_CH), 0)
    has_left = (place[1] > 0).astype(f32)
    has_right = (place[1] < place[3] - 1).astype(f32)
    return jnp.where(column < EDGE, has_left, jnp.where(column >= TILE + EDGE, has_right, 1.0))


def keep(line, target, at, values):
    length = values.shape[0]
    start = EDGE + at
    line[start : start + length, :] = values
    target[at : at + length, 0:HID_CH] = line[start - 1 : start - 1 + length, :].astype(bf16)
    target[at : at + length, HID_CH : 2 * HID_CH] = values.astype(bf16)
    target[at : at + length, 2 * HID_CH :] = line[start + 1 : start + 1 + length, :].astype(bf16)


def around(target, at, length):
    return [target[at + a * SPAN : at + a * SPAN + length, :] for a in (-1, 0, 1)]


def chunks(low, high, most):
    count = high - low + 1
    parts = -(-count // most)
    out = []
    for i in range(parts):
        size = count // parts + (1 if i < count % parts else 0)
        out.append((low, size))
        low += size
    return out


def first_conv_kernel(place, hidden_all, hidden_side, hid_weight, out, line, taps, tiles, sides, sems):
    last = hidden_side.shape[0] - 1
    copies = [
        pltpu.make_async_copy(
            hidden_side.at[0, :, pl.ds(TILE - 16, 16)], sides.at[0], sems.at[0]
        ),
        pltpu.make_async_copy(hidden_side.at[last, :, pl.ds(0, 16)], sides.at[1], sems.at[1]),
        pltpu.make_async_copy(hidden_all, tiles, sems.at[2]),
    ]
    for copy in copies:
        copy.start()
    column_ok = column_inside(place)
    line[...] = jnp.zeros_like(line)
    for copy in copies:
        copy.wait()
    for r in range(ROWS):
        held, row_ok = spot(place, r)
        values = jnp.concatenate(
            [
                sides[0, held].astype(f32)[16 - EDGE :],
                tiles[held].astype(f32),
                sides[1, held].astype(f32)[:EDGE],
            ],
            axis=0,
        )
        values = values * (column_ok * row_ok)
        keep(line, taps, r * SPAN, values)
        if 1 <= r <= ROWS - 2:
            out[(r - 1) * SPAN : r * SPAN, 2 * HID_CH :] = values
    for r, count in chunks(1, ROWS - 2, 4):
        at, length = r * SPAN, count * SPAN
        lhs = jnp.concatenate(around(taps, at, length), axis=1)
        out[at - SPAN : at - SPAN + length, : 2 * HID_CH] = dot(
            lhs, hid_weight[:, : 2 * HID_CH]
        )


def refine_kernel(
    place,
    packed_all,
    packed_side,
    conv_first,
    hid_weight,
    in_weight,
    disparity_out,
    hidden_out,
    line,
    weight,
    head_row,
    looked,
    taps,
    reset_taps,
    gate,
    inputs,
    level,
    sems,
):
    weight_copies = [
        pltpu.make_async_copy(hid_weight, weight.at[pl.ds(0, 9 * HID_CH)], sems.at[0]),
        pltpu.make_async_copy(
            in_weight.at[pl.ds(0, HID_CH)], weight.at[pl.ds(9 * HID_CH, HID_CH)], sems.at[1]
        ),
        pltpu.make_async_copy(
            in_weight.at[pl.ds(HID_CH, 16), pl.ds(0, HID_CH)], head_row, sems.at[2]
        ),
    ]
    for copy in weight_copies:
        copy.start()

    column_ok = column_inside(place)
    has_left, has_right = column_ok[0:1, 0:1], column_ok[SPAN - 1 :, 0:1]
    tap = lax.broadcasted_iota(jnp.int32, (SPAN, HID_CH), 1) - 9 * GROUPS
    at_sub = lax.broadcasted_iota(jnp.int32, (SPAN, 2 * TILE), 0)
    at_lane = lax.broadcasted_iota(jnp.int32, (SPAN, 2 * TILE), 1)
    spread = jnp.where(
        ((at_sub >= EDGE) & (at_lane == at_sub - EDGE))
        | ((at_sub < EDGE) & (at_lane == at_sub - EDGE + 2 * TILE)),
        1.0,
        0.0,
    ).astype(bf16)
    lane_pack = lax.broadcasted_iota(jnp.int32, (PACK, TILE), 1)

    last = packed_side.shape[0] - 1
    shifted = []
    for r in range(ROWS):
        held, row_ok = spot(place, r)
        centre = packed_all[held].astype(f32) * row_ok
        halo = jnp.where(
            lane_pack < TILE // 2,
            packed_side[last, held].astype(f32) * (has_right * row_ok),
            packed_side[0, held].astype(f32) * (has_left * row_ok),
        )
        both = jnp.concatenate([centre, halo], axis=1)
        shifted.append((pltpu.roll(both, 1, 1), both, pltpu.roll(both, 2 * TILE - 1, 1)))
    levels = [
        [feature_scale * (x[3 * GROUPS : 3 * GROUPS + 1] + x[3 * GROUPS + 1 : 3 * GROUPS + 2])
         for x in shifted[r]]
        for r in range(ROWS)
    ]
    sub = lax.broadcasted_iota(jnp.int32, (16, 2 * TILE), 0)
    fill = jnp.zeros((HID_CH - 9 * GROUPS - 16, 2 * TILE), f32)

    def taken(t, r):
        pieces = []
        ends = jnp.zeros((16, 2 * TILE), f32)
        for a in range(3):
            for b in range(3):
                pieces.append(shifted[r + a - 1][b][t * GROUPS : (t + 1) * GROUPS])
                if t == 0:
                    ends = jnp.where(sub == 3 * a + b, levels[r + a - 1][b], ends)
        return jnp.concatenate(pieces + [ends, fill], axis=0).astype(bf16)

    wanted = [(t, r) for t in range(ITERS) for r in range(1 + 2 * t, ROWS - 1 - 2 * t)]
    for i in range(0, len(wanted), 2):
        pair = wanted[i : i + 2]
        both = dot_nt(spread, jnp.concatenate([taken(t, r) for t, r in pair], axis=0))
        for j, (t, r) in enumerate(pair):
            part = both[:, j * HID_CH : (j + 1) * HID_CH]
            if t == 0:
                inputs[r * SPAN : (r + 1) * SPAN, :] = part.astype(bf16)
            else:
                looked[t - 1, r * SPAN : (r + 1) * SPAN, :] = part
    blank = jnp.zeros((EDGE, HID_CH), f32)
    level[EDGE + 2 * SPAN - EDGE : EDGE + 2 * SPAN, :] = blank
    level[EDGE + (ROWS - 2) * SPAN : EDGE + (ROWS - 2) * SPAN + EDGE, :] = blank
    twice = jnp.concatenate([spread, spread], axis=1)
    for r in range(2, ROWS - 2, 2):
        pair = range(r, min(r + 2, ROWS - 2))
        ends = [
            jnp.concatenate(
                [
                    jnp.broadcast_to(shifted[i][1][at : at + 1], (HID_CH, 2 * TILE))
                    for at in (3 * GROUPS, 3 * GROUPS + 1)
                ],
                axis=1,
            )
            for i in pair
        ]
        both = dot_nt(twice, (feature_scale * jnp.concatenate(ends, axis=0)).astype(bf16))
        for j, i in enumerate(pair):
            level[EDGE + i * SPAN : EDGE + (i + 1) * SPAN, :] = both[
                :, j * HID_CH : (j + 1) * HID_CH
            ]
    line[...] = jnp.zeros_like(line)
    for copy in weight_copies:
        copy.wait()
    head = head_row[...].astype(f32)[0:1] * feature_scale
    head = jnp.broadcast_to(head, (HID_CH, HID_CH)).astype(bf16)

    for t in range(ITERS):
        low, high = 1 + 2 * t, ROWS - 2 - 2 * t
        if t > 0:
            spread_level = {}
            for r in range(low - 1, high + 2):
                at = EDGE + r * SPAN
                spread_level[r] = jnp.where(
                    tap % 3 == 0,
                    level[at - 1 : at - 1 + SPAN, :],
                    jnp.where(
                        tap % 3 == 1, level[at : at + SPAN, :], level[at + 1 : at + 1 + SPAN, :]
                    ),
                )
            for r in range(low, high + 1):
                value = looked[t - 1, r * SPAN : (r + 1) * SPAN, :]
                for a in range(3):
                    value = jnp.where(
                        (tap >= 3 * a) & (tap < 3 * a + 3), spread_level[r + a - 1], value
                    )
                inputs[r * SPAN : (r + 1) * SPAN, :] = value.astype(bf16)

        def held(at, length):
            if t == 0:
                return conv_first[at - SPAN : at - SPAN + length, 2 * HID_CH :]
            return taps[at : at + length, HID_CH : 2 * HID_CH].astype(f32)

        for r, count in chunks(low, high, 4):
            at, length = r * SPAN, count * SPAN
            if t == 0:
                both = conv_first[at - SPAN : at - SPAN + length, : 2 * HID_CH] + dot(
                    inputs[at : at + length, :], weight[9 * HID_CH :, : 2 * HID_CH]
                )
            else:
                lhs = around(taps, at, length) + [inputs[at : at + length, :]]
                both = dot(jnp.concatenate(lhs, axis=1), weight[:, : 2 * HID_CH])
            skip, until = (SPAN if r == low else 0), (SPAN if r + count - 1 == high else 0)
            update = both[skip : length - until, :HID_CH]
            gate[at + skip : at + length - until, :] = 0.5 * jnp.tanh(0.5 * update) + 0.5
            reset = 0.5 * jnp.tanh(0.5 * both[:, HID_CH:]) + 0.5
            keep(line, reset_taps, at, reset * held(at, length))
        for r, count in chunks(low + 1, high - 1, 4):
            at, length = r * SPAN, count * SPAN
            lhs = around(reset_taps, at, length) + [inputs[at : at + length, :]]
            candidate = jnp.tanh(dot(jnp.concatenate(lhs, axis=1), weight[:, 2 * HID_CH :]))
            hidden = held(at, length)
            hidden = hidden + gate[at : at + length, :] * (candidate - hidden)
            mask = [column_ok * spot(place, r + i)[1] for i in range(count)]
            hidden = (hidden * jnp.concatenate(mask, axis=0)).astype(bf16)
            level[EDGE + at : EDGE + at + length, :] += dot_nt(hidden, head)
            if t < ITERS - 1:
                keep(line, taps, at, hidden.astype(f32))
            else:
                hidden_out[0] = hidden.astype(f32)[EDGE : EDGE + TILE].astype(bf16)
    at = EDGE + REACH * SPAN + EDGE
    disparity_out[...] = level[at : at + TILE, :].T[0:1] * (1.0 / feature_scale)


def in_hbm(value):
    return pltpu.with_memory_space_constraint(value, pltpu.HBM)


def to_sides(value):
    disps = lax.axis_size("disp")
    right = [(d, d + 1) for d in range(disps - 1)]
    left = [(d + 1, d) for d in range(disps - 1)]
    if disps == 2:
        return lax.ppermute(value, "disp", right + left)[None]
    return jnp.stack([lax.ppermute(value, "disp", right), lax.ppermute(value, "disp", left)])


def to_rows(value, shift):
    bands = lax.axis_size("band")
    return lax.ppermute(
        value, "band", [(i, shift(i)) for i in range(bands) if 0 <= shift(i) < bands]
    )


def odd_pair(i):
    return i ^ 1


def even_pair(i):
    return i - 1 if i % 2 == 0 else i + 1


def local(
    feat_left,
    feat_right,
    limit,
    indices,
    hidden_start,
    vol_kernel,
    group_gain,
    hid_kernel,
    in_kernel,
    head_weight,
):
    bands, disps = lax.axis_size("band"), lax.axis_size("disp")
    place = jnp.stack(
        [lax.axis_index("band"), lax.axis_index("disp"), jnp.int32(bands), jnp.int32(disps)]
    ).astype(jnp.int32)
    smem = pl.BlockSpec(memory_space=pltpu.SMEM)
    vmem = pl.BlockSpec(memory_space=pltpu.VMEM)
    hbm = pl.BlockSpec(memory_space=pltpu.HBM)
    anywhere = pl.BlockSpec(memory_space=pl.ANY)
    padded = (DISPS + 2) * GROUPS

    feats = jnp.concatenate([feat_left[0], feat_right[0]], axis=0)
    odd_own, even_own = to_rows(feats, odd_pair), to_rows(feats, even_pair)
    across = to_sides(feats)
    raw_own, taps = pl.pallas_call(
        own_row_kernel,
        out_shape=(
            jax.ShapeDtypeStruct((padded, 2 * TILE), bf16),
            jax.ShapeDtypeStruct((3 * OUT_SLAB, 3 * SLAB), bf16),
        ),
        in_specs=[smem, vmem, vmem, hbm],
        out_specs=(vmem, vmem),
        scratch_shapes=[
            pltpu.VMEM((padded, TILE), f32),
            pltpu.VMEM((padded, TILE), f32),
            pltpu.VMEM((27, GROUPS, GROUPS), bf16),
            pltpu.SemaphoreType.DMA((1,)),
        ],
        compiler_params=pltpu.CompilerParams(vmem_limit_bytes=16 * 2**20),
        cost_estimate=pl.CostEstimate(flops=2 * 10**9, bytes_accessed=4 * 2**20, transcendentals=0),
    )(place, feats, across, in_hbm(vol_kernel.reshape(27, GROUPS, GROUPS)))
    hidden = jnp.broadcast_to(hidden_start, (bands, TILE, HID_CH))
    odd_own, even_own, hidden = lax.optimization_barrier((odd_own, even_own, hidden))
    odd_across, even_across = to_sides(odd_own), to_sides(even_own)
    hidden_all = lax.all_to_all(hidden, "band", 0, 0, tiled=True)

    in_weight = jnp.concatenate(
        [
            in_kernel[:, :, :GROUPS].reshape(9 * GROUPS, 3 * HID_CH),
            in_kernel[:, :, GROUPS].reshape(9, 3 * HID_CH),
            jnp.zeros((HID_CH - 9 * (GROUPS + 1), 3 * HID_CH), bf16),
            jnp.pad(head_weight.reshape(1, HID_CH), ((0, 15), (0, 2 * HID_CH))),
        ],
        axis=0,
    )

    packed = pl.pallas_call(
        volume_kernel,
        out_shape=jax.ShapeDtypeStruct((bands, PACK, TILE), bf16),
        in_specs=[smem, smem] + [vmem] * 6 + [hbm, hbm],
        out_specs=vmem,
        scratch_shapes=[
            pltpu.VMEM((padded, 2 * TILE), bf16),
            pltpu.VMEM((3 * OUT_SLAB, 3 * SLAB), bf16),
            pltpu.VMEM((2, padded, TILE), f32),
            pltpu.VMEM((2, padded, TILE), f32),
            pltpu.VMEM((DISPS, TILE), f32),
            pltpu.SemaphoreType.DMA((2,)),
        ],
        compiler_params=pltpu.CompilerParams(vmem_limit_bytes=24 * 2**20),
        cost_estimate=pl.CostEstimate(
            flops=5 * 10**9, bytes_accessed=16 * 2**20, transcendentals=DISPS * TILE
        ),
    )(
        place, group_gain, odd_own, odd_across, even_own, even_across,
        limit, indices[:, 0], raw_own, taps,
    )

    packed, hidden_all = lax.optimization_barrier((packed, hidden_all))
    packed_all = lax.all_to_all(packed, "band", 0, 0, tiled=True)
    hidden_side = to_sides(hidden_all)
    area = ROWS * SPAN
    hid_weight = hid_kernel.reshape(9 * HID_CH, 3 * HID_CH)
    conv_first = pl.pallas_call(
        first_conv_kernel,
        out_shape=jax.ShapeDtypeStruct((area - 2 * SPAN, 3 * HID_CH), f32),
        in_specs=[smem, hbm, hbm, vmem],
        out_specs=vmem,
        scratch_shapes=[
            pltpu.VMEM((area + 2 * EDGE, HID_CH), f32),
            pltpu.VMEM((area, 3 * HID_CH), bf16),
            pltpu.VMEM((bands, TILE, HID_CH), bf16),
            pltpu.VMEM((2, bands, 16, HID_CH), bf16),
            pltpu.SemaphoreType.DMA((3,)),
        ],
        compiler_params=pltpu.CompilerParams(vmem_limit_bytes=24 * 2**20),
        cost_estimate=pl.CostEstimate(
            flops=2 * 11 * SPAN * 9 * HID_CH * 2 * HID_CH, bytes_accessed=6 * 2**20, transcendentals=0
        ),
    )(place, in_hbm(hidden_all), in_hbm(hidden_side), hid_weight)
    packed_all, conv_first, in_weight = lax.optimization_barrier(
        (packed_all, conv_first, in_weight)
    )
    packed_side = to_sides(packed_all)
    disparity, hidden = pl.pallas_call(
        refine_kernel,
        out_shape=(
            jax.ShapeDtypeStruct((1, TILE), f32),
            jax.ShapeDtypeStruct((1, TILE, HID_CH), bf16),
        ),
        in_specs=[smem] + [vmem] * 3 + [anywhere, hbm],
        out_specs=(vmem, vmem),
        scratch_shapes=[
            pltpu.VMEM((area + 2 * EDGE, HID_CH), f32),
            pltpu.VMEM((10 * HID_CH, 3 * HID_CH), bf16),
            pltpu.VMEM((16, HID_CH), bf16),
            pltpu.VMEM((ITERS - 1, area, HID_CH), f32),
            pltpu.VMEM((area, 3 * HID_CH), bf16),
            pltpu.VMEM((area, 3 * HID_CH), bf16),
            pltpu.VMEM((area, HID_CH), f32),
            pltpu.VMEM((area, HID_CH), bf16),
            pltpu.VMEM((area + 2 * EDGE, HID_CH), f32),
            pltpu.SemaphoreType.DMA((3,)),
        ],
        compiler_params=pltpu.CompilerParams(vmem_limit_bytes=32 * 2**20),
    )(place, packed_all, packed_side, conv_first, hid_weight, in_hbm(in_weight))
    return (disparity, hidden)


def solution(mesh):
    in_specs = (
        P("band", None, "disp"),
        P("band", None, "disp"),
        P("band", "disp"),
        P(None, "band", "disp"),
        P("band", "disp", None),
        P(),
        P(),
        P(),
        P(),
        P(),
    )
    out_specs = (P("band", "disp"), P("band", "disp", None))
    return jax.shard_map(local, mesh=mesh, in_specs=in_specs, out_specs=out_specs, check_vma=False)
```

```python
import jax
import jax.numpy as jnp
from jax import lax
from jax.experimental import pallas as pl
from jax.experimental.pallas import tpu as pltpu
from jax.sharding import PartitionSpec as P

GROUPS = 8
DISPS = 96
FEAT_CH = 96
HID_CH = 128
ITERS = 3
TILE = 128
REACH = 2 * ITERS
EDGE = 8
WINDOW = 24
PACK = 32
BLOCK = 8
SLAB = (BLOCK + 2) * GROUPS
OUT_SLAB = BLOCK * GROUPS

pixel_unit = 8.0
feature_scale = 0.25
floor_logit = -1e30

f32 = jnp.float32
bf16 = jnp.bfloat16


def dot(a, b):
    return jnp.dot(a, b, preferred_element_type=f32)


def dot_nt(a, b):
    return lax.dot_general(a, b, (((1,), (1,)), ((), ())), preferred_element_type=f32)


def copy_all(copies):
    for copy in copies:
        copy.start()
    for copy in copies:
        copy.wait()


def toeplitz(vol_kernel):
    size = 27 * GROUPS
    flat = vol_kernel[...].astype(f32).reshape(size, GROUPS)
    flat = jnp.concatenate([flat, jnp.zeros((size, TILE - GROUPS), f32)], axis=1).T[:GROUPS]
    row = lax.broadcasted_iota(jnp.int32, (9 * GROUPS, size), 0) >> 3
    tap = lax.broadcasted_iota(jnp.int32, (9 * GROUPS, size), 1) >> 3
    tap_a = (tap >= 9).astype(jnp.int32) + (tap >= 18).astype(jnp.int32)
    within = tap - 9 * tap_a
    tap_b = (within >= 3).astype(jnp.int32) + (within >= 6).astype(jnp.int32)
    tap_e = within - 3 * tap_b
    pairs = jnp.where(
        row == 3 * tap_a + tap_e, jnp.concatenate([flat] * 9, axis=0), 0.0
    ).astype(bf16)
    from_row = lax.broadcasted_iota(jnp.int32, (size, 3 * SLAB), 0)
    to = lax.broadcasted_iota(jnp.int32, (size, 3 * SLAB), 1)
    from_tap = from_row >> 3
    from_in = from_tap - 9 * ((from_tap >= 9).astype(jnp.int32) + (from_tap >= 18).astype(jnp.int32))
    from_b = (from_in >= 3).astype(jnp.int32) + (from_in >= 6).astype(jnp.int32)
    to_b = (to >= SLAB).astype(jnp.int32) + (to >= 2 * SLAB).astype(jnp.int32)
    repeat = jnp.where((from_b == to_b) & ((from_row & 7) == (to & 7)), 1.0, 0.0).astype(bf16)
    spread = dot(pairs, repeat)
    to = lax.broadcasted_iota(jnp.int32, (GROUPS, 3 * SLAB), 1)
    to_b = (to >= SLAB).astype(jnp.int32) + (to >= 2 * SLAB).astype(jnp.int32)
    to_d = (to - SLAB * to_b) >> 3
    rows = []
    for e in range(3):
        for d in range(BLOCK):
            value = jnp.zeros((GROUPS, 3 * SLAB), f32)
            for a in range(3):
                at = (3 * a + e) * GROUPS
                value = jnp.where(to_d == d + a, spread[at : at + GROUPS], value)
            rows.append(value)
    return jnp.concatenate(rows, axis=0).astype(bf16)


def correlate(lefts, rights, place, row_ok, wide, extra):
    has_left = (place[1] > 0).astype(f32)
    has_right = (place[1] < place[3] - 1).astype(f32)
    lane = lax.broadcasted_iota(jnp.int32, (TILE, TILE), 1)
    sub = lax.broadcasted_iota(jnp.int32, (TILE, TILE), 0)
    flip = jnp.where(lane + sub == TILE - 1, 1.0, 0.0).astype(bf16)
    per_group = FEAT_CH // GROUPS
    channel = lax.broadcasted_iota(jnp.int32, (32, FEAT_CH), 1)
    group_masks = [
        (channel >= g * per_group) & (channel < (g + 1) * per_group) for g in range(GROUPS)
    ]
    lane96 = lax.broadcasted_iota(jnp.int32, (FEAT_CH, TILE), 1)
    zero_slab = jnp.zeros((GROUPS, TILE), f32)
    for at in (0, (DISPS + 1) * GROUPS):
        wide[pl.ds(at, GROUPS), :] = zero_slab
        extra[pl.ds(at, GROUPS), :] = zero_slab

    own_t = (lefts[1] * row_ok).T
    side_t = jnp.where(
        lane96 < EDGE,
        lefts[2] * (has_right * row_ok),
        jnp.where(lane96 >= TILE - EDGE, lefts[0] * (has_left * row_ok), 0.0),
    ).T
    sources = jnp.concatenate([rights[2] * has_right, rights[1], rights[0] * has_left], axis=0)
    flipped = dot(sources.astype(bf16), flip)
    reverse = jnp.concatenate(
        [flipped[i * FEAT_CH : (i + 1) * FEAT_CH] for i in range(3)], axis=1
    )
    windows = [
        reverse[:, 2 * TILE - 32 - 32 * k : 3 * TILE - 32 - 32 * k].astype(bf16)
        for k in range(-1, 5)
    ]

    def by_group(rows):
        count = rows.shape[0]
        parts = [jnp.where(m[:count], rows, 0.0) for m in group_masks]
        return jnp.concatenate(parts, axis=0).astype(bf16)

    def shear(product, g, count, first):
        rows = product[count * g : count * g + count]
        return pltpu.roll(rows, TILE - 31 + first, 1, stride=1, stride_axis=0)

    products = [
        dot(by_group(own_t[32 * k : 32 * k + 32]), windows[k + 1]) for k in range(TILE // 32)
    ]
    after = dot(by_group(side_t[:EDGE]), windows[5])
    before = dot(by_group(side_t[TILE - EDGE :]), windows[0])
    sides = []
    for g in range(GROUPS):
        part = jnp.concatenate([shear(product, g, 32, 0) for product in products], axis=0)
        wide[pl.ds(GROUPS + g, DISPS, stride=GROUPS), :] = part.T[:DISPS] * (1.0 / per_group)
        sides += [shear(after, g, EDGE, 0), shear(before, g, EDGE, 32 - EDGE)]
    part = jnp.concatenate(sides, axis=0).T[:DISPS] * (1.0 / per_group)
    for g in range(GROUPS):
        extra[pl.ds(GROUPS + g, DISPS, stride=GROUPS), :] = (
            part if g == 0 else pltpu.roll(part, TILE - 2 * EDGE * g, 1)
        )


def own_row_kernel(place, own, across, vol_kernel, raw_out, taps_out, wide, extra, kernel, sem):
    copy = pltpu.make_async_copy(vol_kernel, kernel, sem.at[0])
    copy.start()
    tiles = [across[0], own[...], across[across.shape[0] - 1]]
    tiles = [tile.astype(f32) for tile in tiles]
    correlate(
        [tile[:FEAT_CH] for tile in tiles], [tile[FEAT_CH:] for tile in tiles],
        place, 1.0, wide, extra,
    )
    raw_out[...] = jnp.concatenate([wide[...], extra[...]], axis=1).astype(bf16)
    copy.wait()
    taps_out[...] = toeplitz(kernel)


def volume_kernel(
    place, gain, odd_own, odd_across, even_own, even_across, limit, indices, hidden, raw_own,
    taps_own, out, raw, taps, wide, extra, logit, padded, sems,
):
    band, bands = place[0], place[2]
    is_even = band % 2 == 0
    copies = [
        pltpu.make_async_copy(raw_own, raw, sems.at[0]),
        pltpu.make_async_copy(taps_own, taps, sems.at[1]),
    ]
    for copy in copies:
        copy.start()

    last = odd_across.shape[0] - 1
    odd = [tile.astype(f32) for tile in (odd_across[0], odd_own[...], odd_across[last])]
    even = [tile.astype(f32) for tile in (even_across[0], even_own[...], even_across[last])]
    for b in range(2):
        row = band + 2 * b - 1
        row_ok = ((row >= 0) & (row < bands)).astype(f32)
        tiles = [
            jnp.where(is_even, y, x) if b == 0 else jnp.where(is_even, x, y)
            for x, y in zip(odd, even)
        ]
        correlate(
            [tile[:FEAT_CH] for tile in tiles], [tile[FEAT_CH:] for tile in tiles],
            place, row_ok, wide.at[b], extra.at[b],
        )
    for copy in copies:
        copy.wait()

    lane8 = lax.broadcasted_iota(jnp.int32, (OUT_SLAB, TILE), 1)
    group_at = lax.broadcasted_iota(jnp.int32, (GROUPS, TILE), 0)
    gains = jnp.zeros((GROUPS, TILE), f32)
    for g in range(GROUPS):
        gains = jnp.where(group_at == g, gain[g], gains)
    wanted = [jnp.broadcast_to(indices[t : t + 1, :], (GROUPS, TILE)) for t in range(ITERS)]
    found = [jnp.zeros((GROUPS, TILE), f32) for _ in range(ITERS)]
    for q in range(DISPS // BLOCK):
        at = q * OUT_SLAB
        slabs = [
            jnp.concatenate(
                [wide[b, at : at + SLAB, :], extra[b, at : at + SLAB, :]], axis=1
            ).astype(bf16)
            for b in range(2)
        ]
        slabs.insert(1, raw[at : at + SLAB, :])
        product = dot(taps[...], jnp.concatenate(slabs, axis=0))
        first, middle, last = (
            product[:OUT_SLAB],
            product[OUT_SLAB : 2 * OUT_SLAB],
            product[2 * OUT_SLAB :],
        )
        conv = (
            middle[:, :TILE]
            + jnp.where(
                lane8 == 0,
                pltpu.roll(first[:, TILE:], TILE - 2 * EDGE + 1, 1),
                pltpu.roll(first[:, :TILE], 1, 1),
            )
            + jnp.where(
                lane8 == TILE - 1,
                pltpu.roll(last[:, TILE:], TILE - 1, 1),
                pltpu.roll(last[:, :TILE], TILE - 1, 1),
            )
        )
        centre = slabs[1][:, :TILE].astype(f32)[GROUPS : GROUPS + OUT_SLAB]
        volume = (centre + jnp.maximum(conv, 0.0)).astype(bf16).astype(f32)
        volume = volume.reshape(BLOCK, GROUPS, TILE)
        logit[q * BLOCK : (q + 1) * BLOCK, :] = jnp.sum(volume * gains[None], axis=1)
        for d in range(BLOCK):
            for t in range(ITERS):
                found[t] = found[t] + jnp.where(wanted[t] == q * BLOCK + d, volume[d], 0.0)

    level = lax.broadcasted_iota(jnp.int32, (DISPS, TILE), 0)
    valid = level < limit[...]
    masked = jnp.where(valid, logit[...], floor_logit)
    top = jnp.max(masked, axis=0, keepdims=True)
    weights = jnp.where(valid, jnp.exp(masked - top), 0.0)
    moment = jnp.sum(weights * level.astype(f32), axis=0, keepdims=True)
    start = moment / jnp.sum(weights, axis=0, keepdims=True) / pixel_unit
    high = start.astype(bf16).astype(f32)
    low = (start - high).astype(bf16).astype(f32)
    ends = jnp.where(
        group_at == 0,
        jnp.broadcast_to(high, (GROUPS, TILE)),
        jnp.where(group_at == 1, jnp.broadcast_to(low, (GROUPS, TILE)), 0.0),
    )

    strip = TILE // out.shape[0]
    padded[:EDGE, :] = jnp.zeros((EDGE, HID_CH), f32)
    padded[EDGE : EDGE + TILE, :] = hidden[...].astype(f32)
    padded[EDGE + TILE :, :] = jnp.zeros((WINDOW - EDGE, HID_CH), f32)
    lane = lax.broadcasted_iota(jnp.int32, (GROUPS, TILE), 1)
    for j in range(out.shape[0]):
        part = jnp.zeros((GROUPS, TILE), f32)
        for q, group in enumerate(found + [ends]):
            moved = pltpu.roll(group, (PACK * q + EDGE - strip * j) % TILE, 1)
            part = jnp.where((lane >= PACK * q) & (lane < PACK * q + WINDOW), moved, part)
        block = [padded[strip * j : strip * j + WINDOW, :], part]
        out[j] = jnp.concatenate(block, axis=0).astype(bf16)


def keep(line, target, at, values, rows):
    length = values.shape[0]
    start = EDGE + at
    row = lax.broadcasted_iota(jnp.int32, (length, HID_CH), 0) % rows
    line[start : start + length, :] = values
    before = jnp.where(row == 0, 0.0, line[start - 1 : start - 1 + length, :])
    after = jnp.where(row == rows - 1, 0.0, line[start + 1 : start + 1 + length, :])
    target[at : at + length, 0:HID_CH] = before.astype(bf16)
    target[at : at + length, HID_CH : 2 * HID_CH] = values.astype(bf16)
    target[at : at + length, 2 * HID_CH :] = after.astype(bf16)


def refine_kernel(
    place,
    blocks,
    beside,
    hid_weight,
    in_weight,
    out,
    line,
    weight,
    head_row,
    looked,
    hidden_at,
    taps,
    reset_taps,
    in_taps,
    gate,
    level,
    sems,
):
    rows = blocks.shape[0]
    strip = TILE // rows
    copies = [
        pltpu.make_async_copy(
            hid_weight.at[pl.ds((3 * a + b) * HID_CH, HID_CH)],
            weight.at[pl.ds((3 * b + a) * HID_CH, HID_CH)],
            sems.at[3 * a + b],
        )
        for a in range(3)
        for b in range(3)
    ]
    copies.append(
        pltpu.make_async_copy(
            in_weight.at[pl.ds(0, 3 * HID_CH)],
            weight.at[pl.ds(9 * HID_CH, 3 * HID_CH)],
            sems.at[9],
        )
    )
    copies.append(
        pltpu.make_async_copy(
            in_weight.at[pl.ds(3 * HID_CH, 16), pl.ds(0, HID_CH)], head_row, sems.at[10]
        )
    )
    for copy in copies:
        copy.start()

    band, disp, bands, disps = place[0], place[1], place[2], place[3]
    reach = -(-REACH // strip)
    at_left = (band < reach) & (disp > 0)
    at_right = (band >= bands - reach) & (disp < disps - 1)
    off = strip * (2 * jnp.where(band < reach, band, bands - 1 - band) + 1)
    first = strip * band - EDGE

    def joined(own, other, axis, size, column):
        column = column + first
        ahead = pltpu.roll(other, lax.rem(size - off, size), axis)
        behind = pltpu.roll(other, off, axis)
        value = jnp.where((column < 0) & at_left, ahead, 0.0)
        value = jnp.where((column >= TILE) & at_right, behind, value)
        return jnp.where((column >= 0) & (column < TILE), own, value)

    column_h = lax.broadcasted_iota(jnp.int32, (PACK, HID_CH), 0)
    lane = lax.broadcasted_iota(jnp.int32, (GROUPS, TILE), 1)
    column_p = lane % PACK
    at_sub = lax.broadcasted_iota(jnp.int32, (PACK, TILE), 0)
    at_lane = lax.broadcasted_iota(jnp.int32, (PACK, TILE), 1)
    spread = jnp.where(at_sub == at_lane % PACK, 1.0, 0.0).astype(bf16)
    fill = jnp.zeros((PACK, TILE), f32)
    zeros = jnp.zeros((GROUPS, TILE), f32)
    lines = []
    for r in range(rows):
        own, other = blocks[r].astype(f32), beside[r].astype(f32)
        packed = joined(own[WINDOW:], other[WINDOW:], 1, TILE, column_p)
        hidden = joined(own, other, 0, PACK, column_h)[:WINDOW]
        hidden_at[pl.ds(r, WINDOW, stride=rows), :] = hidden
        pieces = []
        for b in range(3):
            moved = packed if b == 1 else pltpu.roll(packed, (1 - b) % TILE, 1)
            for q in range(4):
                pieces.append(
                    jnp.where((lane >= PACK * q) & (lane < PACK * (q + 1)), moved, zeros)
                )
        lines.append(jnp.concatenate(pieces + [fill], axis=0).astype(bf16))
    for r in range(0, rows, 2):
        both = dot_nt(spread, jnp.concatenate(lines[r : r + 2], axis=0))
        for i in range(2):
            part = both[:WINDOW, i * HID_CH : (i + 1) * HID_CH]
            looked[pl.ds(r + i, WINDOW, stride=rows), :] = part
    sub = lax.broadcasted_iota(jnp.int32, (HID_CH, HID_CH), 0)
    ends = jnp.where((sub == PACK + 24) | (sub == PACK + 25), feature_scale, 0.0).astype(bf16)
    level[...] = dot(looked[...].astype(bf16), ends)
    blank = jnp.zeros((EDGE, HID_CH), f32)
    line[:EDGE, :] = blank
    line[EDGE + WINDOW * rows :, :] = blank
    start = EDGE - REACH
    width = strip + 2 * REACH
    keep(line, taps, start * rows, hidden_at[start * rows : (start + width) * rows, :], rows)
    for copy in copies:
        copy.wait()
    head = head_row[...].astype(f32)[0:1] * feature_scale
    head = jnp.broadcast_to(head, (HID_CH, HID_CH)).astype(bf16)

    def beside_columns(target, at, length):
        return [target[at + b * rows : at + b * rows + length, :] for b in (-1, 0, 1)]

    for t in range(ITERS):
        halo = REACH - 1 - 2 * t
        at, length = (EDGE - halo) * rows, (strip + 2 * halo) * rows
        lane_at = lax.broadcasted_iota(jnp.int32, (length, HID_CH), 1)
        tap, channel = lane_at // PACK, lane_at % PACK
        near = [level[at + b * rows : at + b * rows + length, :] for b in (-1, 0, 1)]
        value = jnp.where(tap == 0, near[0], jnp.where(tap == 1, near[1], near[2]))
        at_lookup = (channel >= t * GROUPS) & (channel < (t + 1) * GROUPS)
        value = jnp.where(
            (channel == 3 * GROUPS) & (tap < 3),
            value,
            jnp.where(at_lookup, looked[at : at + length, :], 0.0),
        )
        keep(line, in_taps, at, value, rows)
        lhs = beside_columns(taps, at, length) + [in_taps[at : at + length, :]]
        both = dot(jnp.concatenate(lhs, axis=1), weight[:, : 2 * HID_CH])
        gate[at + rows : at + length - rows, :] = (
            0.5 * jnp.tanh(0.5 * both[rows : length - rows, :HID_CH]) + 0.5
        )
        reset = 0.5 * jnp.tanh(0.5 * both[:, HID_CH:]) + 0.5
        keep(line, reset_taps, at, reset * hidden_at[at : at + length, :], rows)

        at, length = at + rows, length - 2 * rows
        lhs = beside_columns(reset_taps, at, length) + [in_taps[at : at + length, :]]
        candidate = jnp.tanh(dot(jnp.concatenate(lhs, axis=1), weight[:, 2 * HID_CH :]))
        hidden = hidden_at[at : at + length, :]
        hidden = hidden + gate[at : at + length, :] * (candidate - hidden)
        column = lax.broadcasted_iota(jnp.int32, (length, HID_CH), 0) // rows
        column = column + (at // rows + first)
        inside = ((column >= 0) | (disp > 0)) & ((column < TILE) | (disp < disps - 1))
        hidden = jnp.where(inside, hidden, 0.0).astype(bf16)
        level[at : at + length, :] += dot_nt(hidden, head)
        hidden_at[at : at + length, :] = hidden.astype(f32)
        if t < ITERS - 1:
            keep(line, taps, at, hidden.astype(f32), rows)

    lane = lax.broadcasted_iota(jnp.int32, (strip, HID_CH), 1)
    gap = [] if strip == EDGE else [jnp.zeros((EDGE - strip, HID_CH), f32)]
    for r in range(rows):
        here = pl.ds(EDGE * rows + r, strip, stride=rows)
        value = level[here, :] * (1.0 / feature_scale)
        high = value.astype(bf16).astype(f32)
        middle = (value - high).astype(bf16).astype(f32)
        parts = jnp.where(lane == 0, high, jnp.where(lane == 1, middle, value - high - middle))
        parts = jnp.where(lane < 3, parts, 0.0)
        block = [hidden_at[here, :]] + gap + [parts] + gap
        out[r] = jnp.concatenate(block, axis=0).astype(bf16)


def unpack_kernel(blocks, disparity_out, hidden_out):
    count = blocks.shape[0]
    strip = TILE // count
    held = [blocks[j].astype(f32) for j in range(count)]
    hidden = jnp.concatenate([block[:strip] for block in held], axis=0)
    hidden_out[0] = hidden.astype(bf16)
    parts = jnp.concatenate([block[EDGE : EDGE + strip] for block in held], axis=0).T
    disparity_out[...] = parts[0:1] + parts[1:2] + parts[2:3]


def in_hbm(value):
    return pltpu.with_memory_space_constraint(value, pltpu.HBM)


def to_sides(value):
    disps = lax.axis_size("disp")
    right = [(d, d + 1) for d in range(disps - 1)]
    left = [(d + 1, d) for d in range(disps - 1)]
    if disps == 2:
        return lax.ppermute(value, "disp", right + left)[None]
    return jnp.stack([lax.ppermute(value, "disp", right), lax.ppermute(value, "disp", left)])


def across_border(value):
    bands, disps = lax.axis_size("band"), lax.axis_size("disp")
    pairs = []
    for i in range(-(-REACH * bands // TILE)):
        for d in range(disps - 1):
            left, right = (bands - 1 - i) * disps + d, i * disps + d + 1
            pairs += [(left, right), (right, left)]
    return lax.ppermute(value, ("band", "disp"), pairs)


def to_rows(value, shift):
    bands = lax.axis_size("band")
    return lax.ppermute(
        value, "band", [(i, shift(i)) for i in range(bands) if 0 <= shift(i) < bands]
    )


def odd_pair(i):
    return i ^ 1


def even_pair(i):
    return i - 1 if i % 2 == 0 else i + 1


def local(
    feat_left,
    feat_right,
    limit,
    indices,
    hidden_start,
    vol_kernel,
    group_gain,
    hid_kernel,
    in_kernel,
    head_weight,
):
    bands, disps = lax.axis_size("band"), lax.axis_size("disp")
    place = jnp.stack(
        [lax.axis_index("band"), lax.axis_index("disp"), jnp.int32(bands), jnp.int32(disps)]
    ).astype(jnp.int32)
    smem = pl.BlockSpec(memory_space=pltpu.SMEM)
    vmem = pl.BlockSpec(memory_space=pltpu.VMEM)
    hbm = pl.BlockSpec(memory_space=pltpu.HBM)
    anywhere = pl.BlockSpec(memory_space=pl.ANY)
    padded = (DISPS + 2) * GROUPS

    feats = jnp.concatenate([feat_left[0], feat_right[0]], axis=0)
    odd_own, even_own = to_rows(feats, odd_pair), to_rows(feats, even_pair)
    across = to_sides(feats)
    raw_own, taps = pl.pallas_call(
        own_row_kernel,
        out_shape=(
            jax.ShapeDtypeStruct((padded, 2 * TILE), bf16),
            jax.ShapeDtypeStruct((3 * OUT_SLAB, 3 * SLAB), bf16),
        ),
        in_specs=[smem, vmem, vmem, hbm],
        out_specs=(vmem, vmem),
        scratch_shapes=[
            pltpu.VMEM((padded, TILE), f32),
            pltpu.VMEM((padded, TILE), f32),
            pltpu.VMEM((27, GROUPS, GROUPS), bf16),
            pltpu.SemaphoreType.DMA((1,)),
        ],
        compiler_params=pltpu.CompilerParams(vmem_limit_bytes=16 * 2**20),
        cost_estimate=pl.CostEstimate(flops=2 * 10**9, bytes_accessed=4 * 2**20, transcendentals=0),
    )(place, feats, across, in_hbm(vol_kernel.reshape(27, GROUPS, GROUPS)))
    odd_own, even_own, raw_own, taps = lax.optimization_barrier(
        (odd_own, even_own, raw_own, taps)
    )
    odd_across, even_across = to_sides(odd_own), to_sides(even_own)

    in_weight = jnp.concatenate(
        [in_kernel[:, :, :GROUPS]] * ITERS + [in_kernel[:, :, GROUPS:]], axis=2
    )
    in_weight = jnp.pad(in_weight, ((0, 0), (0, 1), (0, PACK - in_weight.shape[2]), (0, 0)))
    in_weight = jnp.concatenate(
        [
            in_weight.reshape(3 * HID_CH, 3 * HID_CH),
            jnp.pad(head_weight.reshape(1, HID_CH), ((0, 15), (0, 2 * HID_CH))),
        ],
        axis=0,
    )

    packed = pl.pallas_call(
        volume_kernel,
        out_shape=jax.ShapeDtypeStruct((bands, PACK, TILE), bf16),
        in_specs=[smem, smem] + [vmem] * 7 + [hbm, hbm],
        out_specs=vmem,
        scratch_shapes=[
            pltpu.VMEM((padded, 2 * TILE), bf16),
            pltpu.VMEM((3 * OUT_SLAB, 3 * SLAB), bf16),
            pltpu.VMEM((2, padded, TILE), f32),
            pltpu.VMEM((2, padded, TILE), f32),
            pltpu.VMEM((DISPS, TILE), f32),
            pltpu.VMEM((TILE + WINDOW, HID_CH), f32),
            pltpu.SemaphoreType.DMA((2,)),
        ],
        compiler_params=pltpu.CompilerParams(vmem_limit_bytes=24 * 2**20),
        cost_estimate=pl.CostEstimate(
            flops=5 * 10**9, bytes_accessed=16 * 2**20, transcendentals=DISPS * TILE
        ),
    )(
        place, group_gain, odd_own, odd_across, even_own, even_across,
        limit, indices[:, 0], hidden_start[0], raw_own, taps,
    )

    packed = lax.all_to_all(packed, "band", 0, 0, tiled=True)
    beside = across_border(packed)

    pixels = WINDOW * bands
    refined = pl.pallas_call(
        refine_kernel,
        out_shape=jax.ShapeDtypeStruct((bands, 2 * EDGE, HID_CH), bf16),
        in_specs=[smem, vmem, vmem, anywhere, hbm],
        out_specs=vmem,
        scratch_shapes=[
            pltpu.VMEM((pixels + 2 * EDGE, HID_CH), f32),
            pltpu.VMEM((12 * HID_CH, 3 * HID_CH), bf16),
            pltpu.VMEM((16, HID_CH), bf16),
            pltpu.VMEM((pixels, HID_CH), f32),
            pltpu.VMEM((pixels, HID_CH), f32),
            pltpu.VMEM((pixels, 3 * HID_CH), bf16),
            pltpu.VMEM((pixels, 3 * HID_CH), bf16),
            pltpu.VMEM((pixels, 3 * HID_CH), bf16),
            pltpu.VMEM((pixels, HID_CH), f32),
            pltpu.VMEM((pixels, HID_CH), f32),
            pltpu.SemaphoreType.DMA((11,)),
        ],
        compiler_params=pltpu.CompilerParams(vmem_limit_bytes=32 * 2**20),
    )(
        place, packed, beside,
        hid_kernel.reshape(9 * HID_CH, 3 * HID_CH), in_hbm(in_weight),
    )
    refined = lax.all_to_all(refined, "band", 0, 0, tiled=True)
    disparity, hidden = pl.pallas_call(
        unpack_kernel,
        out_shape=(
            jax.ShapeDtypeStruct((1, TILE), f32),
            jax.ShapeDtypeStruct((1, TILE, HID_CH), bf16),
        ),
        in_specs=[vmem],
        out_specs=(vmem, vmem),
    )(refined)
    return (disparity, hidden)


def solution(mesh):
    in_specs = (
        P("band", None, "disp"),
        P("band", None, "disp"),
        P("band", "disp"),
        P(None, "band", "disp"),
        P("band", "disp", None),
        P(),
        P(),
        P(),
        P(),
        P(),
    )
    out_specs = (P("band", "disp"), P("band", "disp", None))
    return jax.shard_map(local, mesh=mesh, in_specs=in_specs, out_specs=out_specs, check_vma=False)
```

```python
import jax
import jax.numpy as jnp
from jax import lax
from jax.experimental import pallas as pl
from jax.experimental.pallas import tpu as pltpu
from jax.sharding import PartitionSpec as P

GROUPS = 8
DISPS = 96
FEAT_CH = 96
HID_CH = 128
ITERS = 3
TILE = 128
REACH = 2 * ITERS
EDGE = 8
WINDOW = 24
PACK = 32
BLOCK = 8
SLAB = (BLOCK + 2) * GROUPS
OUT_SLAB = BLOCK * GROUPS

pixel_unit = 8.0
feature_scale = 0.25
floor_logit = -1e30

f32 = jnp.float32
bf16 = jnp.bfloat16


def dot(a, b):
    return jnp.dot(a, b, preferred_element_type=f32)


def dot_nt(a, b):
    return lax.dot_general(a, b, (((1,), (1,)), ((), ())), preferred_element_type=f32)


def copy_all(copies):
    for copy in copies:
        copy.start()
    for copy in copies:
        copy.wait()


def toeplitz(vol_kernel):
    size = 27 * GROUPS
    flat = vol_kernel[...].astype(f32).reshape(size, GROUPS)
    flat = jnp.concatenate([flat, jnp.zeros((size, TILE - GROUPS), f32)], axis=1).T[:GROUPS]
    row = lax.broadcasted_iota(jnp.int32, (9 * GROUPS, size), 0) >> 3
    tap = lax.broadcasted_iota(jnp.int32, (9 * GROUPS, size), 1) >> 3
    tap_a = (tap >= 9).astype(jnp.int32) + (tap >= 18).astype(jnp.int32)
    within = tap - 9 * tap_a
    tap_b = (within >= 3).astype(jnp.int32) + (within >= 6).astype(jnp.int32)
    tap_e = within - 3 * tap_b
    pairs = jnp.where(
        row == 3 * tap_a + tap_e, jnp.concatenate([flat] * 9, axis=0), 0.0
    ).astype(bf16)
    from_row = lax.broadcasted_iota(jnp.int32, (size, 3 * SLAB), 0)
    to = lax.broadcasted_iota(jnp.int32, (size, 3 * SLAB), 1)
    from_tap = from_row >> 3
    from_in = from_tap - 9 * ((from_tap >= 9).astype(jnp.int32) + (from_tap >= 18).astype(jnp.int32))
    from_b = (from_in >= 3).astype(jnp.int32) + (from_in >= 6).astype(jnp.int32)
    to_b = (to >= SLAB).astype(jnp.int32) + (to >= 2 * SLAB).astype(jnp.int32)
    repeat = jnp.where((from_b == to_b) & ((from_row & 7) == (to & 7)), 1.0, 0.0).astype(bf16)
    spread = dot(pairs, repeat)
    to = lax.broadcasted_iota(jnp.int32, (GROUPS, 3 * SLAB), 1)
    to_b = (to >= SLAB).astype(jnp.int32) + (to >= 2 * SLAB).astype(jnp.int32)
    to_d = (to - SLAB * to_b) >> 3
    rows = []
    for e in range(3):
        for d in range(BLOCK):
            value = jnp.zeros((GROUPS, 3 * SLAB), f32)
            for a in range(3):
                at = (3 * a + e) * GROUPS
                value = jnp.where(to_d == d + a, spread[at : at + GROUPS], value)
            rows.append(value)
    return jnp.concatenate(rows, axis=0).astype(bf16)


def correlate(lefts, rights, place, row_ok, wide, extra):
    has_left = (place[1] > 0).astype(f32)
    has_right = (place[1] < place[3] - 1).astype(f32)
    lane = lax.broadcasted_iota(jnp.int32, (TILE, TILE), 1)
    sub = lax.broadcasted_iota(jnp.int32, (TILE, TILE), 0)
    flip = jnp.where(lane + sub == TILE - 1, 1.0, 0.0).astype(bf16)
    per_group = FEAT_CH // GROUPS
    channel = lax.broadcasted_iota(jnp.int32, (32, FEAT_CH), 1)
    group_masks = [
        (channel >= g * per_group) & (channel < (g + 1) * per_group) for g in range(GROUPS)
    ]
    lane96 = lax.broadcasted_iota(jnp.int32, (FEAT_CH, TILE), 1)
    zero_slab = jnp.zeros((GROUPS, TILE), f32)
    for at in (0, (DISPS + 1) * GROUPS):
        wide[pl.ds(at, GROUPS), :] = zero_slab
        extra[pl.ds(at, GROUPS), :] = zero_slab

    own_t = (lefts[1] * row_ok).T
    side_t = jnp.where(
        lane96 < EDGE,
        lefts[2] * (has_right * row_ok),
        jnp.where(lane96 >= TILE - EDGE, lefts[0] * (has_left * row_ok), 0.0),
    ).T
    sources = jnp.concatenate([rights[2] * has_right, rights[1], rights[0] * has_left], axis=0)
    flipped = dot(sources.astype(bf16), flip)
    reverse = jnp.concatenate(
        [flipped[i * FEAT_CH : (i + 1) * FEAT_CH] for i in range(3)], axis=1
    )
    windows = [
        reverse[:, 2 * TILE - 32 - 32 * k : 3 * TILE - 32 - 32 * k].astype(bf16)
        for k in range(-1, 5)
    ]

    def by_group(rows):
        count = rows.shape[0]
        parts = [jnp.where(m[:count], rows, 0.0) for m in group_masks]
        return jnp.concatenate(parts, axis=0).astype(bf16)

    def shear(product, g, count, first):
        rows = product[count * g : count * g + count]
        return pltpu.roll(rows, TILE - 31 + first, 1, stride=1, stride_axis=0)

    products = [
        dot(by_group(own_t[32 * k : 32 * k + 32]), windows[k + 1]) for k in range(TILE // 32)
    ]
    after = dot(by_group(side_t[:EDGE]), windows[5])
    before = dot(by_group(side_t[TILE - EDGE :]), windows[0])
    sides = []
    for g in range(GROUPS):
        part = jnp.concatenate([shear(product, g, 32, 0) for product in products], axis=0)
        wide[pl.ds(GROUPS + g, DISPS, stride=GROUPS), :] = part.T[:DISPS] * (1.0 / per_group)
        sides += [shear(after, g, EDGE, 0), shear(before, g, EDGE, 32 - EDGE)]
    part = jnp.concatenate(sides, axis=0).T[:DISPS] * (1.0 / per_group)
    for g in range(GROUPS):
        extra[pl.ds(GROUPS + g, DISPS, stride=GROUPS), :] = (
            part if g == 0 else pltpu.roll(part, TILE - 2 * EDGE * g, 1)
        )


def own_row_kernel(place, own, across, vol_kernel, raw_out, taps_out, wide, extra, kernel, sem):
    copy = pltpu.make_async_copy(vol_kernel, kernel, sem.at[0])
    copy.start()
    tiles = [across[0], own[...], across[across.shape[0] - 1]]
    tiles = [tile.astype(f32) for tile in tiles]
    correlate(
        [tile[:FEAT_CH] for tile in tiles], [tile[FEAT_CH:] for tile in tiles],
        place, 1.0, wide, extra,
    )
    raw_out[...] = jnp.concatenate([wide[...], extra[...]], axis=1).astype(bf16)
    copy.wait()
    taps_out[...] = toeplitz(kernel)


def volume_kernel(
    place, gain, odd_own, odd_across, even_own, even_across, limit, indices, hidden, raw_own,
    taps_own, out, raw, taps, wide, extra, logit, padded, sems,
):
    band, bands = place[0], place[2]
    is_even = band % 2 == 0
    copies = [
        pltpu.make_async_copy(raw_own, raw, sems.at[0]),
        pltpu.make_async_copy(taps_own, taps, sems.at[1]),
    ]
    for copy in copies:
        copy.start()

    last = odd_across.shape[0] - 1
    odd = [tile.astype(f32) for tile in (odd_across[0], odd_own[...], odd_across[last])]
    even = [tile.astype(f32) for tile in (even_across[0], even_own[...], even_across[last])]
    for b in range(2):
        row = band + 2 * b - 1
        row_ok = ((row >= 0) & (row < bands)).astype(f32)
        tiles = [
            jnp.where(is_even, y, x) if b == 0 else jnp.where(is_even, x, y)
            for x, y in zip(odd, even)
        ]
        correlate(
            [tile[:FEAT_CH] for tile in tiles], [tile[FEAT_CH:] for tile in tiles],
            place, row_ok, wide.at[b], extra.at[b],
        )
    for copy in copies:
        copy.wait()

    lane8 = lax.broadcasted_iota(jnp.int32, (OUT_SLAB, TILE), 1)
    group_at = lax.broadcasted_iota(jnp.int32, (GROUPS, TILE), 0)
    gains = jnp.zeros((GROUPS, TILE), f32)
    for g in range(GROUPS):
        gains = jnp.where(group_at == g, gain[g], gains)
    wanted = [jnp.broadcast_to(indices[t : t + 1, :], (GROUPS, TILE)) for t in range(ITERS)]
    found = [jnp.zeros((GROUPS, TILE), f32) for _ in range(ITERS)]
    for q in range(DISPS // BLOCK):
        at = q * OUT_SLAB
        slabs = [
            jnp.concatenate(
                [wide[b, at : at + SLAB, :], extra[b, at : at + SLAB, :]], axis=1
            ).astype(bf16)
            for b in range(2)
        ]
        slabs.insert(1, raw[at : at + SLAB, :])
        product = dot(taps[...], jnp.concatenate(slabs, axis=0))
        first, middle, last = (
            product[:OUT_SLAB],
            product[OUT_SLAB : 2 * OUT_SLAB],
            product[2 * OUT_SLAB :],
        )
        conv = (
            middle[:, :TILE]
            + jnp.where(
                lane8 == 0,
                pltpu.roll(first[:, TILE:], TILE - 2 * EDGE + 1, 1),
                pltpu.roll(first[:, :TILE], 1, 1),
            )
            + jnp.where(
                lane8 == TILE - 1,
                pltpu.roll(last[:, TILE:], TILE - 1, 1),
                pltpu.roll(last[:, :TILE], TILE - 1, 1),
            )
        )
        centre = slabs[1][:, :TILE].astype(f32)[GROUPS : GROUPS + OUT_SLAB]
        volume = (centre + jnp.maximum(conv, 0.0)).astype(bf16).astype(f32)
        volume = volume.reshape(BLOCK, GROUPS, TILE)
        logit[q * BLOCK : (q + 1) * BLOCK, :] = jnp.sum(volume * gains[None], axis=1)
        for d in range(BLOCK):
            for t in range(ITERS):
                found[t] = found[t] + jnp.where(wanted[t] == q * BLOCK + d, volume[d], 0.0)

    level = lax.broadcasted_iota(jnp.int32, (DISPS, TILE), 0)
    valid = level < limit[...]
    masked = jnp.where(valid, logit[...], floor_logit)
    top = jnp.max(masked, axis=0, keepdims=True)
    weights = jnp.where(valid, jnp.exp(masked - top), 0.0)
    moment = jnp.sum(weights * level.astype(f32), axis=0, keepdims=True)
    start = moment / jnp.sum(weights, axis=0, keepdims=True) / pixel_unit
    high = start.astype(bf16).astype(f32)
    low = (start - high).astype(bf16).astype(f32)
    ends = jnp.where(
        group_at == 0,
        jnp.broadcast_to(high, (GROUPS, TILE)),
        jnp.where(group_at == 1, jnp.broadcast_to(low, (GROUPS, TILE)), 0.0),
    )

    strip = TILE // out.shape[0]
    padded[:EDGE, :] = jnp.zeros((EDGE, HID_CH), f32)
    padded[EDGE : EDGE + TILE, :] = hidden[...].astype(f32)
    padded[EDGE + TILE :, :] = jnp.zeros((WINDOW - EDGE, HID_CH), f32)
    lane = lax.broadcasted_iota(jnp.int32, (GROUPS, TILE), 1)
    for j in range(out.shape[0]):
        part = jnp.zeros((GROUPS, TILE), f32)
        for q, group in enumerate(found + [ends]):
            moved = pltpu.roll(group, (PACK * q + EDGE - strip * j) % TILE, 1)
            part = jnp.where((lane >= PACK * q) & (lane < PACK * q + WINDOW), moved, part)
        block = [padded[strip * j : strip * j + WINDOW, :], part]
        out[j] = jnp.concatenate(block, axis=0).astype(bf16)


def keep(line, target, at, values, rows):
    length = values.shape[0]
    start = EDGE + at
    row = lax.broadcasted_iota(jnp.int32, (length, HID_CH), 0) % rows
    line[start : start + length, :] = values
    before = jnp.where(row == 0, 0.0, line[start - 1 : start - 1 + length, :])
    after = jnp.where(row == rows - 1, 0.0, line[start + 1 : start + 1 + length, :])
    target[at : at + length, 0:HID_CH] = before.astype(bf16)
    target[at : at + length, HID_CH : 2 * HID_CH] = values.astype(bf16)
    target[at : at + length, 2 * HID_CH :] = after.astype(bf16)


def refine_kernel(
    place,
    blocks,
    beside,
    hid_weight,
    in_weight,
    out,
    line,
    weight,
    head_row,
    looked,
    hidden_at,
    taps,
    reset_taps,
    in_taps,
    gate,
    level,
    sems,
):
    rows = blocks.shape[0]
    strip = TILE // rows
    copies = [
        pltpu.make_async_copy(
            hid_weight.at[pl.ds((3 * a + b) * HID_CH, HID_CH)],
            weight.at[pl.ds((3 * b + a) * HID_CH, HID_CH)],
            sems.at[3 * a + b],
        )
        for a in range(3)
        for b in range(3)
    ]
    copies.append(
        pltpu.make_async_copy(
            in_weight.at[pl.ds(0, 3 * HID_CH)],
            weight.at[pl.ds(9 * HID_CH, 3 * HID_CH)],
            sems.at[9],
        )
    )
    copies.append(
        pltpu.make_async_copy(
            in_weight.at[pl.ds(3 * HID_CH, 16), pl.ds(0, HID_CH)], head_row, sems.at[10]
        )
    )
    for copy in copies:
        copy.start()

    band, disp, bands, disps = place[0], place[1], place[2], place[3]
    reach = -(-REACH // strip)
    at_left = (band < reach) & (disp > 0)
    at_right = (band >= bands - reach) & (disp < disps - 1)
    off = strip
    if reach > 1:
        off = strip * (2 * jnp.where(band < reach, band, bands - 1 - band) + 1)
    first = strip * band - EDGE

    def joined(own, other, axis, size, column):
        column = column + first
        ahead = pltpu.roll(other, (size - off) % size, axis)
        behind = pltpu.roll(other, off, axis)
        value = jnp.where((column < 0) & at_left, ahead, 0.0)
        value = jnp.where((column >= TILE) & at_right, behind, value)
        return jnp.where((column >= 0) & (column < TILE), own, value)

    column_h = lax.broadcasted_iota(jnp.int32, (PACK, HID_CH), 0)
    lane = lax.broadcasted_iota(jnp.int32, (GROUPS, TILE), 1)
    column_p = lane % PACK
    at_sub = lax.broadcasted_iota(jnp.int32, (PACK, TILE), 0)
    at_lane = lax.broadcasted_iota(jnp.int32, (PACK, TILE), 1)
    spread = jnp.where(at_sub == at_lane % PACK, 1.0, 0.0).astype(bf16)
    fill = jnp.zeros((PACK, TILE), f32)
    zeros = jnp.zeros((GROUPS, TILE), f32)
    lines = []
    for r in range(rows):
        own, other = blocks[r].astype(f32), beside[r].astype(f32)
        packed = joined(own[WINDOW:], other[WINDOW:], 1, TILE, column_p)
        hidden = joined(own, other, 0, PACK, column_h)[:WINDOW]
        hidden_at[pl.ds(r, WINDOW, stride=rows), :] = hidden
        pieces = []
        for b in range(3):
            moved = packed if b == 1 else pltpu.roll(packed, (1 - b) % TILE, 1)
            for q in range(4):
                pieces.append(
                    jnp.where((lane >= PACK * q) & (lane < PACK * (q + 1)), moved, zeros)
                )
        lines.append(jnp.concatenate(pieces + [fill], axis=0).astype(bf16))
    for r in range(0, rows, 2):
        both = dot_nt(spread, jnp.concatenate(lines[r : r + 2], axis=0))
        for i in range(2):
            part = both[:WINDOW, i * HID_CH : (i + 1) * HID_CH]
            looked[pl.ds(r + i, WINDOW, stride=rows), :] = part
    sub = lax.broadcasted_iota(jnp.int32, (HID_CH, HID_CH), 0)
    ends = jnp.where((sub == PACK + 24) | (sub == PACK + 25), feature_scale, 0.0).astype(bf16)
    level[...] = dot(looked[...].astype(bf16), ends)
    blank = jnp.zeros((EDGE, HID_CH), f32)
    line[:EDGE, :] = blank
    line[EDGE + WINDOW * rows :, :] = blank
    start = EDGE - REACH
    width = strip + 2 * REACH
    keep(line, taps, start * rows, hidden_at[start * rows : (start + width) * rows, :], rows)
    for copy in copies:
        copy.wait()
    head = head_row[...].astype(f32)[0:1] * feature_scale
    head = jnp.broadcast_to(head, (HID_CH, HID_CH)).astype(bf16)

    def beside_columns(target, at, length):
        return [target[at + b * rows : at + b * rows + length, :] for b in (-1, 0, 1)]

    for t in range(ITERS):
        halo = REACH - 1 - 2 * t
        at, length = (EDGE - halo) * rows, (strip + 2 * halo) * rows
        lane_at = lax.broadcasted_iota(jnp.int32, (length, HID_CH), 1)
        tap, channel = lane_at // PACK, lane_at % PACK
        near = [level[at + b * rows : at + b * rows + length, :] for b in (-1, 0, 1)]
        value = jnp.where(tap == 0, near[0], jnp.where(tap == 1, near[1], near[2]))
        at_lookup = (channel >= t * GROUPS) & (channel < (t + 1) * GROUPS)
        value = jnp.where(
            (channel == 3 * GROUPS) & (tap < 3),
            value,
            jnp.where(at_lookup, looked[at : at + length, :], 0.0),
        )
        keep(line, in_taps, at, value, rows)
        lhs = beside_columns(taps, at, length) + [in_taps[at : at + length, :]]
        both = dot(jnp.concatenate(lhs, axis=1), weight[:, : 2 * HID_CH])
        gate[at + rows : at + length - rows, :] = (
            0.5 * jnp.tanh(0.5 * both[rows : length - rows, :HID_CH]) + 0.5
        )
        reset = 0.5 * jnp.tanh(0.5 * both[:, HID_CH:]) + 0.5
        keep(line, reset_taps, at, reset * hidden_at[at : at + length, :], rows)

        at, length = at + rows, length - 2 * rows
        lhs = beside_columns(reset_taps, at, length) + [in_taps[at : at + length, :]]
        candidate = jnp.tanh(dot(jnp.concatenate(lhs, axis=1), weight[:, 2 * HID_CH :]))
        hidden = hidden_at[at : at + length, :]
        hidden = hidden + gate[at : at + length, :] * (candidate - hidden)
        column = lax.broadcasted_iota(jnp.int32, (length, HID_CH), 0) // rows
        column = column + (at // rows + first)
        inside = ((column >= 0) | (disp > 0)) & ((column < TILE) | (disp < disps - 1))
        hidden = jnp.where(inside, hidden, 0.0).astype(bf16)
        level[at : at + length, :] += dot_nt(hidden, head)
        hidden_at[at : at + length, :] = hidden.astype(f32)
        if t < ITERS - 1:
            keep(line, taps, at, hidden.astype(f32), rows)

    lane = lax.broadcasted_iota(jnp.int32, (strip, HID_CH), 1)
    gap = [] if strip == EDGE else [jnp.zeros((EDGE - strip, HID_CH), f32)]
    for r in range(rows):
        here = pl.ds(EDGE * rows + r, strip, stride=rows)
        value = level[here, :] * (1.0 / feature_scale)
        high = value.astype(bf16).astype(f32)
        middle = (value - high).astype(bf16).astype(f32)
        parts = jnp.where(lane == 0, high, jnp.where(lane == 1, middle, value - high - middle))
        parts = jnp.where(lane < 3, parts, 0.0)
        block = [hidden_at[here, :]] + gap + [parts] + gap
        out[r] = jnp.concatenate(block, axis=0).astype(bf16)


def stays_kernel(place, blocks, out):
    out[...] = blocks[place[0]].astype(f32)


def unpack_kernel(place, blocks, stays, disparity_out, hidden_out):
    count = blocks.shape[0]
    strip = TILE // count
    held = [
        jnp.where(place[0] == j, stays[...], blocks[j].astype(f32)) for j in range(count)
    ]
    hidden = jnp.concatenate([block[:strip] for block in held], axis=0)
    hidden_out[0] = hidden.astype(bf16)
    parts = jnp.concatenate([block[EDGE : EDGE + strip] for block in held], axis=0).T
    disparity_out[...] = parts[0:1] + parts[1:2] + parts[2:3]


def in_hbm(value):
    return pltpu.with_memory_space_constraint(value, pltpu.HBM)


def to_sides(value):
    disps = lax.axis_size("disp")
    right = [(d, d + 1) for d in range(disps - 1)]
    left = [(d + 1, d) for d in range(disps - 1)]
    if disps == 2:
        return lax.ppermute(value, "disp", right + left)[None]
    return jnp.stack([lax.ppermute(value, "disp", right), lax.ppermute(value, "disp", left)])


def across_border(value):
    bands, disps = lax.axis_size("band"), lax.axis_size("disp")
    pairs = []
    for i in range(-(-REACH * bands // TILE)):
        for d in range(disps - 1):
            left, right = (bands - 1 - i) * disps + d, i * disps + d + 1
            pairs += [(left, right), (right, left)]
    return lax.ppermute(value, ("band", "disp"), pairs)


def to_rows(value, shift):
    bands = lax.axis_size("band")
    return lax.ppermute(
        value, "band", [(i, shift(i)) for i in range(bands) if 0 <= shift(i) < bands]
    )


def odd_pair(i):
    return i ^ 1


def even_pair(i):
    return i - 1 if i % 2 == 0 else i + 1


def local(
    feat_left,
    feat_right,
    limit,
    indices,
    hidden_start,
    vol_kernel,
    group_gain,
    hid_kernel,
    in_kernel,
    head_weight,
):
    bands, disps = lax.axis_size("band"), lax.axis_size("disp")
    place = jnp.stack(
        [lax.axis_index("band"), lax.axis_index("disp"), jnp.int32(bands), jnp.int32(disps)]
    ).astype(jnp.int32)
    smem = pl.BlockSpec(memory_space=pltpu.SMEM)
    vmem = pl.BlockSpec(memory_space=pltpu.VMEM)
    hbm = pl.BlockSpec(memory_space=pltpu.HBM)
    anywhere = pl.BlockSpec(memory_space=pl.ANY)
    padded = (DISPS + 2) * GROUPS

    feats = jnp.concatenate([feat_left[0], feat_right[0]], axis=0)
    odd_own, even_own = to_rows(feats, odd_pair), to_rows(feats, even_pair)
    across = to_sides(feats)
    raw_own, taps = pl.pallas_call(
        own_row_kernel,
        out_shape=(
            jax.ShapeDtypeStruct((padded, 2 * TILE), bf16),
            jax.ShapeDtypeStruct((3 * OUT_SLAB, 3 * SLAB), bf16),
        ),
        in_specs=[smem, vmem, vmem, hbm],
        out_specs=(vmem, vmem),
        scratch_shapes=[
            pltpu.VMEM((padded, TILE), f32),
            pltpu.VMEM((padded, TILE), f32),
            pltpu.VMEM((27, GROUPS, GROUPS), bf16),
            pltpu.SemaphoreType.DMA((1,)),
        ],
        compiler_params=pltpu.CompilerParams(vmem_limit_bytes=16 * 2**20),
        cost_estimate=pl.CostEstimate(flops=2 * 10**9, bytes_accessed=4 * 2**20, transcendentals=0),
    )(place, feats, across, in_hbm(vol_kernel.reshape(27, GROUPS, GROUPS)))
    odd_own, even_own, raw_own, taps = lax.optimization_barrier(
        (odd_own, even_own, raw_own, taps)
    )
    odd_across, even_across = to_sides(odd_own), to_sides(even_own)

    in_weight = jnp.concatenate(
        [in_kernel[:, :, :GROUPS]] * ITERS + [in_kernel[:, :, GROUPS:]], axis=2
    )
    in_weight = jnp.pad(in_weight, ((0, 0), (0, 1), (0, PACK - in_weight.shape[2]), (0, 0)))
    in_weight = jnp.concatenate(
        [
            in_weight.reshape(3 * HID_CH, 3 * HID_CH),
            jnp.pad(head_weight.reshape(1, HID_CH), ((0, 15), (0, 2 * HID_CH))),
        ],
        axis=0,
    )

    packed = pl.pallas_call(
        volume_kernel,
        out_shape=jax.ShapeDtypeStruct((bands, PACK, TILE), bf16),
        in_specs=[smem, smem] + [vmem] * 7 + [hbm, hbm],
        out_specs=vmem,
        scratch_shapes=[
            pltpu.VMEM((padded, 2 * TILE), bf16),
            pltpu.VMEM((3 * OUT_SLAB, 3 * SLAB), bf16),
            pltpu.VMEM((2, padded, TILE), f32),
            pltpu.VMEM((2, padded, TILE), f32),
            pltpu.VMEM((DISPS, TILE), f32),
            pltpu.VMEM((TILE + WINDOW, HID_CH), f32),
            pltpu.SemaphoreType.DMA((2,)),
        ],
        compiler_params=pltpu.CompilerParams(vmem_limit_bytes=24 * 2**20),
        cost_estimate=pl.CostEstimate(
            flops=5 * 10**9, bytes_accessed=16 * 2**20, transcendentals=DISPS * TILE
        ),
    )(
        place, group_gain, odd_own, odd_across, even_own, even_across,
        limit, indices[:, 0], hidden_start[0], raw_own, taps,
    )

    packed = lax.all_to_all(packed, "band", 0, 0, tiled=True)
    packed, in_weight = lax.optimization_barrier((packed, in_weight))
    beside = across_border(packed)

    pixels = WINDOW * bands
    refined = pl.pallas_call(
        refine_kernel,
        out_shape=jax.ShapeDtypeStruct((bands, 2 * EDGE, HID_CH), bf16),
        in_specs=[smem, vmem, vmem, anywhere, hbm],
        out_specs=vmem,
        scratch_shapes=[
            pltpu.VMEM((pixels + 2 * EDGE, HID_CH), f32),
            pltpu.VMEM((12 * HID_CH, 3 * HID_CH), bf16),
            pltpu.VMEM((16, HID_CH), bf16),
            pltpu.VMEM((pixels, HID_CH), f32),
            pltpu.VMEM((pixels, HID_CH), f32),
            pltpu.VMEM((pixels, 3 * HID_CH), bf16),
            pltpu.VMEM((pixels, 3 * HID_CH), bf16),
            pltpu.VMEM((pixels, 3 * HID_CH), bf16),
            pltpu.VMEM((pixels, HID_CH), f32),
            pltpu.VMEM((pixels, HID_CH), f32),
            pltpu.SemaphoreType.DMA((11,)),
        ],
        compiler_params=pltpu.CompilerParams(vmem_limit_bytes=32 * 2**20),
    )(
        place, packed, beside,
        hid_kernel.reshape(9 * HID_CH, 3 * HID_CH), in_hbm(in_weight),
    )
    stays = pl.pallas_call(
        stays_kernel,
        out_shape=jax.ShapeDtypeStruct((2 * EDGE, HID_CH), f32),
        in_specs=[smem, vmem],
        out_specs=vmem,
        cost_estimate=pl.CostEstimate(flops=10**9, bytes_accessed=2**20, transcendentals=0),
    )(place, refined)
    refined = lax.all_to_all(refined, "band", 0, 0, tiled=True)
    disparity, hidden = pl.pallas_call(
        unpack_kernel,
        out_shape=(
            jax.ShapeDtypeStruct((1, TILE), f32),
            jax.ShapeDtypeStruct((1, TILE, HID_CH), bf16),
        ),
        in_specs=[smem, vmem, vmem],
        out_specs=(vmem, vmem),
    )(place, refined, stays)
    return (disparity, hidden)


def solution(mesh):
    in_specs = (
        P("band", None, "disp"),
        P("band", None, "disp"),
        P("band", "disp"),
        P(None, "band", "disp"),
        P("band", "disp", None),
        P(),
        P(),
        P(),
        P(),
        P(),
    )
    out_specs = (P("band", "disp"), P("band", "disp", None))
    return jax.shard_map(local, mesh=mesh, in_specs=in_specs, out_specs=out_specs, check_vma=False)
```

```python
import jax
import jax.numpy as jnp
from jax import lax
from jax.experimental import pallas as pl
from jax.experimental.pallas import tpu as pltpu
from jax.sharding import PartitionSpec as P

GROUPS = 8
DISPS = 96
FEAT_CH = 96
HID_CH = 128
ITERS = 3
TILE = 128
REACH = 2 * ITERS
EDGE = 8
WINDOW = 24
PACK = 32
BLOCK = 8
SLAB = (BLOCK + 2) * GROUPS
OUT_SLAB = BLOCK * GROUPS

pixel_unit = 8.0
feature_scale = 0.25
floor_logit = -1e30

f32 = jnp.float32
bf16 = jnp.bfloat16


def dot(a, b):
    return jnp.dot(a, b, preferred_element_type=f32)


def dot_nt(a, b):
    return lax.dot_general(a, b, (((1,), (1,)), ((), ())), preferred_element_type=f32)


def copy_all(copies):
    for copy in copies:
        copy.start()
    for copy in copies:
        copy.wait()


def toeplitz(vol_kernel):
    size = 27 * GROUPS
    flat = vol_kernel[...].astype(f32).reshape(size, GROUPS)
    flat = jnp.concatenate([flat, jnp.zeros((size, TILE - GROUPS), f32)], axis=1).T[:GROUPS]
    row = lax.broadcasted_iota(jnp.int32, (9 * GROUPS, size), 0) >> 3
    tap = lax.broadcasted_iota(jnp.int32, (9 * GROUPS, size), 1) >> 3
    tap_a = (tap >= 9).astype(jnp.int32) + (tap >= 18).astype(jnp.int32)
    within = tap - 9 * tap_a
    tap_b = (within >= 3).astype(jnp.int32) + (within >= 6).astype(jnp.int32)
    tap_e = within - 3 * tap_b
    pairs = jnp.where(
        row == 3 * tap_a + tap_e, jnp.concatenate([flat] * 9, axis=0), 0.0
    ).astype(bf16)
    from_row = lax.broadcasted_iota(jnp.int32, (size, 3 * SLAB), 0)
    to = lax.broadcasted_iota(jnp.int32, (size, 3 * SLAB), 1)
    from_tap = from_row >> 3
    from_in = from_tap - 9 * ((from_tap >= 9).astype(jnp.int32) + (from_tap >= 18).astype(jnp.int32))
    from_b = (from_in >= 3).astype(jnp.int32) + (from_in >= 6).astype(jnp.int32)
    to_b = (to >= SLAB).astype(jnp.int32) + (to >= 2 * SLAB).astype(jnp.int32)
    repeat = jnp.where((from_b == to_b) & ((from_row & 7) == (to & 7)), 1.0, 0.0).astype(bf16)
    spread = dot(pairs, repeat)
    to = lax.broadcasted_iota(jnp.int32, (GROUPS, 3 * SLAB), 1)
    to_b = (to >= SLAB).astype(jnp.int32) + (to >= 2 * SLAB).astype(jnp.int32)
    to_d = (to - SLAB * to_b) >> 3
    rows = []
    for e in range(3):
        for d in range(BLOCK):
            value = jnp.zeros((GROUPS, 3 * SLAB), f32)
            for a in range(3):
                at = (3 * a + e) * GROUPS
                value = jnp.where(to_d == d + a, spread[at : at + GROUPS], value)
            rows.append(value)
    return jnp.concatenate(rows, axis=0).astype(bf16)


def correlate(lefts, rights, place, row_ok, wide, extra):
    has_left = (place[1] > 0).astype(f32)
    has_right = (place[1] < place[3] - 1).astype(f32)
    lane = lax.broadcasted_iota(jnp.int32, (TILE, TILE), 1)
    sub = lax.broadcasted_iota(jnp.int32, (TILE, TILE), 0)
    flip = jnp.where(lane + sub == TILE - 1, 1.0, 0.0).astype(bf16)
    per_group = FEAT_CH // GROUPS
    channel = lax.broadcasted_iota(jnp.int32, (32, FEAT_CH), 1)
    group_masks = [
        (channel >= g * per_group) & (channel < (g + 1) * per_group) for g in range(GROUPS)
    ]
    lane96 = lax.broadcasted_iota(jnp.int32, (FEAT_CH, TILE), 1)
    zero_slab = jnp.zeros((GROUPS, TILE), f32)
    for at in (0, (DISPS + 1) * GROUPS):
        wide[pl.ds(at, GROUPS), :] = zero_slab
        extra[pl.ds(at, GROUPS), :] = zero_slab

    own_t = (lefts[1] * row_ok).T
    side_t = jnp.where(
        lane96 < EDGE,
        lefts[2] * (has_right * row_ok),
        jnp.where(lane96 >= TILE - EDGE, lefts[0] * (has_left * row_ok), 0.0),
    ).T
    sources = jnp.concatenate([rights[2] * has_right, rights[1], rights[0] * has_left], axis=0)
    flipped = dot(sources.astype(bf16), flip)
    reverse = jnp.concatenate(
        [flipped[i * FEAT_CH : (i + 1) * FEAT_CH] for i in range(3)], axis=1
    )
    windows = [
        reverse[:, 2 * TILE - 32 - 32 * k : 3 * TILE - 32 - 32 * k].astype(bf16)
        for k in range(-1, 5)
    ]

    def by_group(rows):
        count = rows.shape[0]
        parts = [jnp.where(m[:count], rows, 0.0) for m in group_masks]
        return jnp.concatenate(parts, axis=0).astype(bf16)

    def shear(product, g, count, first):
        rows = product[count * g : count * g + count]
        return pltpu.roll(rows, TILE - 31 + first, 1, stride=1, stride_axis=0)

    products = [
        dot(by_group(own_t[32 * k : 32 * k + 32]), windows[k + 1]) for k in range(TILE // 32)
    ]
    after = dot(by_group(side_t[:EDGE]), windows[5])
    before = dot(by_group(side_t[TILE - EDGE :]), windows[0])
    sides = []
    for g in range(GROUPS):
        part = jnp.concatenate([shear(product, g, 32, 0) for product in products], axis=0)
        wide[pl.ds(GROUPS + g, DISPS, stride=GROUPS), :] = part.T[:DISPS] * (1.0 / per_group)
        sides += [shear(after, g, EDGE, 0), shear(before, g, EDGE, 32 - EDGE)]
    part = jnp.concatenate(sides, axis=0).T[:DISPS] * (1.0 / per_group)
    for g in range(GROUPS):
        extra[pl.ds(GROUPS + g, DISPS, stride=GROUPS), :] = (
            part if g == 0 else pltpu.roll(part, TILE - 2 * EDGE * g, 1)
        )


def own_row_kernel(place, own, across, vol_kernel, raw_out, taps_out, wide, extra, kernel, sem):
    copy = pltpu.make_async_copy(vol_kernel, kernel, sem.at[0])
    copy.start()
    tiles = [across[0], own[...], across[across.shape[0] - 1]]
    tiles = [tile.astype(f32) for tile in tiles]
    correlate(
        [tile[:FEAT_CH] for tile in tiles], [tile[FEAT_CH:] for tile in tiles],
        place, 1.0, wide, extra,
    )
    raw_out[...] = jnp.concatenate([wide[...], extra[...]], axis=1).astype(bf16)
    copy.wait()
    taps_out[...] = toeplitz(kernel)


def volume_kernel(
    place, gain, odd_own, odd_across, even_own, even_across, limit, indices, hidden, raw_own,
    taps_own, out, raw, taps, wide, extra, logit, padded, sems,
):
    band, bands = place[0], place[2]
    is_even = band % 2 == 0
    copies = [
        pltpu.make_async_copy(raw_own, raw, sems.at[0]),
        pltpu.make_async_copy(taps_own, taps, sems.at[1]),
    ]
    for copy in copies:
        copy.start()

    last = odd_across.shape[0] - 1
    odd = [tile.astype(f32) for tile in (odd_across[0], odd_own[...], odd_across[last])]
    even = [tile.astype(f32) for tile in (even_across[0], even_own[...], even_across[last])]
    for b in range(2):
        row = band + 2 * b - 1
        row_ok = ((row >= 0) & (row < bands)).astype(f32)
        tiles = [
            jnp.where(is_even, y, x) if b == 0 else jnp.where(is_even, x, y)
            for x, y in zip(odd, even)
        ]
        correlate(
            [tile[:FEAT_CH] for tile in tiles], [tile[FEAT_CH:] for tile in tiles],
            place, row_ok, wide.at[b], extra.at[b],
        )
    for copy in copies:
        copy.wait()

    lane8 = lax.broadcasted_iota(jnp.int32, (OUT_SLAB, TILE), 1)
    group_at = lax.broadcasted_iota(jnp.int32, (GROUPS, TILE), 0)
    gains = jnp.zeros((GROUPS, TILE), f32)
    for g in range(GROUPS):
        gains = jnp.where(group_at == g, gain[g], gains)
    wanted = [jnp.broadcast_to(indices[t : t + 1, :], (GROUPS, TILE)) for t in range(ITERS)]
    found = [jnp.zeros((GROUPS, TILE), f32) for _ in range(ITERS)]
    for q in range(DISPS // BLOCK):
        at = q * OUT_SLAB
        slabs = [
            jnp.concatenate(
                [wide[b, at : at + SLAB, :], extra[b, at : at + SLAB, :]], axis=1
            ).astype(bf16)
            for b in range(2)
        ]
        slabs.insert(1, raw[at : at + SLAB, :])
        product = dot(taps[...], jnp.concatenate(slabs, axis=0))
        first, middle, last = (
            product[:OUT_SLAB],
            product[OUT_SLAB : 2 * OUT_SLAB],
            product[2 * OUT_SLAB :],
        )
        conv = (
            middle[:, :TILE]
            + jnp.where(
                lane8 == 0,
                pltpu.roll(first[:, TILE:], TILE - 2 * EDGE + 1, 1),
                pltpu.roll(first[:, :TILE], 1, 1),
            )
            + jnp.where(
                lane8 == TILE - 1,
                pltpu.roll(last[:, TILE:], TILE - 1, 1),
                pltpu.roll(last[:, :TILE], TILE - 1, 1),
            )
        )
        centre = slabs[1][:, :TILE].astype(f32)[GROUPS : GROUPS + OUT_SLAB]
        volume = (centre + jnp.maximum(conv, 0.0)).astype(bf16).astype(f32)
        volume = volume.reshape(BLOCK, GROUPS, TILE)
        logit[q * BLOCK : (q + 1) * BLOCK, :] = jnp.sum(volume * gains[None], axis=1)
        for d in range(BLOCK):
            for t in range(ITERS):
                found[t] = found[t] + jnp.where(wanted[t] == q * BLOCK + d, volume[d], 0.0)

    level = lax.broadcasted_iota(jnp.int32, (DISPS, TILE), 0)
    valid = level < limit[...]
    masked = jnp.where(valid, logit[...], floor_logit)
    top = jnp.max(masked, axis=0, keepdims=True)
    weights = jnp.where(valid, jnp.exp(masked - top), 0.0)
    moment = jnp.sum(weights * level.astype(f32), axis=0, keepdims=True)
    start = moment / jnp.sum(weights, axis=0, keepdims=True) / pixel_unit
    high = start.astype(bf16).astype(f32)
    low = (start - high).astype(bf16).astype(f32)
    ends = jnp.where(
        group_at == 0,
        jnp.broadcast_to(high, (GROUPS, TILE)),
        jnp.where(group_at == 1, jnp.broadcast_to(low, (GROUPS, TILE)), 0.0),
    )

    strip = TILE // out.shape[0]
    padded[:EDGE, :] = jnp.zeros((EDGE, HID_CH), f32)
    padded[EDGE : EDGE + TILE, :] = hidden[...].astype(f32)
    padded[EDGE + TILE :, :] = jnp.zeros((WINDOW - EDGE, HID_CH), f32)
    lane = lax.broadcasted_iota(jnp.int32, (GROUPS, TILE), 1)
    for j in range(out.shape[0]):
        part = jnp.zeros((GROUPS, TILE), f32)
        for q, group in enumerate(found + [ends]):
            moved = pltpu.roll(group, (PACK * q + EDGE - strip * j) % TILE, 1)
            part = jnp.where((lane >= PACK * q) & (lane < PACK * q + WINDOW), moved, part)
        block = [padded[strip * j : strip * j + WINDOW, :], part]
        out[strip_at(place, j)] = jnp.concatenate(block, axis=0).astype(bf16)


def strip_at(place, band):
    return jnp.where(place[1] % 2 == 0, band, place[2] - 1 - band)


def keep(line, target, at, values, rows):
    length = values.shape[0]
    start = EDGE + at
    row = lax.broadcasted_iota(jnp.int32, (length, HID_CH), 0) % rows
    line[start : start + length, :] = values
    before = jnp.where(row == 0, 0.0, line[start - 1 : start - 1 + length, :])
    after = jnp.where(row == rows - 1, 0.0, line[start + 1 : start + 1 + length, :])
    target[at : at + length, 0:HID_CH] = before.astype(bf16)
    target[at : at + length, HID_CH : 2 * HID_CH] = values.astype(bf16)
    target[at : at + length, 2 * HID_CH :] = after.astype(bf16)


def refine_kernel(
    place,
    blocks,
    beside,
    hid_weight,
    in_weight,
    out,
    line,
    weight,
    head_row,
    looked,
    hidden_at,
    taps,
    reset_taps,
    in_taps,
    gate,
    level,
    sems,
):
    rows = blocks.shape[0]
    strip = TILE // rows
    copies = [
        pltpu.make_async_copy(
            hid_weight.at[pl.ds((3 * a + b) * HID_CH, HID_CH)],
            weight.at[pl.ds((3 * b + a) * HID_CH, HID_CH)],
            sems.at[3 * a + b],
        )
        for a in range(3)
        for b in range(3)
    ]
    copies.append(
        pltpu.make_async_copy(
            in_weight.at[pl.ds(0, 3 * HID_CH)],
            weight.at[pl.ds(9 * HID_CH, 3 * HID_CH)],
            sems.at[9],
        )
    )
    copies.append(
        pltpu.make_async_copy(
            in_weight.at[pl.ds(3 * HID_CH, 16), pl.ds(0, HID_CH)], head_row, sems.at[10]
        )
    )
    for copy in copies:
        copy.start()

    band, disp, bands, disps = place[0], place[1], place[2], place[3]
    reach = -(-REACH // strip)
    at = strip_at(place, band)
    at_left = (at < reach) & (disp > 0)
    at_right = (at >= bands - reach) & (disp < disps - 1)
    off = strip
    if reach > 1:
        off = strip * (2 * jnp.where(at < reach, at, bands - 1 - at) + 1)
    first = strip * at - EDGE

    def joined(own, other, axis, size, column):
        column = column + first
        ahead = pltpu.roll(other, (size - off) % size, axis)
        behind = pltpu.roll(other, off, axis)
        value = jnp.where((column < 0) & at_left, ahead, 0.0)
        value = jnp.where((column >= TILE) & at_right, behind, value)
        return jnp.where((column >= 0) & (column < TILE), own, value)

    column_h = lax.broadcasted_iota(jnp.int32, (PACK, HID_CH), 0)
    lane = lax.broadcasted_iota(jnp.int32, (GROUPS, TILE), 1)
    column_p = lane % PACK
    at_sub = lax.broadcasted_iota(jnp.int32, (PACK, TILE), 0)
    at_lane = lax.broadcasted_iota(jnp.int32, (PACK, TILE), 1)
    spread = jnp.where(at_sub == at_lane % PACK, 1.0, 0.0).astype(bf16)
    fill = jnp.zeros((PACK, TILE), f32)
    zeros = jnp.zeros((GROUPS, TILE), f32)
    lines = []
    for r in range(rows):
        own, other = blocks[r].astype(f32), beside[r].astype(f32)
        packed = joined(own[WINDOW:], other[WINDOW:], 1, TILE, column_p)
        hidden = joined(own, other, 0, PACK, column_h)[:WINDOW]
        hidden_at[pl.ds(r, WINDOW, stride=rows), :] = hidden
        pieces = []
        for b in range(3):
            moved = packed if b == 1 else pltpu.roll(packed, (1 - b) % TILE, 1)
            for q in range(4):
                pieces.append(
                    jnp.where((lane >= PACK * q) & (lane < PACK * (q + 1)), moved, zeros)
                )
        lines.append(jnp.concatenate(pieces + [fill], axis=0).astype(bf16))
    for r in range(0, rows, 2):
        both = dot_nt(spread, jnp.concatenate(lines[r : r + 2], axis=0))
        for i in range(2):
            part = both[:WINDOW, i * HID_CH : (i + 1) * HID_CH]
            looked[pl.ds(r + i, WINDOW, stride=rows), :] = part
    sub = lax.broadcasted_iota(jnp.int32, (HID_CH, HID_CH), 0)
    ends = jnp.where((sub == PACK + 24) | (sub == PACK + 25), feature_scale, 0.0).astype(bf16)
    level[...] = dot(looked[...].astype(bf16), ends)
    blank = jnp.zeros((EDGE, HID_CH), f32)
    line[:EDGE, :] = blank
    line[EDGE + WINDOW * rows :, :] = blank
    start = EDGE - REACH
    width = strip + 2 * REACH
    keep(line, taps, start * rows, hidden_at[start * rows : (start + width) * rows, :], rows)
    for copy in copies:
        copy.wait()
    head = head_row[...].astype(f32)[0:1] * feature_scale
    head = jnp.broadcast_to(head, (HID_CH, HID_CH)).astype(bf16)

    def beside_columns(target, at, length):
        return [target[at + b * rows : at + b * rows + length, :] for b in (-1, 0, 1)]

    for t in range(ITERS):
        halo = REACH - 1 - 2 * t
        at, length = (EDGE - halo) * rows, (strip + 2 * halo) * rows
        lane_at = lax.broadcasted_iota(jnp.int32, (length, HID_CH), 1)
        tap, channel = lane_at // PACK, lane_at % PACK
        near = [level[at + b * rows : at + b * rows + length, :] for b in (-1, 0, 1)]
        value = jnp.where(tap == 0, near[0], jnp.where(tap == 1, near[1], near[2]))
        at_lookup = (channel >= t * GROUPS) & (channel < (t + 1) * GROUPS)
        value = jnp.where(
            (channel == 3 * GROUPS) & (tap < 3),
            value,
            jnp.where(at_lookup, looked[at : at + length, :], 0.0),
        )
        keep(line, in_taps, at, value, rows)
        lhs = beside_columns(taps, at, length) + [in_taps[at : at + length, :]]
        both = dot(jnp.concatenate(lhs, axis=1), weight[:, : 2 * HID_CH])
        gate[at + rows : at + length - rows, :] = (
            0.5 * jnp.tanh(0.5 * both[rows : length - rows, :HID_CH]) + 0.5
        )
        reset = 0.5 * jnp.tanh(0.5 * both[:, HID_CH:]) + 0.5
        keep(line, reset_taps, at, reset * hidden_at[at : at + length, :], rows)

        at, length = at + rows, length - 2 * rows
        lhs = beside_columns(reset_taps, at, length) + [in_taps[at : at + length, :]]
        candidate = jnp.tanh(dot(jnp.concatenate(lhs, axis=1), weight[:, 2 * HID_CH :]))
        hidden = hidden_at[at : at + length, :]
        hidden = hidden + gate[at : at + length, :] * (candidate - hidden)
        column = lax.broadcasted_iota(jnp.int32, (length, HID_CH), 0) // rows
        column = column + (at // rows + first)
        inside = ((column >= 0) | (disp > 0)) & ((column < TILE) | (disp < disps - 1))
        hidden = jnp.where(inside, hidden, 0.0).astype(bf16)
        level[at : at + length, :] += dot_nt(hidden, head)
        hidden_at[at : at + length, :] = hidden.astype(f32)
        if t < ITERS - 1:
            keep(line, taps, at, hidden.astype(f32), rows)

    lane = lax.broadcasted_iota(jnp.int32, (strip, HID_CH), 1)
    gap = [] if strip == EDGE else [jnp.zeros((EDGE - strip, HID_CH), f32)]
    for r in range(rows):
        here = pl.ds(EDGE * rows + r, strip, stride=rows)
        value = level[here, :] * (1.0 / feature_scale)
        high = value.astype(bf16).astype(f32)
        middle = (value - high).astype(bf16).astype(f32)
        parts = jnp.where(lane == 0, high, jnp.where(lane == 1, middle, value - high - middle))
        parts = jnp.where(lane < 3, parts, 0.0)
        block = [hidden_at[here, :]] + gap + [parts] + gap
        out[r] = jnp.concatenate(block, axis=0).astype(bf16)


def stays_kernel(place, blocks, out):
    out[...] = blocks[place[0]].astype(f32)


def unpack_kernel(place, blocks, stays, disparity_out, hidden_out):
    count = blocks.shape[0]
    strip = TILE // count
    bands = [strip_at(place, j) for j in range(count)]
    held = [jnp.where(place[0] == j, stays[...], blocks[j].astype(f32)) for j in bands]
    hidden = jnp.concatenate([block[:strip] for block in held], axis=0)
    hidden_out[0] = hidden.astype(bf16)
    parts = jnp.concatenate([block[EDGE : EDGE + strip] for block in held], axis=0).T
    disparity_out[...] = parts[0:1] + parts[1:2] + parts[2:3]


def in_hbm(value):
    return pltpu.with_memory_space_constraint(value, pltpu.HBM)


def to_sides(value):
    disps = lax.axis_size("disp")
    right = [(d, d + 1) for d in range(disps - 1)]
    left = [(d + 1, d) for d in range(disps - 1)]
    if disps == 2:
        return lax.ppermute(value, "disp", right + left)[None]
    return jnp.stack([lax.ppermute(value, "disp", right), lax.ppermute(value, "disp", left)])


def across_border(value):
    bands, disps = lax.axis_size("band"), lax.axis_size("disp")
    pairs = []
    for i in range(-(-REACH * bands // TILE)):
        for d in range(disps - 1):
            band = bands - 1 - i if d % 2 == 0 else i
            pairs += [
                (band * disps + d, band * disps + d + 1),
                (band * disps + d + 1, band * disps + d),
            ]
    return lax.ppermute(value, ("band", "disp"), pairs)


def to_rows(value, shift):
    bands = lax.axis_size("band")
    return lax.ppermute(
        value, "band", [(i, shift(i)) for i in range(bands) if 0 <= shift(i) < bands]
    )


def odd_pair(i):
    return i ^ 1


def even_pair(i):
    return i - 1 if i % 2 == 0 else i + 1


def local(
    feat_left,
    feat_right,
    limit,
    indices,
    hidden_start,
    vol_kernel,
    group_gain,
    hid_kernel,
    in_kernel,
    head_weight,
):
    bands, disps = lax.axis_size("band"), lax.axis_size("disp")
    place = jnp.stack(
        [lax.axis_index("band"), lax.axis_index("disp"), jnp.int32(bands), jnp.int32(disps)]
    ).astype(jnp.int32)
    smem = pl.BlockSpec(memory_space=pltpu.SMEM)
    vmem = pl.BlockSpec(memory_space=pltpu.VMEM)
    hbm = pl.BlockSpec(memory_space=pltpu.HBM)
    anywhere = pl.BlockSpec(memory_space=pl.ANY)
    padded = (DISPS + 2) * GROUPS

    feats = jnp.concatenate([feat_left[0], feat_right[0]], axis=0)
    odd_own, even_own = to_rows(feats, odd_pair), to_rows(feats, even_pair)
    across = to_sides(feats)
    raw_own, taps = pl.pallas_call(
        own_row_kernel,
        out_shape=(
            jax.ShapeDtypeStruct((padded, 2 * TILE), bf16),
            jax.ShapeDtypeStruct((3 * OUT_SLAB, 3 * SLAB), bf16),
        ),
        in_specs=[smem, vmem, vmem, hbm],
        out_specs=(vmem, vmem),
        scratch_shapes=[
            pltpu.VMEM((padded, TILE), f32),
            pltpu.VMEM((padded, TILE), f32),
            pltpu.VMEM((27, GROUPS, GROUPS), bf16),
            pltpu.SemaphoreType.DMA((1,)),
        ],
        compiler_params=pltpu.CompilerParams(vmem_limit_bytes=16 * 2**20),
        cost_estimate=pl.CostEstimate(flops=2 * 10**9, bytes_accessed=4 * 2**20, transcendentals=0),
    )(place, feats, across, in_hbm(vol_kernel.reshape(27, GROUPS, GROUPS)))
    odd_own, even_own, raw_own, taps = lax.optimization_barrier(
        (odd_own, even_own, raw_own, taps)
    )
    odd_across, even_across = to_sides(odd_own), to_sides(even_own)

    in_weight = jnp.concatenate(
        [in_kernel[:, :, :GROUPS]] * ITERS + [in_kernel[:, :, GROUPS:]], axis=2
    )
    in_weight = jnp.pad(in_weight, ((0, 0), (0, 1), (0, PACK - in_weight.shape[2]), (0, 0)))
    in_weight = jnp.concatenate(
        [
            in_weight.reshape(3 * HID_CH, 3 * HID_CH),
            jnp.pad(head_weight.reshape(1, HID_CH), ((0, 15), (0, 2 * HID_CH))),
        ],
        axis=0,
    )

    packed = pl.pallas_call(
        volume_kernel,
        out_shape=jax.ShapeDtypeStruct((bands, PACK, TILE), bf16),
        in_specs=[smem, smem] + [vmem] * 7 + [hbm, hbm],
        out_specs=vmem,
        scratch_shapes=[
            pltpu.VMEM((padded, 2 * TILE), bf16),
            pltpu.VMEM((3 * OUT_SLAB, 3 * SLAB), bf16),
            pltpu.VMEM((2, padded, TILE), f32),
            pltpu.VMEM((2, padded, TILE), f32),
            pltpu.VMEM((DISPS, TILE), f32),
            pltpu.VMEM((TILE + WINDOW, HID_CH), f32),
            pltpu.SemaphoreType.DMA((2,)),
        ],
        compiler_params=pltpu.CompilerParams(vmem_limit_bytes=24 * 2**20),
        cost_estimate=pl.CostEstimate(
            flops=5 * 10**9, bytes_accessed=16 * 2**20, transcendentals=DISPS * TILE
        ),
    )(
        place, group_gain, odd_own, odd_across, even_own, even_across,
        limit, indices[:, 0], hidden_start[0], raw_own, taps,
    )

    packed = lax.all_to_all(packed, "band", 0, 0, tiled=True)
    packed, in_weight = lax.optimization_barrier((packed, in_weight))
    beside = across_border(packed)

    pixels = WINDOW * bands
    refined = pl.pallas_call(
        refine_kernel,
        out_shape=jax.ShapeDtypeStruct((bands, 2 * EDGE, HID_CH), bf16),
        in_specs=[smem, vmem, vmem, anywhere, hbm],
        out_specs=vmem,
        scratch_shapes=[
            pltpu.VMEM((pixels + 2 * EDGE, HID_CH), f32),
            pltpu.VMEM((12 * HID_CH, 3 * HID_CH), bf16),
            pltpu.VMEM((16, HID_CH), bf16),
            pltpu.VMEM((pixels, HID_CH), f32),
            pltpu.VMEM((pixels, HID_CH), f32),
            pltpu.VMEM((pixels, 3 * HID_CH), bf16),
            pltpu.VMEM((pixels, 3 * HID_CH), bf16),
            pltpu.VMEM((pixels, 3 * HID_CH), bf16),
            pltpu.VMEM((pixels, HID_CH), f32),
            pltpu.VMEM((pixels, HID_CH), f32),
            pltpu.SemaphoreType.DMA((11,)),
        ],
        compiler_params=pltpu.CompilerParams(vmem_limit_bytes=32 * 2**20),
    )(
        place, packed, beside,
        hid_kernel.reshape(9 * HID_CH, 3 * HID_CH), in_hbm(in_weight),
    )
    stays = pl.pallas_call(
        stays_kernel,
        out_shape=jax.ShapeDtypeStruct((2 * EDGE, HID_CH), f32),
        in_specs=[smem, vmem],
        out_specs=vmem,
        cost_estimate=pl.CostEstimate(flops=10**9, bytes_accessed=2**20, transcendentals=0),
    )(place, refined)
    refined = lax.all_to_all(refined, "band", 0, 0, tiled=True)
    disparity, hidden = pl.pallas_call(
        unpack_kernel,
        out_shape=(
            jax.ShapeDtypeStruct((1, TILE), f32),
            jax.ShapeDtypeStruct((1, TILE, HID_CH), bf16),
        ),
        in_specs=[smem, vmem, vmem],
        out_specs=(vmem, vmem),
    )(place, refined, stays)
    return (disparity, hidden)


def solution(mesh):
    in_specs = (
        P("band", None, "disp"),
        P("band", None, "disp"),
        P("band", "disp"),
        P(None, "band", "disp"),
        P("band", "disp", None),
        P(),
        P(),
        P(),
        P(),
        P(),
    )
    out_specs = (P("band", "disp"), P("band", "disp", None))
    return jax.shard_map(local, mesh=mesh, in_specs=in_specs, out_specs=out_specs, check_vma=False)
```

```python
import jax
import jax.numpy as jnp
from jax import lax
from jax.experimental import pallas as pl
from jax.experimental.pallas import tpu as pltpu
from jax.sharding import PartitionSpec as P

GROUPS = 8
DISPS = 96
FEAT_CH = 96
HID_CH = 128
ITERS = 3
TILE = 128
REACH = 2 * ITERS
EDGE = 8
WINDOW = 24
PACK = 32
BLOCK = 8
SLAB = (BLOCK + 2) * GROUPS
OUT_SLAB = BLOCK * GROUPS

pixel_unit = 8.0
feature_scale = 0.25
floor_logit = -1e30

f32 = jnp.float32
bf16 = jnp.bfloat16


def dot(a, b):
    return jnp.dot(a, b, preferred_element_type=f32)


def dot_nt(a, b):
    return lax.dot_general(a, b, (((1,), (1,)), ((), ())), preferred_element_type=f32)


def copy_all(copies):
    for copy in copies:
        copy.start()
    for copy in copies:
        copy.wait()


def toeplitz(vol_kernel):
    size = 27 * GROUPS
    flat = vol_kernel[...].astype(f32).reshape(size, GROUPS)
    flat = jnp.concatenate([flat, jnp.zeros((size, TILE - GROUPS), f32)], axis=1).T[:GROUPS]
    row = lax.broadcasted_iota(jnp.int32, (9 * GROUPS, size), 0) >> 3
    tap = lax.broadcasted_iota(jnp.int32, (9 * GROUPS, size), 1) >> 3
    tap_a = (tap >= 9).astype(jnp.int32) + (tap >= 18).astype(jnp.int32)
    within = tap - 9 * tap_a
    tap_b = (within >= 3).astype(jnp.int32) + (within >= 6).astype(jnp.int32)
    tap_e = within - 3 * tap_b
    pairs = jnp.where(
        row == 3 * tap_a + tap_e, jnp.concatenate([flat] * 9, axis=0), 0.0
    ).astype(bf16)
    from_row = lax.broadcasted_iota(jnp.int32, (size, 3 * SLAB), 0)
    to = lax.broadcasted_iota(jnp.int32, (size, 3 * SLAB), 1)
    from_tap = from_row >> 3
    from_in = from_tap - 9 * ((from_tap >= 9).astype(jnp.int32) + (from_tap >= 18).astype(jnp.int32))
    from_b = (from_in >= 3).astype(jnp.int32) + (from_in >= 6).astype(jnp.int32)
    to_b = (to >= SLAB).astype(jnp.int32) + (to >= 2 * SLAB).astype(jnp.int32)
    repeat = jnp.where((from_b == to_b) & ((from_row & 7) == (to & 7)), 1.0, 0.0).astype(bf16)
    spread = dot(pairs, repeat)
    to = lax.broadcasted_iota(jnp.int32, (GROUPS, 3 * SLAB), 1)
    to_b = (to >= SLAB).astype(jnp.int32) + (to >= 2 * SLAB).astype(jnp.int32)
    to_d = (to - SLAB * to_b) >> 3
    rows = []
    for e in range(3):
        for d in range(BLOCK):
            value = jnp.zeros((GROUPS, 3 * SLAB), f32)
            for a in range(3):
                at = (3 * a + e) * GROUPS
                value = jnp.where(to_d == d + a, spread[at : at + GROUPS], value)
            rows.append(value)
    return jnp.concatenate(rows, axis=0).astype(bf16)


def interleaved(values):
    stacked = jnp.swapaxes(jnp.stack(values), 0, 1)
    return stacked.reshape(values[0].shape[0] * len(values), values[0].shape[1])


def correlate(lefts, rights, place, row_ok, wide, extra):
    has_left = (place[1] > 0).astype(f32)
    has_right = (place[1] < place[3] - 1).astype(f32)
    lane = lax.broadcasted_iota(jnp.int32, (TILE, TILE), 1)
    sub = lax.broadcasted_iota(jnp.int32, (TILE, TILE), 0)
    flip = jnp.where(lane + sub == TILE - 1, 1.0, 0.0).astype(bf16)
    per_group = FEAT_CH // GROUPS
    channel = lax.broadcasted_iota(jnp.int32, (32, FEAT_CH), 1)
    group_masks = [
        (channel >= g * per_group) & (channel < (g + 1) * per_group) for g in range(GROUPS)
    ]
    lane96 = lax.broadcasted_iota(jnp.int32, (FEAT_CH, TILE), 1)
    zero_slab = jnp.zeros((GROUPS, TILE), f32)
    for at in (0, (DISPS + 1) * GROUPS):
        wide[pl.ds(at, GROUPS), :] = zero_slab
        extra[pl.ds(at, GROUPS), :] = zero_slab

    own_t = (lefts[1] * row_ok).T
    side_t = jnp.where(
        lane96 < EDGE,
        lefts[2] * (has_right * row_ok),
        jnp.where(lane96 >= TILE - EDGE, lefts[0] * (has_left * row_ok), 0.0),
    ).T
    sources = jnp.concatenate([rights[2] * has_right, rights[1], rights[0] * has_left], axis=0)
    flipped = dot(sources.astype(bf16), flip)
    reverse = jnp.concatenate(
        [flipped[i * FEAT_CH : (i + 1) * FEAT_CH] for i in range(3)], axis=1
    )
    windows = [
        reverse[:, 2 * TILE - 32 - 32 * k : 3 * TILE - 32 - 32 * k].astype(bf16)
        for k in range(-1, 5)
    ]

    def by_group(rows):
        count = rows.shape[0]
        parts = [jnp.where(m[:count], rows, 0.0) for m in group_masks]
        return jnp.concatenate(parts, axis=0).astype(bf16)

    def shear(product, g, count, first):
        rows = product[count * g : count * g + count]
        return pltpu.roll(rows, TILE - 31 + first, 1, stride=1, stride_axis=0)

    products = [
        dot(by_group(own_t[32 * k : 32 * k + 32]), windows[k + 1]) for k in range(TILE // 32)
    ]
    after = dot(by_group(side_t[:EDGE]), windows[5])
    before = dot(by_group(side_t[TILE - EDGE :]), windows[0])
    parts, sides = [], []
    for g in range(GROUPS):
        part = jnp.concatenate([shear(product, g, 32, 0) for product in products], axis=0)
        parts.append(part.T[:DISPS])
        sides += [shear(after, g, EDGE, 0), shear(before, g, EDGE, 32 - EDGE)]
    part = jnp.concatenate(sides, axis=0).T[:DISPS]
    sides = [part if g == 0 else pltpu.roll(part, TILE - 2 * EDGE * g, 1) for g in range(GROUPS)]
    for target, values in ((wide, parts), (extra, sides)):
        target[GROUPS : GROUPS + DISPS * GROUPS, :] = interleaved(values) * (1.0 / per_group)


def own_row_kernel(place, own, across, vol_kernel, raw_out, taps_out, wide, extra, kernel, sem):
    copy = pltpu.make_async_copy(vol_kernel, kernel, sem.at[0])
    copy.start()
    tiles = [across[0], own[...], across[across.shape[0] - 1]]
    tiles = [tile.astype(f32) for tile in tiles]
    correlate(
        [tile[:FEAT_CH] for tile in tiles], [tile[FEAT_CH:] for tile in tiles],
        place, 1.0, wide, extra,
    )
    raw_out[...] = jnp.concatenate([wide[...], extra[...]], axis=1).astype(bf16)
    copy.wait()
    taps_out[...] = toeplitz(kernel)


def volume_kernel(
    place, gain, odd_own, odd_across, even_own, even_across, limit, indices, hidden, raw_own,
    taps_own, out, raw, taps, wide, extra, logit, padded, sems,
):
    band, bands = place[0], place[2]
    is_even = band % 2 == 0
    copies = [
        pltpu.make_async_copy(raw_own, raw, sems.at[0]),
        pltpu.make_async_copy(taps_own, taps, sems.at[1]),
    ]
    for copy in copies:
        copy.start()

    last = odd_across.shape[0] - 1
    odd = [tile.astype(f32) for tile in (odd_across[0], odd_own[...], odd_across[last])]
    even = [tile.astype(f32) for tile in (even_across[0], even_own[...], even_across[last])]
    for b in range(2):
        row = band + 2 * b - 1
        row_ok = ((row >= 0) & (row < bands)).astype(f32)
        tiles = [
            jnp.where(is_even, y, x) if b == 0 else jnp.where(is_even, x, y)
            for x, y in zip(odd, even)
        ]
        correlate(
            [tile[:FEAT_CH] for tile in tiles], [tile[FEAT_CH:] for tile in tiles],
            place, row_ok, wide.at[b], extra.at[b],
        )
    for copy in copies:
        copy.wait()

    lane8 = lax.broadcasted_iota(jnp.int32, (OUT_SLAB, TILE), 1)
    group_at = lax.broadcasted_iota(jnp.int32, (GROUPS, TILE), 0)
    gains = jnp.zeros((GROUPS, TILE), f32)
    for g in range(GROUPS):
        gains = jnp.where(group_at == g, gain[g], gains)
    wanted = [jnp.broadcast_to(indices[t : t + 1, :], (GROUPS, TILE)) for t in range(ITERS)]
    found = [jnp.zeros((GROUPS, TILE), f32) for _ in range(ITERS)]
    for q in range(DISPS // BLOCK):
        at = q * OUT_SLAB
        slabs = [
            jnp.concatenate(
                [wide[b, at : at + SLAB, :], extra[b, at : at + SLAB, :]], axis=1
            ).astype(bf16)
            for b in range(2)
        ]
        slabs.insert(1, raw[at : at + SLAB, :])
        product = dot(taps[...], jnp.concatenate(slabs, axis=0))
        first, middle, last = (
            product[:OUT_SLAB],
            product[OUT_SLAB : 2 * OUT_SLAB],
            product[2 * OUT_SLAB :],
        )
        conv = (
            middle[:, :TILE]
            + jnp.where(
                lane8 == 0,
                pltpu.roll(first[:, TILE:], TILE - 2 * EDGE + 1, 1),
                pltpu.roll(first[:, :TILE], 1, 1),
            )
            + jnp.where(
                lane8 == TILE - 1,
                pltpu.roll(last[:, TILE:], TILE - 1, 1),
                pltpu.roll(last[:, :TILE], TILE - 1, 1),
            )
        )
        centre = slabs[1][:, :TILE].astype(f32)[GROUPS : GROUPS + OUT_SLAB]
        volume = (centre + jnp.maximum(conv, 0.0)).astype(bf16).astype(f32)
        volume = volume.reshape(BLOCK, GROUPS, TILE)
        logit[q * BLOCK : (q + 1) * BLOCK, :] = jnp.sum(volume * gains[None], axis=1)
        for d in range(BLOCK):
            for t in range(ITERS):
                found[t] = found[t] + jnp.where(wanted[t] == q * BLOCK + d, volume[d], 0.0)

    level = lax.broadcasted_iota(jnp.int32, (DISPS, TILE), 0)
    valid = level < limit[...]
    masked = jnp.where(valid, logit[...], floor_logit)
    top = jnp.max(masked, axis=0, keepdims=True)
    weights = jnp.where(valid, jnp.exp(masked - top), 0.0)
    moment = jnp.sum(weights * level.astype(f32), axis=0, keepdims=True)
    start = moment / jnp.sum(weights, axis=0, keepdims=True) / pixel_unit
    high = start.astype(bf16).astype(f32)
    low = (start - high).astype(bf16).astype(f32)
    ends = jnp.where(
        group_at == 0,
        jnp.broadcast_to(high, (GROUPS, TILE)),
        jnp.where(group_at == 1, jnp.broadcast_to(low, (GROUPS, TILE)), 0.0),
    )

    strip = TILE // out.shape[0]
    padded[:EDGE, :] = jnp.zeros((EDGE, HID_CH), f32)
    padded[EDGE : EDGE + TILE, :] = hidden[...].astype(f32)
    padded[EDGE + TILE :, :] = jnp.zeros((WINDOW - EDGE, HID_CH), f32)
    lane = lax.broadcasted_iota(jnp.int32, (GROUPS, TILE), 1)
    for j in range(out.shape[0]):
        part = jnp.zeros((GROUPS, TILE), f32)
        for q, group in enumerate(found + [ends]):
            moved = pltpu.roll(group, (PACK * q + EDGE - strip * j) % TILE, 1)
            part = jnp.where((lane >= PACK * q) & (lane < PACK * q + WINDOW), moved, part)
        block = [padded[strip * j : strip * j + WINDOW, :], part]
        out[strip_at(place, j)] = jnp.concatenate(block, axis=0).astype(bf16)


def strip_at(place, band):
    return jnp.where(place[1] % 2 == 0, band, place[2] - 1 - band)


def keep(line, target, at, values, rows):
    length = values.shape[0]
    start = EDGE + at
    row = lax.broadcasted_iota(jnp.int32, (length, HID_CH), 0) % rows
    line[start : start + length, :] = values
    before = jnp.where(row == 0, 0.0, line[start - 1 : start - 1 + length, :])
    after = jnp.where(row == rows - 1, 0.0, line[start + 1 : start + 1 + length, :])
    target[at : at + length, 0:HID_CH] = before.astype(bf16)
    target[at : at + length, HID_CH : 2 * HID_CH] = values.astype(bf16)
    target[at : at + length, 2 * HID_CH :] = after.astype(bf16)


def refine_kernel(
    place,
    blocks,
    beside,
    hid_weight,
    in_weight,
    out,
    line,
    weight,
    head_row,
    looked,
    hidden_at,
    taps,
    reset_taps,
    in_taps,
    gate,
    level,
    sems,
):
    rows = blocks.shape[0]
    strip = TILE // rows
    copies = [
        pltpu.make_async_copy(
            hid_weight.at[pl.ds((3 * a + b) * HID_CH, HID_CH)],
            weight.at[pl.ds((3 * b + a) * HID_CH, HID_CH)],
            sems.at[3 * a + b],
        )
        for a in range(3)
        for b in range(3)
    ]
    copies.append(
        pltpu.make_async_copy(
            in_weight.at[pl.ds(0, 3 * HID_CH)],
            weight.at[pl.ds(9 * HID_CH, 3 * HID_CH)],
            sems.at[9],
        )
    )
    copies.append(
        pltpu.make_async_copy(
            in_weight.at[pl.ds(3 * HID_CH, 16), pl.ds(0, HID_CH)], head_row, sems.at[10]
        )
    )
    for copy in copies:
        copy.start()

    band, disp, bands, disps = place[0], place[1], place[2], place[3]
    reach = -(-REACH // strip)
    at = strip_at(place, band)
    at_left = (at < reach) & (disp > 0)
    at_right = (at >= bands - reach) & (disp < disps - 1)
    off = strip
    if reach > 1:
        off = strip * (2 * jnp.where(at < reach, at, bands - 1 - at) + 1)
    first = strip * at - EDGE

    def joined(own, other, axis, size, column):
        column = column + first
        ahead = pltpu.roll(other, (size - off) % size, axis)
        behind = pltpu.roll(other, off, axis)
        value = jnp.where((column < 0) & at_left, ahead, 0.0)
        value = jnp.where((column >= TILE) & at_right, behind, value)
        return jnp.where((column >= 0) & (column < TILE), own, value)

    column_h = lax.broadcasted_iota(jnp.int32, (PACK, HID_CH), 0)
    lane = lax.broadcasted_iota(jnp.int32, (GROUPS, TILE), 1)
    column_p = lane % PACK
    at_sub = lax.broadcasted_iota(jnp.int32, (PACK, TILE), 0)
    at_lane = lax.broadcasted_iota(jnp.int32, (PACK, TILE), 1)
    spread = jnp.where(at_sub == at_lane % PACK, 1.0, 0.0).astype(bf16)
    fill = jnp.zeros((PACK, TILE), f32)
    zeros = jnp.zeros((GROUPS, TILE), f32)
    lines, hiddens, found = [], [], []
    for r in range(rows):
        own, other = blocks[r].astype(f32), beside[r].astype(f32)
        packed = joined(own[WINDOW:], other[WINDOW:], 1, TILE, column_p)
        hidden = joined(own, other, 0, PACK, column_h)[:WINDOW]
        hiddens.append(hidden)
        pieces = []
        for b in range(3):
            moved = packed if b == 1 else pltpu.roll(packed, (1 - b) % TILE, 1)
            for q in range(4):
                pieces.append(
                    jnp.where((lane >= PACK * q) & (lane < PACK * (q + 1)), moved, zeros)
                )
        lines.append(jnp.concatenate(pieces + [fill], axis=0).astype(bf16))
    for r in range(0, rows, 2):
        both = dot_nt(spread, jnp.concatenate(lines[r : r + 2], axis=0))
        for i in range(2):
            found.append(both[:WINDOW, i * HID_CH : (i + 1) * HID_CH])
    hidden_at[...] = interleaved(hiddens)
    looked[...] = interleaved(found)
    sub = lax.broadcasted_iota(jnp.int32, (HID_CH, HID_CH), 0)
    ends = jnp.where((sub == PACK + 24) | (sub == PACK + 25), feature_scale, 0.0).astype(bf16)
    level[...] = dot(looked[...].astype(bf16), ends)
    blank = jnp.zeros((EDGE, HID_CH), f32)
    line[:EDGE, :] = blank
    line[EDGE + WINDOW * rows :, :] = blank
    start = EDGE - REACH
    width = strip + 2 * REACH
    keep(line, taps, start * rows, hidden_at[start * rows : (start + width) * rows, :], rows)
    for copy in copies:
        copy.wait()
    head = head_row[...].astype(f32)[0:1] * feature_scale
    head = jnp.broadcast_to(head, (HID_CH, HID_CH)).astype(bf16)

    def beside_columns(target, at, length):
        return [target[at + b * rows : at + b * rows + length, :] for b in (-1, 0, 1)]

    for t in range(ITERS):
        halo = REACH - 1 - 2 * t
        at, length = (EDGE - halo) * rows, (strip + 2 * halo) * rows
        lane_at = lax.broadcasted_iota(jnp.int32, (length, HID_CH), 1)
        tap, channel = lane_at // PACK, lane_at % PACK
        near = [level[at + b * rows : at + b * rows + length, :] for b in (-1, 0, 1)]
        value = jnp.where(tap == 0, near[0], jnp.where(tap == 1, near[1], near[2]))
        at_lookup = (channel >= t * GROUPS) & (channel < (t + 1) * GROUPS)
        value = jnp.where(
            (channel == 3 * GROUPS) & (tap < 3),
            value,
            jnp.where(at_lookup, looked[at : at + length, :], 0.0),
        )
        keep(line, in_taps, at, value, rows)
        lhs = beside_columns(taps, at, length) + [in_taps[at : at + length, :]]
        both = dot(jnp.concatenate(lhs, axis=1), weight[:, : 2 * HID_CH])
        gate[at + rows : at + length - rows, :] = (
            0.5 * jnp.tanh(0.5 * both[rows : length - rows, :HID_CH]) + 0.5
        )
        reset = 0.5 * jnp.tanh(0.5 * both[:, HID_CH:]) + 0.5
        keep(line, reset_taps, at, reset * hidden_at[at : at + length, :], rows)

        at, length = at + rows, length - 2 * rows
        lhs = beside_columns(reset_taps, at, length) + [in_taps[at : at + length, :]]
        candidate = jnp.tanh(dot(jnp.concatenate(lhs, axis=1), weight[:, 2 * HID_CH :]))
        hidden = hidden_at[at : at + length, :]
        hidden = hidden + gate[at : at + length, :] * (candidate - hidden)
        column = lax.broadcasted_iota(jnp.int32, (length, HID_CH), 0) // rows
        column = column + (at // rows + first)
        inside = ((column >= 0) | (disp > 0)) & ((column < TILE) | (disp < disps - 1))
        hidden = jnp.where(inside, hidden, 0.0).astype(bf16)
        level[at : at + length, :] += dot_nt(hidden, head)
        hidden_at[at : at + length, :] = hidden.astype(f32)
        if t < ITERS - 1:
            keep(line, taps, at, hidden.astype(f32), rows)

    lane = lax.broadcasted_iota(jnp.int32, (strip, HID_CH), 1)
    gap = [] if strip == EDGE else [jnp.zeros((EDGE - strip, HID_CH), f32)]
    final = slice(EDGE * rows, (EDGE + strip) * rows)
    hidden = jnp.swapaxes(hidden_at[final, :].reshape(strip, rows, HID_CH), 0, 1)
    levels = jnp.swapaxes(level[final, :].reshape(strip, rows, HID_CH), 0, 1)
    for r in range(rows):
        value = levels[r] * (1.0 / feature_scale)
        high = value.astype(bf16).astype(f32)
        middle = (value - high).astype(bf16).astype(f32)
        parts = jnp.where(lane == 0, high, jnp.where(lane == 1, middle, value - high - middle))
        parts = jnp.where(lane < 3, parts, 0.0)
        block = [hidden[r]] + gap + [parts] + gap
        out[r] = jnp.concatenate(block, axis=0).astype(bf16)


def unpack_kernel(place, blocks, disparity_out, hidden_out):
    count = blocks.shape[0]
    strip = TILE // count
    held = [blocks[strip_at(place, j)].astype(f32) for j in range(count)]
    hidden = jnp.concatenate([block[:strip] for block in held], axis=0)
    hidden_out[0] = hidden.astype(bf16)
    parts = jnp.concatenate([block[EDGE : EDGE + strip] for block in held], axis=0).T
    disparity_out[...] = parts[0:1] + parts[1:2] + parts[2:3]


def in_hbm(value):
    return pltpu.with_memory_space_constraint(value, pltpu.HBM)


def to_sides(value):
    disps = lax.axis_size("disp")
    right = [(d, d + 1) for d in range(disps - 1)]
    left = [(d + 1, d) for d in range(disps - 1)]
    if disps == 2:
        return lax.ppermute(value, "disp", right + left)[None]
    return jnp.stack([lax.ppermute(value, "disp", right), lax.ppermute(value, "disp", left)])


def across_border(value):
    bands, disps = lax.axis_size("band"), lax.axis_size("disp")
    pairs = []
    for i in range(-(-REACH * bands // TILE)):
        for d in range(disps - 1):
            band = bands - 1 - i if d % 2 == 0 else i
            pairs += [
                (band * disps + d, band * disps + d + 1),
                (band * disps + d + 1, band * disps + d),
            ]
    return lax.ppermute(value, ("band", "disp"), pairs)


def to_rows(value, shift):
    bands = lax.axis_size("band")
    return lax.ppermute(
        value, "band", [(i, shift(i)) for i in range(bands) if 0 <= shift(i) < bands]
    )


def odd_pair(i):
    return i ^ 1


def even_pair(i):
    return i - 1 if i % 2 == 0 else i + 1


def local(
    feat_left,
    feat_right,
    limit,
    indices,
    hidden_start,
    vol_kernel,
    group_gain,
    hid_kernel,
    in_kernel,
    head_weight,
):
    bands, disps = lax.axis_size("band"), lax.axis_size("disp")
    place = jnp.stack(
        [lax.axis_index("band"), lax.axis_index("disp"), jnp.int32(bands), jnp.int32(disps)]
    ).astype(jnp.int32)
    smem = pl.BlockSpec(memory_space=pltpu.SMEM)
    vmem = pl.BlockSpec(memory_space=pltpu.VMEM)
    hbm = pl.BlockSpec(memory_space=pltpu.HBM)
    anywhere = pl.BlockSpec(memory_space=pl.ANY)
    padded = (DISPS + 2) * GROUPS

    feats = jnp.concatenate([feat_left[0], feat_right[0]], axis=0)
    odd_own, even_own = to_rows(feats, odd_pair), to_rows(feats, even_pair)
    across = to_sides(feats)
    raw_own, taps = pl.pallas_call(
        own_row_kernel,
        out_shape=(
            jax.ShapeDtypeStruct((padded, 2 * TILE), bf16),
            jax.ShapeDtypeStruct((3 * OUT_SLAB, 3 * SLAB), bf16),
        ),
        in_specs=[smem, vmem, vmem, hbm],
        out_specs=(vmem, vmem),
        scratch_shapes=[
            pltpu.VMEM((padded, TILE), f32),
            pltpu.VMEM((padded, TILE), f32),
            pltpu.VMEM((27, GROUPS, GROUPS), bf16),
            pltpu.SemaphoreType.DMA((1,)),
        ],
        compiler_params=pltpu.CompilerParams(vmem_limit_bytes=16 * 2**20),
        cost_estimate=pl.CostEstimate(flops=2 * 10**9, bytes_accessed=4 * 2**20, transcendentals=0),
    )(place, feats, across, in_hbm(vol_kernel.reshape(27, GROUPS, GROUPS)))
    odd_own, even_own, raw_own, taps = lax.optimization_barrier(
        (odd_own, even_own, raw_own, taps)
    )
    odd_across, even_across = to_sides(odd_own), to_sides(even_own)

    in_weight = jnp.concatenate(
        [in_kernel[:, :, :GROUPS]] * ITERS + [in_kernel[:, :, GROUPS:]], axis=2
    )
    in_weight = jnp.pad(in_weight, ((0, 0), (0, 1), (0, PACK - in_weight.shape[2]), (0, 0)))
    in_weight = jnp.concatenate(
        [
            in_weight.reshape(3 * HID_CH, 3 * HID_CH),
            jnp.pad(head_weight.reshape(1, HID_CH), ((0, 15), (0, 2 * HID_CH))),
        ],
        axis=0,
    )

    packed = pl.pallas_call(
        volume_kernel,
        out_shape=jax.ShapeDtypeStruct((bands, PACK, TILE), bf16),
        in_specs=[smem, smem] + [vmem] * 7 + [hbm, hbm],
        out_specs=vmem,
        scratch_shapes=[
            pltpu.VMEM((padded, 2 * TILE), bf16),
            pltpu.VMEM((3 * OUT_SLAB, 3 * SLAB), bf16),
            pltpu.VMEM((2, padded, TILE), f32),
            pltpu.VMEM((2, padded, TILE), f32),
            pltpu.VMEM((DISPS, TILE), f32),
            pltpu.VMEM((TILE + WINDOW, HID_CH), f32),
            pltpu.SemaphoreType.DMA((2,)),
        ],
        compiler_params=pltpu.CompilerParams(vmem_limit_bytes=24 * 2**20),
        cost_estimate=pl.CostEstimate(
            flops=5 * 10**9, bytes_accessed=16 * 2**20, transcendentals=DISPS * TILE
        ),
    )(
        place, in_hbm(group_gain), odd_own, odd_across, even_own, even_across,
        in_hbm(limit), in_hbm(indices[:, 0]), in_hbm(hidden_start[0]), raw_own, taps,
    )

    packed = lax.all_to_all(packed, "band", 0, 0, tiled=True)
    packed, in_weight = lax.optimization_barrier((packed, in_weight))
    beside = across_border(packed)

    pixels = WINDOW * bands
    refined = pl.pallas_call(
        refine_kernel,
        out_shape=jax.ShapeDtypeStruct((bands, 2 * EDGE, HID_CH), bf16),
        in_specs=[smem, vmem, vmem, anywhere, hbm],
        out_specs=vmem,
        scratch_shapes=[
            pltpu.VMEM((pixels + 2 * EDGE, HID_CH), f32),
            pltpu.VMEM((12 * HID_CH, 3 * HID_CH), bf16),
            pltpu.VMEM((16, HID_CH), bf16),
            pltpu.VMEM((pixels, HID_CH), f32),
            pltpu.VMEM((pixels, HID_CH), f32),
            pltpu.VMEM((pixels, 3 * HID_CH), bf16),
            pltpu.VMEM((pixels, 3 * HID_CH), bf16),
            pltpu.VMEM((pixels, 3 * HID_CH), bf16),
            pltpu.VMEM((pixels, HID_CH), f32),
            pltpu.VMEM((pixels, HID_CH), f32),
            pltpu.SemaphoreType.DMA((11,)),
        ],
        compiler_params=pltpu.CompilerParams(vmem_limit_bytes=32 * 2**20),
    )(
        place, packed, beside,
        hid_kernel.reshape(9 * HID_CH, 3 * HID_CH), in_hbm(in_weight),
    )
    refined = lax.all_to_all(refined, "band", 0, 0, tiled=True)
    disparity, hidden = pl.pallas_call(
        unpack_kernel,
        out_shape=(
            jax.ShapeDtypeStruct((1, TILE), f32),
            jax.ShapeDtypeStruct((1, TILE, HID_CH), bf16),
        ),
        in_specs=[smem, vmem],
        out_specs=(vmem, vmem),
    )(place, refined)
    return (disparity, hidden)


def solution(mesh):
    in_specs = (
        P("band", None, "disp"),
        P("band", None, "disp"),
        P("band", "disp"),
        P(None, "band", "disp"),
        P("band", "disp", None),
        P(),
        P(),
        P(),
        P(),
        P(),
    )
    out_specs = (P("band", "disp"), P("band", "disp", None))
    return jax.shard_map(local, mesh=mesh, in_specs=in_specs, out_specs=out_specs, check_vma=False)
```

```python
import jax
import jax.numpy as jnp
from jax import lax
from jax.experimental import pallas as pl
from jax.experimental.pallas import tpu as pltpu
from jax.sharding import PartitionSpec as P

GROUPS = 8
DISPS = 96
FEAT_CH = 96
HID_CH = 128
ITERS = 3
TILE = 128
REACH = 2 * ITERS
EDGE = 8
SPAN = TILE + 2 * EDGE
ROWS = 2 * REACH + 1
PACK = 32
BLOCK = 8
SLAB = (BLOCK + 2) * GROUPS
OUT_SLAB = BLOCK * GROUPS

pixel_unit = 8.0
feature_scale = 0.25
floor_logit = -1e30

f32 = jnp.float32
bf16 = jnp.bfloat16


def dot(a, b):
    return jnp.dot(a, b, preferred_element_type=f32)


def dot_nt(a, b):
    return lax.dot_general(a, b, (((1,), (1,)), ((), ())), preferred_element_type=f32)


def copy_all(copies):
    for copy in copies:
        copy.start()
    for copy in copies:
        copy.wait()


def toeplitz(vol_kernel):
    size = 27 * GROUPS
    flat = vol_kernel[...].astype(f32).reshape(size, GROUPS)
    flat = jnp.concatenate([flat, jnp.zeros((size, TILE - GROUPS), f32)], axis=1).T[:GROUPS]
    row = lax.broadcasted_iota(jnp.int32, (9 * GROUPS, size), 0) >> 3
    tap = lax.broadcasted_iota(jnp.int32, (9 * GROUPS, size), 1) >> 3
    tap_a = (tap >= 9).astype(jnp.int32) + (tap >= 18).astype(jnp.int32)
    within = tap - 9 * tap_a
    tap_b = (within >= 3).astype(jnp.int32) + (within >= 6).astype(jnp.int32)
    tap_e = within - 3 * tap_b
    pairs = jnp.where(
        row == 3 * tap_a + tap_e, jnp.concatenate([flat] * 9, axis=0), 0.0
    ).astype(bf16)
    from_row = lax.broadcasted_iota(jnp.int32, (size, 3 * SLAB), 0)
    to = lax.broadcasted_iota(jnp.int32, (size, 3 * SLAB), 1)
    from_tap = from_row >> 3
    from_in = from_tap - 9 * ((from_tap >= 9).astype(jnp.int32) + (from_tap >= 18).astype(jnp.int32))
    from_b = (from_in >= 3).astype(jnp.int32) + (from_in >= 6).astype(jnp.int32)
    to_b = (to >= SLAB).astype(jnp.int32) + (to >= 2 * SLAB).astype(jnp.int32)
    repeat = jnp.where((from_b == to_b) & ((from_row & 7) == (to & 7)), 1.0, 0.0).astype(bf16)
    spread = dot(pairs, repeat)
    to = lax.broadcasted_iota(jnp.int32, (GROUPS, 3 * SLAB), 1)
    to_b = (to >= SLAB).astype(jnp.int32) + (to >= 2 * SLAB).astype(jnp.int32)
    to_d = (to - SLAB * to_b) >> 3
    rows = []
    for e in range(3):
        for d in range(BLOCK):
            value = jnp.zeros((GROUPS, 3 * SLAB), f32)
            for a in range(3):
                at = (3 * a + e) * GROUPS
                value = jnp.where(to_d == d + a, spread[at : at + GROUPS], value)
            rows.append(value)
    return jnp.concatenate(rows, axis=0).astype(bf16)


def correlate(lefts, rights, place, row_ok, wide, extra):
    has_left = (place[1] > 0).astype(f32)
    has_right = (place[1] < place[3] - 1).astype(f32)
    lane = lax.broadcasted_iota(jnp.int32, (TILE, TILE), 1)
    sub = lax.broadcasted_iota(jnp.int32, (TILE, TILE), 0)
    flip = jnp.where(lane + sub == TILE - 1, 1.0, 0.0).astype(bf16)
    per_group = FEAT_CH // GROUPS
    channel = lax.broadcasted_iota(jnp.int32, (32, FEAT_CH), 1)
    group_masks = [
        (channel >= g * per_group) & (channel < (g + 1) * per_group) for g in range(GROUPS)
    ]
    lane96 = lax.broadcasted_iota(jnp.int32, (FEAT_CH, TILE), 1)
    zero_slab = jnp.zeros((GROUPS, TILE), f32)
    for at in (0, (DISPS + 1) * GROUPS):
        wide[pl.ds(at, GROUPS), :] = zero_slab
        extra[pl.ds(at, GROUPS), :] = zero_slab

    own_t = (lefts[1] * row_ok).T
    side_t = jnp.where(
        lane96 < EDGE,
        lefts[2] * (has_right * row_ok),
        jnp.where(lane96 >= TILE - EDGE, lefts[0] * (has_left * row_ok), 0.0),
    ).T
    sources = jnp.concatenate([rights[2] * has_right, rights[1], rights[0] * has_left], axis=0)
    flipped = dot(sources.astype(bf16), flip)
    reverse = jnp.concatenate(
        [flipped[i * FEAT_CH : (i + 1) * FEAT_CH] for i in range(3)], axis=1
    )
    windows = [
        reverse[:, 2 * TILE - 32 - 32 * k : 3 * TILE - 32 - 32 * k].astype(bf16)
        for k in range(-1, 5)
    ]

    def by_group(rows):
        count = rows.shape[0]
        parts = [jnp.where(m[:count], rows, 0.0) for m in group_masks]
        return jnp.concatenate(parts, axis=0).astype(bf16)

    def shear(product, g, count, first):
        rows = product[count * g : count * g + count]
        return pltpu.roll(rows, TILE - 31 + first, 1, stride=1, stride_axis=0)

    products = [
        dot(by_group(own_t[32 * k : 32 * k + 32]), windows[k + 1]) for k in range(TILE // 32)
    ]
    after = dot(by_group(side_t[:EDGE]), windows[5])
    before = dot(by_group(side_t[TILE - EDGE :]), windows[0])
    sides = []
    for g in range(GROUPS):
        part = jnp.concatenate([shear(product, g, 32, 0) for product in products], axis=0)
        wide[pl.ds(GROUPS + g, DISPS, stride=GROUPS), :] = part.T[:DISPS] * (1.0 / per_group)
        sides += [shear(after, g, EDGE, 0), shear(before, g, EDGE, 32 - EDGE)]
    part = jnp.concatenate(sides, axis=0).T[:DISPS] * (1.0 / per_group)
    for g in range(GROUPS):
        extra[pl.ds(GROUPS + g, DISPS, stride=GROUPS), :] = (
            part if g == 0 else pltpu.roll(part, TILE - 2 * EDGE * g, 1)
        )


def features(tiles):
    tiles = [tile[: 2 * FEAT_CH].astype(f32) for tile in tiles]
    return [tile[:FEAT_CH] for tile in tiles], [tile[FEAT_CH:] for tile in tiles]


def own_row_kernel(place, own, across, vol_kernel, raw_out, taps_out, wide, extra, kernel, sem):
    copy = pltpu.make_async_copy(vol_kernel, kernel, sem.at[0])
    copy.start()
    tiles = [across[0], own[...], across[across.shape[0] - 1]]
    correlate(*features(tiles), place, 1.0, wide, extra)
    raw_out[...] = jnp.concatenate([wide[...], extra[...]], axis=1).astype(bf16)
    copy.wait()
    taps_out[...] = toeplitz(kernel)


def volume_kernel(
    place, gain, own, across, odd_own, odd_across, even_own, even_across, limit, indices, raw_own,
    taps_own, out, window, raw, taps, wide, extra, logit, sems,
):
    band, bands = place[0], place[2]
    is_even = band % 2 == 0
    copies = [
        pltpu.make_async_copy(raw_own, raw, sems.at[0]),
        pltpu.make_async_copy(taps_own, taps, sems.at[1]),
    ]
    for copy in copies:
        copy.start()

    last = odd_across.shape[0] - 1
    at = 2 * FEAT_CH
    for i, (centre, sides) in enumerate(
        ((odd_own, odd_across), (own, across), (even_own, even_across))
    ):
        window[i, :TILE] = centre[at:]
        window[i, TILE : TILE + 16] = sides[0, at + TILE - 16 :]
        window[i, TILE + 16 :] = sides[last, at : at + 16]

    odd = features([odd_across[0], odd_own[...], odd_across[last]])
    even = features([even_across[0], even_own[...], even_across[last]])
    for b in range(2):
        row = band + 2 * b - 1
        row_ok = ((row >= 0) & (row < bands)).astype(f32)
        lefts, rights = [
            [
                jnp.where(is_even, y, x) if b == 0 else jnp.where(is_even, x, y)
                for x, y in zip(*pair)
            ]
            for pair in zip(odd, even)
        ]
        correlate(lefts, rights, place, row_ok, wide.at[b], extra.at[b])
    for copy in copies:
        copy.wait()

    lane8 = lax.broadcasted_iota(jnp.int32, (OUT_SLAB, TILE), 1)
    group_at = lax.broadcasted_iota(jnp.int32, (GROUPS, TILE), 0)
    gains = jnp.zeros((GROUPS, TILE), f32)
    for g in range(GROUPS):
        gains = jnp.where(group_at == g, gain[g], gains)
    wanted = [jnp.broadcast_to(indices[t : t + 1, :], (GROUPS, TILE)) for t in range(ITERS)]
    found = [jnp.zeros((GROUPS, TILE), f32) for _ in range(ITERS)]
    for q in range(DISPS // BLOCK):
        at = q * OUT_SLAB
        slabs = [
            jnp.concatenate(
                [wide[b, at : at + SLAB, :], extra[b, at : at + SLAB, :]], axis=1
            ).astype(bf16)
            for b in range(2)
        ]
        slabs.insert(1, raw[at : at + SLAB, :])
        product = dot(taps[...], jnp.concatenate(slabs, axis=0))
        first, middle, last = (
            product[:OUT_SLAB],
            product[OUT_SLAB : 2 * OUT_SLAB],
            product[2 * OUT_SLAB :],
        )
        conv = (
            middle[:, :TILE]
            + jnp.where(
                lane8 == 0,
                pltpu.roll(first[:, TILE:], TILE - 2 * EDGE + 1, 1),
                pltpu.roll(first[:, :TILE], 1, 1),
            )
            + jnp.where(
                lane8 == TILE - 1,
                pltpu.roll(last[:, TILE:], TILE - 1, 1),
                pltpu.roll(last[:, :TILE], TILE - 1, 1),
            )
        )
        centre = slabs[1][:, :TILE].astype(f32)[GROUPS : GROUPS + OUT_SLAB]
        volume = (centre + jnp.maximum(conv, 0.0)).astype(bf16).astype(f32)
        volume = volume.reshape(BLOCK, GROUPS, TILE)
        logit[q * BLOCK : (q + 1) * BLOCK, :] = jnp.sum(volume * gains[None], axis=1)
        for d in range(BLOCK):
            for t in range(ITERS):
                found[t] = found[t] + jnp.where(wanted[t] == q * BLOCK + d, volume[d], 0.0)

    level = lax.broadcasted_iota(jnp.int32, (DISPS, TILE), 0)
    valid = level < limit[...]
    masked = jnp.where(valid, logit[...], floor_logit)
    top = jnp.max(masked, axis=0, keepdims=True)
    weights = jnp.where(valid, jnp.exp(masked - top), 0.0)
    moment = jnp.sum(weights * level.astype(f32), axis=0, keepdims=True)
    start = moment / jnp.sum(weights, axis=0, keepdims=True) / pixel_unit
    high = start.astype(bf16).astype(f32)
    low = (start - high).astype(bf16).astype(f32)
    ends = jnp.where(
        group_at == 0,
        jnp.broadcast_to(high, (GROUPS, TILE)),
        jnp.where(group_at == 1, jnp.broadcast_to(low, (GROUPS, TILE)), 0.0),
    )
    packed = jnp.concatenate(found + [ends], axis=0).astype(bf16)
    for i in range(out.shape[0]):
        out[i] = packed


def spot(place, r):
    band, bands = place[0], place[2]
    row = band - REACH + r
    return jnp.clip(row, 0, bands - 1), ((row >= 0) & (row < bands)).astype(f32)


def column_inside(place):
    column = lax.broadcasted_iota(jnp.int32, (SPAN, HID_CH), 0)
    has_left = (place[1] > 0).astype(f32)
    has_right = (place[1] < place[3] - 1).astype(f32)
    return jnp.where(column < EDGE, has_left, jnp.where(column >= TILE + EDGE, has_right, 1.0))


def keep(line, target, at, values):
    length = values.shape[0]
    start = EDGE + at
    line[start : start + length, :] = values
    target[at : at + length, 0:HID_CH] = line[start - 1 : start - 1 + length, :].astype(bf16)
    target[at : at + length, HID_CH : 2 * HID_CH] = values.astype(bf16)
    target[at : at + length, 2 * HID_CH :] = line[start + 1 : start + 1 + length, :].astype(bf16)


def around(target, at, length):
    return [target[at + a * SPAN : at + a * SPAN + length, :] for a in (-1, 0, 1)]


def chunks(low, high, most):
    count = high - low + 1
    parts = -(-count // most)
    out = []
    for i in range(parts):
        size = count // parts + (1 if i < count % parts else 0)
        out.append((low, size))
        low += size
    return out


def first_conv_kernel(
    place, here, below_3, above_3, below_5, above_5, border, hid_weight, out, line, taps
):
    band, bands = place[0], place[2]
    column_ok = column_inside(place)
    line[...] = jnp.zeros_like(line)
    for r in range(ROWS):
        away = r - REACH
        if abs(away) <= 1:
            window, step, parity = here, away, band % 2
        elif abs(away) <= 4:
            window, parity = (below_3 if away < 0 else above_3), (band + 1) % 2
            step = away + 3 if away < 0 else away - 3
        else:
            window, parity = (below_5 if away < 0 else above_5), (band + 1) % 2
            step = away + 5 if away < 0 else away - 5
        if step == 0:
            tile = window[1]
        else:
            tile = window[jnp.where(parity == (0 if step == 1 else 1), 0, 2)]
        tile = tile.astype(f32)
        if abs(away) == 2:
            at_border = (band == 2) if away < 0 else (band == bands - 3)
            tile = jnp.where(at_border, border[1].astype(f32), tile)
        values = jnp.concatenate(
            [tile[TILE + 16 - EDGE : TILE + 16], tile[:TILE], tile[TILE + 16 : TILE + 16 + EDGE]],
            axis=0,
        )
        values = values * (column_ok * spot(place, r)[1])
        keep(line, taps, r * SPAN, values)
        if 1 <= r <= ROWS - 2:
            out[(r - 1) * SPAN : r * SPAN, 2 * HID_CH :] = values
    for r, count in chunks(1, ROWS - 2, 4):
        at, length = r * SPAN, count * SPAN
        lhs = jnp.concatenate(around(taps, at, length), axis=1)
        out[at - SPAN : at - SPAN + length, : 2 * HID_CH] = dot(
            lhs, hid_weight[:, : 2 * HID_CH]
        )


def refine_kernel(
    place,
    packed_all,
    packed_side,
    conv_first,
    hid_weight,
    in_weight,
    disparity_out,
    hidden_out,
    line,
    weight,
    head_row,
    looked,
    taps,
    reset_taps,
    gate,
    inputs,
    level,
    sems,
):
    weight_copies = [
        pltpu.make_async_copy(hid_weight, weight.at[pl.ds(0, 9 * HID_CH)], sems.at[0]),
        pltpu.make_async_copy(
            in_weight.at[pl.ds(0, HID_CH)], weight.at[pl.ds(9 * HID_CH, HID_CH)], sems.at[1]
        ),
        pltpu.make_async_copy(
            in_weight.at[pl.ds(HID_CH, 16), pl.ds(0, HID_CH)], head_row, sems.at[2]
        ),
    ]
    for copy in weight_copies:
        copy.start()

    column_ok = column_inside(place)
    has_left, has_right = column_ok[0:1, 0:1], column_ok[SPAN - 1 :, 0:1]
    tap = lax.broadcasted_iota(jnp.int32, (SPAN, HID_CH), 1) - 9 * GROUPS
    at_sub = lax.broadcasted_iota(jnp.int32, (SPAN, 2 * TILE), 0)
    at_lane = lax.broadcasted_iota(jnp.int32, (SPAN, 2 * TILE), 1)
    spread = jnp.where(
        ((at_sub >= EDGE) & (at_lane == at_sub - EDGE))
        | ((at_sub < EDGE) & (at_lane == at_sub - EDGE + 2 * TILE)),
        1.0,
        0.0,
    ).astype(bf16)
    lane_pack = lax.broadcasted_iota(jnp.int32, (PACK, TILE), 1)

    last = packed_side.shape[0] - 1
    shifted = []
    for r in range(ROWS):
        held, row_ok = spot(place, r)
        centre = packed_all[held].astype(f32) * row_ok
        halo = jnp.where(
            lane_pack < TILE // 2,
            packed_side[last, held].astype(f32) * (has_right * row_ok),
            packed_side[0, held].astype(f32) * (has_left * row_ok),
        )
        both = jnp.concatenate([centre, halo], axis=1)
        shifted.append((pltpu.roll(both, 1, 1), both, pltpu.roll(both, 2 * TILE - 1, 1)))
    levels = [
        [feature_scale * (x[3 * GROUPS : 3 * GROUPS + 1] + x[3 * GROUPS + 1 : 3 * GROUPS + 2])
         for x in shifted[r]]
        for r in range(ROWS)
    ]
    sub = lax.broadcasted_iota(jnp.int32, (16, 2 * TILE), 0)
    fill = jnp.zeros((HID_CH - 9 * GROUPS - 16, 2 * TILE), f32)

    def taken(t, r):
        pieces = []
        ends = jnp.zeros((16, 2 * TILE), f32)
        for a in range(3):
            for b in range(3):
                pieces.append(shifted[r + a - 1][b][t * GROUPS : (t + 1) * GROUPS])
                if t == 0:
                    ends = jnp.where(sub == 3 * a + b, levels[r + a - 1][b], ends)
        return jnp.concatenate(pieces + [ends, fill], axis=0).astype(bf16)

    wanted = [(t, r) for t in range(ITERS) for r in range(1 + 2 * t, ROWS - 1 - 2 * t)]
    for i in range(0, len(wanted), 2):
        pair = wanted[i : i + 2]
        both = dot_nt(spread, jnp.concatenate([taken(t, r) for t, r in pair], axis=0))
        for j, (t, r) in enumerate(pair):
            part = both[:, j * HID_CH : (j + 1) * HID_CH]
            if t == 0:
                inputs[r * SPAN : (r + 1) * SPAN, :] = part.astype(bf16)
            else:
                looked[t - 1, r * SPAN : (r + 1) * SPAN, :] = part
    blank = jnp.zeros((EDGE, HID_CH), f32)
    level[EDGE + 2 * SPAN - EDGE : EDGE + 2 * SPAN, :] = blank
    level[EDGE + (ROWS - 2) * SPAN : EDGE + (ROWS - 2) * SPAN + EDGE, :] = blank
    twice = jnp.concatenate([spread, spread], axis=1)
    for r in range(2, ROWS - 2, 2):
        pair = range(r, min(r + 2, ROWS - 2))
        ends = [
            jnp.concatenate(
                [
                    jnp.broadcast_to(shifted[i][1][at : at + 1], (HID_CH, 2 * TILE))
                    for at in (3 * GROUPS, 3 * GROUPS + 1)
                ],
                axis=1,
            )
            for i in pair
        ]
        both = dot_nt(twice, (feature_scale * jnp.concatenate(ends, axis=0)).astype(bf16))
        for j, i in enumerate(pair):
            level[EDGE + i * SPAN : EDGE + (i + 1) * SPAN, :] = both[
                :, j * HID_CH : (j + 1) * HID_CH
            ]
    line[...] = jnp.zeros_like(line)
    for copy in weight_copies:
        copy.wait()
    head = head_row[...].astype(f32)[0:1] * feature_scale
    head = jnp.broadcast_to(head, (HID_CH, HID_CH)).astype(bf16)

    for t in range(ITERS):
        low, high = 1 + 2 * t, ROWS - 2 - 2 * t
        if t > 0:
            spread_level = {}
            for r in range(low - 1, high + 2):
                at = EDGE + r * SPAN
                spread_level[r] = jnp.where(
                    tap % 3 == 0,
                    level[at - 1 : at - 1 + SPAN, :],
                    jnp.where(
                        tap % 3 == 1, level[at : at + SPAN, :], level[at + 1 : at + 1 + SPAN, :]
                    ),
                )
            for r in range(low, high + 1):
                value = looked[t - 1, r * SPAN : (r + 1) * SPAN, :]
                for a in range(3):
                    value = jnp.where(
                        (tap >= 3 * a) & (tap < 3 * a + 3), spread_level[r + a - 1], value
                    )
                inputs[r * SPAN : (r + 1) * SPAN, :] = value.astype(bf16)

        def held(at, length):
            if t == 0:
                return conv_first[at - SPAN : at - SPAN + length, 2 * HID_CH :]
            return taps[at : at + length, HID_CH : 2 * HID_CH].astype(f32)

        for r, count in chunks(low, high, 4):
            at, length = r * SPAN, count * SPAN
            if t == 0:
                both = conv_first[at - SPAN : at - SPAN + length, : 2 * HID_CH] + dot(
                    inputs[at : at + length, :], weight[9 * HID_CH :, : 2 * HID_CH]
                )
            else:
                lhs = around(taps, at, length) + [inputs[at : at + length, :]]
                both = dot(jnp.concatenate(lhs, axis=1), weight[:, : 2 * HID_CH])
            skip, until = (SPAN if r == low else 0), (SPAN if r + count - 1 == high else 0)
            update = both[skip : length - until, :HID_CH]
            gate[at + skip : at + length - until, :] = 0.5 * jnp.tanh(0.5 * update) + 0.5
            reset = 0.5 * jnp.tanh(0.5 * both[:, HID_CH:]) + 0.5
            keep(line, reset_taps, at, reset * held(at, length))
        for r, count in chunks(low + 1, high - 1, 4):
            at, length = r * SPAN, count * SPAN
            lhs = around(reset_taps, at, length) + [inputs[at : at + length, :]]
            candidate = jnp.tanh(dot(jnp.concatenate(lhs, axis=1), weight[:, 2 * HID_CH :]))
            hidden = held(at, length)
            hidden = hidden + gate[at : at + length, :] * (candidate - hidden)
            mask = [column_ok * spot(place, r + i)[1] for i in range(count)]
            hidden = (hidden * jnp.concatenate(mask, axis=0)).astype(bf16)
            level[EDGE + at : EDGE + at + length, :] += dot_nt(hidden, head)
            if t < ITERS - 1:
                keep(line, taps, at, hidden.astype(f32))
            else:
                hidden_out[0] = hidden.astype(f32)[EDGE : EDGE + TILE].astype(bf16)
    at = EDGE + REACH * SPAN + EDGE
    disparity_out[...] = level[at : at + TILE, :].T[0:1] * (1.0 / feature_scale)


def in_hbm(value):
    return pltpu.with_memory_space_constraint(value, pltpu.HBM)


def to_sides(value):
    disps = lax.axis_size("disp")
    right = [(d, d + 1) for d in range(disps - 1)]
    left = [(d + 1, d) for d in range(disps - 1)]
    if disps == 2:
        return lax.ppermute(value, "disp", right + left)[None]
    return jnp.stack([lax.ppermute(value, "disp", right), lax.ppermute(value, "disp", left)])


def to_rows(value, shift):
    bands = lax.axis_size("band")
    return lax.ppermute(
        value, "band", [(i, shift(i)) for i in range(bands) if 0 <= shift(i) < bands]
    )


def odd_pair(i):
    return i ^ 1


def even_pair(i):
    return i - 1 if i % 2 == 0 else i + 1


def local(
    feat_left,
    feat_right,
    limit,
    indices,
    hidden_start,
    vol_kernel,
    group_gain,
    hid_kernel,
    in_kernel,
    head_weight,
):
    bands, disps = lax.axis_size("band"), lax.axis_size("disp")
    place = jnp.stack(
        [lax.axis_index("band"), lax.axis_index("disp"), jnp.int32(bands), jnp.int32(disps)]
    ).astype(jnp.int32)
    smem = pl.BlockSpec(memory_space=pltpu.SMEM)
    vmem = pl.BlockSpec(memory_space=pltpu.VMEM)
    hbm = pl.BlockSpec(memory_space=pltpu.HBM)
    anywhere = pl.BlockSpec(memory_space=pl.ANY)
    padded = (DISPS + 2) * GROUPS

    feats = jnp.concatenate([feat_left[0], feat_right[0], hidden_start[0]], axis=0)
    odd_own, even_own = to_rows(feats, odd_pair), to_rows(feats, even_pair)
    across = to_sides(feats)
    raw_own, taps = pl.pallas_call(
        own_row_kernel,
        out_shape=(
            jax.ShapeDtypeStruct((padded, 2 * TILE), bf16),
            jax.ShapeDtypeStruct((3 * OUT_SLAB, 3 * SLAB), bf16),
        ),
        in_specs=[smem, vmem, vmem, hbm],
        out_specs=(vmem, vmem),
        scratch_shapes=[
            pltpu.VMEM((padded, TILE), f32),
            pltpu.VMEM((padded, TILE), f32),
            pltpu.VMEM((27, GROUPS, GROUPS), bf16),
            pltpu.SemaphoreType.DMA((1,)),
        ],
        compiler_params=pltpu.CompilerParams(vmem_limit_bytes=16 * 2**20),
        cost_estimate=pl.CostEstimate(flops=2 * 10**9, bytes_accessed=4 * 2**20, transcendentals=0),
    )(place, feats, across, in_hbm(vol_kernel.reshape(27, GROUPS, GROUPS)))
    odd_own, even_own, raw_own, taps = lax.optimization_barrier(
        (odd_own, even_own, raw_own, taps)
    )
    odd_across, even_across = to_sides(odd_own), to_sides(even_own)

    in_weight = jnp.concatenate(
        [
            in_kernel[:, :, :GROUPS].reshape(9 * GROUPS, 3 * HID_CH),
            in_kernel[:, :, GROUPS].reshape(9, 3 * HID_CH),
            jnp.zeros((HID_CH - 9 * (GROUPS + 1), 3 * HID_CH), bf16),
            jnp.pad(head_weight.reshape(1, HID_CH), ((0, 15), (0, 2 * HID_CH))),
        ],
        axis=0,
    )

    packed, window = pl.pallas_call(
        volume_kernel,
        out_shape=(
            jax.ShapeDtypeStruct((bands, PACK, TILE), bf16),
            jax.ShapeDtypeStruct((3, TILE + 32, HID_CH), bf16),
        ),
        in_specs=[smem, smem] + [vmem] * 8 + [hbm, hbm],
        out_specs=(vmem, vmem),
        scratch_shapes=[
            pltpu.VMEM((padded, 2 * TILE), bf16),
            pltpu.VMEM((3 * OUT_SLAB, 3 * SLAB), bf16),
            pltpu.VMEM((2, padded, TILE), f32),
            pltpu.VMEM((2, padded, TILE), f32),
            pltpu.VMEM((DISPS, TILE), f32),
            pltpu.SemaphoreType.DMA((2,)),
        ],
        compiler_params=pltpu.CompilerParams(vmem_limit_bytes=24 * 2**20),
        cost_estimate=pl.CostEstimate(
            flops=5 * 10**9, bytes_accessed=16 * 2**20, transcendentals=DISPS * TILE
        ),
    )(
        place, group_gain, feats, across, odd_own, odd_across, even_own, even_across,
        limit, indices[:, 0], raw_own, taps,
    )

    packed_all = lax.all_to_all(packed, "band", 0, 0, tiled=True)
    windows = [to_rows(window, lambda i, step=step: i + step) for step in (3, -3, 5, -5)]
    border = lax.ppermute(window, "band", [(0, 2), (bands - 1, bands - 3)])
    area = ROWS * SPAN
    hid_weight = hid_kernel.reshape(9 * HID_CH, 3 * HID_CH)
    conv_first = pl.pallas_call(
        first_conv_kernel,
        out_shape=jax.ShapeDtypeStruct((area - 2 * SPAN, 3 * HID_CH), f32),
        in_specs=[smem] + [vmem] * 7,
        out_specs=vmem,
        scratch_shapes=[
            pltpu.VMEM((area + 2 * EDGE, HID_CH), f32),
            pltpu.VMEM((area, 3 * HID_CH), bf16),
        ],
        compiler_params=pltpu.CompilerParams(vmem_limit_bytes=24 * 2**20),
        cost_estimate=pl.CostEstimate(
            flops=2 * 11 * SPAN * 9 * HID_CH * 2 * HID_CH, bytes_accessed=6 * 2**20, transcendentals=0
        ),
    )(place, window, *windows, border, hid_weight)
    packed_all, conv_first, in_weight = lax.optimization_barrier(
        (packed_all, conv_first, in_weight)
    )
    packed_side = to_sides(packed_all)
    disparity, hidden = pl.pallas_call(
        refine_kernel,
        out_shape=(
            jax.ShapeDtypeStruct((1, TILE), f32),
            jax.ShapeDtypeStruct((1, TILE, HID_CH), bf16),
        ),
        in_specs=[smem] + [vmem] * 3 + [anywhere, hbm],
        out_specs=(vmem, vmem),
        scratch_shapes=[
            pltpu.VMEM((area + 2 * EDGE, HID_CH), f32),
            pltpu.VMEM((10 * HID_CH, 3 * HID_CH), bf16),
            pltpu.VMEM((16, HID_CH), bf16),
            pltpu.VMEM((ITERS - 1, area, HID_CH), f32),
            pltpu.VMEM((area, 3 * HID_CH), bf16),
            pltpu.VMEM((area, 3 * HID_CH), bf16),
            pltpu.VMEM((area, HID_CH), f32),
            pltpu.VMEM((area, HID_CH), bf16),
            pltpu.VMEM((area + 2 * EDGE, HID_CH), f32),
            pltpu.SemaphoreType.DMA((3,)),
        ],
        compiler_params=pltpu.CompilerParams(vmem_limit_bytes=32 * 2**20),
    )(place, packed_all, packed_side, conv_first, hid_weight, in_hbm(in_weight))
    return (disparity, hidden)


def solution(mesh):
    in_specs = (
        P("band", None, "disp"),
        P("band", None, "disp"),
        P("band", "disp"),
        P(None, "band", "disp"),
        P("band", "disp", None),
        P(),
        P(),
        P(),
        P(),
        P(),
    )
    out_specs = (P("band", "disp"), P("band", "disp", None))
    return jax.shard_map(local, mesh=mesh, in_specs=in_specs, out_specs=out_specs, check_vma=False)
```

```python
import jax
import jax.numpy as jnp
from jax import lax
from jax.experimental import pallas as pl
from jax.experimental.pallas import tpu as pltpu
from jax.sharding import PartitionSpec as P

GROUPS = 8
DISPS = 96
FEAT_CH = 96
HID_CH = 128
ITERS = 3
TILE = 128
REACH = 2 * ITERS
EDGE = 8
QUAD = 4
STRIP = TILE // QUAD
WINDOW = STRIP + 2 * EDGE
PACK = 32
PITCH = 64
BLOCK_ROWS = WINDOW + 2 * GROUPS
AROUND = QUAD + 2 * REACH
BLOCK = 8
SLAB = (BLOCK + 2) * GROUPS
OUT_SLAB = BLOCK * GROUPS

pixel_unit = 8.0
feature_scale = 0.25
floor_logit = -1e30

f32 = jnp.float32
bf16 = jnp.bfloat16


def dot(a, b):
    return jnp.dot(a, b, preferred_element_type=f32)


def dot_nt(a, b):
    return lax.dot_general(a, b, (((1,), (1,)), ((), ())), preferred_element_type=f32)


def copy_all(copies):
    for copy in copies:
        copy.start()
    for copy in copies:
        copy.wait()


def toeplitz(vol_kernel):
    size = 27 * GROUPS
    flat = vol_kernel[...].astype(f32).reshape(size, GROUPS)
    flat = jnp.concatenate([flat, jnp.zeros((size, TILE - GROUPS), f32)], axis=1).T[:GROUPS]
    row = lax.broadcasted_iota(jnp.int32, (9 * GROUPS, size), 0) >> 3
    tap = lax.broadcasted_iota(jnp.int32, (9 * GROUPS, size), 1) >> 3
    tap_a = (tap >= 9).astype(jnp.int32) + (tap >= 18).astype(jnp.int32)
    within = tap - 9 * tap_a
    tap_b = (within >= 3).astype(jnp.int32) + (within >= 6).astype(jnp.int32)
    tap_e = within - 3 * tap_b
    pairs = jnp.where(
        row == 3 * tap_a + tap_e, jnp.concatenate([flat] * 9, axis=0), 0.0
    ).astype(bf16)
    from_row = lax.broadcasted_iota(jnp.int32, (size, 3 * SLAB), 0)
    to = lax.broadcasted_iota(jnp.int32, (size, 3 * SLAB), 1)
    from_tap = from_row >> 3
    from_in = from_tap - 9 * ((from_tap >= 9).astype(jnp.int32) + (from_tap >= 18).astype(jnp.int32))
    from_b = (from_in >= 3).astype(jnp.int32) + (from_in >= 6).astype(jnp.int32)
    to_b = (to >= SLAB).astype(jnp.int32) + (to >= 2 * SLAB).astype(jnp.int32)
    repeat = jnp.where((from_b == to_b) & ((from_row & 7) == (to & 7)), 1.0, 0.0).astype(bf16)
    spread = dot(pairs, repeat)
    to = lax.broadcasted_iota(jnp.int32, (GROUPS, 3 * SLAB), 1)
    to_b = (to >= SLAB).astype(jnp.int32) + (to >= 2 * SLAB).astype(jnp.int32)
    to_d = (to - SLAB * to_b) >> 3
    rows = []
    for e in range(3):
        for d in range(BLOCK):
            value = jnp.zeros((GROUPS, 3 * SLAB), f32)
            for a in range(3):
                at = (3 * a + e) * GROUPS
                value = jnp.where(to_d == d + a, spread[at : at + GROUPS], value)
            rows.append(value)
    return jnp.concatenate(rows, axis=0).astype(bf16)


def interleaved(values):
    stacked = jnp.swapaxes(jnp.stack(values), 0, 1)
    return stacked.reshape(values[0].shape[0] * len(values), values[0].shape[1])


def correlate(lefts, rights, place, row_ok, wide, extra):
    has_left = (place[1] > 0).astype(f32)
    has_right = (place[1] < place[3] - 1).astype(f32)
    lane = lax.broadcasted_iota(jnp.int32, (TILE, TILE), 1)
    sub = lax.broadcasted_iota(jnp.int32, (TILE, TILE), 0)
    flip = jnp.where(lane + sub == TILE - 1, 1.0, 0.0).astype(bf16)
    per_group = FEAT_CH // GROUPS
    channel = lax.broadcasted_iota(jnp.int32, (32, FEAT_CH), 1)
    group_masks = [
        (channel >= g * per_group) & (channel < (g + 1) * per_group) for g in range(GROUPS)
    ]
    lane96 = lax.broadcasted_iota(jnp.int32, (FEAT_CH, TILE), 1)
    zero_slab = jnp.zeros((GROUPS, TILE), f32)
    for at in (0, (DISPS + 1) * GROUPS):
        wide[pl.ds(at, GROUPS), :] = zero_slab
        extra[pl.ds(at, GROUPS), :] = zero_slab

    own_t = (lefts[1] * row_ok).T
    side_t = jnp.where(
        lane96 < EDGE,
        lefts[2] * (has_right * row_ok),
        jnp.where(lane96 >= TILE - EDGE, lefts[0] * (has_left * row_ok), 0.0),
    ).T
    sources = jnp.concatenate([rights[2] * has_right, rights[1], rights[0] * has_left], axis=0)
    flipped = dot(sources.astype(bf16), flip)
    reverse = jnp.concatenate(
        [flipped[i * FEAT_CH : (i + 1) * FEAT_CH] for i in range(3)], axis=1
    )
    windows = [
        reverse[:, 2 * TILE - 32 - 32 * k : 3 * TILE - 32 - 32 * k].astype(bf16)
        for k in range(-1, 5)
    ]

    def by_group(rows):
        count = rows.shape[0]
        parts = [jnp.where(m[:count], rows, 0.0) for m in group_masks]
        return jnp.concatenate(parts, axis=0).astype(bf16)

    def shear(product, g, count, first):
        rows = product[count * g : count * g + count]
        return pltpu.roll(rows, TILE - 31 + first, 1, stride=1, stride_axis=0)

    products = [
        dot(by_group(own_t[32 * k : 32 * k + 32]), windows[k + 1]) for k in range(TILE // 32)
    ]
    after = dot(by_group(side_t[:EDGE]), windows[5])
    before = dot(by_group(side_t[TILE - EDGE :]), windows[0])
    parts, sides = [], []
    for g in range(GROUPS):
        part = jnp.concatenate([shear(product, g, 32, 0) for product in products], axis=0)
        parts.append(part.T[:DISPS])
        sides += [shear(after, g, EDGE, 0), shear(before, g, EDGE, 32 - EDGE)]
    part = jnp.concatenate(sides, axis=0).T[:DISPS]
    sides = [part if g == 0 else pltpu.roll(part, TILE - 2 * EDGE * g, 1) for g in range(GROUPS)]
    for target, values in ((wide, parts), (extra, sides)):
        target[GROUPS : GROUPS + DISPS * GROUPS, :] = interleaved(values) * (1.0 / per_group)


def own_row_kernel(place, own, across, vol_kernel, raw_out, taps_out, wide, extra, kernel, sem):
    copy = pltpu.make_async_copy(vol_kernel, kernel, sem.at[0])
    copy.start()
    tiles = [across[0], own[...], across[across.shape[0] - 1]]
    tiles = [tile.astype(f32) for tile in tiles]
    correlate(
        [tile[:FEAT_CH] for tile in tiles], [tile[FEAT_CH:] for tile in tiles],
        place, 1.0, wide, extra,
    )
    raw_out[...] = jnp.concatenate([wide[...], extra[...]], axis=1).astype(bf16)
    copy.wait()
    taps_out[...] = toeplitz(kernel)


def volume_kernel(
    place, gain, odd_own, odd_across, even_own, even_across, limit, indices, hidden, raw_own,
    taps_own, out_0, out_1, out_2, out_3, raw, taps, wide, extra, logit, padded, blocks, sems,
):
    band, bands = place[0], place[2]
    is_even = band % 2 == 0
    copies = [
        pltpu.make_async_copy(raw_own, raw, sems.at[0]),
        pltpu.make_async_copy(taps_own, taps, sems.at[1]),
    ]
    for copy in copies:
        copy.start()

    last = odd_across.shape[0] - 1
    odd = [tile.astype(f32) for tile in (odd_across[0], odd_own[...], odd_across[last])]
    even = [tile.astype(f32) for tile in (even_across[0], even_own[...], even_across[last])]
    for b in range(2):
        row = band + 2 * b - 1
        row_ok = ((row >= 0) & (row < bands)).astype(f32)
        tiles = [
            jnp.where(is_even, y, x) if b == 0 else jnp.where(is_even, x, y)
            for x, y in zip(odd, even)
        ]
        correlate(
            [tile[:FEAT_CH] for tile in tiles], [tile[FEAT_CH:] for tile in tiles],
            place, row_ok, wide.at[b], extra.at[b],
        )
    for copy in copies:
        copy.wait()

    lane8 = lax.broadcasted_iota(jnp.int32, (OUT_SLAB, TILE), 1)
    group_at = lax.broadcasted_iota(jnp.int32, (GROUPS, TILE), 0)
    gains = jnp.zeros((GROUPS, TILE), f32)
    for g in range(GROUPS):
        gains = jnp.where(group_at == g, gain[g], gains)
    wanted = [jnp.broadcast_to(indices[t : t + 1, :], (GROUPS, TILE)) for t in range(ITERS)]
    found = [jnp.zeros((GROUPS, TILE), f32) for _ in range(ITERS)]
    for q in range(DISPS // BLOCK):
        at = q * OUT_SLAB
        slabs = [
            jnp.concatenate(
                [wide[b, at : at + SLAB, :], extra[b, at : at + SLAB, :]], axis=1
            ).astype(bf16)
            for b in range(2)
        ]
        slabs.insert(1, raw[at : at + SLAB, :])
        product = dot(taps[...], jnp.concatenate(slabs, axis=0))
        first, middle, last = (
            product[:OUT_SLAB],
            product[OUT_SLAB : 2 * OUT_SLAB],
            product[2 * OUT_SLAB :],
        )
        conv = (
            middle[:, :TILE]
            + jnp.where(
                lane8 == 0,
                pltpu.roll(first[:, TILE:], TILE - 2 * EDGE + 1, 1),
                pltpu.roll(first[:, :TILE], 1, 1),
            )
            + jnp.where(
                lane8 == TILE - 1,
                pltpu.roll(last[:, TILE:], TILE - 1, 1),
                pltpu.roll(last[:, :TILE], TILE - 1, 1),
            )
        )
        centre = slabs[1][:, :TILE].astype(f32)[GROUPS : GROUPS + OUT_SLAB]
        volume = (centre + jnp.maximum(conv, 0.0)).astype(bf16).astype(f32)
        volume = volume.reshape(BLOCK, GROUPS, TILE)
        logit[q * BLOCK : (q + 1) * BLOCK, :] = jnp.sum(volume * gains[None], axis=1)
        for d in range(BLOCK):
            for t in range(ITERS):
                found[t] = found[t] + jnp.where(wanted[t] == q * BLOCK + d, volume[d], 0.0)

    level = lax.broadcasted_iota(jnp.int32, (DISPS, TILE), 0)
    valid = level < limit[...]
    masked = jnp.where(valid, logit[...], floor_logit)
    top = jnp.max(masked, axis=0, keepdims=True)
    weights = jnp.where(valid, jnp.exp(masked - top), 0.0)
    moment = jnp.sum(weights * level.astype(f32), axis=0, keepdims=True)
    start = moment / jnp.sum(weights, axis=0, keepdims=True) / pixel_unit
    high = start.astype(bf16).astype(f32)
    low = (start - high).astype(bf16).astype(f32)
    ends = jnp.where(
        group_at == 0,
        jnp.broadcast_to(high, (GROUPS, TILE)),
        jnp.where(group_at == 1, jnp.broadcast_to(low, (GROUPS, TILE)), 0.0),
    )

    padded[:EDGE, :] = jnp.zeros((EDGE, HID_CH), f32)
    padded[EDGE : EDGE + TILE, :] = hidden[...].astype(f32)
    padded[EDGE + TILE :, :] = jnp.zeros((EDGE, HID_CH), f32)
    lane = lax.broadcasted_iota(jnp.int32, (GROUPS, TILE), 1)
    packed = found + [ends]
    for strip in range(QUAD):
        block = [padded[STRIP * strip : STRIP * strip + WINDOW, :]]
        for half in range(2):
            low, high = [
                pltpu.roll(packed[2 * half + i], (PITCH * i + EDGE - STRIP * strip) % TILE, 1)
                for i in range(2)
            ]
            part = jnp.where(lane < PITCH, low, high)
            block.append(jnp.where(lane % PITCH < WINDOW, part, 0.0))
        blocks[strip] = jnp.concatenate(block, axis=0).astype(bf16)
    member = band % QUAD
    for i, out in enumerate((out_0, out_1, out_2, out_3)):
        out[...] = blocks[strip_at(place, member ^ i)]


def strip_at(place, member):
    return jnp.where(place[1] % 2 == 0, member, QUAD - 1 - member)


def keep(line, target, at, values, rows):
    length = values.shape[0]
    start = EDGE + at
    row = lax.broadcasted_iota(jnp.int32, (length, HID_CH), 0) % rows
    line[start : start + length, :] = values
    before = jnp.where(row == 0, 0.0, line[start - 1 : start - 1 + length, :])
    after = jnp.where(row == rows - 1, 0.0, line[start + 1 : start + 1 + length, :])
    target[at : at + length, 0:HID_CH] = before.astype(bf16)
    target[at : at + length, HID_CH : 2 * HID_CH] = values.astype(bf16)
    target[at : at + length, 2 * HID_CH :] = after.astype(bf16)


def refine_kernel(
    place,
    own,
    near_a,
    near_b,
    far_c,
    far_d,
    own_beside,
    near_a_beside,
    near_b_beside,
    far_c_beside,
    far_d_beside,
    hid_weight,
    in_weight,
    out_0,
    out_1,
    out_2,
    out_3,
    line,
    weight,
    head_row,
    looked,
    hidden_at,
    taps,
    reset_taps,
    in_taps,
    gate,
    level,
    blocks,
    sems,
):
    rows, strip = AROUND, STRIP
    copies = [
        pltpu.make_async_copy(
            hid_weight.at[pl.ds((3 * a + b) * HID_CH, HID_CH)],
            weight.at[pl.ds((3 * b + a) * HID_CH, HID_CH)],
            sems.at[3 * a + b],
        )
        for a in range(3)
        for b in range(3)
    ]
    copies.append(
        pltpu.make_async_copy(
            in_weight.at[pl.ds(0, 3 * HID_CH)],
            weight.at[pl.ds(9 * HID_CH, 3 * HID_CH)],
            sems.at[9],
        )
    )
    copies.append(
        pltpu.make_async_copy(
            in_weight.at[pl.ds(3 * HID_CH, 16), pl.ds(0, HID_CH)], head_row, sems.at[10]
        )
    )
    for copy in copies:
        copy.start()

    band, disp, bands, disps = place[0], place[1], place[2], place[3]
    member, layer = band % QUAD, band // QUAD
    at = strip_at(place, member)
    at_left = (at == 0) & (disp > 0)
    at_right = (at == QUAD - 1) & (disp < disps - 1)
    off = strip
    first = strip * at - EDGE
    first_row = layer * QUAD - REACH

    def block_of(r):
        step, row = (r + 2 * QUAD - REACH) // QUAD - 2, (r + 2 * QUAD - REACH) % QUAD
        slot = row ^ member
        if step == 0:
            return own[slot].astype(f32), own_beside[slot].astype(f32)
        if abs(step) == 1:
            choice, pairs = (layer % 2 == 0) == (step > 0), ((near_a, near_b), (near_a_beside, near_b_beside))
        else:
            choice, pairs = (layer % 4 < 2) == (step > 0), ((far_c, far_d), (far_c_beside, far_d_beside))
        inside = (first_row + r >= 0) & (first_row + r < bands)
        return [
            jnp.where(inside, jnp.where(choice, x[slot].astype(f32), y[slot].astype(f32)), 0.0)
            for x, y in pairs
        ]

    def joined(own, other, axis, size, column):
        column = column + first
        ahead = pltpu.roll(other, (size - off) % size, axis)
        behind = pltpu.roll(other, off, axis)
        value = jnp.where((column < 0) & at_left, ahead, 0.0)
        value = jnp.where((column >= TILE) & at_right, behind, value)
        return jnp.where((column >= 0) & (column < TILE), own, value)

    column_h = lax.broadcasted_iota(jnp.int32, (BLOCK_ROWS, HID_CH), 0)
    lane = lax.broadcasted_iota(jnp.int32, (GROUPS, TILE), 1)
    column_p = lax.broadcasted_iota(jnp.int32, (2 * GROUPS, TILE), 1) % PITCH
    at_sub = lax.broadcasted_iota(jnp.int32, (WINDOW, TILE), 0)
    at_lane = lax.broadcasted_iota(jnp.int32, (WINDOW, TILE), 1)
    spread = jnp.where(at_sub == at_lane % PITCH, 1.0, 0.0).astype(bf16)
    fill = jnp.zeros((PACK, TILE), f32)
    zeros = jnp.zeros((GROUPS, TILE), f32)
    lines, hiddens, found = [], [], []
    for r in range(rows):
        here, other = block_of(r)
        packed = joined(here[WINDOW:], other[WINDOW:], 1, TILE, column_p)
        hiddens.append(joined(here, other, 0, BLOCK_ROWS, column_h)[:WINDOW])
        pieces = []
        for b in range(3):
            moved = packed if b == 1 else pltpu.roll(packed, (1 - b) % TILE, 1)
            for q in range(4):
                part = moved[GROUPS * (q // 2) : GROUPS * (q // 2 + 1)]
                pieces.append(jnp.where((lane >= PITCH) == (q % 2 == 1), part, zeros))
        lines.append(jnp.concatenate(pieces + [fill], axis=0).astype(bf16))
    for r in range(0, rows, 2):
        both = dot_nt(spread, jnp.concatenate(lines[r : r + 2], axis=0))
        for i in range(2):
            found.append(both[:, i * HID_CH : (i + 1) * HID_CH])
    hidden_at[...] = interleaved(hiddens)
    looked[...] = interleaved(found)
    sub = lax.broadcasted_iota(jnp.int32, (HID_CH, HID_CH), 0)
    ends = jnp.where((sub == PACK + 24) | (sub == PACK + 25), feature_scale, 0.0).astype(bf16)
    level[...] = dot(looked[...].astype(bf16), ends)
    blank = jnp.zeros((EDGE, HID_CH), f32)
    line[:EDGE, :] = blank
    line[EDGE + WINDOW * rows :, :] = blank
    start = EDGE - REACH
    width = strip + 2 * REACH
    keep(line, taps, start * rows, hidden_at[start * rows : (start + width) * rows, :], rows)
    for copy in copies:
        copy.wait()
    head = head_row[...].astype(f32)[0:1] * feature_scale
    head = jnp.broadcast_to(head, (HID_CH, HID_CH)).astype(bf16)

    def beside_columns(target, at, length):
        return [target[at + b * rows : at + b * rows + length, :] for b in (-1, 0, 1)]

    for t in range(ITERS):
        halo = REACH - 1 - 2 * t
        at, length = (EDGE - halo) * rows, (strip + 2 * halo) * rows
        lane_at = lax.broadcasted_iota(jnp.int32, (length, HID_CH), 1)
        tap, channel = lane_at // PACK, lane_at % PACK
        near = [level[at + b * rows : at + b * rows + length, :] for b in (-1, 0, 1)]
        value = jnp.where(tap == 0, near[0], jnp.where(tap == 1, near[1], near[2]))
        at_lookup = (channel >= t * GROUPS) & (channel < (t + 1) * GROUPS)
        value = jnp.where(
            (channel == 3 * GROUPS) & (tap < 3),
            value,
            jnp.where(at_lookup, looked[at : at + length, :], 0.0),
        )
        keep(line, in_taps, at, value, rows)
        lhs = beside_columns(taps, at, length) + [in_taps[at : at + length, :]]
        both = dot(jnp.concatenate(lhs, axis=1), weight[:, : 2 * HID_CH])
        gate[at + rows : at + length - rows, :] = (
            0.5 * jnp.tanh(0.5 * both[rows : length - rows, :HID_CH]) + 0.5
        )
        reset = 0.5 * jnp.tanh(0.5 * both[:, HID_CH:]) + 0.5
        keep(line, reset_taps, at, reset * hidden_at[at : at + length, :], rows)

        at, length = at + rows, length - 2 * rows
        lhs = beside_columns(reset_taps, at, length) + [in_taps[at : at + length, :]]
        candidate = jnp.tanh(dot(jnp.concatenate(lhs, axis=1), weight[:, 2 * HID_CH :]))
        hidden = hidden_at[at : at + length, :]
        hidden = hidden + gate[at : at + length, :] * (candidate - hidden)
        pixel = lax.broadcasted_iota(jnp.int32, (length, HID_CH), 0)
        column, row = pixel // rows + (at // rows + first), pixel % rows + first_row
        inside = ((column >= 0) | (disp > 0)) & ((column < TILE) | (disp < disps - 1))
        inside = inside & (row >= 0) & (row < bands)
        hidden = jnp.where(inside, hidden, 0.0).astype(bf16)
        level[at : at + length, :] += dot_nt(hidden, head)
        hidden_at[at : at + length, :] = hidden.astype(f32)
        if t < ITERS - 1:
            keep(line, taps, at, hidden.astype(f32), rows)

    lane = lax.broadcasted_iota(jnp.int32, (strip, HID_CH), 1)
    final = slice(EDGE * rows, (EDGE + strip) * rows)
    hidden = jnp.swapaxes(hidden_at[final, :].reshape(strip, rows, HID_CH), 0, 1)
    levels = jnp.swapaxes(level[final, :].reshape(strip, rows, HID_CH), 0, 1)
    for r in range(QUAD):
        value = levels[REACH + r] * (1.0 / feature_scale)
        high = value.astype(bf16).astype(f32)
        middle = (value - high).astype(bf16).astype(f32)
        parts = jnp.where(lane == 0, high, jnp.where(lane == 1, middle, value - high - middle))
        parts = jnp.where(lane < 3, parts, 0.0)
        blocks[r] = jnp.concatenate([hidden[REACH + r], parts], axis=0).astype(bf16)
    for i, out in enumerate((out_0, out_1, out_2, out_3)):
        out[...] = blocks[member ^ i]


def unpack_kernel(place, from_0, from_1, from_2, from_3, disparity_out, hidden_out, blocks):
    for i, block in enumerate((from_0, from_1, from_2, from_3)):
        blocks[i] = block[...]
    member = place[0] % QUAD
    held = [blocks[strip_at(place, strip) ^ member].astype(f32) for strip in range(QUAD)]
    hidden_out[0] = jnp.concatenate([block[:STRIP] for block in held], axis=0).astype(bf16)
    parts = jnp.concatenate([block[STRIP:] for block in held], axis=0).T
    disparity_out[...] = parts[0:1] + parts[1:2] + parts[2:3]


def in_hbm(value):
    return pltpu.with_memory_space_constraint(value, pltpu.HBM)


def to_sides(value):
    disps = lax.axis_size("disp")
    right = [(d, d + 1) for d in range(disps - 1)]
    left = [(d + 1, d) for d in range(disps - 1)]
    if disps == 2:
        return lax.ppermute(value, "disp", right + left)[None]
    return jnp.stack([lax.ppermute(value, "disp", right), lax.ppermute(value, "disp", left)])


def across_border(value):
    bands, disps = lax.axis_size("band"), lax.axis_size("disp")
    pairs = []
    for band in range(bands):
        for d in range(disps - 1):
            if band % QUAD == (QUAD - 1 if d % 2 == 0 else 0):
                left, right = band * disps + d, band * disps + d + 1
                pairs += [(left, right), (right, left)]
    return lax.ppermute(value, ("band", "disp"), pairs)


def in_group(blocks):
    return [blocks[0]] + [
        to_rows(block, lambda band, i=i: band ^ i) for i, block in enumerate(blocks) if i > 0
    ]


def to_layers(value, partner):
    groups = lax.axis_size("band") // QUAD
    if not any(0 <= partner(g) < groups for g in range(groups)):
        return None
    return to_rows(value, lambda band: partner(band // QUAD) * QUAD + band % QUAD)


def to_rows(value, shift):
    bands = lax.axis_size("band")
    return lax.ppermute(
        value, "band", [(i, shift(i)) for i in range(bands) if 0 <= shift(i) < bands]
    )


def odd_pair(i):
    return i ^ 1


def even_pair(i):
    return i - 1 if i % 2 == 0 else i + 1


def local(
    feat_left,
    feat_right,
    limit,
    indices,
    hidden_start,
    vol_kernel,
    group_gain,
    hid_kernel,
    in_kernel,
    head_weight,
):
    bands, disps = lax.axis_size("band"), lax.axis_size("disp")
    place = jnp.stack(
        [lax.axis_index("band"), lax.axis_index("disp"), jnp.int32(bands), jnp.int32(disps)]
    ).astype(jnp.int32)
    smem = pl.BlockSpec(memory_space=pltpu.SMEM)
    vmem = pl.BlockSpec(memory_space=pltpu.VMEM)
    hbm = pl.BlockSpec(memory_space=pltpu.HBM)
    anywhere = pl.BlockSpec(memory_space=pl.ANY)
    padded = (DISPS + 2) * GROUPS

    feats = jnp.concatenate([feat_left[0], feat_right[0]], axis=0)
    odd_own, even_own = to_rows(feats, odd_pair), to_rows(feats, even_pair)
    across = to_sides(feats)
    raw_own, taps = pl.pallas_call(
        own_row_kernel,
        out_shape=(
            jax.ShapeDtypeStruct((padded, 2 * TILE), bf16),
            jax.ShapeDtypeStruct((3 * OUT_SLAB, 3 * SLAB), bf16),
        ),
        in_specs=[smem, vmem, vmem, hbm],
        out_specs=(vmem, vmem),
        scratch_shapes=[
            pltpu.VMEM((padded, TILE), f32),
            pltpu.VMEM((padded, TILE), f32),
            pltpu.VMEM((27, GROUPS, GROUPS), bf16),
            pltpu.SemaphoreType.DMA((1,)),
        ],
        compiler_params=pltpu.CompilerParams(vmem_limit_bytes=16 * 2**20),
        cost_estimate=pl.CostEstimate(flops=2 * 10**9, bytes_accessed=4 * 2**20, transcendentals=0),
    )(place, feats, across, in_hbm(vol_kernel.reshape(27, GROUPS, GROUPS)))
    odd_own, even_own, raw_own, taps = lax.optimization_barrier(
        (odd_own, even_own, raw_own, taps)
    )
    odd_across, even_across = to_sides(odd_own), to_sides(even_own)

    in_weight = jnp.concatenate(
        [in_kernel[:, :, :GROUPS]] * ITERS + [in_kernel[:, :, GROUPS:]], axis=2
    )
    in_weight = jnp.pad(in_weight, ((0, 0), (0, 1), (0, PACK - in_weight.shape[2]), (0, 0)))
    in_weight = jnp.concatenate(
        [
            in_weight.reshape(3 * HID_CH, 3 * HID_CH),
            jnp.pad(head_weight.reshape(1, HID_CH), ((0, 15), (0, 2 * HID_CH))),
        ],
        axis=0,
    )

    blocks = pl.pallas_call(
        volume_kernel,
        out_shape=(jax.ShapeDtypeStruct((BLOCK_ROWS, TILE), bf16),) * QUAD,
        in_specs=[smem, smem] + [vmem] * 7 + [hbm, hbm],
        out_specs=(vmem,) * QUAD,
        scratch_shapes=[
            pltpu.VMEM((padded, 2 * TILE), bf16),
            pltpu.VMEM((3 * OUT_SLAB, 3 * SLAB), bf16),
            pltpu.VMEM((2, padded, TILE), f32),
            pltpu.VMEM((2, padded, TILE), f32),
            pltpu.VMEM((DISPS, TILE), f32),
            pltpu.VMEM((TILE + 2 * EDGE, HID_CH), f32),
            pltpu.VMEM((QUAD, BLOCK_ROWS, TILE), bf16),
            pltpu.SemaphoreType.DMA((2,)),
        ],
        compiler_params=pltpu.CompilerParams(vmem_limit_bytes=24 * 2**20),
        cost_estimate=pl.CostEstimate(
            flops=5 * 10**9, bytes_accessed=16 * 2**20, transcendentals=DISPS * TILE
        ),
    )(
        place, in_hbm(group_gain), odd_own, odd_across, even_own, even_across,
        in_hbm(limit), in_hbm(indices[:, 0]), in_hbm(hidden_start[0]), raw_own, taps,
    )

    own = jnp.stack(in_group(blocks))
    around = [
        to_layers(own, lambda g: g ^ 1),
        to_layers(own, lambda g: (g - 1 ^ 1) + 1),
        to_layers(own, lambda g: g ^ 2),
        to_layers(own, lambda g: (g - 2 ^ 2) + 2),
    ]
    beside = [across_border(value) for value in [own] + around if value is not None]
    if around[3] is None:
        around[3], beside = around[2], beside + beside[-1:]

    pixels = WINDOW * AROUND
    refined = pl.pallas_call(
        refine_kernel,
        out_shape=(jax.ShapeDtypeStruct((2 * STRIP, HID_CH), bf16),) * QUAD,
        in_specs=[smem] + [vmem] * 10 + [anywhere, hbm],
        out_specs=(vmem,) * QUAD,
        scratch_shapes=[
            pltpu.VMEM((pixels + 2 * EDGE, HID_CH), f32),
            pltpu.VMEM((12 * HID_CH, 3 * HID_CH), bf16),
            pltpu.VMEM((16, HID_CH), bf16),
            pltpu.VMEM((pixels, HID_CH), f32),
            pltpu.VMEM((pixels, HID_CH), f32),
            pltpu.VMEM((pixels, 3 * HID_CH), bf16),
            pltpu.VMEM((pixels, 3 * HID_CH), bf16),
            pltpu.VMEM((pixels, 3 * HID_CH), bf16),
            pltpu.VMEM((pixels, HID_CH), f32),
            pltpu.VMEM((pixels, HID_CH), f32),
            pltpu.VMEM((QUAD, 2 * STRIP, HID_CH), bf16),
            pltpu.SemaphoreType.DMA((11,)),
        ],
        compiler_params=pltpu.CompilerParams(vmem_limit_bytes=32 * 2**20),
    )(
        place, own, *around, *beside,
        hid_kernel.reshape(9 * HID_CH, 3 * HID_CH), in_hbm(in_weight),
    )
    disparity, hidden = pl.pallas_call(
        unpack_kernel,
        out_shape=(
            jax.ShapeDtypeStruct((1, TILE), f32),
            jax.ShapeDtypeStruct((1, TILE, HID_CH), bf16),
        ),
        in_specs=[smem] + [vmem] * QUAD,
        out_specs=(vmem, vmem),
        scratch_shapes=[pltpu.VMEM((QUAD, 2 * STRIP, HID_CH), bf16)],
    )(place, *in_group(refined))
    return (disparity, hidden)


def solution(mesh):
    in_specs = (
        P("band", None, "disp"),
        P("band", None, "disp"),
        P("band", "disp"),
        P(None, "band", "disp"),
        P("band", "disp", None),
        P(),
        P(),
        P(),
        P(),
        P(),
    )
    out_specs = (P("band", "disp"), P("band", "disp", None))
    return jax.shard_map(local, mesh=mesh, in_specs=in_specs, out_specs=out_specs, check_vma=False)
```

```python
import jax
import jax.numpy as jnp
from jax import lax
from jax.experimental import pallas as pl
from jax.experimental.pallas import tpu as pltpu
from jax.sharding import PartitionSpec as P

GROUPS = 8
DISPS = 96
FEAT_CH = 96
HID_CH = 128
ITERS = 3
TILE = 128
REACH = 2 * ITERS
EDGE = 8
QUAD = 4
STRIP = TILE // QUAD
WINDOW = STRIP + 2 * EDGE
PACK = 32
PITCH = 64
BLOCK_ROWS = WINDOW + 2 * GROUPS
AROUND = QUAD + 2 * REACH
BLOCK = 8
SLAB = (BLOCK + 2) * GROUPS
OUT_SLAB = BLOCK * GROUPS

pixel_unit = 8.0
feature_scale = 0.25
floor_logit = -1e30

f32 = jnp.float32
bf16 = jnp.bfloat16


def dot(a, b):
    return jnp.dot(a, b, preferred_element_type=f32)


def dot_nt(a, b):
    return lax.dot_general(a, b, (((1,), (1,)), ((), ())), preferred_element_type=f32)


def copy_all(copies):
    for copy in copies:
        copy.start()
    for copy in copies:
        copy.wait()


def toeplitz(vol_kernel):
    size = 27 * GROUPS
    flat = vol_kernel[...].astype(f32).reshape(size, GROUPS)
    flat = jnp.concatenate([flat, jnp.zeros((size, TILE - GROUPS), f32)], axis=1).T[:GROUPS]
    row = lax.broadcasted_iota(jnp.int32, (9 * GROUPS, size), 0) >> 3
    tap = lax.broadcasted_iota(jnp.int32, (9 * GROUPS, size), 1) >> 3
    tap_a = (tap >= 9).astype(jnp.int32) + (tap >= 18).astype(jnp.int32)
    within = tap - 9 * tap_a
    tap_b = (within >= 3).astype(jnp.int32) + (within >= 6).astype(jnp.int32)
    tap_e = within - 3 * tap_b
    pairs = jnp.where(
        row == 3 * tap_a + tap_e, jnp.concatenate([flat] * 9, axis=0), 0.0
    ).astype(bf16)
    from_row = lax.broadcasted_iota(jnp.int32, (size, 3 * SLAB), 0)
    to = lax.broadcasted_iota(jnp.int32, (size, 3 * SLAB), 1)
    from_tap = from_row >> 3
    from_in = from_tap - 9 * ((from_tap >= 9).astype(jnp.int32) + (from_tap >= 18).astype(jnp.int32))
    from_b = (from_in >= 3).astype(jnp.int32) + (from_in >= 6).astype(jnp.int32)
    to_b = (to >= SLAB).astype(jnp.int32) + (to >= 2 * SLAB).astype(jnp.int32)
    repeat = jnp.where((from_b == to_b) & ((from_row & 7) == (to & 7)), 1.0, 0.0).astype(bf16)
    spread = dot(pairs, repeat)
    to = lax.broadcasted_iota(jnp.int32, (GROUPS, 3 * SLAB), 1)
    to_b = (to >= SLAB).astype(jnp.int32) + (to >= 2 * SLAB).astype(jnp.int32)
    to_d = (to - SLAB * to_b) >> 3
    rows = []
    for e in range(3):
        for d in range(BLOCK):
            value = jnp.zeros((GROUPS, 3 * SLAB), f32)
            for a in range(3):
                at = (3 * a + e) * GROUPS
                value = jnp.where(to_d == d + a, spread[at : at + GROUPS], value)
            rows.append(value)
    return jnp.concatenate(rows, axis=0).astype(bf16)


def interleaved(values):
    stacked = jnp.swapaxes(jnp.stack(values), 0, 1)
    return stacked.reshape(values[0].shape[0] * len(values), values[0].shape[1])


def correlate(lefts, rights, place, row_ok, wide, extra):
    has_left = (place[1] > 0).astype(f32)
    has_right = (place[1] < place[3] - 1).astype(f32)
    lane = lax.broadcasted_iota(jnp.int32, (TILE, TILE), 1)
    sub = lax.broadcasted_iota(jnp.int32, (TILE, TILE), 0)
    flip = jnp.where(lane + sub == TILE - 1, 1.0, 0.0).astype(bf16)
    per_group = FEAT_CH // GROUPS
    channel = lax.broadcasted_iota(jnp.int32, (32, FEAT_CH), 1)
    group_masks = [
        (channel >= g * per_group) & (channel < (g + 1) * per_group) for g in range(GROUPS)
    ]
    lane96 = lax.broadcasted_iota(jnp.int32, (FEAT_CH, TILE), 1)
    zero_slab = jnp.zeros((GROUPS, TILE), f32)
    for at in (0, (DISPS + 1) * GROUPS):
        wide[pl.ds(at, GROUPS), :] = zero_slab
        extra[pl.ds(at, GROUPS), :] = zero_slab

    own_t = (lefts[1] * row_ok).T
    side_t = jnp.where(
        lane96 < EDGE,
        lefts[2] * (has_right * row_ok),
        jnp.where(lane96 >= TILE - EDGE, lefts[0] * (has_left * row_ok), 0.0),
    ).T
    sources = jnp.concatenate([rights[2] * has_right, rights[1], rights[0] * has_left], axis=0)
    flipped = dot(sources.astype(bf16), flip)
    reverse = jnp.concatenate(
        [flipped[i * FEAT_CH : (i + 1) * FEAT_CH] for i in range(3)], axis=1
    )
    windows = [
        reverse[:, 2 * TILE - 32 - 32 * k : 3 * TILE - 32 - 32 * k].astype(bf16)
        for k in range(-1, 5)
    ]

    def by_group(rows):
        count = rows.shape[0]
        parts = [jnp.where(m[:count], rows, 0.0) for m in group_masks]
        return jnp.concatenate(parts, axis=0).astype(bf16)

    def shear(product, g, count, first):
        rows = product[count * g : count * g + count]
        return pltpu.roll(rows, TILE - 31 + first, 1, stride=1, stride_axis=0)

    products = [
        dot(by_group(own_t[32 * k : 32 * k + 32]), windows[k + 1]) for k in range(TILE // 32)
    ]
    after = dot(by_group(side_t[:EDGE]), windows[5])
    before = dot(by_group(side_t[TILE - EDGE :]), windows[0])
    parts, sides = [], []
    for g in range(GROUPS):
        part = jnp.concatenate([shear(product, g, 32, 0) for product in products], axis=0)
        parts.append(part.T[:DISPS])
        sides += [shear(after, g, EDGE, 0), shear(before, g, EDGE, 32 - EDGE)]
    part = jnp.concatenate(sides, axis=0).T[:DISPS]
    sides = [part if g == 0 else pltpu.roll(part, TILE - 2 * EDGE * g, 1) for g in range(GROUPS)]
    for target, values in ((wide, parts), (extra, sides)):
        target[GROUPS : GROUPS + DISPS * GROUPS, :] = interleaved(values) * (1.0 / per_group)


def own_row_kernel(place, own, across, vol_kernel, raw_out, taps_out, wide, extra, kernel, sem):
    copy = pltpu.make_async_copy(vol_kernel, kernel, sem.at[0])
    copy.start()
    tiles = [across[0], own[...], across[across.shape[0] - 1]]
    tiles = [tile.astype(f32) for tile in tiles]
    correlate(
        [tile[:FEAT_CH] for tile in tiles], [tile[FEAT_CH:] for tile in tiles],
        place, 1.0, wide, extra,
    )
    raw_out[...] = jnp.concatenate([wide[...], extra[...]], axis=1).astype(bf16)
    copy.wait()
    taps_out[...] = toeplitz(kernel)


def volume_kernel(
    place, gain, odd_own, odd_across, even_own, even_across, limit, indices, hidden, raw_own,
    taps_own, out_0, out_1, out_2, out_3, raw, taps, wide, extra, logit, padded, blocks, sems,
):
    band, bands = place[0], place[2]
    is_even = band % 2 == 0
    copies = [
        pltpu.make_async_copy(raw_own, raw, sems.at[0]),
        pltpu.make_async_copy(taps_own, taps, sems.at[1]),
    ]
    for copy in copies:
        copy.start()

    last = odd_across.shape[0] - 1
    odd = [tile.astype(f32) for tile in (odd_across[0], odd_own[...], odd_across[last])]
    even = [tile.astype(f32) for tile in (even_across[0], even_own[...], even_across[last])]
    for b in range(2):
        row = band + 2 * b - 1
        row_ok = ((row >= 0) & (row < bands)).astype(f32)
        tiles = [
            jnp.where(is_even, y, x) if b == 0 else jnp.where(is_even, x, y)
            for x, y in zip(odd, even)
        ]
        correlate(
            [tile[:FEAT_CH] for tile in tiles], [tile[FEAT_CH:] for tile in tiles],
            place, row_ok, wide.at[b], extra.at[b],
        )
    for copy in copies:
        copy.wait()

    lane8 = lax.broadcasted_iota(jnp.int32, (OUT_SLAB, TILE), 1)
    group_at = lax.broadcasted_iota(jnp.int32, (GROUPS, TILE), 0)
    gains = jnp.zeros((GROUPS, TILE), f32)
    for g in range(GROUPS):
        gains = jnp.where(group_at == g, gain[g], gains)
    wanted = [jnp.broadcast_to(indices[t : t + 1, :], (GROUPS, TILE)) for t in range(ITERS)]
    found = [jnp.zeros((GROUPS, TILE), f32) for _ in range(ITERS)]
    for q in range(DISPS // BLOCK):
        at = q * OUT_SLAB
        slabs = [
            jnp.concatenate(
                [wide[b, at : at + SLAB, :], extra[b, at : at + SLAB, :]], axis=1
            ).astype(bf16)
            for b in range(2)
        ]
        slabs.insert(1, raw[at : at + SLAB, :])
        product = dot(taps[...], jnp.concatenate(slabs, axis=0))
        first, middle, last = (
            product[:OUT_SLAB],
            product[OUT_SLAB : 2 * OUT_SLAB],
            product[2 * OUT_SLAB :],
        )
        conv = (
            middle[:, :TILE]
            + jnp.where(
                lane8 == 0,
                pltpu.roll(first[:, TILE:], TILE - 2 * EDGE + 1, 1),
                pltpu.roll(first[:, :TILE], 1, 1),
            )
            + jnp.where(
                lane8 == TILE - 1,
                pltpu.roll(last[:, TILE:], TILE - 1, 1),
                pltpu.roll(last[:, :TILE], TILE - 1, 1),
            )
        )
        centre = slabs[1][:, :TILE].astype(f32)[GROUPS : GROUPS + OUT_SLAB]
        volume = (centre + jnp.maximum(conv, 0.0)).astype(bf16).astype(f32)
        volume = volume.reshape(BLOCK, GROUPS, TILE)
        logit[q * BLOCK : (q + 1) * BLOCK, :] = jnp.sum(volume * gains[None], axis=1)
        for d in range(BLOCK):
            for t in range(ITERS):
                found[t] = found[t] + jnp.where(wanted[t] == q * BLOCK + d, volume[d], 0.0)

    level = lax.broadcasted_iota(jnp.int32, (DISPS, TILE), 0)
    valid = level < limit[...]
    masked = jnp.where(valid, logit[...], floor_logit)
    top = jnp.max(masked, axis=0, keepdims=True)
    weights = jnp.where(valid, jnp.exp(masked - top), 0.0)
    moment = jnp.sum(weights * level.astype(f32), axis=0, keepdims=True)
    start = moment / jnp.sum(weights, axis=0, keepdims=True) / pixel_unit
    high = start.astype(bf16).astype(f32)
    low = (start - high).astype(bf16).astype(f32)
    ends = jnp.where(
        group_at == 0,
        jnp.broadcast_to(high, (GROUPS, TILE)),
        jnp.where(group_at == 1, jnp.broadcast_to(low, (GROUPS, TILE)), 0.0),
    )

    padded[:EDGE, :] = jnp.zeros((EDGE, HID_CH), f32)
    padded[EDGE : EDGE + TILE, :] = hidden[...].astype(f32)
    padded[EDGE + TILE :, :] = jnp.zeros((EDGE, HID_CH), f32)
    lane = lax.broadcasted_iota(jnp.int32, (GROUPS, TILE), 1)
    packed = found + [ends]
    for strip in range(QUAD):
        block = [padded[STRIP * strip : STRIP * strip + WINDOW, :]]
        for half in range(2):
            low, high = [
                pltpu.roll(packed[2 * half + i], (PITCH * i + EDGE - STRIP * strip) % TILE, 1)
                for i in range(2)
            ]
            part = jnp.where(lane < PITCH, low, high)
            block.append(jnp.where(lane % PITCH < WINDOW, part, 0.0))
        blocks[strip] = jnp.concatenate(block, axis=0).astype(bf16)
    member = band % QUAD
    for i, out in enumerate((out_0, out_1, out_2, out_3)):
        out[...] = blocks[strip_at(place, member ^ i)]


def strip_at(place, member):
    return jnp.where(place[1] % 2 == 0, member, QUAD - 1 - member)


def keep(line, target, at, values):
    length = values.shape[0]
    start = EDGE + at
    line[start : start + length, :] = values
    target[at : at + length, 0:HID_CH] = line[start - 1 : start - 1 + length, :].astype(bf16)
    target[at : at + length, HID_CH : 2 * HID_CH] = values.astype(bf16)
    target[at : at + length, 2 * HID_CH :] = line[start + 1 : start + 1 + length, :].astype(bf16)


def around(target, at, length):
    return [target[at + a * WINDOW : at + a * WINDOW + length, :] for a in (-1, 0, 1)]


def refine_kernel(
    place,
    own,
    near_a,
    near_b,
    far_c,
    far_d,
    own_beside,
    near_a_beside,
    near_b_beside,
    far_c_beside,
    far_d_beside,
    hid_weight,
    in_weight,
    out_0,
    out_1,
    out_2,
    out_3,
    line,
    weight,
    head_row,
    looked,
    hidden_at,
    taps,
    reset_taps,
    inputs,
    gate,
    level,
    blocks,
    sems,
):
    rows, strip = AROUND, STRIP
    copies = [
        pltpu.make_async_copy(hid_weight, weight.at[pl.ds(0, 9 * HID_CH)], sems.at[0])
    ]
    copies.append(
        pltpu.make_async_copy(
            in_weight.at[pl.ds(0, 3 * HID_CH)],
            weight.at[pl.ds(9 * HID_CH, 3 * HID_CH)],
            sems.at[1],
        )
    )
    copies.append(
        pltpu.make_async_copy(
            in_weight.at[pl.ds(3 * HID_CH, 16), pl.ds(0, HID_CH)], head_row, sems.at[2]
        )
    )
    for copy in copies:
        copy.start()

    band, disp, bands, disps = place[0], place[1], place[2], place[3]
    member, layer = band % QUAD, band // QUAD
    at = strip_at(place, member)
    at_left = (at == 0) & (disp > 0)
    at_right = (at == QUAD - 1) & (disp < disps - 1)
    off = strip
    first = strip * at - EDGE
    first_row = layer * QUAD - REACH

    def block_of(r):
        step, row = (r + 2 * QUAD - REACH) // QUAD - 2, (r + 2 * QUAD - REACH) % QUAD
        slot = row ^ member
        if step == 0:
            return own[slot].astype(f32), own_beside[slot].astype(f32)
        if abs(step) == 1:
            choice, pairs = (layer % 2 == 0) == (step > 0), ((near_a, near_b), (near_a_beside, near_b_beside))
        else:
            choice, pairs = (layer % 4 < 2) == (step > 0), ((far_c, far_d), (far_c_beside, far_d_beside))
        inside = (first_row + r >= 0) & (first_row + r < bands)
        return [
            jnp.where(inside, jnp.where(choice, x[slot].astype(f32), y[slot].astype(f32)), 0.0)
            for x, y in pairs
        ]

    def joined(own, other, axis, size, column):
        column = column + first
        ahead = pltpu.roll(other, (size - off) % size, axis)
        behind = pltpu.roll(other, off, axis)
        value = jnp.where((column < 0) & at_left, ahead, 0.0)
        value = jnp.where((column >= TILE) & at_right, behind, value)
        return jnp.where((column >= 0) & (column < TILE), own, value)

    column_h = lax.broadcasted_iota(jnp.int32, (BLOCK_ROWS, HID_CH), 0)
    lane = lax.broadcasted_iota(jnp.int32, (GROUPS, TILE), 1)
    column_p = lax.broadcasted_iota(jnp.int32, (2 * GROUPS, TILE), 1) % PITCH
    at_sub = lax.broadcasted_iota(jnp.int32, (WINDOW, TILE), 0)
    at_lane = lax.broadcasted_iota(jnp.int32, (WINDOW, TILE), 1)
    spread = jnp.where(at_sub == at_lane % PITCH, 1.0, 0.0).astype(bf16)
    fill = jnp.zeros((PACK, TILE), f32)
    zeros = jnp.zeros((GROUPS, TILE), f32)
    lines = []
    for r in range(rows):
        here, other = block_of(r)
        packed = joined(here[WINDOW:], other[WINDOW:], 1, TILE, column_p)
        hidden = joined(here, other, 0, BLOCK_ROWS, column_h)[:WINDOW]
        hidden_at[r * WINDOW : (r + 1) * WINDOW, :] = hidden
        pieces = []
        for b in range(3):
            moved = packed if b == 1 else pltpu.roll(packed, (1 - b) % TILE, 1)
            for q in range(4):
                part = moved[GROUPS * (q // 2) : GROUPS * (q // 2 + 1)]
                pieces.append(jnp.where((lane >= PITCH) == (q % 2 == 1), part, zeros))
        lines.append(jnp.concatenate(pieces + [fill], axis=0).astype(bf16))
    for r in range(0, rows, 2):
        both = dot_nt(spread, jnp.concatenate(lines[r : r + 2], axis=0))
        for i in range(2):
            at = (r + i) * WINDOW
            looked[at : at + WINDOW, :] = both[:, i * HID_CH : (i + 1) * HID_CH]
    sub = lax.broadcasted_iota(jnp.int32, (HID_CH, HID_CH), 0)
    ends = jnp.where((sub == PACK + 24) | (sub == PACK + 25), feature_scale, 0.0).astype(bf16)
    blank = jnp.zeros((EDGE, HID_CH), f32)
    level[:EDGE, :] = blank
    level[EDGE + WINDOW * rows :, :] = blank
    level[EDGE : EDGE + WINDOW * rows, :] = dot(looked[...].astype(bf16), ends)
    line[...] = jnp.zeros_like(line)
    keep(line, taps, 0, hidden_at[...])
    for copy in copies:
        copy.wait()
    head = head_row[...].astype(f32)[0:1] * feature_scale
    head = jnp.broadcast_to(head, (HID_CH, HID_CH)).astype(bf16)

    for t in range(ITERS):
        low, high = 1 + 2 * t, rows - 2 - 2 * t
        at, length = (low - 1) * WINDOW, (high - low + 3) * WINDOW
        lane_at = lax.broadcasted_iota(jnp.int32, (length, HID_CH), 1)
        tap, channel = lane_at // PACK, lane_at % PACK
        near = [level[EDGE + at + b : EDGE + at + b + length, :] for b in (-1, 0, 1)]
        value = jnp.where(tap == 0, near[0], jnp.where(tap == 1, near[1], near[2]))
        at_lookup = (channel >= t * GROUPS) & (channel < (t + 1) * GROUPS)
        value = jnp.where(
            (channel == 3 * GROUPS) & (tap < 3),
            value,
            jnp.where(at_lookup, looked[at : at + length, :], 0.0),
        )
        inputs[at : at + length, :] = value.astype(bf16)

        at, length = low * WINDOW, (high - low + 1) * WINDOW
        lhs = around(taps, at, length) + around(inputs, at, length)
        both = dot(jnp.concatenate(lhs, axis=1), weight[:, : 2 * HID_CH])
        gate[at + WINDOW : at + length - WINDOW, :] = (
            0.5 * jnp.tanh(0.5 * both[WINDOW : length - WINDOW, :HID_CH]) + 0.5
        )
        reset = 0.5 * jnp.tanh(0.5 * both[:, HID_CH:]) + 0.5
        keep(line, reset_taps, at, reset * hidden_at[at : at + length, :])

        at, length = at + WINDOW, length - 2 * WINDOW
        lhs = around(reset_taps, at, length) + around(inputs, at, length)
        candidate = jnp.tanh(dot(jnp.concatenate(lhs, axis=1), weight[:, 2 * HID_CH :]))
        hidden = hidden_at[at : at + length, :]
        hidden = hidden + gate[at : at + length, :] * (candidate - hidden)
        pixel = lax.broadcasted_iota(jnp.int32, (length, HID_CH), 0)
        column, row = pixel % WINDOW + first, pixel // WINDOW + (low + 1 + first_row)
        inside = ((column >= 0) | (disp > 0)) & ((column < TILE) | (disp < disps - 1))
        inside = inside & (row >= 0) & (row < bands)
        hidden = jnp.where(inside, hidden, 0.0).astype(bf16)
        level[EDGE + at : EDGE + at + length, :] += dot_nt(hidden, head)
        hidden_at[at : at + length, :] = hidden.astype(f32)
        if t < ITERS - 1:
            keep(line, taps, at, hidden.astype(f32))

    lane = lax.broadcasted_iota(jnp.int32, (strip, HID_CH), 1)
    for r in range(QUAD):
        at = (REACH + r) * WINDOW + EDGE
        hidden = hidden_at[at : at + strip, :]
        value = level[EDGE + at : EDGE + at + strip, :] * (1.0 / feature_scale)
        high = value.astype(bf16).astype(f32)
        middle = (value - high).astype(bf16).astype(f32)
        parts = jnp.where(lane == 0, high, jnp.where(lane == 1, middle, value - high - middle))
        parts = jnp.where(lane < 3, parts, 0.0)
        blocks[r] = jnp.concatenate([hidden, parts], axis=0).astype(bf16)
    for i, out in enumerate((out_0, out_1, out_2, out_3)):
        out[...] = blocks[member ^ i]


def unpack_kernel(place, from_0, from_1, from_2, from_3, disparity_out, hidden_out, blocks):
    for i, block in enumerate((from_0, from_1, from_2, from_3)):
        blocks[i] = block[...]
    member = place[0] % QUAD
    held = [blocks[strip_at(place, strip) ^ member].astype(f32) for strip in range(QUAD)]
    hidden_out[0] = jnp.concatenate([block[:STRIP] for block in held], axis=0).astype(bf16)
    parts = jnp.concatenate([block[STRIP:] for block in held], axis=0).T
    disparity_out[...] = parts[0:1] + parts[1:2] + parts[2:3]


def in_hbm(value):
    return pltpu.with_memory_space_constraint(value, pltpu.HBM)


def to_sides(value):
    disps = lax.axis_size("disp")
    right = [(d, d + 1) for d in range(disps - 1)]
    left = [(d + 1, d) for d in range(disps - 1)]
    if disps == 2:
        return lax.ppermute(value, "disp", right + left)[None]
    return jnp.stack([lax.ppermute(value, "disp", right), lax.ppermute(value, "disp", left)])


def across_border(value):
    bands, disps = lax.axis_size("band"), lax.axis_size("disp")
    pairs = []
    for band in range(bands):
        for d in range(disps - 1):
            if disps == 2 or band % QUAD == (QUAD - 1 if d % 2 == 0 else 0):
                left, right = band * disps + d, band * disps + d + 1
                pairs += [(left, right), (right, left)]
    return lax.ppermute(value, ("band", "disp"), pairs)


def in_group(blocks):
    return [blocks[0]] + [
        to_rows(block, lambda band, i=i: band ^ i) for i, block in enumerate(blocks) if i > 0
    ]


def to_layers(value, partner):
    groups = lax.axis_size("band") // QUAD
    if not any(0 <= partner(g) < groups for g in range(groups)):
        return None
    return to_rows(value, lambda band: partner(band // QUAD) * QUAD + band % QUAD)


def to_rows(value, shift):
    bands = lax.axis_size("band")
    return lax.ppermute(
        value, "band", [(i, shift(i)) for i in range(bands) if 0 <= shift(i) < bands]
    )


def odd_pair(i):
    return i ^ 1


def even_pair(i):
    return i - 1 if i % 2 == 0 else i + 1


def local(
    feat_left,
    feat_right,
    limit,
    indices,
    hidden_start,
    vol_kernel,
    group_gain,
    hid_kernel,
    in_kernel,
    head_weight,
):
    bands, disps = lax.axis_size("band"), lax.axis_size("disp")
    place = jnp.stack(
        [lax.axis_index("band"), lax.axis_index("disp"), jnp.int32(bands), jnp.int32(disps)]
    ).astype(jnp.int32)
    smem = pl.BlockSpec(memory_space=pltpu.SMEM)
    vmem = pl.BlockSpec(memory_space=pltpu.VMEM)
    hbm = pl.BlockSpec(memory_space=pltpu.HBM)
    anywhere = pl.BlockSpec(memory_space=pl.ANY)
    padded = (DISPS + 2) * GROUPS

    feats = jnp.concatenate([feat_left[0], feat_right[0]], axis=0)
    odd_own, even_own = to_rows(feats, odd_pair), to_rows(feats, even_pair)
    across = to_sides(feats)
    raw_own, taps = pl.pallas_call(
        own_row_kernel,
        out_shape=(
            jax.ShapeDtypeStruct((padded, 2 * TILE), bf16),
            jax.ShapeDtypeStruct((3 * OUT_SLAB, 3 * SLAB), bf16),
        ),
        in_specs=[smem, vmem, vmem, hbm],
        out_specs=(vmem, vmem),
        scratch_shapes=[
            pltpu.VMEM((padded, TILE), f32),
            pltpu.VMEM((padded, TILE), f32),
            pltpu.VMEM((27, GROUPS, GROUPS), bf16),
            pltpu.SemaphoreType.DMA((1,)),
        ],
        compiler_params=pltpu.CompilerParams(vmem_limit_bytes=16 * 2**20),
        cost_estimate=pl.CostEstimate(flops=2 * 10**9, bytes_accessed=4 * 2**20, transcendentals=0),
    )(place, feats, across, in_hbm(vol_kernel.reshape(27, GROUPS, GROUPS)))
    odd_own, even_own, raw_own, taps = lax.optimization_barrier(
        (odd_own, even_own, raw_own, taps)
    )
    odd_across, even_across = to_sides(odd_own), to_sides(even_own)

    in_weight = jnp.concatenate(
        [in_kernel[:, :, :GROUPS]] * ITERS + [in_kernel[:, :, GROUPS:]], axis=2
    )
    in_weight = jnp.pad(in_weight, ((0, 0), (0, 1), (0, PACK - in_weight.shape[2]), (0, 0)))
    in_weight = jnp.concatenate(
        [
            in_weight.reshape(3 * HID_CH, 3 * HID_CH),
            jnp.pad(head_weight.reshape(1, HID_CH), ((0, 15), (0, 2 * HID_CH))),
        ],
        axis=0,
    )

    blocks = pl.pallas_call(
        volume_kernel,
        out_shape=(jax.ShapeDtypeStruct((BLOCK_ROWS, TILE), bf16),) * QUAD,
        in_specs=[smem, smem] + [vmem] * 7 + [hbm, hbm],
        out_specs=(vmem,) * QUAD,
        scratch_shapes=[
            pltpu.VMEM((padded, 2 * TILE), bf16),
            pltpu.VMEM((3 * OUT_SLAB, 3 * SLAB), bf16),
            pltpu.VMEM((2, padded, TILE), f32),
            pltpu.VMEM((2, padded, TILE), f32),
            pltpu.VMEM((DISPS, TILE), f32),
            pltpu.VMEM((TILE + 2 * EDGE, HID_CH), f32),
            pltpu.VMEM((QUAD, BLOCK_ROWS, TILE), bf16),
            pltpu.SemaphoreType.DMA((2,)),
        ],
        compiler_params=pltpu.CompilerParams(vmem_limit_bytes=24 * 2**20),
        cost_estimate=pl.CostEstimate(
            flops=5 * 10**9, bytes_accessed=16 * 2**20, transcendentals=DISPS * TILE
        ),
    )(
        place, in_hbm(group_gain), odd_own, odd_across, even_own, even_across,
        in_hbm(limit), in_hbm(indices[:, 0]), in_hbm(hidden_start[0]), raw_own, taps,
    )

    own, in_weight = lax.optimization_barrier((jnp.stack(in_group(blocks)), in_weight))
    around = [
        to_layers(own, lambda g: g ^ 1),
        to_layers(own, lambda g: (g - 1 ^ 1) + 1),
        to_layers(own, lambda g: g ^ 2),
        to_layers(own, lambda g: (g - 2 ^ 2) + 2),
    ]
    beside = [across_border(value) for value in [own] + around if value is not None]
    if around[3] is None:
        around[3], beside = around[2], beside + beside[-1:]

    pixels = WINDOW * AROUND
    refined = pl.pallas_call(
        refine_kernel,
        out_shape=(jax.ShapeDtypeStruct((2 * STRIP, HID_CH), bf16),) * QUAD,
        in_specs=[smem] + [vmem] * 10 + [anywhere, hbm],
        out_specs=(vmem,) * QUAD,
        scratch_shapes=[
            pltpu.VMEM((pixels + 2 * EDGE, HID_CH), f32),
            pltpu.VMEM((12 * HID_CH, 3 * HID_CH), bf16),
            pltpu.VMEM((16, HID_CH), bf16),
            pltpu.VMEM((pixels, HID_CH), f32),
            pltpu.VMEM((pixels, HID_CH), f32),
            pltpu.VMEM((pixels, 3 * HID_CH), bf16),
            pltpu.VMEM((pixels, 3 * HID_CH), bf16),
            pltpu.VMEM((pixels, HID_CH), bf16),
            pltpu.VMEM((pixels, HID_CH), f32),
            pltpu.VMEM((pixels + 2 * EDGE, HID_CH), f32),
            pltpu.VMEM((QUAD, 2 * STRIP, HID_CH), bf16),
            pltpu.SemaphoreType.DMA((3,)),
        ],
        compiler_params=pltpu.CompilerParams(vmem_limit_bytes=32 * 2**20),
    )(
        place, own, *around, *beside,
        hid_kernel.reshape(9 * HID_CH, 3 * HID_CH), in_hbm(in_weight),
    )
    disparity, hidden = pl.pallas_call(
        unpack_kernel,
        out_shape=(
            jax.ShapeDtypeStruct((1, TILE), f32),
            jax.ShapeDtypeStruct((1, TILE, HID_CH), bf16),
        ),
        in_specs=[smem] + [vmem] * QUAD,
        out_specs=(vmem, vmem),
        scratch_shapes=[pltpu.VMEM((QUAD, 2 * STRIP, HID_CH), bf16)],
    )(place, *in_group(refined))
    return (disparity, hidden)


def solution(mesh):
    in_specs = (
        P("band", None, "disp"),
        P("band", None, "disp"),
        P("band", "disp"),
        P(None, "band", "disp"),
        P("band", "disp", None),
        P(),
        P(),
        P(),
        P(),
        P(),
    )
    out_specs = (P("band", "disp"), P("band", "disp", None))
    return jax.shard_map(local, mesh=mesh, in_specs=in_specs, out_specs=out_specs, check_vma=False)
```

```python
import jax
import jax.numpy as jnp
from jax import lax
from jax.experimental import pallas as pl
from jax.experimental.pallas import tpu as pltpu
from jax.sharding import PartitionSpec as P

GROUPS = 8
DISPS = 96
FEAT_CH = 96
HID_CH = 128
ITERS = 3
TILE = 128
REACH = 2 * ITERS
EDGE = 8
QUAD = 4
STRIP = TILE // QUAD
WINDOW = STRIP + 2 * EDGE
PACK = 32
PITCH = 64
BLOCK_ROWS = WINDOW + 2 * GROUPS
AROUND = QUAD + 2 * REACH
BLOCK = 8
SLAB = (BLOCK + 2) * GROUPS
OUT_SLAB = BLOCK * GROUPS

pixel_unit = 8.0
feature_scale = 0.25
floor_logit = -1e30

f32 = jnp.float32
bf16 = jnp.bfloat16


def dot(a, b):
    return jnp.dot(a, b, preferred_element_type=f32)


def dot_nt(a, b):
    return lax.dot_general(a, b, (((1,), (1,)), ((), ())), preferred_element_type=f32)


def copy_all(copies):
    for copy in copies:
        copy.start()
    for copy in copies:
        copy.wait()


def toeplitz(vol_kernel):
    size = 27 * GROUPS
    flat = vol_kernel[...].astype(f32).reshape(size, GROUPS)
    flat = jnp.concatenate([flat, jnp.zeros((size, TILE - GROUPS), f32)], axis=1).T[:GROUPS]
    row = lax.broadcasted_iota(jnp.int32, (9 * GROUPS, size), 0) >> 3
    tap = lax.broadcasted_iota(jnp.int32, (9 * GROUPS, size), 1) >> 3
    tap_a = (tap >= 9).astype(jnp.int32) + (tap >= 18).astype(jnp.int32)
    within = tap - 9 * tap_a
    tap_b = (within >= 3).astype(jnp.int32) + (within >= 6).astype(jnp.int32)
    tap_e = within - 3 * tap_b
    pairs = jnp.where(
        row == 3 * tap_a + tap_e, jnp.concatenate([flat] * 9, axis=0), 0.0
    ).astype(bf16)
    from_row = lax.broadcasted_iota(jnp.int32, (size, 3 * SLAB), 0)
    to = lax.broadcasted_iota(jnp.int32, (size, 3 * SLAB), 1)
    from_tap = from_row >> 3
    from_in = from_tap - 9 * ((from_tap >= 9).astype(jnp.int32) + (from_tap >= 18).astype(jnp.int32))
    from_b = (from_in >= 3).astype(jnp.int32) + (from_in >= 6).astype(jnp.int32)
    to_b = (to >= SLAB).astype(jnp.int32) + (to >= 2 * SLAB).astype(jnp.int32)
    repeat = jnp.where((from_b == to_b) & ((from_row & 7) == (to & 7)), 1.0, 0.0).astype(bf16)
    spread = dot(pairs, repeat)
    to = lax.broadcasted_iota(jnp.int32, (GROUPS, 3 * SLAB), 1)
    to_b = (to >= SLAB).astype(jnp.int32) + (to >= 2 * SLAB).astype(jnp.int32)
    to_d = (to - SLAB * to_b) >> 3
    rows = []
    for e in range(3):
        for d in range(BLOCK):
            value = jnp.zeros((GROUPS, 3 * SLAB), f32)
            for a in range(3):
                at = (3 * a + e) * GROUPS
                value = jnp.where(to_d == d + a, spread[at : at + GROUPS], value)
            rows.append(value)
    return jnp.concatenate(rows, axis=0).astype(bf16)


def interleaved(values):
    stacked = jnp.swapaxes(jnp.stack(values), 0, 1)
    return stacked.reshape(values[0].shape[0] * len(values), values[0].shape[1])


def correlate(lefts, rights, place, row_ok, wide, extra):
    has_left = (place[1] > 0).astype(f32)
    has_right = (place[1] < place[3] - 1).astype(f32)
    lane = lax.broadcasted_iota(jnp.int32, (TILE, TILE), 1)
    sub = lax.broadcasted_iota(jnp.int32, (TILE, TILE), 0)
    flip = jnp.where(lane + sub == TILE - 1, 1.0, 0.0).astype(bf16)
    per_group = FEAT_CH // GROUPS
    channel = lax.broadcasted_iota(jnp.int32, (32, FEAT_CH), 1)
    group_masks = [
        (channel >= g * per_group) & (channel < (g + 1) * per_group) for g in range(GROUPS)
    ]
    lane96 = lax.broadcasted_iota(jnp.int32, (FEAT_CH, TILE), 1)
    zero_slab = jnp.zeros((GROUPS, TILE), f32)
    for at in (0, (DISPS + 1) * GROUPS):
        wide[pl.ds(at, GROUPS), :] = zero_slab
        extra[pl.ds(at, GROUPS), :] = zero_slab

    own_t = (lefts[1] * row_ok).T
    side_t = jnp.where(
        lane96 < EDGE,
        lefts[2] * (has_right * row_ok),
        jnp.where(lane96 >= TILE - EDGE, lefts[0] * (has_left * row_ok), 0.0),
    ).T
    sources = jnp.concatenate([rights[2] * has_right, rights[1], rights[0] * has_left], axis=0)
    flipped = dot(sources.astype(bf16), flip)
    reverse = jnp.concatenate(
        [flipped[i * FEAT_CH : (i + 1) * FEAT_CH] for i in range(3)], axis=1
    )
    windows = [
        reverse[:, 2 * TILE - 32 - 32 * k : 3 * TILE - 32 - 32 * k].astype(bf16)
        for k in range(-1, 5)
    ]

    def by_group(rows):
        count = rows.shape[0]
        parts = [jnp.where(m[:count], rows, 0.0) for m in group_masks]
        return jnp.concatenate(parts, axis=0).astype(bf16)

    def shear(product, g, count, first):
        rows = product[count * g : count * g + count]
        return pltpu.roll(rows, TILE - 31 + first, 1, stride=1, stride_axis=0)

    products = [
        dot(by_group(own_t[32 * k : 32 * k + 32]), windows[k + 1]) for k in range(TILE // 32)
    ]
    after = dot(by_group(side_t[:EDGE]), windows[5])
    before = dot(by_group(side_t[TILE - EDGE :]), windows[0])
    parts, sides = [], []
    for g in range(GROUPS):
        part = jnp.concatenate([shear(product, g, 32, 0) for product in products], axis=0)
        parts.append(part.T[:DISPS])
        sides += [shear(after, g, EDGE, 0), shear(before, g, EDGE, 32 - EDGE)]
    part = jnp.concatenate(sides, axis=0).T[:DISPS]
    sides = [part if g == 0 else pltpu.roll(part, TILE - 2 * EDGE * g, 1) for g in range(GROUPS)]
    for target, values in ((wide, parts), (extra, sides)):
        target[GROUPS : GROUPS + DISPS * GROUPS, :] = interleaved(values) * (1.0 / per_group)


def own_row_kernel(place, own, across, vol_kernel, raw_out, taps_out, wide, extra, kernel, sem):
    copy = pltpu.make_async_copy(vol_kernel, kernel, sem.at[0])
    copy.start()
    tiles = [across[0], own[...], across[across.shape[0] - 1]]
    tiles = [tile.astype(f32) for tile in tiles]
    correlate(
        [tile[:FEAT_CH] for tile in tiles], [tile[FEAT_CH:] for tile in tiles],
        place, 1.0, wide, extra,
    )
    raw_out[...] = jnp.concatenate([wide[...], extra[...]], axis=1).astype(bf16)
    copy.wait()
    taps_out[...] = toeplitz(kernel)


def volume_kernel(
    place, gain, odd_own, odd_across, even_own, even_across, marks, marks_across, hidden,
    hidden_across, raw_own, taps_own, out_0, out_1, out_2, out_3, raw, taps, wide, extra, logit, padded, blocks, sems,
):
    band, bands = place[0], place[2]
    is_even = band % 2 == 0
    copies = [
        pltpu.make_async_copy(raw_own, raw, sems.at[0]),
        pltpu.make_async_copy(taps_own, taps, sems.at[1]),
    ]
    for copy in copies:
        copy.start()

    last = odd_across.shape[0] - 1
    odd = [tile.astype(f32) for tile in (odd_across[0], odd_own[...], odd_across[last])]
    even = [tile.astype(f32) for tile in (even_across[0], even_own[...], even_across[last])]
    for b in range(2):
        row = band + 2 * b - 1
        row_ok = ((row >= 0) & (row < bands)).astype(f32)
        tiles = [
            jnp.where(is_even, y, x) if b == 0 else jnp.where(is_even, x, y)
            for x, y in zip(odd, even)
        ]
        correlate(
            [tile[:FEAT_CH] for tile in tiles], [tile[FEAT_CH:] for tile in tiles],
            place, row_ok, wide.at[b], extra.at[b],
        )
    for copy in copies:
        copy.wait()

    lane = lax.broadcasted_iota(jnp.int32, (GROUPS, TILE), 1)
    left_marks = pltpu.roll(marks_across[0], 2 * EDGE, 1)
    levels_of = [marks[...], jnp.where(lane < EDGE, marks_across[last], left_marks)]
    lane8 = lax.broadcasted_iota(jnp.int32, (OUT_SLAB, TILE), 1)
    group_at = lax.broadcasted_iota(jnp.int32, (GROUPS, TILE), 0)
    gains = jnp.zeros((GROUPS, TILE), f32)
    for g in range(GROUPS):
        gains = jnp.where(group_at == g, gain[g], gains)
    wanted = [
        [jnp.broadcast_to(rows[t + 1 : t + 2], (GROUPS, TILE)) for t in range(ITERS)]
        for rows in levels_of
    ]
    found = [[jnp.zeros((GROUPS, TILE), f32) for _ in range(ITERS)] for _ in range(2)]
    for q in range(DISPS // BLOCK):
        at = q * OUT_SLAB
        slabs = [
            jnp.concatenate(
                [wide[b, at : at + SLAB, :], extra[b, at : at + SLAB, :]], axis=1
            ).astype(bf16)
            for b in range(2)
        ]
        slabs.insert(1, raw[at : at + SLAB, :])
        product = dot(taps[...], jnp.concatenate(slabs, axis=0))
        halves = [product[:, :TILE], product[:, TILE:]]
        first = [half[:OUT_SLAB] for half in halves]
        middle = [half[OUT_SLAB : 2 * OUT_SLAB] for half in halves]
        after = [half[2 * OUT_SLAB :] for half in halves]
        first_on = pltpu.roll(first[0], 1, 1)
        convs = [
            middle[0]
            + jnp.where(lane8 == 0, pltpu.roll(first[1], TILE - 2 * EDGE + 1, 1), first_on)
            + jnp.where(
                lane8 == TILE - 1,
                pltpu.roll(after[1], TILE - 1, 1),
                pltpu.roll(after[0], TILE - 1, 1),
            ),
            middle[1]
            + jnp.where(lane8 == 0, first_on, pltpu.roll(first[1], 1, 1))
            + jnp.where(
                lane8 == 2 * EDGE - 1,
                pltpu.roll(after[0], 2 * EDGE - 1, 1),
                pltpu.roll(after[1], TILE - 1, 1),
            ),
        ]
        centre = slabs[1].astype(f32)[GROUPS : GROUPS + OUT_SLAB]
        for i in range(2):
            volume = centre[:, i * TILE : (i + 1) * TILE] + jnp.maximum(convs[i], 0.0)
            volume = volume.astype(bf16).astype(f32).reshape(BLOCK, GROUPS, TILE)
            logit[i, q * BLOCK : (q + 1) * BLOCK, :] = jnp.sum(volume * gains[None], axis=1)
            for d in range(BLOCK):
                for t in range(ITERS):
                    hit = wanted[i][t] == q * BLOCK + d
                    found[i][t] = found[i][t] + jnp.where(hit, volume[d], 0.0)

    level = lax.broadcasted_iota(jnp.int32, (DISPS, TILE), 0)
    for i in range(2):
        valid = level < levels_of[i][0:1]
        masked = jnp.where(valid, logit[i], floor_logit)
        top = jnp.max(masked, axis=0, keepdims=True)
        weights = jnp.where(valid, jnp.exp(masked - top), 0.0)
        moment = jnp.sum(weights * level.astype(f32), axis=0, keepdims=True)
        start = moment / jnp.sum(weights, axis=0, keepdims=True) / pixel_unit
        high = start.astype(bf16).astype(f32)
        low = (start - high).astype(bf16).astype(f32)
        ends = jnp.where(
            group_at == 0,
            jnp.broadcast_to(high, (GROUPS, TILE)),
            jnp.where(group_at == 1, jnp.broadcast_to(low, (GROUPS, TILE)), 0.0),
        )
        found[i].append(ends)
    has_left, has_right = place[1] > 0, place[1] < place[3] - 1
    is_beside = ((lane < EDGE) & has_right) | ((lane >= EDGE) & (lane < 2 * EDGE) & has_left)
    packed, packed_beside = found[0], [jnp.where(is_beside, x, 0.0) for x in found[1]]

    before = hidden_across[0, TILE - 2 * EDGE :, :].astype(f32)[EDGE:]
    after = hidden_across[last, : 2 * EDGE, :].astype(f32)[:EDGE]
    padded[:EDGE, :] = jnp.where(has_left, before, 0.0)
    padded[EDGE : EDGE + TILE, :] = hidden[...].astype(f32)
    padded[EDGE + TILE :, :] = jnp.where(has_right, after, 0.0)
    for strip in range(QUAD):
        block = [padded[STRIP * strip : STRIP * strip + WINDOW, :]]
        for half in range(2):
            part = jnp.zeros((GROUPS, TILE), f32)
            for i in range(2):
                q, base = 2 * half + i, PITCH * i
                at = lane - base
                moved = pltpu.roll(packed[q], (base + EDGE - STRIP * strip) % TILE, 1)
                if strip == 0:
                    other = pltpu.roll(packed_beside[q], (base - EDGE) % TILE, 1)
                    moved = jnp.where(at < EDGE, other, moved)
                if strip == QUAD - 1:
                    other = pltpu.roll(packed_beside[q], base + WINDOW - EDGE, 1)
                    moved = jnp.where(at >= WINDOW - EDGE, other, moved)
                part = jnp.where((at >= 0) & (at < WINDOW), moved, part)
            block.append(part)
        blocks[strip] = jnp.concatenate(block, axis=0).astype(bf16)
    member = band % QUAD
    for i, out in enumerate((out_0, out_1, out_2, out_3)):
        out[...] = blocks[strip_at(place, member ^ i)]


def strip_at(place, member):
    return jnp.where(place[1] % 2 == 0, member, QUAD - 1 - member)


def keep(line, target, at, values):
    length = values.shape[0]
    start = EDGE + at
    line[start : start + length, :] = values
    target[at : at + length, 0:HID_CH] = line[start - 1 : start - 1 + length, :].astype(bf16)
    target[at : at + length, HID_CH : 2 * HID_CH] = values.astype(bf16)
    target[at : at + length, 2 * HID_CH :] = line[start + 1 : start + 1 + length, :].astype(bf16)


def around(target, at, length):
    return [target[at + a * WINDOW : at + a * WINDOW + length, :] for a in (-1, 0, 1)]


def refine_kernel(
    place,
    own,
    near_a,
    near_b,
    far_c,
    far_d,
    hid_weight,
    in_weight,
    head,
    out_0,
    out_1,
    out_2,
    out_3,
    line,
    weight,
    looked,
    hidden_at,
    taps,
    reset_taps,
    inputs,
    gate,
    level,
    blocks,
    sems,
):
    rows, strip = AROUND, STRIP
    copies = [
        pltpu.make_async_copy(hid_weight, weight.at[pl.ds(0, 9 * HID_CH)], sems.at[0])
    ]
    copies.append(
        pltpu.make_async_copy(
            in_weight, weight.at[pl.ds(9 * HID_CH, 3 * HID_CH)], sems.at[1]
        )
    )
    for copy in copies:
        copy.start()

    band, disp, bands, disps = place[0], place[1], place[2], place[3]
    member, layer = band % QUAD, band // QUAD
    at = strip_at(place, member)
    first = strip * at - EDGE
    first_row = layer * QUAD - REACH

    def block_of(r):
        step, row = (r + 2 * QUAD - REACH) // QUAD - 2, (r + 2 * QUAD - REACH) % QUAD
        slot = row ^ member
        if step == 0:
            return own[slot].astype(f32)
        if abs(step) == 1:
            choice, x, y = (layer % 2 == 0) == (step > 0), near_a, near_b
        else:
            choice, x, y = (layer % 4 < 2) == (step > 0), far_c, far_d
        inside = (first_row + r >= 0) & (first_row + r < bands)
        block = jnp.where(choice, x[slot].astype(f32), y[slot].astype(f32))
        return jnp.where(inside, block, 0.0)

    lane = lax.broadcasted_iota(jnp.int32, (GROUPS, TILE), 1)
    at_sub = lax.broadcasted_iota(jnp.int32, (WINDOW, TILE), 0)
    at_lane = lax.broadcasted_iota(jnp.int32, (WINDOW, TILE), 1)
    spread = jnp.where(at_sub == at_lane % PITCH, 1.0, 0.0).astype(bf16)
    fill = jnp.zeros((PACK, TILE), f32)
    zeros = jnp.zeros((GROUPS, TILE), f32)
    lines = []
    for r in range(rows):
        block = block_of(r)
        packed = block[WINDOW:]
        hidden_at[r * WINDOW : (r + 1) * WINDOW, :] = block[:WINDOW]
        pieces = []
        for b in range(3):
            moved = packed if b == 1 else pltpu.roll(packed, (1 - b) % TILE, 1)
            for q in range(4):
                part = moved[GROUPS * (q // 2) : GROUPS * (q // 2 + 1)]
                pieces.append(jnp.where((lane >= PITCH) == (q % 2 == 1), part, zeros))
        lines.append(jnp.concatenate(pieces + [fill], axis=0).astype(bf16))
    for r in range(0, rows, 2):
        both = dot_nt(spread, jnp.concatenate(lines[r : r + 2], axis=0))
        for i in range(2):
            at = (r + i) * WINDOW
            looked[at : at + WINDOW, :] = both[:, i * HID_CH : (i + 1) * HID_CH]
    sub = lax.broadcasted_iota(jnp.int32, (HID_CH, HID_CH), 0)
    ends = jnp.where((sub == PACK + 24) | (sub == PACK + 25), feature_scale, 0.0).astype(bf16)
    blank = jnp.zeros((EDGE, HID_CH), f32)
    level[:EDGE, :] = blank
    level[EDGE + WINDOW * rows :, :] = blank
    level[EDGE : EDGE + WINDOW * rows, :] = dot(looked[...].astype(bf16), ends)
    line[...] = jnp.zeros_like(line)
    keep(line, taps, 0, hidden_at[...])
    for copy in copies:
        copy.wait()
    heads = jnp.broadcast_to(head[...].astype(f32) * feature_scale, (HID_CH, HID_CH)).astype(bf16)

    for t in range(ITERS):
        low, high = 1 + 2 * t, rows - 2 - 2 * t
        at, length = (low - 1) * WINDOW, (high - low + 3) * WINDOW
        lane_at = lax.broadcasted_iota(jnp.int32, (length, HID_CH), 1)
        tap, channel = lane_at // PACK, lane_at % PACK
        near = [level[EDGE + at + b : EDGE + at + b + length, :] for b in (-1, 0, 1)]
        value = jnp.where(tap == 0, near[0], jnp.where(tap == 1, near[1], near[2]))
        at_lookup = (channel >= t * GROUPS) & (channel < (t + 1) * GROUPS)
        value = jnp.where(
            (channel == 3 * GROUPS) & (tap < 3),
            value,
            jnp.where(at_lookup, looked[at : at + length, :], 0.0),
        )
        inputs[at : at + length, :] = value.astype(bf16)

        at, length = low * WINDOW, (high - low + 1) * WINDOW
        lhs = around(taps, at, length) + around(inputs, at, length)
        both = dot(jnp.concatenate(lhs, axis=1), weight[:, : 2 * HID_CH])
        gate[at + WINDOW : at + length - WINDOW, :] = (
            0.5 * jnp.tanh(0.5 * both[WINDOW : length - WINDOW, :HID_CH]) + 0.5
        )
        reset = 0.5 * jnp.tanh(0.5 * both[:, HID_CH:]) + 0.5
        keep(line, reset_taps, at, reset * hidden_at[at : at + length, :])

        at, length = at + WINDOW, length - 2 * WINDOW
        lhs = around(reset_taps, at, length) + around(inputs, at, length)
        candidate = jnp.tanh(dot(jnp.concatenate(lhs, axis=1), weight[:, 2 * HID_CH :]))
        hidden = hidden_at[at : at + length, :]
        hidden = hidden + gate[at : at + length, :] * (candidate - hidden)
        pixel = lax.broadcasted_iota(jnp.int32, (length, HID_CH), 0)
        column, row = pixel % WINDOW + first, pixel // WINDOW + (low + 1 + first_row)
        inside = ((column >= 0) | (disp > 0)) & ((column < TILE) | (disp < disps - 1))
        inside = inside & (row >= 0) & (row < bands)
        hidden = jnp.where(inside, hidden, 0.0).astype(bf16)
        level[EDGE + at : EDGE + at + length, :] += dot_nt(hidden, heads)
        hidden_at[at : at + length, :] = hidden.astype(f32)
        if t < ITERS - 1:
            keep(line, taps, at, hidden.astype(f32))

    lane = lax.broadcasted_iota(jnp.int32, (strip, HID_CH), 1)
    for r in range(QUAD):
        at = (REACH + r) * WINDOW + EDGE
        hidden = hidden_at[at : at + strip, :]
        value = level[EDGE + at : EDGE + at + strip, :] * (1.0 / feature_scale)
        high = value.astype(bf16).astype(f32)
        middle = (value - high).astype(bf16).astype(f32)
        parts = jnp.where(lane == 0, high, jnp.where(lane == 1, middle, value - high - middle))
        parts = jnp.where(lane < 3, parts, 0.0)
        blocks[r] = jnp.concatenate([hidden, parts], axis=0).astype(bf16)
    for i, out in enumerate((out_0, out_1, out_2, out_3)):
        out[...] = blocks[member ^ i]


def unpack_kernel(place, from_0, from_1, from_2, from_3, disparity_out, hidden_out, blocks):
    for i, block in enumerate((from_0, from_1, from_2, from_3)):
        blocks[i] = block[...]
    member = place[0] % QUAD
    held = [blocks[strip_at(place, strip) ^ member].astype(f32) for strip in range(QUAD)]
    hidden_out[0] = jnp.concatenate([block[:STRIP] for block in held], axis=0).astype(bf16)
    parts = jnp.concatenate([block[STRIP:] for block in held], axis=0).T
    disparity_out[...] = parts[0:1] + parts[1:2] + parts[2:3]


def in_hbm(value):
    return pltpu.with_memory_space_constraint(value, pltpu.HBM)


def to_sides(value):
    disps = lax.axis_size("disp")
    right = [(d, d + 1) for d in range(disps - 1)]
    left = [(d + 1, d) for d in range(disps - 1)]
    if disps == 2:
        return lax.ppermute(value, "disp", right + left)[None]
    return jnp.stack([lax.ppermute(value, "disp", right), lax.ppermute(value, "disp", left)])


def in_group(blocks):
    return [blocks[0]] + [
        to_rows(block, lambda band, i=i: band ^ i) for i, block in enumerate(blocks) if i > 0
    ]


def to_layers(value, partner):
    groups = lax.axis_size("band") // QUAD
    if not any(0 <= partner(g) < groups for g in range(groups)):
        return None
    return to_rows(value, lambda band: partner(band // QUAD) * QUAD + band % QUAD)


def to_rows(value, shift):
    bands = lax.axis_size("band")
    return lax.ppermute(
        value, "band", [(i, shift(i)) for i in range(bands) if 0 <= shift(i) < bands]
    )


def odd_pair(i):
    return i ^ 1


def even_pair(i):
    return i - 1 if i % 2 == 0 else i + 1


def local(
    feat_left,
    feat_right,
    limit,
    indices,
    hidden_start,
    vol_kernel,
    group_gain,
    hid_kernel,
    in_kernel,
    head_weight,
):
    bands, disps = lax.axis_size("band"), lax.axis_size("disp")
    place = jnp.stack(
        [lax.axis_index("band"), lax.axis_index("disp"), jnp.int32(bands), jnp.int32(disps)]
    ).astype(jnp.int32)
    smem = pl.BlockSpec(memory_space=pltpu.SMEM)
    vmem = pl.BlockSpec(memory_space=pltpu.VMEM)
    hbm = pl.BlockSpec(memory_space=pltpu.HBM)
    anywhere = pl.BlockSpec(memory_space=pl.ANY)
    padded = (DISPS + 2) * GROUPS

    feats = jnp.concatenate([feat_left[0], feat_right[0]], axis=0)
    odd_own, even_own = to_rows(feats, odd_pair), to_rows(feats, even_pair)
    across = to_sides(feats)
    raw_own, taps = pl.pallas_call(
        own_row_kernel,
        out_shape=(
            jax.ShapeDtypeStruct((padded, 2 * TILE), bf16),
            jax.ShapeDtypeStruct((3 * OUT_SLAB, 3 * SLAB), bf16),
        ),
        in_specs=[smem, vmem, vmem, hbm],
        out_specs=(vmem, vmem),
        scratch_shapes=[
            pltpu.VMEM((padded, TILE), f32),
            pltpu.VMEM((padded, TILE), f32),
            pltpu.VMEM((27, GROUPS, GROUPS), bf16),
            pltpu.SemaphoreType.DMA((1,)),
        ],
        compiler_params=pltpu.CompilerParams(vmem_limit_bytes=16 * 2**20),
        cost_estimate=pl.CostEstimate(flops=2 * 10**9, bytes_accessed=4 * 2**20, transcendentals=0),
    )(place, feats, across, in_hbm(vol_kernel.reshape(27, GROUPS, GROUPS)))
    marks = jnp.concatenate([limit, indices[:, 0]], axis=0)
    marks = jnp.pad(marks, ((0, GROUPS - marks.shape[0]), (0, 0)))
    hidden = hidden_start[0]
    hidden_across, marks_across = to_sides(hidden), to_sides(marks)
    odd_own, even_own, raw_own, taps, hidden_across, marks_across = lax.optimization_barrier(
        (odd_own, even_own, raw_own, taps, hidden_across, marks_across)
    )
    odd_across, even_across = to_sides(odd_own), to_sides(even_own)

    in_weight = jnp.concatenate(
        [in_kernel[:, :, :GROUPS]] * ITERS + [in_kernel[:, :, GROUPS:]], axis=2
    )
    in_weight = jnp.pad(in_weight, ((0, 0), (0, 1), (0, PACK - in_weight.shape[2]), (0, 0)))
    in_weight = in_weight.reshape(3 * HID_CH, 3 * HID_CH)

    blocks = pl.pallas_call(
        volume_kernel,
        out_shape=(jax.ShapeDtypeStruct((BLOCK_ROWS, TILE), bf16),) * QUAD,
        in_specs=[smem, smem] + [vmem] * 8 + [hbm, hbm],
        out_specs=(vmem,) * QUAD,
        scratch_shapes=[
            pltpu.VMEM((padded, 2 * TILE), bf16),
            pltpu.VMEM((3 * OUT_SLAB, 3 * SLAB), bf16),
            pltpu.VMEM((2, padded, TILE), f32),
            pltpu.VMEM((2, padded, TILE), f32),
            pltpu.VMEM((2, DISPS, TILE), f32),
            pltpu.VMEM((TILE + 2 * EDGE, HID_CH), f32),
            pltpu.VMEM((QUAD, BLOCK_ROWS, TILE), bf16),
            pltpu.SemaphoreType.DMA((2,)),
        ],
        compiler_params=pltpu.CompilerParams(vmem_limit_bytes=24 * 2**20),
        cost_estimate=pl.CostEstimate(
            flops=5 * 10**9, bytes_accessed=16 * 2**20, transcendentals=DISPS * TILE
        ),
    )(
        place, in_hbm(group_gain), odd_own, odd_across, even_own, even_across,
        marks, marks_across, in_hbm(hidden), hidden_across, raw_own, taps,
    )

    own, in_weight = lax.optimization_barrier((jnp.stack(in_group(blocks)), in_weight))
    around = [
        to_layers(own, lambda g: g ^ 1),
        to_layers(own, lambda g: (g - 1 ^ 1) + 1),
        to_layers(own, lambda g: g ^ 2),
        to_layers(own, lambda g: (g - 2 ^ 2) + 2),
    ]
    if around[3] is None:
        around[3] = around[2]

    pixels = WINDOW * AROUND
    refined = pl.pallas_call(
        refine_kernel,
        out_shape=(jax.ShapeDtypeStruct((2 * STRIP, HID_CH), bf16),) * QUAD,
        in_specs=[smem] + [vmem] * 5 + [anywhere, anywhere, vmem],
        out_specs=(vmem,) * QUAD,
        scratch_shapes=[
            pltpu.VMEM((pixels + 2 * EDGE, HID_CH), f32),
            pltpu.VMEM((12 * HID_CH, 3 * HID_CH), bf16),
            pltpu.VMEM((pixels, HID_CH), f32),
            pltpu.VMEM((pixels, HID_CH), f32),
            pltpu.VMEM((pixels, 3 * HID_CH), bf16),
            pltpu.VMEM((pixels, 3 * HID_CH), bf16),
            pltpu.VMEM((pixels, HID_CH), bf16),
            pltpu.VMEM((pixels, HID_CH), f32),
            pltpu.VMEM((pixels + 2 * EDGE, HID_CH), f32),
            pltpu.VMEM((QUAD, 2 * STRIP, HID_CH), bf16),
            pltpu.SemaphoreType.DMA((2,)),
        ],
        compiler_params=pltpu.CompilerParams(vmem_limit_bytes=32 * 2**20),
    )(
        place, own, *around,
        hid_kernel.reshape(9 * HID_CH, 3 * HID_CH), in_weight,
        in_hbm(head_weight.reshape(1, HID_CH)),
    )
    disparity, hidden = pl.pallas_call(
        unpack_kernel,
        out_shape=(
            jax.ShapeDtypeStruct((1, TILE), f32),
            jax.ShapeDtypeStruct((1, TILE, HID_CH), bf16),
        ),
        in_specs=[smem] + [vmem] * QUAD,
        out_specs=(vmem, vmem),
        scratch_shapes=[pltpu.VMEM((QUAD, 2 * STRIP, HID_CH), bf16)],
        compiler_params=pltpu.CompilerParams(vmem_limit_bytes=4 * 2**20),
    )(place, *in_group(refined))
    return (disparity, hidden)


def solution(mesh):
    in_specs = (
        P("band", None, "disp"),
        P("band", None, "disp"),
        P("band", "disp"),
        P(None, "band", "disp"),
        P("band", "disp", None),
        P(),
        P(),
        P(),
        P(),
        P(),
    )
    out_specs = (P("band", "disp"), P("band", "disp", None))
    return jax.shard_map(local, mesh=mesh, in_specs=in_specs, out_specs=out_specs, check_vma=False)
```

```python
import jax
import jax.numpy as jnp
from jax import lax
from jax.experimental import pallas as pl
from jax.experimental.pallas import tpu as pltpu
from jax.sharding import PartitionSpec as P

GROUPS = 8
DISPS = 96
FEAT_CH = 96
HID_CH = 128
ITERS = 3
TILE = 128
REACH = 2 * ITERS
EDGE = 8
QUAD = 4
STRIP = TILE // QUAD
WINDOW = STRIP + 2 * EDGE
PACK = 32
PITCH = 64
ORDER = (0, 3, 1, 2)
BLOCK_ROWS = WINDOW + 2 * GROUPS
AROUND = QUAD + 2 * REACH
BLOCK = 8
SLAB = (BLOCK + 2) * GROUPS
OUT_SLAB = BLOCK * GROUPS

pixel_unit = 8.0
feature_scale = 0.25
floor_logit = -1e30

f32 = jnp.float32
bf16 = jnp.bfloat16


def dot(a, b):
    return jnp.dot(a, b, preferred_element_type=f32)


def dot_nt(a, b):
    return lax.dot_general(a, b, (((1,), (1,)), ((), ())), preferred_element_type=f32)


def copy_all(copies):
    for copy in copies:
        copy.start()
    for copy in copies:
        copy.wait()


def toeplitz(vol_kernel):
    size = 27 * GROUPS
    flat = vol_kernel[...].astype(f32).reshape(size, GROUPS)
    flat = jnp.concatenate([flat, jnp.zeros((size, TILE - GROUPS), f32)], axis=1).T[:GROUPS]
    row = lax.broadcasted_iota(jnp.int32, (9 * GROUPS, size), 0) >> 3
    tap = lax.broadcasted_iota(jnp.int32, (9 * GROUPS, size), 1) >> 3
    tap_a = (tap >= 9).astype(jnp.int32) + (tap >= 18).astype(jnp.int32)
    within = tap - 9 * tap_a
    tap_b = (within >= 3).astype(jnp.int32) + (within >= 6).astype(jnp.int32)
    tap_e = within - 3 * tap_b
    pairs = jnp.where(
        row == 3 * tap_a + tap_e, jnp.concatenate([flat] * 9, axis=0), 0.0
    ).astype(bf16)
    from_row = lax.broadcasted_iota(jnp.int32, (size, 3 * SLAB), 0)
    to = lax.broadcasted_iota(jnp.int32, (size, 3 * SLAB), 1)
    from_tap = from_row >> 3
    from_in = from_tap - 9 * ((from_tap >= 9).astype(jnp.int32) + (from_tap >= 18).astype(jnp.int32))
    from_b = (from_in >= 3).astype(jnp.int32) + (from_in >= 6).astype(jnp.int32)
    to_b = (to >= SLAB).astype(jnp.int32) + (to >= 2 * SLAB).astype(jnp.int32)
    repeat = jnp.where((from_b == to_b) & ((from_row & 7) == (to & 7)), 1.0, 0.0).astype(bf16)
    spread = dot(pairs, repeat)
    to = lax.broadcasted_iota(jnp.int32, (GROUPS, 3 * SLAB), 1)
    to_b = (to >= SLAB).astype(jnp.int32) + (to >= 2 * SLAB).astype(jnp.int32)
    to_d = (to - SLAB * to_b) >> 3
    rows = []
    for e in range(3):
        for d in range(BLOCK):
            value = jnp.zeros((GROUPS, 3 * SLAB), f32)
            for a in range(3):
                at = (3 * a + e) * GROUPS
                value = jnp.where(to_d == d + a, spread[at : at + GROUPS], value)
            rows.append(value)
    return jnp.concatenate(rows, axis=0).astype(bf16)


def interleaved(values):
    stacked = jnp.swapaxes(jnp.stack(values), 0, 1)
    return stacked.reshape(values[0].shape[0] * len(values), values[0].shape[1])


def correlate(lefts, rights, place, row_ok, wide, extra):
    has_left = (place[1] > 0).astype(f32)
    has_right = (place[1] < place[3] - 1).astype(f32)
    lane = lax.broadcasted_iota(jnp.int32, (TILE, TILE), 1)
    sub = lax.broadcasted_iota(jnp.int32, (TILE, TILE), 0)
    flip = jnp.where(lane + sub == TILE - 1, 1.0, 0.0).astype(bf16)
    per_group = FEAT_CH // GROUPS
    channel = lax.broadcasted_iota(jnp.int32, (32, FEAT_CH), 1)
    group_masks = [
        (channel >= g * per_group) & (channel < (g + 1) * per_group) for g in range(GROUPS)
    ]
    lane96 = lax.broadcasted_iota(jnp.int32, (FEAT_CH, TILE), 1)
    zero_slab = jnp.zeros((GROUPS, TILE), f32)
    for at in (0, (DISPS + 1) * GROUPS):
        wide[pl.ds(at, GROUPS), :] = zero_slab
        extra[pl.ds(at, GROUPS), :] = zero_slab

    own_t = (lefts[1] * row_ok).T
    side_t = jnp.where(
        lane96 < EDGE,
        lefts[2] * (has_right * row_ok),
        jnp.where(lane96 >= TILE - EDGE, lefts[0] * (has_left * row_ok), 0.0),
    ).T
    sources = jnp.concatenate([rights[2] * has_right, rights[1], rights[0] * has_left], axis=0)
    flipped = dot(sources.astype(bf16), flip)
    reverse = jnp.concatenate(
        [flipped[i * FEAT_CH : (i + 1) * FEAT_CH] for i in range(3)], axis=1
    )
    windows = [
        reverse[:, 2 * TILE - 32 - 32 * k : 3 * TILE - 32 - 32 * k].astype(bf16)
        for k in range(-1, 5)
    ]

    def by_group(rows):
        count = rows.shape[0]
        parts = [jnp.where(m[:count], rows, 0.0) for m in group_masks]
        return jnp.concatenate(parts, axis=0).astype(bf16)

    def shear(product, g, count, first):
        rows = product[count * g : count * g + count]
        return pltpu.roll(rows, TILE - 31 + first, 1, stride=1, stride_axis=0)

    products = [
        dot(by_group(own_t[32 * k : 32 * k + 32]), windows[k + 1]) for k in range(TILE // 32)
    ]
    after = dot(by_group(side_t[:EDGE]), windows[5])
    before = dot(by_group(side_t[TILE - EDGE :]), windows[0])
    parts, sides = [], []
    for g in range(GROUPS):
        part = jnp.concatenate([shear(product, g, 32, 0) for product in products], axis=0)
        parts.append(part.T[:DISPS])
        sides += [shear(after, g, EDGE, 0), shear(before, g, EDGE, 32 - EDGE)]
    part = jnp.concatenate(sides, axis=0).T[:DISPS]
    sides = [part if g == 0 else pltpu.roll(part, TILE - 2 * EDGE * g, 1) for g in range(GROUPS)]
    for target, values in ((wide, parts), (extra, sides)):
        target[GROUPS : GROUPS + DISPS * GROUPS, :] = interleaved(values) * (1.0 / per_group)


def own_row_kernel(
    place, own, across, limit, indices, vol_kernel, raw_out, taps_out, marks_out, wide, extra,
    kernel, sem,
):
    copy = pltpu.make_async_copy(vol_kernel, kernel, sem.at[0])
    copy.start()
    tiles = [across[0], own[...], across[across.shape[0] - 1]]
    tiles = [tile.astype(f32) for tile in tiles]
    correlate(
        [tile[:FEAT_CH] for tile in tiles], [tile[FEAT_CH:] for tile in tiles],
        place, 1.0, wide, extra,
    )
    raw_out[...] = jnp.concatenate([wide[...], extra[...]], axis=1).astype(bf16)
    marks = [limit[...]] + [indices[t] for t in range(ITERS)]
    blank = jnp.zeros((GROUPS - len(marks), TILE), jnp.int32)
    marks_out[...] = jnp.concatenate(marks + [blank], axis=0)
    copy.wait()
    taps_out[...] = toeplitz(kernel)


def volume_kernel(
    place, gain, odd_own, odd_across, even_own, even_across, marks, marks_across, hidden,
    hidden_across, raw_own, taps_own, out_0, out_1, out_2, out_3, raw, taps, wide, extra, logit, padded, blocks, sems,
):
    band, bands = place[0], place[2]
    is_even = band % 2 == 0
    copies = [
        pltpu.make_async_copy(raw_own, raw, sems.at[0]),
        pltpu.make_async_copy(taps_own, taps, sems.at[1]),
    ]
    for copy in copies:
        copy.start()

    last = odd_across.shape[0] - 1
    odd = [tile.astype(f32) for tile in (odd_across[0], odd_own[...], odd_across[last])]
    even = [tile.astype(f32) for tile in (even_across[0], even_own[...], even_across[last])]
    for b in range(2):
        row = band + 2 * b - 1
        row_ok = ((row >= 0) & (row < bands)).astype(f32)
        tiles = [
            jnp.where(is_even, y, x) if b == 0 else jnp.where(is_even, x, y)
            for x, y in zip(odd, even)
        ]
        correlate(
            [tile[:FEAT_CH] for tile in tiles], [tile[FEAT_CH:] for tile in tiles],
            place, row_ok, wide.at[b], extra.at[b],
        )
    for copy in copies:
        copy.wait()

    lane = lax.broadcasted_iota(jnp.int32, (GROUPS, TILE), 1)
    left_marks = pltpu.roll(marks_across[0], 2 * EDGE, 1)
    levels_of = [marks[...], jnp.where(lane < EDGE, marks_across[last], left_marks)]
    lane8 = lax.broadcasted_iota(jnp.int32, (OUT_SLAB, TILE), 1)
    group_at = lax.broadcasted_iota(jnp.int32, (GROUPS, TILE), 0)
    gains = jnp.zeros((GROUPS, TILE), f32)
    for g in range(GROUPS):
        gains = jnp.where(group_at == g, gain[g], gains)
    wanted = [
        [jnp.broadcast_to(rows[t + 1 : t + 2], (GROUPS, TILE)) for t in range(ITERS)]
        for rows in levels_of
    ]
    found = [[jnp.zeros((GROUPS, TILE), f32) for _ in range(ITERS)] for _ in range(2)]
    for q in range(DISPS // BLOCK):
        at = q * OUT_SLAB
        slabs = [
            jnp.concatenate(
                [wide[b, at : at + SLAB, :], extra[b, at : at + SLAB, :]], axis=1
            ).astype(bf16)
            for b in range(2)
        ]
        slabs.insert(1, raw[at : at + SLAB, :])
        product = dot(taps[...], jnp.concatenate(slabs, axis=0))
        halves = [product[:, :TILE], product[:, TILE:]]
        first = [half[:OUT_SLAB] for half in halves]
        middle = [half[OUT_SLAB : 2 * OUT_SLAB] for half in halves]
        after = [half[2 * OUT_SLAB :] for half in halves]
        first_on = pltpu.roll(first[0], 1, 1)
        convs = [
            middle[0]
            + jnp.where(lane8 == 0, pltpu.roll(first[1], TILE - 2 * EDGE + 1, 1), first_on)
            + jnp.where(
                lane8 == TILE - 1,
                pltpu.roll(after[1], TILE - 1, 1),
                pltpu.roll(after[0], TILE - 1, 1),
            ),
            middle[1]
            + jnp.where(lane8 == 0, first_on, pltpu.roll(first[1], 1, 1))
            + jnp.where(
                lane8 == 2 * EDGE - 1,
                pltpu.roll(after[0], 2 * EDGE - 1, 1),
                pltpu.roll(after[1], TILE - 1, 1),
            ),
        ]
        centre = slabs[1].astype(f32)[GROUPS : GROUPS + OUT_SLAB]
        for i in range(2):
            volume = centre[:, i * TILE : (i + 1) * TILE] + jnp.maximum(convs[i], 0.0)
            volume = volume.astype(bf16).astype(f32).reshape(BLOCK, GROUPS, TILE)
            logit[i, q * BLOCK : (q + 1) * BLOCK, :] = jnp.sum(volume * gains[None], axis=1)
            for d in range(BLOCK):
                for t in range(ITERS):
                    hit = wanted[i][t] == q * BLOCK + d
                    found[i][t] = found[i][t] + jnp.where(hit, volume[d], 0.0)

    level = lax.broadcasted_iota(jnp.int32, (DISPS, TILE), 0)
    for i in range(2):
        valid = level < levels_of[i][0:1]
        masked = jnp.where(valid, logit[i], floor_logit)
        top = jnp.max(masked, axis=0, keepdims=True)
        weights = jnp.where(valid, jnp.exp(masked - top), 0.0)
        moment = jnp.sum(weights * level.astype(f32), axis=0, keepdims=True)
        start = moment / jnp.sum(weights, axis=0, keepdims=True) / pixel_unit
        high = start.astype(bf16).astype(f32)
        low = (start - high).astype(bf16).astype(f32)
        ends = jnp.where(
            group_at == 0,
            jnp.broadcast_to(high, (GROUPS, TILE)),
            jnp.where(group_at == 1, jnp.broadcast_to(low, (GROUPS, TILE)), 0.0),
        )
        found[i].append(ends)
    has_left, has_right = place[1] > 0, place[1] < place[3] - 1
    is_beside = ((lane < EDGE) & has_right) | ((lane >= EDGE) & (lane < 2 * EDGE) & has_left)
    packed, packed_beside = found[0], [jnp.where(is_beside, x, 0.0) for x in found[1]]

    before = hidden_across[0, TILE - 2 * EDGE :, :].astype(f32)[EDGE:]
    after = hidden_across[last, : 2 * EDGE, :].astype(f32)[:EDGE]
    padded[:EDGE, :] = jnp.where(has_left, before, 0.0)
    padded[EDGE : EDGE + TILE, :] = hidden[...].astype(f32)
    padded[EDGE + TILE :, :] = jnp.where(has_right, after, 0.0)
    for strip in range(QUAD):
        block = [padded[STRIP * strip : STRIP * strip + WINDOW, :]]
        for half in range(2):
            part = jnp.zeros((GROUPS, TILE), f32)
            for i in range(2):
                q, base = 2 * half + i, PITCH * i
                at = lane - base
                moved = pltpu.roll(packed[q], (base + EDGE - STRIP * strip) % TILE, 1)
                if strip == 0:
                    other = pltpu.roll(packed_beside[q], (base - EDGE) % TILE, 1)
                    moved = jnp.where(at < EDGE, other, moved)
                if strip == QUAD - 1:
                    other = pltpu.roll(packed_beside[q], base + WINDOW - EDGE, 1)
                    moved = jnp.where(at >= WINDOW - EDGE, other, moved)
                part = jnp.where((at >= 0) & (at < WINDOW), moved, part)
            block.append(part)
        blocks[strip] = jnp.concatenate(block, axis=0).astype(bf16)
    member = band % QUAD
    for i, out in zip(ORDER, (out_0, out_1, out_2, out_3)):
        out[...] = blocks[strip_at(place, member ^ i)]


def slot_of(member_xor):
    return jnp.where(member_xor == 0, 0, jnp.where(member_xor == 3, 1, member_xor + 1))


def strip_at(place, member):
    return jnp.where(place[1] % 2 == 0, member, QUAD - 1 - member)


def keep(line, target, at, values):
    length = values.shape[0]
    start = EDGE + at
    line[start : start + length, :] = values
    target[at : at + length, 0:HID_CH] = line[start - 1 : start - 1 + length, :].astype(bf16)
    target[at : at + length, HID_CH : 2 * HID_CH] = values.astype(bf16)
    target[at : at + length, 2 * HID_CH :] = line[start + 1 : start + 1 + length, :].astype(bf16)


def around(target, at, length):
    return [target[at + a * WINDOW : at + a * WINDOW + length, :] for a in (-1, 0, 1)]


def refine_kernel(
    place,
    own,
    far_c,
    far_d,
    near_a,
    near_b,
    hid_weight,
    in_weight,
    head,
    out_0,
    out_1,
    out_2,
    out_3,
    line,
    weight,
    looked,
    hidden_at,
    taps,
    reset_taps,
    inputs,
    gate,
    level,
    blocks,
    sems,
):
    rows, strip = AROUND, STRIP
    copies = [
        pltpu.make_async_copy(hid_weight, weight.at[pl.ds(0, 9 * HID_CH)], sems.at[0])
    ]
    copies.append(
        pltpu.make_async_copy(
            in_weight, weight.at[pl.ds(9 * HID_CH, 3 * HID_CH)], sems.at[1]
        )
    )
    for copy in copies:
        copy.start()

    band, disp, bands, disps = place[0], place[1], place[2], place[3]
    member, layer = band % QUAD, band // QUAD
    at = strip_at(place, member)
    first = strip * at - EDGE
    first_row = layer * QUAD - REACH

    def block_of(r):
        step, row = (r + 2 * QUAD - REACH) // QUAD - 2, (r + 2 * QUAD - REACH) % QUAD
        slot = slot_of(row ^ member)
        if step == 0:
            return own[slot].astype(f32)
        if abs(step) == 1:
            choice, x, y = (layer % 2 == 0) == (step > 0), near_a, near_b
        else:
            choice, x, y = (layer % 4 < 2) == (step > 0), far_c, far_d
        inside = (first_row + r >= 0) & (first_row + r < bands)
        block = jnp.where(choice, x[slot].astype(f32), y[slot].astype(f32))
        return jnp.where(inside, block, 0.0)

    lane = lax.broadcasted_iota(jnp.int32, (GROUPS, TILE), 1)
    at_sub = lax.broadcasted_iota(jnp.int32, (WINDOW, TILE), 0)
    at_lane = lax.broadcasted_iota(jnp.int32, (WINDOW, TILE), 1)
    spread = jnp.where(at_sub == at_lane % PITCH, 1.0, 0.0).astype(bf16)
    fill = jnp.zeros((PACK, TILE), f32)
    zeros = jnp.zeros((GROUPS, TILE), f32)
    lines = []
    for r in range(rows):
        block = block_of(r)
        packed = block[WINDOW:]
        hidden_at[r * WINDOW : (r + 1) * WINDOW, :] = block[:WINDOW]
        pieces = []
        for b in range(3):
            moved = packed if b == 1 else pltpu.roll(packed, (1 - b) % TILE, 1)
            for q in range(4):
                part = moved[GROUPS * (q // 2) : GROUPS * (q // 2 + 1)]
                pieces.append(jnp.where((lane >= PITCH) == (q % 2 == 1), part, zeros))
        lines.append(jnp.concatenate(pieces + [fill], axis=0).astype(bf16))
    for r in range(0, rows, 2):
        both = dot_nt(spread, jnp.concatenate(lines[r : r + 2], axis=0))
        for i in range(2):
            at = (r + i) * WINDOW
            looked[at : at + WINDOW, :] = both[:, i * HID_CH : (i + 1) * HID_CH]
    sub = lax.broadcasted_iota(jnp.int32, (HID_CH, HID_CH), 0)
    ends = jnp.where((sub == PACK + 24) | (sub == PACK + 25), feature_scale, 0.0).astype(bf16)
    blank = jnp.zeros((EDGE, HID_CH), f32)
    level[:EDGE, :] = blank
    level[EDGE + WINDOW * rows :, :] = blank
    level[EDGE : EDGE + WINDOW * rows, :] = dot(looked[...].astype(bf16), ends)
    line[...] = jnp.zeros_like(line)
    keep(line, taps, 0, hidden_at[...])
    for copy in copies:
        copy.wait()
    heads = jnp.broadcast_to(head[...].astype(f32) * feature_scale, (HID_CH, HID_CH)).astype(bf16)

    for t in range(ITERS):
        low, high = 1 + 2 * t, rows - 2 - 2 * t
        at, length = (low - 1) * WINDOW, (high - low + 3) * WINDOW
        lane_at = lax.broadcasted_iota(jnp.int32, (length, HID_CH), 1)
        tap, channel = lane_at // PACK, lane_at % PACK
        near = [level[EDGE + at + b : EDGE + at + b + length, :] for b in (-1, 0, 1)]
        value = jnp.where(tap == 0, near[0], jnp.where(tap == 1, near[1], near[2]))
        at_lookup = (channel >= t * GROUPS) & (channel < (t + 1) * GROUPS)
        value = jnp.where(
            (channel == 3 * GROUPS) & (tap < 3),
            value,
            jnp.where(at_lookup, looked[at : at + length, :], 0.0),
        )
        inputs[at : at + length, :] = value.astype(bf16)

        at, length = low * WINDOW, (high - low + 1) * WINDOW
        lhs = around(taps, at, length) + around(inputs, at, length)
        both = dot(jnp.concatenate(lhs, axis=1), weight[:, : 2 * HID_CH])
        gate[at + WINDOW : at + length - WINDOW, :] = (
            0.5 * jnp.tanh(0.5 * both[WINDOW : length - WINDOW, :HID_CH]) + 0.5
        )
        reset = 0.5 * jnp.tanh(0.5 * both[:, HID_CH:]) + 0.5
        keep(line, reset_taps, at, reset * hidden_at[at : at + length, :])

        at, length = at + WINDOW, length - 2 * WINDOW
        lhs = around(reset_taps, at, length) + around(inputs, at, length)
        candidate = jnp.tanh(dot(jnp.concatenate(lhs, axis=1), weight[:, 2 * HID_CH :]))
        hidden = hidden_at[at : at + length, :]
        hidden = hidden + gate[at : at + length, :] * (candidate - hidden)
        pixel = lax.broadcasted_iota(jnp.int32, (length, HID_CH), 0)
        column, row = pixel % WINDOW + first, pixel // WINDOW + (low + 1 + first_row)
        inside = ((column >= 0) | (disp > 0)) & ((column < TILE) | (disp < disps - 1))
        inside = inside & (row >= 0) & (row < bands)
        hidden = jnp.where(inside, hidden, 0.0).astype(bf16)
        level[EDGE + at : EDGE + at + length, :] += dot_nt(hidden, heads)
        hidden_at[at : at + length, :] = hidden.astype(f32)
        if t < ITERS - 1:
            keep(line, taps, at, hidden.astype(f32))

    lane = lax.broadcasted_iota(jnp.int32, (strip, HID_CH), 1)
    for r in range(QUAD):
        at = (REACH + r) * WINDOW + EDGE
        hidden = hidden_at[at : at + strip, :]
        value = level[EDGE + at : EDGE + at + strip, :] * (1.0 / feature_scale)
        high = value.astype(bf16).astype(f32)
        middle = (value - high).astype(bf16).astype(f32)
        parts = jnp.where(lane == 0, high, jnp.where(lane == 1, middle, value - high - middle))
        parts = jnp.where(lane < 3, parts, 0.0)
        blocks[r] = jnp.concatenate([hidden, parts], axis=0).astype(bf16)
    for i, out in zip(ORDER, (out_0, out_1, out_2, out_3)):
        out[...] = blocks[member ^ i]


def unpack_kernel(place, from_0, from_1, from_2, from_3, disparity_out, hidden_out, blocks):
    for i, block in enumerate((from_0, from_1, from_2, from_3)):
        blocks[i] = block[...]
    member = place[0] % QUAD
    slots = [slot_of(strip_at(place, strip) ^ member) for strip in range(QUAD)]
    held = [blocks[slot].astype(f32) for slot in slots]
    hidden_out[0] = jnp.concatenate([block[:STRIP] for block in held], axis=0).astype(bf16)
    parts = jnp.concatenate([block[STRIP:] for block in held], axis=0).T
    disparity_out[...] = parts[0:1] + parts[1:2] + parts[2:3]


def in_hbm(value):
    return pltpu.with_memory_space_constraint(value, pltpu.HBM)


def to_sides(value):
    disps = lax.axis_size("disp")
    right = [(d, d + 1) for d in range(disps - 1)]
    left = [(d + 1, d) for d in range(disps - 1)]
    if disps == 2:
        return lax.ppermute(value, "disp", right + left)[None]
    return jnp.stack([lax.ppermute(value, "disp", right), lax.ppermute(value, "disp", left)])


def in_group(blocks):
    return [blocks[0]] + [
        to_rows(block, lambda band, i=i: band ^ i)
        for i, block in list(zip(ORDER, blocks))[1:]
    ]


def to_layers(value, partner):
    groups = lax.axis_size("band") // QUAD
    if not any(0 <= partner(g) < groups for g in range(groups)):
        return None
    return to_rows(value, lambda band: partner(band // QUAD) * QUAD + band % QUAD)


def to_rows(value, shift):
    bands = lax.axis_size("band")
    return lax.ppermute(
        value, "band", [(i, shift(i)) for i in range(bands) if 0 <= shift(i) < bands]
    )


def odd_pair(i):
    return i ^ 1


def even_pair(i):
    return i - 1 if i % 2 == 0 else i + 1


def local(
    feat_left,
    feat_right,
    limit,
    indices,
    hidden_start,
    vol_kernel,
    group_gain,
    hid_kernel,
    in_kernel,
    head_weight,
):
    bands, disps = lax.axis_size("band"), lax.axis_size("disp")
    place = jnp.stack(
        [lax.axis_index("band"), lax.axis_index("disp"), jnp.int32(bands), jnp.int32(disps)]
    ).astype(jnp.int32)
    smem = pl.BlockSpec(memory_space=pltpu.SMEM)
    vmem = pl.BlockSpec(memory_space=pltpu.VMEM)
    hbm = pl.BlockSpec(memory_space=pltpu.HBM)
    anywhere = pl.BlockSpec(memory_space=pl.ANY)
    padded = (DISPS + 2) * GROUPS

    feats = jnp.concatenate([feat_left[0], feat_right[0]], axis=0)
    odd_own, even_own = to_rows(feats, odd_pair), to_rows(feats, even_pair)
    across = to_sides(feats)
    raw_own, taps, marks = pl.pallas_call(
        own_row_kernel,
        out_shape=(
            jax.ShapeDtypeStruct((padded, 2 * TILE), bf16),
            jax.ShapeDtypeStruct((3 * OUT_SLAB, 3 * SLAB), bf16),
            jax.ShapeDtypeStruct((GROUPS, TILE), jnp.int32),
        ),
        in_specs=[smem, vmem, vmem, vmem, vmem, hbm],
        out_specs=(vmem, vmem, vmem),
        scratch_shapes=[
            pltpu.VMEM((padded, TILE), f32),
            pltpu.VMEM((padded, TILE), f32),
            pltpu.VMEM((27, GROUPS, GROUPS), bf16),
            pltpu.SemaphoreType.DMA((1,)),
        ],
        compiler_params=pltpu.CompilerParams(vmem_limit_bytes=16 * 2**20),
        cost_estimate=pl.CostEstimate(flops=2 * 10**9, bytes_accessed=4 * 2**20, transcendentals=0),
    )(
        place, feats, across, in_hbm(limit), in_hbm(indices),
        in_hbm(vol_kernel.reshape(27, GROUPS, GROUPS)),
    )
    hidden = hidden_start[0]
    hidden_across = to_sides(hidden)
    odd_own, even_own, raw_own, taps, hidden_across = lax.optimization_barrier(
        (odd_own, even_own, raw_own, taps, hidden_across)
    )
    marks_across = to_sides(marks)
    odd_across, even_across = to_sides(odd_own), to_sides(even_own)

    in_weight = jnp.concatenate(
        [in_kernel[:, :, :GROUPS]] * ITERS + [in_kernel[:, :, GROUPS:]], axis=2
    )
    in_weight = jnp.pad(in_weight, ((0, 0), (0, 1), (0, PACK - in_weight.shape[2]), (0, 0)))
    in_weight = in_weight.reshape(3 * HID_CH, 3 * HID_CH)

    blocks = pl.pallas_call(
        volume_kernel,
        out_shape=(jax.ShapeDtypeStruct((BLOCK_ROWS, TILE), bf16),) * QUAD,
        in_specs=[smem, smem] + [vmem] * 8 + [hbm, hbm],
        out_specs=(vmem,) * QUAD,
        scratch_shapes=[
            pltpu.VMEM((padded, 2 * TILE), bf16),
            pltpu.VMEM((3 * OUT_SLAB, 3 * SLAB), bf16),
            pltpu.VMEM((2, padded, TILE), f32),
            pltpu.VMEM((2, padded, TILE), f32),
            pltpu.VMEM((2, DISPS, TILE), f32),
            pltpu.VMEM((TILE + 2 * EDGE, HID_CH), f32),
            pltpu.VMEM((QUAD, BLOCK_ROWS, TILE), bf16),
            pltpu.SemaphoreType.DMA((2,)),
        ],
        compiler_params=pltpu.CompilerParams(vmem_limit_bytes=24 * 2**20),
        cost_estimate=pl.CostEstimate(
            flops=5 * 10**9, bytes_accessed=16 * 2**20, transcendentals=DISPS * TILE
        ),
    )(
        place, in_hbm(group_gain), odd_own, odd_across, even_own, even_across,
        marks, marks_across, in_hbm(hidden), hidden_across, raw_own, taps,
    )

    own, in_weight = lax.optimization_barrier((jnp.stack(in_group(blocks)), in_weight))
    around = [
        to_layers(own, lambda g: g ^ 2),
        to_layers(own, lambda g: (g - 2 ^ 2) + 2),
        to_layers(own, lambda g: g ^ 1),
        to_layers(own, lambda g: (g - 1 ^ 1) + 1),
    ]
    if around[1] is None:
        around[1] = around[0]

    pixels = WINDOW * AROUND
    refined = pl.pallas_call(
        refine_kernel,
        out_shape=(jax.ShapeDtypeStruct((2 * STRIP, HID_CH), bf16),) * QUAD,
        in_specs=[smem] + [vmem] * 5 + [anywhere, anywhere, vmem],
        out_specs=(vmem,) * QUAD,
        scratch_shapes=[
            pltpu.VMEM((pixels + 2 * EDGE, HID_CH), f32),
            pltpu.VMEM((12 * HID_CH, 3 * HID_CH), bf16),
            pltpu.VMEM((pixels, HID_CH), f32),
            pltpu.VMEM((pixels, HID_CH), f32),
            pltpu.VMEM((pixels, 3 * HID_CH), bf16),
            pltpu.VMEM((pixels, 3 * HID_CH), bf16),
            pltpu.VMEM((pixels, HID_CH), bf16),
            pltpu.VMEM((pixels, HID_CH), f32),
            pltpu.VMEM((pixels + 2 * EDGE, HID_CH), f32),
            pltpu.VMEM((QUAD, 2 * STRIP, HID_CH), bf16),
            pltpu.SemaphoreType.DMA((2,)),
        ],
        compiler_params=pltpu.CompilerParams(vmem_limit_bytes=32 * 2**20),
    )(
        place, own, *around,
        hid_kernel.reshape(9 * HID_CH, 3 * HID_CH), in_weight,
        in_hbm(head_weight.reshape(1, HID_CH)),
    )
    disparity, hidden = pl.pallas_call(
        unpack_kernel,
        out_shape=(
            jax.ShapeDtypeStruct((1, TILE), f32),
            jax.ShapeDtypeStruct((1, TILE, HID_CH), bf16),
        ),
        in_specs=[smem] + [vmem] * QUAD,
        out_specs=(vmem, vmem),
        scratch_shapes=[pltpu.VMEM((QUAD, 2 * STRIP, HID_CH), bf16)],
        compiler_params=pltpu.CompilerParams(vmem_limit_bytes=4 * 2**20),
    )(place, *in_group(refined))
    return (disparity, hidden)


def solution(mesh):
    in_specs = (
        P("band", None, "disp"),
        P("band", None, "disp"),
        P("band", "disp"),
        P(None, "band", "disp"),
        P("band", "disp", None),
        P(),
        P(),
        P(),
        P(),
        P(),
    )
    out_specs = (P("band", "disp"), P("band", "disp", None))
    return jax.shard_map(local, mesh=mesh, in_specs=in_specs, out_specs=out_specs, check_vma=False)
```

```python
import jax
import jax.numpy as jnp
from jax import lax
from jax.experimental import pallas as pl
from jax.experimental.pallas import tpu as pltpu
from jax.sharding import PartitionSpec as P

GROUPS = 8
DISPS = 96
FEAT_CH = 96
HID_CH = 128
ITERS = 3
TILE = 128
REACH = 2 * ITERS
EDGE = 8
QUAD = 4
STRIP = TILE // QUAD
WINDOW = STRIP + 2 * EDGE
PACK = 32
PITCH = 64
ORDER = (0, 3, 1, 2)
BLOCK_ROWS = WINDOW + 2 * GROUPS
AROUND = QUAD + 2 * REACH
BLOCK = 8
SLAB = (BLOCK + 2) * GROUPS
OUT_SLAB = BLOCK * GROUPS

pixel_unit = 8.0
feature_scale = 0.25
floor_logit = -1e30

f32 = jnp.float32
bf16 = jnp.bfloat16


def position():
    return (
        lax.axis_index("band"), lax.axis_index("disp"),
        lax.axis_size("band"), lax.axis_size("disp"),
    )


def dot(a, b):
    return jnp.dot(a, b, preferred_element_type=f32)


def dot_nt(a, b):
    return lax.dot_general(a, b, (((1,), (1,)), ((), ())), preferred_element_type=f32)


def copy_all(copies):
    for copy in copies:
        copy.start()
    for copy in copies:
        copy.wait()


def toeplitz(vol_kernel):
    size = 27 * GROUPS
    flat = vol_kernel[...].astype(f32).reshape(size, GROUPS)
    flat = jnp.concatenate([flat, jnp.zeros((size, TILE - GROUPS), f32)], axis=1).T[:GROUPS]
    row = lax.broadcasted_iota(jnp.int32, (9 * GROUPS, size), 0) >> 3
    tap = lax.broadcasted_iota(jnp.int32, (9 * GROUPS, size), 1) >> 3
    tap_a = (tap >= 9).astype(jnp.int32) + (tap >= 18).astype(jnp.int32)
    within = tap - 9 * tap_a
    tap_b = (within >= 3).astype(jnp.int32) + (within >= 6).astype(jnp.int32)
    tap_e = within - 3 * tap_b
    pairs = jnp.where(
        row == 3 * tap_a + tap_e, jnp.concatenate([flat] * 9, axis=0), 0.0
    ).astype(bf16)
    from_row = lax.broadcasted_iota(jnp.int32, (size, 3 * SLAB), 0)
    to = lax.broadcasted_iota(jnp.int32, (size, 3 * SLAB), 1)
    from_tap = from_row >> 3
    from_in = from_tap - 9 * ((from_tap >= 9).astype(jnp.int32) + (from_tap >= 18).astype(jnp.int32))
    from_b = (from_in >= 3).astype(jnp.int32) + (from_in >= 6).astype(jnp.int32)
    to_b = (to >= SLAB).astype(jnp.int32) + (to >= 2 * SLAB).astype(jnp.int32)
    repeat = jnp.where((from_b == to_b) & ((from_row & 7) == (to & 7)), 1.0, 0.0).astype(bf16)
    spread = dot(pairs, repeat)
    to = lax.broadcasted_iota(jnp.int32, (GROUPS, 3 * SLAB), 1)
    to_b = (to >= SLAB).astype(jnp.int32) + (to >= 2 * SLAB).astype(jnp.int32)
    to_d = (to - SLAB * to_b) >> 3
    rows = []
    for e in range(3):
        for d in range(BLOCK):
            value = jnp.zeros((GROUPS, 3 * SLAB), f32)
            for a in range(3):
                at = (3 * a + e) * GROUPS
                value = jnp.where(to_d == d + a, spread[at : at + GROUPS], value)
            rows.append(value)
    return jnp.concatenate(rows, axis=0).astype(bf16)


def interleaved(values):
    stacked = jnp.swapaxes(jnp.stack(values), 0, 1)
    return stacked.reshape(values[0].shape[0] * len(values), values[0].shape[1])


def correlate(lefts, rights, place, row_ok, wide, extra):
    has_left = (place[1] > 0).astype(f32)
    has_right = (place[1] < place[3] - 1).astype(f32)
    lane = lax.broadcasted_iota(jnp.int32, (TILE, TILE), 1)
    sub = lax.broadcasted_iota(jnp.int32, (TILE, TILE), 0)
    flip = jnp.where(lane + sub == TILE - 1, 1.0, 0.0).astype(bf16)
    per_group = FEAT_CH // GROUPS
    channel = lax.broadcasted_iota(jnp.int32, (32, FEAT_CH), 1)
    group_masks = [
        (channel >= g * per_group) & (channel < (g + 1) * per_group) for g in range(GROUPS)
    ]
    lane96 = lax.broadcasted_iota(jnp.int32, (FEAT_CH, TILE), 1)
    zero_slab = jnp.zeros((GROUPS, TILE), f32)
    for at in (0, (DISPS + 1) * GROUPS):
        wide[pl.ds(at, GROUPS), :] = zero_slab
        extra[pl.ds(at, GROUPS), :] = zero_slab

    own_t = (lefts[1] * row_ok).T
    side_t = jnp.where(
        lane96 < EDGE,
        lefts[2] * (has_right * row_ok),
        jnp.where(lane96 >= TILE - EDGE, lefts[0] * (has_left * row_ok), 0.0),
    ).T
    sources = jnp.concatenate([rights[2] * has_right, rights[1], rights[0] * has_left], axis=0)
    flipped = dot(sources.astype(bf16), flip)
    reverse = jnp.concatenate(
        [flipped[i * FEAT_CH : (i + 1) * FEAT_CH] for i in range(3)], axis=1
    )
    windows = [
        reverse[:, 2 * TILE - 32 - 32 * k : 3 * TILE - 32 - 32 * k].astype(bf16)
        for k in range(-1, 5)
    ]

    def by_group(rows):
        count = rows.shape[0]
        parts = [jnp.where(m[:count], rows, 0.0) for m in group_masks]
        return jnp.concatenate(parts, axis=0).astype(bf16)

    def shear(product, g, count, first):
        rows = product[count * g : count * g + count]
        return pltpu.roll(rows, TILE - 31 + first, 1, stride=1, stride_axis=0)

    products = [
        dot(by_group(own_t[32 * k : 32 * k + 32]), windows[k + 1]) for k in range(TILE // 32)
    ]
    after = dot(by_group(side_t[:EDGE]), windows[5])
    before = dot(by_group(side_t[TILE - EDGE :]), windows[0])
    parts, sides = [], []
    for g in range(GROUPS):
        part = jnp.concatenate([shear(product, g, 32, 0) for product in products], axis=0)
        parts.append(part.T[:DISPS])
        sides += [shear(after, g, EDGE, 0), shear(before, g, EDGE, 32 - EDGE)]
    part = jnp.concatenate(sides, axis=0).T[:DISPS]
    sides = [part if g == 0 else pltpu.roll(part, TILE - 2 * EDGE * g, 1) for g in range(GROUPS)]
    for target, values in ((wide, parts), (extra, sides)):
        target[GROUPS : GROUPS + DISPS * GROUPS, :] = interleaved(values) * (1.0 / per_group)


def own_row_kernel(
    own, across, limit, indices, gain, head, vol_kernel, raw_out, taps_out, marks_out, gains_out,
    heads_out, wide, extra, limits, index_rows, gain_held, head_held, kernel, sems,
):
    place = position()
    copies = [
        pltpu.make_async_copy(source, target, sems.at[i])
        for i, (source, target) in enumerate(
            (
                (limit, limits), (indices, index_rows), (gain, gain_held), (head, head_held),
                (vol_kernel, kernel),
            )
        )
    ]
    for copy in copies:
        copy.start()
    tiles = [across[0], own[...], across[across.shape[0] - 1]]
    tiles = [tile.astype(f32) for tile in tiles]
    correlate(
        [tile[:FEAT_CH] for tile in tiles], [tile[FEAT_CH:] for tile in tiles],
        place, 1.0, wide, extra,
    )
    raw_out[...] = jnp.concatenate([wide[...], extra[...]], axis=1).astype(bf16)
    for copy in copies:
        copy.wait()
    marks = [limits[...]] + [index_rows[t] for t in range(ITERS)]
    blank = jnp.zeros((GROUPS - len(marks), TILE), jnp.int32)
    marks_out[...] = jnp.concatenate(marks + [blank], axis=0)
    group_at = lax.broadcasted_iota(jnp.int32, (GROUPS, TILE), 0)
    gains = jnp.zeros((GROUPS, TILE), f32)
    for g in range(GROUPS):
        gains = jnp.where(group_at == g, gain_held[g], gains)
    gains_out[...] = gains
    heads = head_held[...].astype(f32) * feature_scale
    heads_out[...] = jnp.broadcast_to(heads, heads_out.shape).astype(bf16)
    taps_out[...] = toeplitz(kernel)


def volume_kernel(
    gains, odd_own, odd_across, even_own, even_across, marks, marks_across, hidden,
    hidden_across, raw_own, taps_own, out_0, out_1, out_2, out_3, raw, taps, wide, extra, logit, padded, blocks, sems,
):
    place = position()
    band, bands = place[0], place[2]
    is_even = band % 2 == 0
    copies = [
        pltpu.make_async_copy(raw_own, raw, sems.at[0]),
        pltpu.make_async_copy(taps_own, taps, sems.at[1]),
    ]
    for copy in copies:
        copy.start()

    last = odd_across.shape[0] - 1
    odd = [tile.astype(f32) for tile in (odd_across[0], odd_own[...], odd_across[last])]
    even = [tile.astype(f32) for tile in (even_across[0], even_own[...], even_across[last])]
    for b in range(2):
        row = band + 2 * b - 1
        row_ok = ((row >= 0) & (row < bands)).astype(f32)
        tiles = [
            jnp.where(is_even, y, x) if b == 0 else jnp.where(is_even, x, y)
            for x, y in zip(odd, even)
        ]
        correlate(
            [tile[:FEAT_CH] for tile in tiles], [tile[FEAT_CH:] for tile in tiles],
            place, row_ok, wide.at[b], extra.at[b],
        )
    for copy in copies:
        copy.wait()

    lane = lax.broadcasted_iota(jnp.int32, (GROUPS, TILE), 1)
    left_marks = pltpu.roll(marks_across[0], 2 * EDGE, 1)
    levels_of = [marks[...], jnp.where(lane < EDGE, marks_across[last], left_marks)]
    lane8 = lax.broadcasted_iota(jnp.int32, (OUT_SLAB, TILE), 1)
    group_at = lax.broadcasted_iota(jnp.int32, (GROUPS, TILE), 0)
    wanted = [
        [jnp.broadcast_to(rows[t + 1 : t + 2], (GROUPS, TILE)) for t in range(ITERS)]
        for rows in levels_of
    ]
    found = [[jnp.zeros((GROUPS, TILE), f32) for _ in range(ITERS)] for _ in range(2)]
    for q in range(DISPS // BLOCK):
        at = q * OUT_SLAB
        slabs = [
            jnp.concatenate(
                [wide[b, at : at + SLAB, :], extra[b, at : at + SLAB, :]], axis=1
            ).astype(bf16)
            for b in range(2)
        ]
        slabs.insert(1, raw[at : at + SLAB, :])
        product = dot(taps[...], jnp.concatenate(slabs, axis=0))
        halves = [product[:, :TILE], product[:, TILE:]]
        first = [half[:OUT_SLAB] for half in halves]
        middle = [half[OUT_SLAB : 2 * OUT_SLAB] for half in halves]
        after = [half[2 * OUT_SLAB :] for half in halves]
        first_on = pltpu.roll(first[0], 1, 1)
        convs = [
            middle[0]
            + jnp.where(lane8 == 0, pltpu.roll(first[1], TILE - 2 * EDGE + 1, 1), first_on)
            + jnp.where(
                lane8 == TILE - 1,
                pltpu.roll(after[1], TILE - 1, 1),
                pltpu.roll(after[0], TILE - 1, 1),
            ),
            middle[1]
            + jnp.where(lane8 == 0, first_on, pltpu.roll(first[1], 1, 1))
            + jnp.where(
                lane8 == 2 * EDGE - 1,
                pltpu.roll(after[0], 2 * EDGE - 1, 1),
                pltpu.roll(after[1], TILE - 1, 1),
            ),
        ]
        centre = slabs[1].astype(f32)[GROUPS : GROUPS + OUT_SLAB]
        for i in range(2):
            volume = centre[:, i * TILE : (i + 1) * TILE] + jnp.maximum(convs[i], 0.0)
            volume = volume.astype(bf16).astype(f32).reshape(BLOCK, GROUPS, TILE)
            logit[i, q * BLOCK : (q + 1) * BLOCK, :] = jnp.sum(volume * gains[...][None], axis=1)
            for d in range(BLOCK):
                for t in range(ITERS):
                    hit = wanted[i][t] == q * BLOCK + d
                    found[i][t] = found[i][t] + jnp.where(hit, volume[d], 0.0)

    level = lax.broadcasted_iota(jnp.int32, (DISPS, TILE), 0)
    for i in range(2):
        valid = level < levels_of[i][0:1]
        masked = jnp.where(valid, logit[i], floor_logit)
        top = jnp.max(masked, axis=0, keepdims=True)
        weights = jnp.where(valid, jnp.exp(masked - top), 0.0)
        moment = jnp.sum(weights * level.astype(f32), axis=0, keepdims=True)
        start = moment / jnp.sum(weights, axis=0, keepdims=True) / pixel_unit
        high = start.astype(bf16).astype(f32)
        low = (start - high).astype(bf16).astype(f32)
        ends = jnp.where(
            group_at == 0,
            jnp.broadcast_to(high, (GROUPS, TILE)),
            jnp.where(group_at == 1, jnp.broadcast_to(low, (GROUPS, TILE)), 0.0),
        )
        found[i].append(ends)
    has_left, has_right = place[1] > 0, place[1] < place[3] - 1
    is_beside = ((lane < EDGE) & has_right) | ((lane >= EDGE) & (lane < 2 * EDGE) & has_left)
    packed, packed_beside = found[0], [jnp.where(is_beside, x, 0.0) for x in found[1]]

    before = hidden_across[0, TILE - 2 * EDGE :, :].astype(f32)[EDGE:]
    after = hidden_across[last, : 2 * EDGE, :].astype(f32)[:EDGE]
    padded[:EDGE, :] = jnp.where(has_left, before, 0.0)
    padded[EDGE : EDGE + TILE, :] = hidden[...].astype(f32)
    padded[EDGE + TILE :, :] = jnp.where(has_right, after, 0.0)
    for strip in range(QUAD):
        block = [padded[STRIP * strip : STRIP * strip + WINDOW, :]]
        for half in range(2):
            part = jnp.zeros((GROUPS, TILE), f32)
            for i in range(2):
                q, base = 2 * half + i, PITCH * i
                at = lane - base
                moved = pltpu.roll(packed[q], (base + EDGE - STRIP * strip) % TILE, 1)
                if strip == 0:
                    other = pltpu.roll(packed_beside[q], (base - EDGE) % TILE, 1)
                    moved = jnp.where(at < EDGE, other, moved)
                if strip == QUAD - 1:
                    other = pltpu.roll(packed_beside[q], base + WINDOW - EDGE, 1)
                    moved = jnp.where(at >= WINDOW - EDGE, other, moved)
                part = jnp.where((at >= 0) & (at < WINDOW), moved, part)
            block.append(part)
        blocks[strip] = jnp.concatenate(block, axis=0).astype(bf16)
    member = band % QUAD
    for i, out in zip(ORDER, (out_0, out_1, out_2, out_3)):
        out[...] = blocks[strip_at(place, member ^ i)]


def slot_of(member_xor):
    return jnp.where(member_xor == 0, 0, jnp.where(member_xor == 3, 1, member_xor + 1))


def strip_at(place, member):
    return jnp.where(place[1] % 2 == 0, member, QUAD - 1 - member)


def keep(line, target, at, values):
    length = values.shape[0]
    start = EDGE + at
    line[start : start + length, :] = values
    target[at : at + length, 0:HID_CH] = line[start - 1 : start - 1 + length, :].astype(bf16)
    target[at : at + length, HID_CH : 2 * HID_CH] = values.astype(bf16)
    target[at : at + length, 2 * HID_CH :] = line[start + 1 : start + 1 + length, :].astype(bf16)


def around(target, at, length):
    return [target[at + a * WINDOW : at + a * WINDOW + length, :] for a in (-1, 0, 1)]


def refine_kernel(
    own,
    far_c,
    far_d,
    near_a,
    near_b,
    hid_weight,
    in_weight,
    heads,
    out_0,
    out_1,
    out_2,
    out_3,
    line,
    weight,
    looked,
    hidden_at,
    taps,
    reset_taps,
    inputs,
    gate,
    level,
    blocks,
    sems,
):
    rows, strip = AROUND, STRIP
    copies = [
        pltpu.make_async_copy(hid_weight, weight.at[pl.ds(0, 9 * HID_CH)], sems.at[0])
    ]
    copies.append(
        pltpu.make_async_copy(
            in_weight, weight.at[pl.ds(9 * HID_CH, 3 * HID_CH)], sems.at[1]
        )
    )
    for copy in copies:
        copy.start()

    place = position()
    band, disp, bands, disps = place
    member, layer = band % QUAD, band // QUAD
    at = strip_at(place, member)
    first = strip * at - EDGE
    first_row = layer * QUAD - REACH

    def block_of(r):
        step, row = (r + 2 * QUAD - REACH) // QUAD - 2, (r + 2 * QUAD - REACH) % QUAD
        slot = slot_of(row ^ member)
        if step == 0:
            return own[slot].astype(f32)
        if abs(step) == 1:
            choice, x, y = (layer % 2 == 0) == (step > 0), near_a, near_b
        else:
            choice, x, y = (layer % 4 < 2) == (step > 0), far_c, far_d
        inside = (first_row + r >= 0) & (first_row + r < bands)
        block = jnp.where(choice, x[slot].astype(f32), y[slot].astype(f32))
        return jnp.where(inside, block, 0.0)

    lane = lax.broadcasted_iota(jnp.int32, (GROUPS, TILE), 1)
    at_sub = lax.broadcasted_iota(jnp.int32, (WINDOW, TILE), 0)
    at_lane = lax.broadcasted_iota(jnp.int32, (WINDOW, TILE), 1)
    spread = jnp.where(at_sub == at_lane % PITCH, 1.0, 0.0).astype(bf16)
    fill = jnp.zeros((PACK, TILE), f32)
    zeros = jnp.zeros((GROUPS, TILE), f32)
    lines = []
    for r in range(rows):
        block = block_of(r)
        packed = block[WINDOW:]
        hidden_at[r * WINDOW : (r + 1) * WINDOW, :] = block[:WINDOW]
        pieces = []
        for b in range(3):
            moved = packed if b == 1 else pltpu.roll(packed, (1 - b) % TILE, 1)
            for q in range(4):
                part = moved[GROUPS * (q // 2) : GROUPS * (q // 2 + 1)]
                pieces.append(jnp.where((lane >= PITCH) == (q % 2 == 1), part, zeros))
        lines.append(jnp.concatenate(pieces + [fill], axis=0).astype(bf16))
    for r in range(0, rows, 2):
        both = dot_nt(spread, jnp.concatenate(lines[r : r + 2], axis=0))
        for i in range(2):
            at = (r + i) * WINDOW
            looked[at : at + WINDOW, :] = both[:, i * HID_CH : (i + 1) * HID_CH]
    sub = lax.broadcasted_iota(jnp.int32, (HID_CH, HID_CH), 0)
    ends = jnp.where((sub == PACK + 24) | (sub == PACK + 25), feature_scale, 0.0).astype(bf16)
    blank = jnp.zeros((EDGE, HID_CH), f32)
    level[:EDGE, :] = blank
    level[EDGE + WINDOW * rows :, :] = blank
    level[EDGE : EDGE + WINDOW * rows, :] = dot(looked[...].astype(bf16), ends)
    line[...] = jnp.zeros_like(line)
    keep(line, taps, 0, hidden_at[...])
    for copy in copies:
        copy.wait()

    for t in range(ITERS):
        low, high = 1 + 2 * t, rows - 2 - 2 * t
        at, length = (low - 1) * WINDOW, (high - low + 3) * WINDOW
        lane_at = lax.broadcasted_iota(jnp.int32, (length, HID_CH), 1)
        tap, channel = lane_at // PACK, lane_at % PACK
        near = [level[EDGE + at + b : EDGE + at + b + length, :] for b in (-1, 0, 1)]
        value = jnp.where(tap == 0, near[0], jnp.where(tap == 1, near[1], near[2]))
        at_lookup = (channel >= t * GROUPS) & (channel < (t + 1) * GROUPS)
        value = jnp.where(
            (channel == 3 * GROUPS) & (tap < 3),
            value,
            jnp.where(at_lookup, looked[at : at + length, :], 0.0),
        )
        inputs[at : at + length, :] = value.astype(bf16)

        at, length = low * WINDOW, (high - low + 1) * WINDOW
        lhs = around(taps, at, length) + around(inputs, at, length)
        both = dot(jnp.concatenate(lhs, axis=1), weight[:, : 2 * HID_CH])
        gate[at + WINDOW : at + length - WINDOW, :] = (
            0.5 * jnp.tanh(0.5 * both[WINDOW : length - WINDOW, :HID_CH]) + 0.5
        )
        reset = 0.5 * jnp.tanh(0.5 * both[:, HID_CH:]) + 0.5
        keep(line, reset_taps, at, reset * hidden_at[at : at + length, :])

        at, length = at + WINDOW, length - 2 * WINDOW
        lhs = around(reset_taps, at, length) + around(inputs, at, length)
        candidate = jnp.tanh(dot(jnp.concatenate(lhs, axis=1), weight[:, 2 * HID_CH :]))
        hidden = hidden_at[at : at + length, :]
        hidden = hidden + gate[at : at + length, :] * (candidate - hidden)
        pixel = lax.broadcasted_iota(jnp.int32, (length, HID_CH), 0)
        column, row = pixel % WINDOW + first, pixel // WINDOW + (low + 1 + first_row)
        inside = ((column >= 0) | (disp > 0)) & ((column < TILE) | (disp < disps - 1))
        inside = inside & (row >= 0) & (row < bands)
        hidden = jnp.where(inside, hidden, 0.0).astype(bf16)
        level[EDGE + at : EDGE + at + length, :] += dot_nt(hidden, heads[...])
        hidden_at[at : at + length, :] = hidden.astype(f32)
        if t < ITERS - 1:
            keep(line, taps, at, hidden.astype(f32))

    lane = lax.broadcasted_iota(jnp.int32, (strip, HID_CH), 1)
    for r in range(QUAD):
        at = (REACH + r) * WINDOW + EDGE
        hidden = hidden_at[at : at + strip, :]
        value = level[EDGE + at : EDGE + at + strip, :] * (1.0 / feature_scale)
        high = value.astype(bf16).astype(f32)
        middle = (value - high).astype(bf16).astype(f32)
        parts = jnp.where(lane == 0, high, jnp.where(lane == 1, middle, value - high - middle))
        parts = jnp.where(lane < 3, parts, 0.0)
        blocks[r] = jnp.concatenate([hidden, parts], axis=0).astype(bf16)
    for i, out in zip(ORDER, (out_0, out_1, out_2, out_3)):
        out[...] = blocks[member ^ i]


def unpack_kernel(from_0, from_1, from_2, from_3, disparity_out, hidden_out, blocks):
    for i, block in enumerate((from_0, from_1, from_2, from_3)):
        blocks[i] = block[...]
    place = position()
    member = place[0] % QUAD
    slots = [slot_of(strip_at(place, strip) ^ member) for strip in range(QUAD)]
    held = [blocks[slot].astype(f32) for slot in slots]
    hidden_out[0] = jnp.concatenate([block[:STRIP] for block in held], axis=0).astype(bf16)
    parts = jnp.concatenate([block[STRIP:] for block in held], axis=0).T
    disparity_out[...] = parts[0:1] + parts[1:2] + parts[2:3]


def in_hbm(value):
    return pltpu.with_memory_space_constraint(value, pltpu.HBM)


def to_sides(value):
    disps = lax.axis_size("disp")
    right = [(d, d + 1) for d in range(disps - 1)]
    left = [(d + 1, d) for d in range(disps - 1)]
    if disps == 2:
        return lax.ppermute(value, "disp", right + left)[None]
    return jnp.stack([lax.ppermute(value, "disp", right), lax.ppermute(value, "disp", left)])


def in_group(blocks):
    return [blocks[0]] + [
        to_rows(block, lambda band, i=i: band ^ i)
        for i, block in list(zip(ORDER, blocks))[1:]
    ]


def to_layers(value, partner):
    groups = lax.axis_size("band") // QUAD
    if not any(0 <= partner(g) < groups for g in range(groups)):
        return None
    return to_rows(value, lambda band: partner(band // QUAD) * QUAD + band % QUAD)


def to_rows(value, shift):
    bands = lax.axis_size("band")
    return lax.ppermute(
        value, "band", [(i, shift(i)) for i in range(bands) if 0 <= shift(i) < bands]
    )


def odd_pair(i):
    return i ^ 1


def even_pair(i):
    return i - 1 if i % 2 == 0 else i + 1


def local(
    feat_left,
    feat_right,
    limit,
    indices,
    hidden_start,
    vol_kernel,
    group_gain,
    hid_kernel,
    in_kernel,
    head_weight,
):
    bands, disps = lax.axis_size("band"), lax.axis_size("disp")
    vmem = pl.BlockSpec(memory_space=pltpu.VMEM)
    hbm = pl.BlockSpec(memory_space=pltpu.HBM)
    anywhere = pl.BlockSpec(memory_space=pl.ANY)
    padded = (DISPS + 2) * GROUPS

    feats = jnp.concatenate([feat_left[0], feat_right[0]], axis=0)
    odd_own, even_own = to_rows(feats, odd_pair), to_rows(feats, even_pair)
    across = to_sides(feats)
    raw_own, taps, marks, gains, heads = pl.pallas_call(
        own_row_kernel,
        out_shape=(
            jax.ShapeDtypeStruct((padded, 2 * TILE), bf16),
            jax.ShapeDtypeStruct((3 * OUT_SLAB, 3 * SLAB), bf16),
            jax.ShapeDtypeStruct((GROUPS, TILE), jnp.int32),
            jax.ShapeDtypeStruct((GROUPS, TILE), f32),
            jax.ShapeDtypeStruct((HID_CH, HID_CH), bf16),
        ),
        in_specs=[vmem, vmem] + [hbm] * 5,
        out_specs=(vmem,) * 5,
        scratch_shapes=[
            pltpu.VMEM((padded, TILE), f32),
            pltpu.VMEM((padded, TILE), f32),
            pltpu.VMEM((1, TILE), jnp.int32),
            pltpu.VMEM((ITERS, 1, TILE), jnp.int32),
            pltpu.SMEM((GROUPS,), f32),
            pltpu.VMEM((1, HID_CH), bf16),
            pltpu.VMEM((27, GROUPS, GROUPS), bf16),
            pltpu.SemaphoreType.DMA((5,)),
        ],
        compiler_params=pltpu.CompilerParams(vmem_limit_bytes=16 * 2**20),
        cost_estimate=pl.CostEstimate(flops=2 * 10**9, bytes_accessed=4 * 2**20, transcendentals=0),
    )(
        feats, across, in_hbm(limit), in_hbm(indices), in_hbm(group_gain),
        in_hbm(head_weight.reshape(1, HID_CH)), in_hbm(vol_kernel.reshape(27, GROUPS, GROUPS)),
    )
    hidden = hidden_start[0]
    hidden_across = to_sides(hidden)
    odd_own, even_own, raw_own, taps, hidden_across = lax.optimization_barrier(
        (odd_own, even_own, raw_own, taps, hidden_across)
    )
    marks_across = to_sides(marks)
    odd_across, even_across = to_sides(odd_own), to_sides(even_own)

    in_weight = jnp.concatenate(
        [in_kernel[:, :, :GROUPS]] * ITERS + [in_kernel[:, :, GROUPS:]], axis=2
    )
    in_weight = jnp.pad(in_weight, ((0, 0), (0, 1), (0, PACK - in_weight.shape[2]), (0, 0)))
    in_weight = in_weight.reshape(3 * HID_CH, 3 * HID_CH)

    blocks = pl.pallas_call(
        volume_kernel,
        out_shape=(jax.ShapeDtypeStruct((BLOCK_ROWS, TILE), bf16),) * QUAD,
        in_specs=[vmem] * 9 + [hbm, hbm],
        out_specs=(vmem,) * QUAD,
        scratch_shapes=[
            pltpu.VMEM((padded, 2 * TILE), bf16),
            pltpu.VMEM((3 * OUT_SLAB, 3 * SLAB), bf16),
            pltpu.VMEM((2, padded, TILE), f32),
            pltpu.VMEM((2, padded, TILE), f32),
            pltpu.VMEM((2, DISPS, TILE), f32),
            pltpu.VMEM((TILE + 2 * EDGE, HID_CH), f32),
            pltpu.VMEM((QUAD, BLOCK_ROWS, TILE), bf16),
            pltpu.SemaphoreType.DMA((2,)),
        ],
        compiler_params=pltpu.CompilerParams(vmem_limit_bytes=24 * 2**20),
        cost_estimate=pl.CostEstimate(
            flops=5 * 10**9, bytes_accessed=16 * 2**20, transcendentals=DISPS * TILE
        ),
    )(
        gains, odd_own, odd_across, even_own, even_across,
        marks, marks_across, hidden, hidden_across, raw_own, taps,
    )

    own, in_weight = lax.optimization_barrier((jnp.stack(in_group(blocks)), in_weight))
    around = [
        to_layers(own, lambda g: g ^ 2),
        to_layers(own, lambda g: (g - 2 ^ 2) + 2),
        to_layers(own, lambda g: g ^ 1),
        to_layers(own, lambda g: (g - 1 ^ 1) + 1),
    ]
    if around[1] is None:
        around[1] = around[0]

    pixels = WINDOW * AROUND
    refined = pl.pallas_call(
        refine_kernel,
        out_shape=(jax.ShapeDtypeStruct((2 * STRIP, HID_CH), bf16),) * QUAD,
        in_specs=[vmem] * 5 + [anywhere, anywhere, vmem],
        out_specs=(vmem,) * QUAD,
        scratch_shapes=[
            pltpu.VMEM((pixels + 2 * EDGE, HID_CH), f32),
            pltpu.VMEM((12 * HID_CH, 3 * HID_CH), bf16),
            pltpu.VMEM((pixels, HID_CH), f32),
            pltpu.VMEM((pixels, HID_CH), f32),
            pltpu.VMEM((pixels, 3 * HID_CH), bf16),
            pltpu.VMEM((pixels, 3 * HID_CH), bf16),
            pltpu.VMEM((pixels, HID_CH), bf16),
            pltpu.VMEM((pixels, HID_CH), f32),
            pltpu.VMEM((pixels + 2 * EDGE, HID_CH), f32),
            pltpu.VMEM((QUAD, 2 * STRIP, HID_CH), bf16),
            pltpu.SemaphoreType.DMA((2,)),
        ],
        compiler_params=pltpu.CompilerParams(vmem_limit_bytes=32 * 2**20),
    )(
        own, *around,
        hid_kernel.reshape(9 * HID_CH, 3 * HID_CH), in_weight, heads,
    )
    disparity, hidden = pl.pallas_call(
        unpack_kernel,
        out_shape=(
            jax.ShapeDtypeStruct((1, TILE), f32),
            jax.ShapeDtypeStruct((1, TILE, HID_CH), bf16),
        ),
        in_specs=[vmem] * QUAD,
        out_specs=(vmem, vmem),
        scratch_shapes=[pltpu.VMEM((QUAD, 2 * STRIP, HID_CH), bf16)],
        compiler_params=pltpu.CompilerParams(vmem_limit_bytes=4 * 2**20),
    )(*in_group(refined))
    return (disparity, hidden)


def solution(mesh):
    in_specs = (
        P("band", None, "disp"),
        P("band", None, "disp"),
        P("band", "disp"),
        P(None, "band", "disp"),
        P("band", "disp", None),
        P(),
        P(),
        P(),
        P(),
        P(),
    )
    out_specs = (P("band", "disp"), P("band", "disp", None))
    return jax.shard_map(local, mesh=mesh, in_specs=in_specs, out_specs=out_specs, check_vma=False)
```

```python
import jax
import jax.numpy as jnp
from jax import lax
from jax.experimental import pallas as pl
from jax.experimental.pallas import tpu as pltpu
from jax.sharding import PartitionSpec as P

GROUPS = 8
DISPS = 96
FEAT_CH = 96
HID_CH = 128
ITERS = 3
TILE = 128
REACH = 2 * ITERS
EDGE = 8
QUAD = 4
STRIP = TILE // QUAD
WINDOW = STRIP + 2 * EDGE
PACK = 32
PITCH = 64
ORDER = (0, 3, 1, 2)
BLOCK_ROWS = WINDOW + 2 * GROUPS
AROUND = QUAD + 2 * REACH
BLOCK = 8
SLAB = (BLOCK + 2) * GROUPS
OUT_SLAB = BLOCK * GROUPS

pixel_unit = 8.0
feature_scale = 0.25
floor_logit = -1e30

f32 = jnp.float32
bf16 = jnp.bfloat16


def position():
    return (
        lax.axis_index("band"), lax.axis_index("disp"),
        lax.axis_size("band"), lax.axis_size("disp"),
    )


def dot(a, b):
    return jnp.dot(a, b, preferred_element_type=f32)


def dot_nt(a, b):
    return lax.dot_general(a, b, (((1,), (1,)), ((), ())), preferred_element_type=f32)


def copy_all(copies):
    for copy in copies:
        copy.start()
    for copy in copies:
        copy.wait()


def toeplitz(vol_kernel):
    size = 27 * GROUPS
    flat = vol_kernel[...].astype(f32).reshape(size, GROUPS)
    flat = jnp.concatenate([flat, jnp.zeros((size, TILE - GROUPS), f32)], axis=1).T[:GROUPS]
    row = lax.broadcasted_iota(jnp.int32, (9 * GROUPS, size), 0) >> 3
    tap = lax.broadcasted_iota(jnp.int32, (9 * GROUPS, size), 1) >> 3
    tap_a = (tap >= 9).astype(jnp.int32) + (tap >= 18).astype(jnp.int32)
    within = tap - 9 * tap_a
    tap_b = (within >= 3).astype(jnp.int32) + (within >= 6).astype(jnp.int32)
    tap_e = within - 3 * tap_b
    pairs = jnp.where(
        row == 3 * tap_a + tap_e, jnp.concatenate([flat] * 9, axis=0), 0.0
    ).astype(bf16)
    from_row = lax.broadcasted_iota(jnp.int32, (size, 3 * SLAB), 0)
    to = lax.broadcasted_iota(jnp.int32, (size, 3 * SLAB), 1)
    from_tap = from_row >> 3
    from_in = from_tap - 9 * ((from_tap >= 9).astype(jnp.int32) + (from_tap >= 18).astype(jnp.int32))
    from_b = (from_in >= 3).astype(jnp.int32) + (from_in >= 6).astype(jnp.int32)
    to_b = (to >= SLAB).astype(jnp.int32) + (to >= 2 * SLAB).astype(jnp.int32)
    repeat = jnp.where((from_b == to_b) & ((from_row & 7) == (to & 7)), 1.0, 0.0).astype(bf16)
    spread = dot(pairs, repeat)
    to = lax.broadcasted_iota(jnp.int32, (GROUPS, 3 * SLAB), 1)
    to_b = (to >= SLAB).astype(jnp.int32) + (to >= 2 * SLAB).astype(jnp.int32)
    to_d = (to - SLAB * to_b) >> 3
    rows = []
    for e in range(3):
        for d in range(BLOCK):
            value = jnp.zeros((GROUPS, 3 * SLAB), f32)
            for a in range(3):
                at = (3 * a + e) * GROUPS
                value = jnp.where(to_d == d + a, spread[at : at + GROUPS], value)
            rows.append(value)
    return jnp.concatenate(rows, axis=0).astype(bf16)


def interleaved(values):
    stacked = jnp.swapaxes(jnp.stack(values), 0, 1)
    return stacked.reshape(values[0].shape[0] * len(values), values[0].shape[1])


def toeplitz_kernel(vol_kernel, out):
    out[...] = toeplitz(vol_kernel)


def correlate(lefts, rights, place, row_ok, wide, extra):
    has_left = (place[1] > 0).astype(f32)
    has_right = (place[1] < place[3] - 1).astype(f32)
    lane = lax.broadcasted_iota(jnp.int32, (TILE, TILE), 1)
    sub = lax.broadcasted_iota(jnp.int32, (TILE, TILE), 0)
    flip = jnp.where(lane + sub == TILE - 1, 1.0, 0.0).astype(bf16)
    per_group = FEAT_CH // GROUPS
    channel = lax.broadcasted_iota(jnp.int32, (32, FEAT_CH), 1)
    group_masks = [
        (channel >= g * per_group) & (channel < (g + 1) * per_group) for g in range(GROUPS)
    ]
    lane96 = lax.broadcasted_iota(jnp.int32, (FEAT_CH, TILE), 1)
    zero_slab = jnp.zeros((GROUPS, TILE), f32)
    for at in (0, (DISPS + 1) * GROUPS):
        wide[pl.ds(at, GROUPS), :] = zero_slab
        extra[pl.ds(at, GROUPS), :] = zero_slab

    own_t = (lefts[1] * row_ok).T
    side_t = jnp.where(
        lane96 < EDGE,
        lefts[2] * (has_right * row_ok),
        jnp.where(lane96 >= TILE - EDGE, lefts[0] * (has_left * row_ok), 0.0),
    ).T
    sources = jnp.concatenate([rights[2] * has_right, rights[1], rights[0] * has_left], axis=0)
    flipped = dot(sources.astype(bf16), flip)
    reverse = jnp.concatenate(
        [flipped[i * FEAT_CH : (i + 1) * FEAT_CH] for i in range(3)], axis=1
    )
    windows = [
        reverse[:, 2 * TILE - 32 - 32 * k : 3 * TILE - 32 - 32 * k].astype(bf16)
        for k in range(-1, 5)
    ]

    def by_group(rows):
        count = rows.shape[0]
        parts = [jnp.where(m[:count], rows, 0.0) for m in group_masks]
        return jnp.concatenate(parts, axis=0).astype(bf16)

    def shear(product, g, count, first):
        rows = product[count * g : count * g + count]
        return pltpu.roll(rows, TILE - 31 + first, 1, stride=1, stride_axis=0)

    products = [
        dot(by_group(own_t[32 * k : 32 * k + 32]), windows[k + 1]) for k in range(TILE // 32)
    ]
    after = dot(by_group(side_t[:EDGE]), windows[5])
    before = dot(by_group(side_t[TILE - EDGE :]), windows[0])
    parts, sides = [], []
    for g in range(GROUPS):
        part = jnp.concatenate([shear(product, g, 32, 0) for product in products], axis=0)
        parts.append(part.T[:DISPS])
        sides += [shear(after, g, EDGE, 0), shear(before, g, EDGE, 32 - EDGE)]
    part = jnp.concatenate(sides, axis=0).T[:DISPS]
    sides = [part if g == 0 else pltpu.roll(part, TILE - 2 * EDGE * g, 1) for g in range(GROUPS)]
    for target, values in ((wide, parts), (extra, sides)):
        target[GROUPS : GROUPS + DISPS * GROUPS, :] = interleaved(values) * (1.0 / per_group)


def own_row_kernel(
    own, across, limit, indices, gain, head, vol_kernel, raw_out, kernel_out, marks_out,
    gains_out, heads_out, wide, extra, limits, index_rows, gain_held, head_held, kernel, sems,
):
    place = position()
    copies = [
        pltpu.make_async_copy(source, target, sems.at[i])
        for i, (source, target) in enumerate(
            (
                (limit, limits), (indices, index_rows), (gain, gain_held), (head, head_held),
                (vol_kernel, kernel),
            )
        )
    ]
    for copy in copies:
        copy.start()
    tiles = [across[0], own[...], across[across.shape[0] - 1]]
    tiles = [tile.astype(f32) for tile in tiles]
    correlate(
        [tile[:FEAT_CH] for tile in tiles], [tile[FEAT_CH:] for tile in tiles],
        place, 1.0, wide, extra,
    )
    raw_out[...] = jnp.concatenate([wide[...], extra[...]], axis=1).astype(bf16)
    for copy in copies:
        copy.wait()
    marks = [limits[...]] + [index_rows[t] for t in range(ITERS)]
    blank = jnp.zeros((GROUPS - len(marks), TILE), jnp.int32)
    marks_out[...] = jnp.concatenate(marks + [blank], axis=0)
    group_at = lax.broadcasted_iota(jnp.int32, (GROUPS, TILE), 0)
    gains = jnp.zeros((GROUPS, TILE), f32)
    for g in range(GROUPS):
        gains = jnp.where(group_at == g, gain_held[g], gains)
    gains_out[...] = gains
    heads = head_held[...].astype(f32) * feature_scale
    heads_out[...] = jnp.broadcast_to(heads, heads_out.shape).astype(bf16)
    kernel_out[...] = kernel[...]


def volume_kernel(
    gains, even_own, even_across, odd_own, odd_across, marks, marks_across, hidden,
    hidden_across, raw_own, taps_own, out_0, out_1, out_2, out_3, raw, taps, wide, extra, logit, padded, blocks, sems,
):
    place = position()
    band, bands = place[0], place[2]
    is_even = band % 2 == 0
    copies = [
        pltpu.make_async_copy(raw_own, raw, sems.at[0]),
        pltpu.make_async_copy(taps_own, taps, sems.at[1]),
    ]
    for copy in copies:
        copy.start()

    last = odd_across.shape[0] - 1
    odd = [tile.astype(f32) for tile in (odd_across[0], odd_own[...], odd_across[last])]
    even = [tile.astype(f32) for tile in (even_across[0], even_own[...], even_across[last])]
    for b in range(2):
        row = band + 2 * b - 1
        row_ok = ((row >= 0) & (row < bands)).astype(f32)
        tiles = [
            jnp.where(is_even, y, x) if b == 0 else jnp.where(is_even, x, y)
            for x, y in zip(odd, even)
        ]
        correlate(
            [tile[:FEAT_CH] for tile in tiles], [tile[FEAT_CH:] for tile in tiles],
            place, row_ok, wide.at[b], extra.at[b],
        )
    for copy in copies:
        copy.wait()

    lane = lax.broadcasted_iota(jnp.int32, (GROUPS, TILE), 1)
    left_marks = pltpu.roll(marks_across[0], 2 * EDGE, 1)
    levels_of = [marks[...], jnp.where(lane < EDGE, marks_across[last], left_marks)]
    lane8 = lax.broadcasted_iota(jnp.int32, (OUT_SLAB, TILE), 1)
    group_at = lax.broadcasted_iota(jnp.int32, (GROUPS, TILE), 0)
    wanted = [
        [jnp.broadcast_to(rows[t + 1 : t + 2], (GROUPS, TILE)) for t in range(ITERS)]
        for rows in levels_of
    ]
    found = [[jnp.zeros((GROUPS, TILE), f32) for _ in range(ITERS)] for _ in range(2)]
    for q in range(DISPS // BLOCK):
        at = q * OUT_SLAB
        slabs = [
            jnp.concatenate(
                [wide[b, at : at + SLAB, :], extra[b, at : at + SLAB, :]], axis=1
            ).astype(bf16)
            for b in range(2)
        ]
        slabs.insert(1, raw[at : at + SLAB, :])
        product = dot(taps[...], jnp.concatenate(slabs, axis=0))
        halves = [product[:, :TILE], product[:, TILE:]]
        first = [half[:OUT_SLAB] for half in halves]
        middle = [half[OUT_SLAB : 2 * OUT_SLAB] for half in halves]
        after = [half[2 * OUT_SLAB :] for half in halves]
        first_on = pltpu.roll(first[0], 1, 1)
        convs = [
            middle[0]
            + jnp.where(lane8 == 0, pltpu.roll(first[1], TILE - 2 * EDGE + 1, 1), first_on)
            + jnp.where(
                lane8 == TILE - 1,
                pltpu.roll(after[1], TILE - 1, 1),
                pltpu.roll(after[0], TILE - 1, 1),
            ),
            middle[1]
            + jnp.where(lane8 == 0, first_on, pltpu.roll(first[1], 1, 1))
            + jnp.where(
                lane8 == 2 * EDGE - 1,
                pltpu.roll(after[0], 2 * EDGE - 1, 1),
                pltpu.roll(after[1], TILE - 1, 1),
            ),
        ]
        centre = slabs[1].astype(f32)[GROUPS : GROUPS + OUT_SLAB]
        for i in range(2):
            volume = centre[:, i * TILE : (i + 1) * TILE] + jnp.maximum(convs[i], 0.0)
            volume = volume.astype(bf16).astype(f32).reshape(BLOCK, GROUPS, TILE)
            logit[i, q * BLOCK : (q + 1) * BLOCK, :] = jnp.sum(volume * gains[...][None], axis=1)
            for d in range(BLOCK):
                for t in range(ITERS):
                    hit = wanted[i][t] == q * BLOCK + d
                    found[i][t] = found[i][t] + jnp.where(hit, volume[d], 0.0)

    level = lax.broadcasted_iota(jnp.int32, (DISPS, TILE), 0)
    for i in range(2):
        valid = level < levels_of[i][0:1]
        masked = jnp.where(valid, logit[i], floor_logit)
        top = jnp.max(masked, axis=0, keepdims=True)
        weights = jnp.where(valid, jnp.exp(masked - top), 0.0)
        moment = jnp.sum(weights * level.astype(f32), axis=0, keepdims=True)
        start = moment / jnp.sum(weights, axis=0, keepdims=True) / pixel_unit
        high = start.astype(bf16).astype(f32)
        low = (start - high).astype(bf16).astype(f32)
        ends = jnp.where(
            group_at == 0,
            jnp.broadcast_to(high, (GROUPS, TILE)),
            jnp.where(group_at == 1, jnp.broadcast_to(low, (GROUPS, TILE)), 0.0),
        )
        found[i].append(ends)
    has_left, has_right = place[1] > 0, place[1] < place[3] - 1
    is_beside = ((lane < EDGE) & has_right) | ((lane >= EDGE) & (lane < 2 * EDGE) & has_left)
    packed, packed_beside = found[0], [jnp.where(is_beside, x, 0.0) for x in found[1]]

    before = hidden_across[0, TILE - 2 * EDGE :, :].astype(f32)[EDGE:]
    after = hidden_across[last, : 2 * EDGE, :].astype(f32)[:EDGE]
    padded[:EDGE, :] = jnp.where(has_left, before, 0.0)
    padded[EDGE : EDGE + TILE, :] = hidden[...].astype(f32)
    padded[EDGE + TILE :, :] = jnp.where(has_right, after, 0.0)
    for strip in range(QUAD):
        block = [padded[STRIP * strip : STRIP * strip + WINDOW, :]]
        for half in range(2):
            part = jnp.zeros((GROUPS, TILE), f32)
            for i in range(2):
                q, base = 2 * half + i, PITCH * i
                at = lane - base
                moved = pltpu.roll(packed[q], (base + EDGE - STRIP * strip) % TILE, 1)
                if strip == 0:
                    other = pltpu.roll(packed_beside[q], (base - EDGE) % TILE, 1)
                    moved = jnp.where(at < EDGE, other, moved)
                if strip == QUAD - 1:
                    other = pltpu.roll(packed_beside[q], base + WINDOW - EDGE, 1)
                    moved = jnp.where(at >= WINDOW - EDGE, other, moved)
                part = jnp.where((at >= 0) & (at < WINDOW), moved, part)
            block.append(part)
        blocks[strip] = jnp.concatenate(block, axis=0).astype(bf16)
    member = band % QUAD
    for i, out in zip(ORDER, (out_0, out_1, out_2, out_3)):
        out[...] = blocks[strip_at(place, member ^ i)]


def slot_of(member_xor):
    return jnp.where(member_xor == 0, 0, jnp.where(member_xor == 3, 1, member_xor + 1))


def strip_at(place, member):
    return jnp.where(place[1] % 2 == 0, member, QUAD - 1 - member)


def keep(line, target, at, values):
    length = values.shape[0]
    start = EDGE + at
    line[start : start + length, :] = values
    target[at : at + length, 0:HID_CH] = line[start - 1 : start - 1 + length, :].astype(bf16)
    target[at : at + length, HID_CH : 2 * HID_CH] = values.astype(bf16)
    target[at : at + length, 2 * HID_CH :] = line[start + 1 : start + 1 + length, :].astype(bf16)


def around(target, at, length):
    return [target[at + a * WINDOW : at + a * WINDOW + length, :] for a in (-1, 0, 1)]


def refine_kernel(
    own,
    far_c,
    far_d,
    near_a,
    near_b,
    hid_weight,
    in_weight,
    heads,
    out_0,
    out_1,
    out_2,
    out_3,
    line,
    weight,
    looked,
    hidden_at,
    taps,
    reset_taps,
    inputs,
    gate,
    level,
    blocks,
    sems,
):
    rows, strip = AROUND, STRIP
    copies = [
        pltpu.make_async_copy(hid_weight, weight.at[pl.ds(0, 9 * HID_CH)], sems.at[0])
    ]
    copies.append(
        pltpu.make_async_copy(
            in_weight, weight.at[pl.ds(9 * HID_CH, 3 * HID_CH)], sems.at[1]
        )
    )
    for copy in copies:
        copy.start()

    place = position()
    band, disp, bands, disps = place
    member, layer = band % QUAD, band // QUAD
    at = strip_at(place, member)
    first = strip * at - EDGE
    first_row = layer * QUAD - REACH

    def block_of(r):
        step, row = (r + 2 * QUAD - REACH) // QUAD - 2, (r + 2 * QUAD - REACH) % QUAD
        slot = slot_of(row ^ member)
        if step == 0:
            return own[slot].astype(f32)
        if abs(step) == 1:
            choice, x, y = (layer % 2 == 0) == (step > 0), near_a, near_b
        else:
            choice, x, y = (layer % 4 < 2) == (step > 0), far_c, far_d
        inside = (first_row + r >= 0) & (first_row + r < bands)
        block = jnp.where(choice, x[slot].astype(f32), y[slot].astype(f32))
        return jnp.where(inside, block, 0.0)

    lane = lax.broadcasted_iota(jnp.int32, (GROUPS, TILE), 1)
    at_sub = lax.broadcasted_iota(jnp.int32, (WINDOW, TILE), 0)
    at_lane = lax.broadcasted_iota(jnp.int32, (WINDOW, TILE), 1)
    spread = jnp.where(at_sub == at_lane % PITCH, 1.0, 0.0).astype(bf16)
    fill = jnp.zeros((PACK, TILE), f32)
    zeros = jnp.zeros((GROUPS, TILE), f32)
    lines = []
    for r in range(rows):
        block = block_of(r)
        packed = block[WINDOW:]
        hidden_at[r * WINDOW : (r + 1) * WINDOW, :] = block[:WINDOW]
        pieces = []
        for b in range(3):
            moved = packed if b == 1 else pltpu.roll(packed, (1 - b) % TILE, 1)
            for q in range(4):
                part = moved[GROUPS * (q // 2) : GROUPS * (q // 2 + 1)]
                pieces.append(jnp.where((lane >= PITCH) == (q % 2 == 1), part, zeros))
        lines.append(jnp.concatenate(pieces + [fill], axis=0).astype(bf16))
    for r in range(0, rows, 2):
        both = dot_nt(spread, jnp.concatenate(lines[r : r + 2], axis=0))
        for i in range(2):
            at = (r + i) * WINDOW
            looked[at : at + WINDOW, :] = both[:, i * HID_CH : (i + 1) * HID_CH]
    sub = lax.broadcasted_iota(jnp.int32, (HID_CH, HID_CH), 0)
    ends = jnp.where((sub == PACK + 24) | (sub == PACK + 25), feature_scale, 0.0).astype(bf16)
    blank = jnp.zeros((EDGE, HID_CH), f32)
    level[:EDGE, :] = blank
    level[EDGE + WINDOW * rows :, :] = blank
    level[EDGE : EDGE + WINDOW * rows, :] = dot(looked[...].astype(bf16), ends)
    line[...] = jnp.zeros_like(line)
    keep(line, taps, 0, hidden_at[...])
    for copy in copies:
        copy.wait()

    for t in range(ITERS):
        low, high = 1 + 2 * t, rows - 2 - 2 * t
        at, length = (low - 1) * WINDOW, (high - low + 3) * WINDOW
        lane_at = lax.broadcasted_iota(jnp.int32, (length, HID_CH), 1)
        tap, channel = lane_at // PACK, lane_at % PACK
        near = [level[EDGE + at + b : EDGE + at + b + length, :] for b in (-1, 0, 1)]
        value = jnp.where(tap == 0, near[0], jnp.where(tap == 1, near[1], near[2]))
        at_lookup = (channel >= t * GROUPS) & (channel < (t + 1) * GROUPS)
        value = jnp.where(
            (channel == 3 * GROUPS) & (tap < 3),
            value,
            jnp.where(at_lookup, looked[at : at + length, :], 0.0),
        )
        inputs[at : at + length, :] = value.astype(bf16)

        at, length = low * WINDOW, (high - low + 1) * WINDOW
        lhs = around(taps, at, length) + around(inputs, at, length)
        both = dot(jnp.concatenate(lhs, axis=1), weight[:, : 2 * HID_CH])
        gate[at + WINDOW : at + length - WINDOW, :] = (
            0.5 * jnp.tanh(0.5 * both[WINDOW : length - WINDOW, :HID_CH]) + 0.5
        )
        reset = 0.5 * jnp.tanh(0.5 * both[:, HID_CH:]) + 0.5
        keep(line, reset_taps, at, reset * hidden_at[at : at + length, :])

        at, length = at + WINDOW, length - 2 * WINDOW
        lhs = around(reset_taps, at, length) + around(inputs, at, length)
        candidate = jnp.tanh(dot(jnp.concatenate(lhs, axis=1), weight[:, 2 * HID_CH :]))
        hidden = hidden_at[at : at + length, :]
        hidden = hidden + gate[at : at + length, :] * (candidate - hidden)
        pixel = lax.broadcasted_iota(jnp.int32, (length, HID_CH), 0)
        column, row = pixel % WINDOW + first, pixel // WINDOW + (low + 1 + first_row)
        inside = ((column >= 0) | (disp > 0)) & ((column < TILE) | (disp < disps - 1))
        inside = inside & (row >= 0) & (row < bands)
        hidden = jnp.where(inside, hidden, 0.0).astype(bf16)
        level[EDGE + at : EDGE + at + length, :] += dot_nt(hidden, heads[...])
        hidden_at[at : at + length, :] = hidden.astype(f32)
        if t < ITERS - 1:
            keep(line, taps, at, hidden.astype(f32))

    lane = lax.broadcasted_iota(jnp.int32, (strip, HID_CH), 1)
    for r in range(QUAD):
        at = (REACH + r) * WINDOW + EDGE
        hidden = hidden_at[at : at + strip, :]
        value = level[EDGE + at : EDGE + at + strip, :] * (1.0 / feature_scale)
        high = value.astype(bf16).astype(f32)
        middle = (value - high).astype(bf16).astype(f32)
        parts = jnp.where(lane == 0, high, jnp.where(lane == 1, middle, value - high - middle))
        parts = jnp.where(lane < 3, parts, 0.0)
        blocks[r] = jnp.concatenate([hidden, parts], axis=0).astype(bf16)
    for i, out in zip(ORDER, (out_0, out_1, out_2, out_3)):
        out[...] = blocks[member ^ i]


def unpack_kernel(from_0, from_1, from_2, from_3, disparity_out, hidden_out, blocks):
    for i, block in enumerate((from_0, from_1, from_2, from_3)):
        blocks[i] = block[...]
    place = position()
    member = place[0] % QUAD
    slots = [slot_of(strip_at(place, strip) ^ member) for strip in range(QUAD)]
    held = [blocks[slot].astype(f32) for slot in slots]
    hidden_out[0] = jnp.concatenate([block[:STRIP] for block in held], axis=0).astype(bf16)
    parts = jnp.concatenate([block[STRIP:] for block in held], axis=0).T
    disparity_out[...] = parts[0:1] + parts[1:2] + parts[2:3]


def in_hbm(value):
    return pltpu.with_memory_space_constraint(value, pltpu.HBM)


def to_sides(value):
    disps = lax.axis_size("disp")
    right = [(d, d + 1) for d in range(disps - 1)]
    left = [(d + 1, d) for d in range(disps - 1)]
    if disps == 2:
        return lax.ppermute(value, "disp", right + left)[None]
    return jnp.stack([lax.ppermute(value, "disp", right), lax.ppermute(value, "disp", left)])


def in_group(blocks):
    return [blocks[0]] + [
        to_rows(block, lambda band, i=i: band ^ i)
        for i, block in list(zip(ORDER, blocks))[1:]
    ]


def to_layers(value, partner):
    groups = lax.axis_size("band") // QUAD
    if not any(0 <= partner(g) < groups for g in range(groups)):
        return None
    return to_rows(value, lambda band: partner(band // QUAD) * QUAD + band % QUAD)


def to_rows(value, shift):
    bands = lax.axis_size("band")
    return lax.ppermute(
        value, "band", [(i, shift(i)) for i in range(bands) if 0 <= shift(i) < bands]
    )


def odd_pair(i):
    return i ^ 1


def even_pair(i):
    return i - 1 if i % 2 == 0 else i + 1


def local(
    feat_left,
    feat_right,
    limit,
    indices,
    hidden_start,
    vol_kernel,
    group_gain,
    hid_kernel,
    in_kernel,
    head_weight,
):
    bands, disps = lax.axis_size("band"), lax.axis_size("disp")
    vmem = pl.BlockSpec(memory_space=pltpu.VMEM)
    hbm = pl.BlockSpec(memory_space=pltpu.HBM)
    anywhere = pl.BlockSpec(memory_space=pl.ANY)
    padded = (DISPS + 2) * GROUPS

    feats = jnp.concatenate([feat_left[0], feat_right[0]], axis=0)
    even_own, odd_own = to_rows(feats, even_pair), to_rows(feats, odd_pair)
    across = to_sides(feats)
    raw_own, kernel_held, marks, gains, heads = pl.pallas_call(
        own_row_kernel,
        out_shape=(
            jax.ShapeDtypeStruct((padded, 2 * TILE), bf16),
            jax.ShapeDtypeStruct((27, GROUPS, GROUPS), bf16),
            jax.ShapeDtypeStruct((GROUPS, TILE), jnp.int32),
            jax.ShapeDtypeStruct((GROUPS, TILE), f32),
            jax.ShapeDtypeStruct((HID_CH, HID_CH), bf16),
        ),
        in_specs=[vmem, vmem] + [hbm] * 5,
        out_specs=(vmem,) * 5,
        scratch_shapes=[
            pltpu.VMEM((padded, TILE), f32),
            pltpu.VMEM((padded, TILE), f32),
            pltpu.VMEM((1, TILE), jnp.int32),
            pltpu.VMEM((ITERS, 1, TILE), jnp.int32),
            pltpu.SMEM((GROUPS,), f32),
            pltpu.VMEM((1, HID_CH), bf16),
            pltpu.VMEM((27, GROUPS, GROUPS), bf16),
            pltpu.SemaphoreType.DMA((5,)),
        ],
        compiler_params=pltpu.CompilerParams(vmem_limit_bytes=16 * 2**20),
        cost_estimate=pl.CostEstimate(flops=2 * 10**9, bytes_accessed=4 * 2**20, transcendentals=0),
    )(
        feats, across, in_hbm(limit), in_hbm(indices), in_hbm(group_gain),
        in_hbm(head_weight.reshape(1, HID_CH)), in_hbm(vol_kernel.reshape(27, GROUPS, GROUPS)),
    )
    hidden = hidden_start[0]
    hidden_across = to_sides(hidden)
    even_own, odd_own, raw_own, hidden_across = lax.optimization_barrier(
        (even_own, odd_own, raw_own, hidden_across)
    )
    taps = pl.pallas_call(
        toeplitz_kernel,
        out_shape=jax.ShapeDtypeStruct((3 * OUT_SLAB, 3 * SLAB), bf16),
        in_specs=[vmem],
        out_specs=vmem,
        compiler_params=pltpu.CompilerParams(vmem_limit_bytes=8 * 2**20),
        cost_estimate=pl.CostEstimate(flops=10**9, bytes_accessed=2**20, transcendentals=0),
    )(kernel_held)
    marks_across = to_sides(marks)
    even_across, odd_across = to_sides(even_own), to_sides(odd_own)

    in_weight = jnp.concatenate(
        [in_kernel[:, :, :GROUPS]] * ITERS + [in_kernel[:, :, GROUPS:]], axis=2
    )
    in_weight = jnp.pad(in_weight, ((0, 0), (0, 1), (0, PACK - in_weight.shape[2]), (0, 0)))
    in_weight = in_weight.reshape(3 * HID_CH, 3 * HID_CH)

    blocks = pl.pallas_call(
        volume_kernel,
        out_shape=(jax.ShapeDtypeStruct((BLOCK_ROWS, TILE), bf16),) * QUAD,
        in_specs=[vmem] * 9 + [hbm, hbm],
        out_specs=(vmem,) * QUAD,
        scratch_shapes=[
            pltpu.VMEM((padded, 2 * TILE), bf16),
            pltpu.VMEM((3 * OUT_SLAB, 3 * SLAB), bf16),
            pltpu.VMEM((2, padded, TILE), f32),
            pltpu.VMEM((2, padded, TILE), f32),
            pltpu.VMEM((2, DISPS, TILE), f32),
            pltpu.VMEM((TILE + 2 * EDGE, HID_CH), f32),
            pltpu.VMEM((QUAD, BLOCK_ROWS, TILE), bf16),
            pltpu.SemaphoreType.DMA((2,)),
        ],
        compiler_params=pltpu.CompilerParams(vmem_limit_bytes=24 * 2**20),
        cost_estimate=pl.CostEstimate(
            flops=5 * 10**9, bytes_accessed=16 * 2**20, transcendentals=DISPS * TILE
        ),
    )(
        gains, even_own, even_across, odd_own, odd_across,
        marks, marks_across, hidden, hidden_across, raw_own, taps,
    )

    own, in_weight = lax.optimization_barrier((jnp.stack(in_group(blocks)), in_weight))
    around = [
        to_layers(own, lambda g: g ^ 2),
        to_layers(own, lambda g: (g - 2 ^ 2) + 2),
        to_layers(own, lambda g: g ^ 1),
        to_layers(own, lambda g: (g - 1 ^ 1) + 1),
    ]
    if around[1] is None:
        around[1] = around[0]

    pixels = WINDOW * AROUND
    refined = pl.pallas_call(
        refine_kernel,
        out_shape=(jax.ShapeDtypeStruct((2 * STRIP, HID_CH), bf16),) * QUAD,
        in_specs=[vmem] * 5 + [anywhere, anywhere, vmem],
        out_specs=(vmem,) * QUAD,
        scratch_shapes=[
            pltpu.VMEM((pixels + 2 * EDGE, HID_CH), f32),
            pltpu.VMEM((12 * HID_CH, 3 * HID_CH), bf16),
            pltpu.VMEM((pixels, HID_CH), f32),
            pltpu.VMEM((pixels, HID_CH), f32),
            pltpu.VMEM((pixels, 3 * HID_CH), bf16),
            pltpu.VMEM((pixels, 3 * HID_CH), bf16),
            pltpu.VMEM((pixels, HID_CH), bf16),
            pltpu.VMEM((pixels, HID_CH), f32),
            pltpu.VMEM((pixels + 2 * EDGE, HID_CH), f32),
            pltpu.VMEM((QUAD, 2 * STRIP, HID_CH), bf16),
            pltpu.SemaphoreType.DMA((2,)),
        ],
        compiler_params=pltpu.CompilerParams(vmem_limit_bytes=32 * 2**20),
    )(
        own, *around,
        hid_kernel.reshape(9 * HID_CH, 3 * HID_CH), in_weight, heads,
    )
    disparity, hidden = pl.pallas_call(
        unpack_kernel,
        out_shape=(
            jax.ShapeDtypeStruct((1, TILE), f32),
            jax.ShapeDtypeStruct((1, TILE, HID_CH), bf16),
        ),
        in_specs=[vmem] * QUAD,
        out_specs=(vmem, vmem),
        scratch_shapes=[pltpu.VMEM((QUAD, 2 * STRIP, HID_CH), bf16)],
        compiler_params=pltpu.CompilerParams(vmem_limit_bytes=4 * 2**20),
    )(*in_group(refined))
    return (disparity, hidden)


def solution(mesh):
    in_specs = (
        P("band", None, "disp"),
        P("band", None, "disp"),
        P("band", "disp"),
        P(None, "band", "disp"),
        P("band", "disp", None),
        P(),
        P(),
        P(),
        P(),
        P(),
    )
    out_specs = (P("band", "disp"), P("band", "disp", None))
    return jax.shard_map(local, mesh=mesh, in_specs=in_specs, out_specs=out_specs, check_vma=False)
```

```python
import jax
import jax.numpy as jnp
from jax import lax
from jax.experimental import pallas as pl
from jax.experimental.pallas import tpu as pltpu
from jax.sharding import PartitionSpec as P

GROUPS = 8
DISPS = 96
FEAT_CH = 96
HID_CH = 128
ITERS = 3
TILE = 128
REACH = 2 * ITERS
EDGE = 8
QUAD = 4
STRIP = TILE // QUAD
WINDOW = STRIP + 2 * EDGE
PACK = 32
PITCH = 64
ORDER = (0, 3, 1, 2)
BLOCK_ROWS = WINDOW + 2 * GROUPS
AROUND = QUAD + 2 * REACH
BLOCK = 8
SLAB = (BLOCK + 2) * GROUPS
OUT_SLAB = BLOCK * GROUPS

pixel_unit = 8.0
feature_scale = 0.25
floor_logit = -1e30

f32 = jnp.float32
bf16 = jnp.bfloat16


def position():
    return (
        lax.axis_index("band"), lax.axis_index("disp"),
        lax.axis_size("band"), lax.axis_size("disp"),
    )


def dot(a, b):
    return jnp.dot(a, b, preferred_element_type=f32)


def dot_nt(a, b):
    return lax.dot_general(a, b, (((1,), (1,)), ((), ())), preferred_element_type=f32)


def copy_all(copies):
    for copy in copies:
        copy.start()
    for copy in copies:
        copy.wait()


def toeplitz(vol_kernel):
    size = 27 * GROUPS
    flat = vol_kernel[...].astype(f32).reshape(size, GROUPS)
    flat = jnp.concatenate([flat, jnp.zeros((size, TILE - GROUPS), f32)], axis=1).T[:GROUPS]
    row = lax.broadcasted_iota(jnp.int32, (9 * GROUPS, size), 0) >> 3
    tap = lax.broadcasted_iota(jnp.int32, (9 * GROUPS, size), 1) >> 3
    tap_a = (tap >= 9).astype(jnp.int32) + (tap >= 18).astype(jnp.int32)
    within = tap - 9 * tap_a
    tap_b = (within >= 3).astype(jnp.int32) + (within >= 6).astype(jnp.int32)
    tap_e = within - 3 * tap_b
    pairs = jnp.where(
        row == 3 * tap_a + tap_e, jnp.concatenate([flat] * 9, axis=0), 0.0
    ).astype(bf16)
    from_row = lax.broadcasted_iota(jnp.int32, (size, 3 * SLAB), 0)
    to = lax.broadcasted_iota(jnp.int32, (size, 3 * SLAB), 1)
    from_tap = from_row >> 3
    from_in = from_tap - 9 * ((from_tap >= 9).astype(jnp.int32) + (from_tap >= 18).astype(jnp.int32))
    from_b = (from_in >= 3).astype(jnp.int32) + (from_in >= 6).astype(jnp.int32)
    to_b = (to >= SLAB).astype(jnp.int32) + (to >= 2 * SLAB).astype(jnp.int32)
    repeat = jnp.where((from_b == to_b) & ((from_row & 7) == (to & 7)), 1.0, 0.0).astype(bf16)
    spread = dot(pairs, repeat)
    to = lax.broadcasted_iota(jnp.int32, (GROUPS, 3 * SLAB), 1)
    to_b = (to >= SLAB).astype(jnp.int32) + (to >= 2 * SLAB).astype(jnp.int32)
    to_d = (to - SLAB * to_b) >> 3
    rows = []
    for e in range(3):
        for d in range(BLOCK):
            value = jnp.zeros((GROUPS, 3 * SLAB), f32)
            for a in range(3):
                at = (3 * a + e) * GROUPS
                value = jnp.where(to_d == d + a, spread[at : at + GROUPS], value)
            rows.append(value)
    return jnp.concatenate(rows, axis=0).astype(bf16)


def interleaved(values):
    stacked = jnp.swapaxes(jnp.stack(values), 0, 1)
    return stacked.reshape(values[0].shape[0] * len(values), values[0].shape[1])


def toeplitz_kernel(vol_kernel, out):
    out[...] = toeplitz(vol_kernel)


def correlate(lefts, rights, place, row_ok, wide, extra):
    has_left = (place[1] > 0).astype(f32)
    has_right = (place[1] < place[3] - 1).astype(f32)
    lane = lax.broadcasted_iota(jnp.int32, (TILE, TILE), 1)
    sub = lax.broadcasted_iota(jnp.int32, (TILE, TILE), 0)
    flip = jnp.where(lane + sub == TILE - 1, 1.0, 0.0).astype(bf16)
    per_group = FEAT_CH // GROUPS
    channel = lax.broadcasted_iota(jnp.int32, (32, FEAT_CH), 1)
    group_masks = [
        (channel >= g * per_group) & (channel < (g + 1) * per_group) for g in range(GROUPS)
    ]
    lane96 = lax.broadcasted_iota(jnp.int32, (FEAT_CH, TILE), 1)
    zero_slab = jnp.zeros((GROUPS, TILE), f32)
    for at in (0, (DISPS + 1) * GROUPS):
        wide[pl.ds(at, GROUPS), :] = zero_slab
        extra[pl.ds(at, GROUPS), :] = zero_slab

    own_t = (lefts[1] * row_ok).T
    side_t = jnp.where(
        lane96 < EDGE,
        lefts[2] * (has_right * row_ok),
        jnp.where(lane96 >= TILE - EDGE, lefts[0] * (has_left * row_ok), 0.0),
    ).T
    sources = jnp.concatenate([rights[2] * has_right, rights[1], rights[0] * has_left], axis=0)
    flipped = dot(sources.astype(bf16), flip)
    reverse = jnp.concatenate(
        [flipped[i * FEAT_CH : (i + 1) * FEAT_CH] for i in range(3)], axis=1
    )
    windows = [
        reverse[:, 2 * TILE - 32 - 32 * k : 3 * TILE - 32 - 32 * k].astype(bf16)
        for k in range(-1, 5)
    ]

    def by_group(rows):
        count = rows.shape[0]
        parts = [jnp.where(m[:count], rows, 0.0) for m in group_masks]
        return jnp.concatenate(parts, axis=0).astype(bf16)

    def shear(product, g, count, first):
        rows = product[count * g : count * g + count]
        return pltpu.roll(rows, TILE - 31 + first, 1, stride=1, stride_axis=0)

    products = [
        dot(by_group(own_t[32 * k : 32 * k + 32]), windows[k + 1]) for k in range(TILE // 32)
    ]
    after = dot(by_group(side_t[:EDGE]), windows[5])
    before = dot(by_group(side_t[TILE - EDGE :]), windows[0])
    parts, sides = [], []
    for g in range(GROUPS):
        part = jnp.concatenate([shear(product, g, 32, 0) for product in products], axis=0)
        parts.append(part.T[:DISPS])
        sides += [shear(after, g, EDGE, 0), shear(before, g, EDGE, 32 - EDGE)]
    part = jnp.concatenate(sides, axis=0).T[:DISPS]
    sides = [part if g == 0 else pltpu.roll(part, TILE - 2 * EDGE * g, 1) for g in range(GROUPS)]
    for target, values in ((wide, parts), (extra, sides)):
        target[GROUPS : GROUPS + DISPS * GROUPS, :] = interleaved(values) * (1.0 / per_group)


def own_row_kernel(
    own, across, limit, indices, gain, head, vol_kernel, raw_out, kernel_out, marks_out,
    gains_out, heads_out, wide, extra, limits, index_rows, gain_held, head_held, kernel, sems,
):
    place = position()
    copies = [
        pltpu.make_async_copy(source, target, sems.at[i])
        for i, (source, target) in enumerate(
            (
                (limit, limits), (indices, index_rows), (gain, gain_held), (head, head_held),
                (vol_kernel, kernel),
            )
        )
    ]
    for copy in copies:
        copy.start()
    tiles = [across[0], own[...], across[across.shape[0] - 1]]
    tiles = [tile.astype(f32) for tile in tiles]
    correlate(
        [tile[:FEAT_CH] for tile in tiles], [tile[FEAT_CH:] for tile in tiles],
        place, 1.0, wide, extra,
    )
    raw_out[...] = jnp.concatenate([wide[...], extra[...]], axis=1).astype(bf16)
    for copy in copies:
        copy.wait()
    marks = [limits[...]] + [index_rows[t] for t in range(ITERS)]
    blank = jnp.zeros((GROUPS - len(marks), TILE), jnp.int32)
    marks_out[...] = jnp.concatenate(marks + [blank], axis=0)
    group_at = lax.broadcasted_iota(jnp.int32, (GROUPS, TILE), 0)
    gains = jnp.zeros((GROUPS, TILE), f32)
    for g in range(GROUPS):
        gains = jnp.where(group_at == g, gain_held[g], gains)
    gains_out[...] = gains
    heads = head_held[...].astype(f32) * feature_scale
    heads_out[...] = jnp.broadcast_to(heads, heads_out.shape).astype(bf16)
    kernel_out[...] = kernel[...]


def volume_kernel(
    gains, even_own, even_across, odd_own, odd_across, marks, marks_across, hidden,
    hidden_across, raw_own, taps_own, out_0, out_1, out_2, out_3, raw, taps, wide, extra, logit, padded, blocks, sems,
):
    place = position()
    band, bands = place[0], place[2]
    is_even = band % 2 == 0
    copies = [
        pltpu.make_async_copy(raw_own, raw, sems.at[0]),
        pltpu.make_async_copy(taps_own, taps, sems.at[1]),
    ]
    for copy in copies:
        copy.start()

    last = odd_across.shape[0] - 1
    odd = [tile.astype(f32) for tile in (odd_across[0], odd_own[...], odd_across[last])]
    even = [tile.astype(f32) for tile in (even_across[0], even_own[...], even_across[last])]
    for b in range(2):
        row = band + 2 * b - 1
        row_ok = ((row >= 0) & (row < bands)).astype(f32)
        tiles = [
            jnp.where(is_even, y, x) if b == 0 else jnp.where(is_even, x, y)
            for x, y in zip(odd, even)
        ]
        correlate(
            [tile[:FEAT_CH] for tile in tiles], [tile[FEAT_CH:] for tile in tiles],
            place, row_ok, wide.at[b], extra.at[b],
        )
    for copy in copies:
        copy.wait()

    lane = lax.broadcasted_iota(jnp.int32, (GROUPS, TILE), 1)
    left_marks = pltpu.roll(marks_across[0], 2 * EDGE, 1)
    levels_of = [marks[...], jnp.where(lane < EDGE, marks_across[last], left_marks)]
    lane8 = lax.broadcasted_iota(jnp.int32, (OUT_SLAB, TILE), 1)
    group_at = lax.broadcasted_iota(jnp.int32, (GROUPS, TILE), 0)
    wanted = [
        [jnp.broadcast_to(rows[t + 1 : t + 2], (GROUPS, TILE)) for t in range(ITERS)]
        for rows in levels_of
    ]
    found = [[jnp.zeros((GROUPS, TILE), f32) for _ in range(ITERS)] for _ in range(2)]
    for q in range(DISPS // BLOCK):
        at = q * OUT_SLAB
        slabs = [
            jnp.concatenate(
                [wide[b, at : at + SLAB, :], extra[b, at : at + SLAB, :]], axis=1
            ).astype(bf16)
            for b in range(2)
        ]
        slabs.insert(1, raw[at : at + SLAB, :])
        product = dot(taps[...], jnp.concatenate(slabs, axis=0))
        halves = [product[:, :TILE], product[:, TILE:]]
        first = [half[:OUT_SLAB] for half in halves]
        middle = [half[OUT_SLAB : 2 * OUT_SLAB] for half in halves]
        after = [half[2 * OUT_SLAB :] for half in halves]
        first_on = pltpu.roll(first[0], 1, 1)
        convs = [
            middle[0]
            + jnp.where(lane8 == 0, pltpu.roll(first[1], TILE - 2 * EDGE + 1, 1), first_on)
            + jnp.where(
                lane8 == TILE - 1,
                pltpu.roll(after[1], TILE - 1, 1),
                pltpu.roll(after[0], TILE - 1, 1),
            ),
            middle[1]
            + jnp.where(lane8 == 0, first_on, pltpu.roll(first[1], 1, 1))
            + jnp.where(
                lane8 == 2 * EDGE - 1,
                pltpu.roll(after[0], 2 * EDGE - 1, 1),
                pltpu.roll(after[1], TILE - 1, 1),
            ),
        ]
        centre = slabs[1].astype(f32)[GROUPS : GROUPS + OUT_SLAB]
        for i in range(2):
            volume = centre[:, i * TILE : (i + 1) * TILE] + jnp.maximum(convs[i], 0.0)
            volume = volume.astype(bf16).astype(f32).reshape(BLOCK, GROUPS, TILE)
            logit[i, q * BLOCK : (q + 1) * BLOCK, :] = jnp.sum(volume * gains[...][None], axis=1)
            for d in range(BLOCK):
                for t in range(ITERS):
                    hit = wanted[i][t] == q * BLOCK + d
                    found[i][t] = found[i][t] + jnp.where(hit, volume[d], 0.0)

    level = lax.broadcasted_iota(jnp.int32, (DISPS, TILE), 0)
    for i in range(2):
        valid = level < levels_of[i][0:1]
        masked = jnp.where(valid, logit[i], floor_logit)
        top = jnp.max(masked, axis=0, keepdims=True)
        weights = jnp.where(valid, jnp.exp(masked - top), 0.0)
        moment = jnp.sum(weights * level.astype(f32), axis=0, keepdims=True)
        start = moment / jnp.sum(weights, axis=0, keepdims=True) / pixel_unit
        high = start.astype(bf16).astype(f32)
        low = (start - high).astype(bf16).astype(f32)
        ends = jnp.where(
            group_at == 0,
            jnp.broadcast_to(high, (GROUPS, TILE)),
            jnp.where(group_at == 1, jnp.broadcast_to(low, (GROUPS, TILE)), 0.0),
        )
        found[i].append(ends)
    has_left, has_right = place[1] > 0, place[1] < place[3] - 1
    is_beside = ((lane < EDGE) & has_right) | ((lane >= EDGE) & (lane < 2 * EDGE) & has_left)
    packed, packed_beside = found[0], [jnp.where(is_beside, x, 0.0) for x in found[1]]

    before = hidden_across[0, TILE - 2 * EDGE :, :].astype(f32)[EDGE:]
    after = hidden_across[last, : 2 * EDGE, :].astype(f32)[:EDGE]
    padded[:EDGE, :] = jnp.where(has_left, before, 0.0)
    padded[EDGE : EDGE + TILE, :] = hidden[...].astype(f32)
    padded[EDGE + TILE :, :] = jnp.where(has_right, after, 0.0)
    for strip in range(QUAD):
        block = [padded[STRIP * strip : STRIP * strip + WINDOW, :]]
        for half in range(2):
            part = jnp.zeros((GROUPS, TILE), f32)
            for i in range(2):
                q, base = 2 * half + i, PITCH * i
                at = lane - base
                moved = pltpu.roll(packed[q], (base + EDGE - STRIP * strip) % TILE, 1)
                if strip == 0:
                    other = pltpu.roll(packed_beside[q], (base - EDGE) % TILE, 1)
                    moved = jnp.where(at < EDGE, other, moved)
                if strip == QUAD - 1:
                    other = pltpu.roll(packed_beside[q], base + WINDOW - EDGE, 1)
                    moved = jnp.where(at >= WINDOW - EDGE, other, moved)
                part = jnp.where((at >= 0) & (at < WINDOW), moved, part)
            block.append(part)
        blocks[strip] = jnp.concatenate(block, axis=0).astype(bf16)
    member = band % QUAD
    for i, out in zip(ORDER, (out_0, out_1, out_2, out_3)):
        out[...] = blocks[strip_at(place, member ^ i)]


def slot_of(member_xor):
    return jnp.where(member_xor == 0, 0, jnp.where(member_xor == 3, 1, member_xor + 1))


def strip_at(place, member):
    return jnp.where(place[1] % 2 == 0, member, QUAD - 1 - member)


def keep(line, target, at, values):
    length = values.shape[0]
    start = EDGE + at
    line[start : start + length, :] = values
    target[at : at + length, 0:HID_CH] = line[start - 1 : start - 1 + length, :].astype(bf16)
    target[at : at + length, HID_CH : 2 * HID_CH] = values.astype(bf16)
    target[at : at + length, 2 * HID_CH :] = line[start + 1 : start + 1 + length, :].astype(bf16)


def around(target, at, length):
    return [target[at + a * WINDOW : at + a * WINDOW + length, :] for a in (-1, 0, 1)]


def weight_kernel(hid_weight, in_weight, out):
    out[: 9 * HID_CH, :] = hid_weight[...]
    out[9 * HID_CH :, :] = in_weight[...]


def refine_kernel(
    own,
    far_c,
    far_d,
    near_a,
    near_b,
    weight,
    heads,
    out_0,
    out_1,
    out_2,
    out_3,
    line,
    looked,
    hidden_at,
    taps,
    reset_taps,
    inputs,
    gate,
    level,
    blocks,
):
    rows, strip = AROUND, STRIP
    place = position()
    band, disp, bands, disps = place
    member, layer = band % QUAD, band // QUAD
    at = strip_at(place, member)
    first = strip * at - EDGE
    first_row = layer * QUAD - REACH

    def block_of(r):
        step, row = (r + 2 * QUAD - REACH) // QUAD - 2, (r + 2 * QUAD - REACH) % QUAD
        slot = slot_of(row ^ member)
        if step == 0:
            return own[slot].astype(f32)
        if abs(step) == 1:
            choice, x, y = (layer % 2 == 0) == (step > 0), near_a, near_b
        else:
            choice, x, y = (layer % 4 < 2) == (step > 0), far_c, far_d
        inside = (first_row + r >= 0) & (first_row + r < bands)
        block = jnp.where(choice, x[slot].astype(f32), y[slot].astype(f32))
        return jnp.where(inside, block, 0.0)

    lane = lax.broadcasted_iota(jnp.int32, (GROUPS, TILE), 1)
    at_sub = lax.broadcasted_iota(jnp.int32, (WINDOW, TILE), 0)
    at_lane = lax.broadcasted_iota(jnp.int32, (WINDOW, TILE), 1)
    spread = jnp.where(at_sub == at_lane % PITCH, 1.0, 0.0).astype(bf16)
    fill = jnp.zeros((PACK, TILE), f32)
    zeros = jnp.zeros((GROUPS, TILE), f32)
    lines = []
    for r in range(rows):
        block = block_of(r)
        packed = block[WINDOW:]
        hidden_at[r * WINDOW : (r + 1) * WINDOW, :] = block[:WINDOW]
        pieces = []
        for b in range(3):
            moved = packed if b == 1 else pltpu.roll(packed, (1 - b) % TILE, 1)
            for q in range(4):
                part = moved[GROUPS * (q // 2) : GROUPS * (q // 2 + 1)]
                pieces.append(jnp.where((lane >= PITCH) == (q % 2 == 1), part, zeros))
        lines.append(jnp.concatenate(pieces + [fill], axis=0).astype(bf16))
    for r in range(0, rows, 2):
        both = dot_nt(spread, jnp.concatenate(lines[r : r + 2], axis=0))
        for i in range(2):
            at = (r + i) * WINDOW
            looked[at : at + WINDOW, :] = both[:, i * HID_CH : (i + 1) * HID_CH]
    sub = lax.broadcasted_iota(jnp.int32, (HID_CH, HID_CH), 0)
    ends = jnp.where((sub == PACK + 24) | (sub == PACK + 25), feature_scale, 0.0).astype(bf16)
    blank = jnp.zeros((EDGE, HID_CH), f32)
    level[:EDGE, :] = blank
    level[EDGE + WINDOW * rows :, :] = blank
    level[EDGE : EDGE + WINDOW * rows, :] = dot(looked[...].astype(bf16), ends)
    line[...] = jnp.zeros_like(line)
    keep(line, taps, 0, hidden_at[...])

    for t in range(ITERS):
        low, high = 1 + 2 * t, rows - 2 - 2 * t
        at, length = (low - 1) * WINDOW, (high - low + 3) * WINDOW
        lane_at = lax.broadcasted_iota(jnp.int32, (length, HID_CH), 1)
        tap, channel = lane_at // PACK, lane_at % PACK
        near = [level[EDGE + at + b : EDGE + at + b + length, :] for b in (-1, 0, 1)]
        value = jnp.where(tap == 0, near[0], jnp.where(tap == 1, near[1], near[2]))
        at_lookup = (channel >= t * GROUPS) & (channel < (t + 1) * GROUPS)
        value = jnp.where(
            (channel == 3 * GROUPS) & (tap < 3),
            value,
            jnp.where(at_lookup, looked[at : at + length, :], 0.0),
        )
        inputs[at : at + length, :] = value.astype(bf16)

        at, length = low * WINDOW, (high - low + 1) * WINDOW
        lhs = around(taps, at, length) + around(inputs, at, length)
        both = dot(jnp.concatenate(lhs, axis=1), weight[:, : 2 * HID_CH])
        gate[at + WINDOW : at + length - WINDOW, :] = (
            0.5 * jnp.tanh(0.5 * both[WINDOW : length - WINDOW, :HID_CH]) + 0.5
        )
        reset = 0.5 * jnp.tanh(0.5 * both[:, HID_CH:]) + 0.5
        keep(line, reset_taps, at, reset * hidden_at[at : at + length, :])

        at, length = at + WINDOW, length - 2 * WINDOW
        lhs = around(reset_taps, at, length) + around(inputs, at, length)
        candidate = jnp.tanh(dot(jnp.concatenate(lhs, axis=1), weight[:, 2 * HID_CH :]))
        hidden = hidden_at[at : at + length, :]
        hidden = hidden + gate[at : at + length, :] * (candidate - hidden)
        pixel = lax.broadcasted_iota(jnp.int32, (length, HID_CH), 0)
        column, row = pixel % WINDOW + first, pixel // WINDOW + (low + 1 + first_row)
        inside = ((column >= 0) | (disp > 0)) & ((column < TILE) | (disp < disps - 1))
        inside = inside & (row >= 0) & (row < bands)
        hidden = jnp.where(inside, hidden, 0.0).astype(bf16)
        level[EDGE + at : EDGE + at + length, :] += dot_nt(hidden, heads[...])
        hidden_at[at : at + length, :] = hidden.astype(f32)
        if t < ITERS - 1:
            keep(line, taps, at, hidden.astype(f32))

    lane = lax.broadcasted_iota(jnp.int32, (strip, HID_CH), 1)
    for r in range(QUAD):
        at = (REACH + r) * WINDOW + EDGE
        hidden = hidden_at[at : at + strip, :]
        value = level[EDGE + at : EDGE + at + strip, :] * (1.0 / feature_scale)
        high = value.astype(bf16).astype(f32)
        middle = (value - high).astype(bf16).astype(f32)
        parts = jnp.where(lane == 0, high, jnp.where(lane == 1, middle, value - high - middle))
        parts = jnp.where(lane < 3, parts, 0.0)
        blocks[r] = jnp.concatenate([hidden, parts], axis=0).astype(bf16)
    for i, out in zip(ORDER, (out_0, out_1, out_2, out_3)):
        out[...] = blocks[member ^ i]


def unpack_kernel(from_0, from_1, from_2, from_3, disparity_out, hidden_out, blocks):
    for i, block in enumerate((from_0, from_1, from_2, from_3)):
        blocks[i] = block[...]
    place = position()
    member = place[0] % QUAD
    slots = [slot_of(strip_at(place, strip) ^ member) for strip in range(QUAD)]
    held = [blocks[slot].astype(f32) for slot in slots]
    hidden_out[0] = jnp.concatenate([block[:STRIP] for block in held], axis=0).astype(bf16)
    parts = jnp.concatenate([block[STRIP:] for block in held], axis=0).T
    disparity_out[...] = parts[0:1] + parts[1:2] + parts[2:3]


def in_hbm(value):
    return pltpu.with_memory_space_constraint(value, pltpu.HBM)


def to_sides(value):
    disps = lax.axis_size("disp")
    right = [(d, d + 1) for d in range(disps - 1)]
    left = [(d + 1, d) for d in range(disps - 1)]
    if disps == 2:
        return lax.ppermute(value, "disp", right + left)[None]
    return jnp.stack([lax.ppermute(value, "disp", right), lax.ppermute(value, "disp", left)])


def in_group(blocks):
    return [blocks[0]] + [
        to_rows(block, lambda band, i=i: band ^ i)
        for i, block in list(zip(ORDER, blocks))[1:]
    ]


def to_layers(value, partner):
    groups = lax.axis_size("band") // QUAD
    if not any(0 <= partner(g) < groups for g in range(groups)):
        return None
    return to_rows(value, lambda band: partner(band // QUAD) * QUAD + band % QUAD)


def to_rows(value, shift):
    bands = lax.axis_size("band")
    return lax.ppermute(
        value, "band", [(i, shift(i)) for i in range(bands) if 0 <= shift(i) < bands]
    )


def odd_pair(i):
    return i ^ 1


def even_pair(i):
    return i - 1 if i % 2 == 0 else i + 1


def local(
    feat_left,
    feat_right,
    limit,
    indices,
    hidden_start,
    vol_kernel,
    group_gain,
    hid_kernel,
    in_kernel,
    head_weight,
):
    bands, disps = lax.axis_size("band"), lax.axis_size("disp")
    vmem = pl.BlockSpec(memory_space=pltpu.VMEM)
    hbm = pl.BlockSpec(memory_space=pltpu.HBM)
    padded = (DISPS + 2) * GROUPS

    feats = jnp.concatenate([feat_left[0], feat_right[0]], axis=0)
    even_own, odd_own = to_rows(feats, even_pair), to_rows(feats, odd_pair)
    across = to_sides(feats)
    raw_own, kernel_held, marks, gains, heads = pl.pallas_call(
        own_row_kernel,
        out_shape=(
            jax.ShapeDtypeStruct((padded, 2 * TILE), bf16),
            jax.ShapeDtypeStruct((27, GROUPS, GROUPS), bf16),
            jax.ShapeDtypeStruct((GROUPS, TILE), jnp.int32),
            jax.ShapeDtypeStruct((GROUPS, TILE), f32),
            jax.ShapeDtypeStruct((HID_CH, HID_CH), bf16),
        ),
        in_specs=[vmem, vmem] + [hbm] * 5,
        out_specs=(vmem,) * 5,
        scratch_shapes=[
            pltpu.VMEM((padded, TILE), f32),
            pltpu.VMEM((padded, TILE), f32),
            pltpu.VMEM((1, TILE), jnp.int32),
            pltpu.VMEM((ITERS, 1, TILE), jnp.int32),
            pltpu.SMEM((GROUPS,), f32),
            pltpu.VMEM((1, HID_CH), bf16),
            pltpu.VMEM((27, GROUPS, GROUPS), bf16),
            pltpu.SemaphoreType.DMA((5,)),
        ],
        compiler_params=pltpu.CompilerParams(vmem_limit_bytes=16 * 2**20),
        cost_estimate=pl.CostEstimate(flops=2 * 10**9, bytes_accessed=4 * 2**20, transcendentals=0),
    )(
        feats, across, in_hbm(limit), in_hbm(indices), in_hbm(group_gain),
        in_hbm(head_weight.reshape(1, HID_CH)), in_hbm(vol_kernel.reshape(27, GROUPS, GROUPS)),
    )
    hidden = hidden_start[0]
    hidden_across = to_sides(hidden)
    even_own, odd_own, raw_own, hidden_across = lax.optimization_barrier(
        (even_own, odd_own, raw_own, hidden_across)
    )
    taps = pl.pallas_call(
        toeplitz_kernel,
        out_shape=jax.ShapeDtypeStruct((3 * OUT_SLAB, 3 * SLAB), bf16),
        in_specs=[vmem],
        out_specs=vmem,
        compiler_params=pltpu.CompilerParams(vmem_limit_bytes=8 * 2**20),
        cost_estimate=pl.CostEstimate(flops=10**9, bytes_accessed=2**20, transcendentals=0),
    )(kernel_held)
    marks_across = to_sides(marks)
    even_across, odd_across = to_sides(even_own), to_sides(odd_own)

    in_weight = jnp.concatenate(
        [in_kernel[:, :, :GROUPS]] * ITERS + [in_kernel[:, :, GROUPS:]], axis=2
    )
    in_weight = jnp.pad(in_weight, ((0, 0), (0, 1), (0, PACK - in_weight.shape[2]), (0, 0)))
    in_weight = in_weight.reshape(3 * HID_CH, 3 * HID_CH)

    blocks = pl.pallas_call(
        volume_kernel,
        out_shape=(jax.ShapeDtypeStruct((BLOCK_ROWS, TILE), bf16),) * QUAD,
        in_specs=[vmem] * 9 + [hbm, hbm],
        out_specs=(vmem,) * QUAD,
        scratch_shapes=[
            pltpu.VMEM((padded, 2 * TILE), bf16),
            pltpu.VMEM((3 * OUT_SLAB, 3 * SLAB), bf16),
            pltpu.VMEM((2, padded, TILE), f32),
            pltpu.VMEM((2, padded, TILE), f32),
            pltpu.VMEM((2, DISPS, TILE), f32),
            pltpu.VMEM((TILE + 2 * EDGE, HID_CH), f32),
            pltpu.VMEM((QUAD, BLOCK_ROWS, TILE), bf16),
            pltpu.SemaphoreType.DMA((2,)),
        ],
        compiler_params=pltpu.CompilerParams(vmem_limit_bytes=24 * 2**20),
        cost_estimate=pl.CostEstimate(
            flops=5 * 10**9, bytes_accessed=16 * 2**20, transcendentals=DISPS * TILE
        ),
    )(
        gains, even_own, even_across, odd_own, odd_across,
        marks, marks_across, hidden, hidden_across, raw_own, taps,
    )

    weight = pl.pallas_call(
        weight_kernel,
        out_shape=jax.ShapeDtypeStruct((12 * HID_CH, 3 * HID_CH), bf16),
        in_specs=[vmem, vmem],
        out_specs=vmem,
        compiler_params=pltpu.CompilerParams(vmem_limit_bytes=8 * 2**20),
        cost_estimate=pl.CostEstimate(flops=10**8, bytes_accessed=2**20, transcendentals=0),
    )(hid_kernel.reshape(9 * HID_CH, 3 * HID_CH), in_weight)
    own, weight = lax.optimization_barrier((jnp.stack(in_group(blocks)), weight))
    around = [
        to_layers(own, lambda g: g ^ 2),
        to_layers(own, lambda g: (g - 2 ^ 2) + 2),
        to_layers(own, lambda g: g ^ 1),
        to_layers(own, lambda g: (g - 1 ^ 1) + 1),
    ]
    if around[1] is None:
        around[1] = around[0]

    pixels = WINDOW * AROUND
    refined = pl.pallas_call(
        refine_kernel,
        out_shape=(jax.ShapeDtypeStruct((2 * STRIP, HID_CH), bf16),) * QUAD,
        in_specs=[vmem] * 7,
        out_specs=(vmem,) * QUAD,
        scratch_shapes=[
            pltpu.VMEM((pixels + 2 * EDGE, HID_CH), f32),
            pltpu.VMEM((pixels, HID_CH), f32),
            pltpu.VMEM((pixels, HID_CH), f32),
            pltpu.VMEM((pixels, 3 * HID_CH), bf16),
            pltpu.VMEM((pixels, 3 * HID_CH), bf16),
            pltpu.VMEM((pixels, HID_CH), bf16),
            pltpu.VMEM((pixels, HID_CH), f32),
            pltpu.VMEM((pixels + 2 * EDGE, HID_CH), f32),
            pltpu.VMEM((QUAD, 2 * STRIP, HID_CH), bf16),
        ],
        compiler_params=pltpu.CompilerParams(vmem_limit_bytes=32 * 2**20),
    )(
        own, *around,
        weight, heads,
    )
    disparity, hidden = pl.pallas_call(
        unpack_kernel,
        out_shape=(
            jax.ShapeDtypeStruct((1, TILE), f32),
            jax.ShapeDtypeStruct((1, TILE, HID_CH), bf16),
        ),
        in_specs=[vmem] * QUAD,
        out_specs=(vmem, vmem),
        scratch_shapes=[pltpu.VMEM((QUAD, 2 * STRIP, HID_CH), bf16)],
        compiler_params=pltpu.CompilerParams(vmem_limit_bytes=4 * 2**20),
    )(*in_group(refined))
    return (disparity, hidden)


def solution(mesh):
    in_specs = (
        P("band", None, "disp"),
        P("band", None, "disp"),
        P("band", "disp"),
        P(None, "band", "disp"),
        P("band", "disp", None),
        P(),
        P(),
        P(),
        P(),
        P(),
    )
    out_specs = (P("band", "disp"), P("band", "disp", None))
    return jax.shard_map(local, mesh=mesh, in_specs=in_specs, out_specs=out_specs, check_vma=False)
```

```python
import jax
import jax.numpy as jnp
from jax import lax
from jax.experimental import pallas as pl
from jax.experimental.pallas import tpu as pltpu
from jax.sharding import PartitionSpec as P

GROUPS = 8
DISPS = 96
FEAT_CH = 96
HID_CH = 128
ITERS = 3
TILE = 128
REACH = 2 * ITERS
EDGE = 8
QUAD = 4
STRIP = TILE // QUAD
WINDOW = STRIP + 2 * EDGE
PACK = 32
PITCH = 64
ORDER = (0, 3, 1, 2)
BLOCK_ROWS = WINDOW + 2 * GROUPS
AROUND = QUAD + 2 * REACH
BLOCK = 8
SLAB = (BLOCK + 2) * GROUPS
OUT_SLAB = BLOCK * GROUPS

pixel_unit = 8.0
feature_scale = 0.25
floor_logit = -1e30

f32 = jnp.float32
bf16 = jnp.bfloat16


def position():
    return (
        lax.axis_index("band"), lax.axis_index("disp"),
        lax.axis_size("band"), lax.axis_size("disp"),
    )


def dot(a, b):
    return jnp.dot(a, b, preferred_element_type=f32)


def dot_nt(a, b):
    return lax.dot_general(a, b, (((1,), (1,)), ((), ())), preferred_element_type=f32)


def copy_all(copies):
    for copy in copies:
        copy.start()
    for copy in copies:
        copy.wait()


def toeplitz(vol_kernel):
    size = 27 * GROUPS
    flat = vol_kernel[...].astype(f32).reshape(size, GROUPS)
    flat = jnp.concatenate([flat, jnp.zeros((size, TILE - GROUPS), f32)], axis=1).T[:GROUPS]
    row = lax.broadcasted_iota(jnp.int32, (9 * GROUPS, size), 0) >> 3
    tap = lax.broadcasted_iota(jnp.int32, (9 * GROUPS, size), 1) >> 3
    tap_a = (tap >= 9).astype(jnp.int32) + (tap >= 18).astype(jnp.int32)
    within = tap - 9 * tap_a
    tap_b = (within >= 3).astype(jnp.int32) + (within >= 6).astype(jnp.int32)
    tap_e = within - 3 * tap_b
    pairs = jnp.where(
        row == 3 * tap_a + tap_e, jnp.concatenate([flat] * 9, axis=0), 0.0
    ).astype(bf16)
    from_row = lax.broadcasted_iota(jnp.int32, (size, 3 * SLAB), 0)
    to = lax.broadcasted_iota(jnp.int32, (size, 3 * SLAB), 1)
    from_tap = from_row >> 3
    from_in = from_tap - 9 * ((from_tap >= 9).astype(jnp.int32) + (from_tap >= 18).astype(jnp.int32))
    from_b = (from_in >= 3).astype(jnp.int32) + (from_in >= 6).astype(jnp.int32)
    to_b = (to >= SLAB).astype(jnp.int32) + (to >= 2 * SLAB).astype(jnp.int32)
    repeat = jnp.where((from_b == to_b) & ((from_row & 7) == (to & 7)), 1.0, 0.0).astype(bf16)
    spread = dot(pairs, repeat)
    to = lax.broadcasted_iota(jnp.int32, (GROUPS, 3 * SLAB), 1)
    to_b = (to >= SLAB).astype(jnp.int32) + (to >= 2 * SLAB).astype(jnp.int32)
    to_d = (to - SLAB * to_b) >> 3
    rows = []
    for e in range(3):
        for d in range(BLOCK):
            value = jnp.zeros((GROUPS, 3 * SLAB), f32)
            for a in range(3):
                at = (3 * a + e) * GROUPS
                value = jnp.where(to_d == d + a, spread[at : at + GROUPS], value)
            rows.append(value)
    return jnp.concatenate(rows, axis=0).astype(bf16)


def interleaved(values):
    stacked = jnp.swapaxes(jnp.stack(values), 0, 1)
    return stacked.reshape(values[0].shape[0] * len(values), values[0].shape[1])


def toeplitz_kernel(vol_kernel, out):
    out[...] = toeplitz(vol_kernel)


def correlate(lefts, rights, place, row_ok, wide, extra):
    has_left = (place[1] > 0).astype(f32)
    has_right = (place[1] < place[3] - 1).astype(f32)
    lane = lax.broadcasted_iota(jnp.int32, (TILE, TILE), 1)
    sub = lax.broadcasted_iota(jnp.int32, (TILE, TILE), 0)
    flip = jnp.where(lane + sub == TILE - 1, 1.0, 0.0).astype(bf16)
    per_group = FEAT_CH // GROUPS
    channel = lax.broadcasted_iota(jnp.int32, (32, FEAT_CH), 1)
    group_masks = [
        (channel >= g * per_group) & (channel < (g + 1) * per_group) for g in range(GROUPS)
    ]
    lane96 = lax.broadcasted_iota(jnp.int32, (FEAT_CH, TILE), 1)
    zero_slab = jnp.zeros((GROUPS, TILE), f32)
    for at in (0, (DISPS + 1) * GROUPS):
        wide[pl.ds(at, GROUPS), :] = zero_slab
        extra[pl.ds(at, GROUPS), :] = zero_slab

    own_t = (lefts[1] * row_ok).T
    side_t = jnp.where(
        lane96 < EDGE,
        lefts[2] * (has_right * row_ok),
        jnp.where(lane96 >= TILE - EDGE, lefts[0] * (has_left * row_ok), 0.0),
    ).T
    sources = jnp.concatenate([rights[2] * has_right, rights[1], rights[0] * has_left], axis=0)
    flipped = dot(sources.astype(bf16), flip)
    reverse = jnp.concatenate(
        [flipped[i * FEAT_CH : (i + 1) * FEAT_CH] for i in range(3)], axis=1
    )
    windows = [
        reverse[:, 2 * TILE - 32 - 32 * k : 3 * TILE - 32 - 32 * k].astype(bf16)
        for k in range(-1, 5)
    ]

    def by_group(rows):
        count = rows.shape[0]
        parts = [jnp.where(m[:count], rows, 0.0) for m in group_masks]
        return jnp.concatenate(parts, axis=0).astype(bf16)

    def shear(product, g, count, first):
        rows = product[count * g : count * g + count]
        return pltpu.roll(rows, TILE - 31 + first, 1, stride=1, stride_axis=0)

    products = [
        dot(by_group(own_t[32 * k : 32 * k + 32]), windows[k + 1]) for k in range(TILE // 32)
    ]
    after = dot(by_group(side_t[:EDGE]), windows[5])
    before = dot(by_group(side_t[TILE - EDGE :]), windows[0])
    parts, sides = [], []
    for g in range(GROUPS):
        part = jnp.concatenate([shear(product, g, 32, 0) for product in products], axis=0)
        parts.append(part.T[:DISPS])
        sides += [shear(after, g, EDGE, 0), shear(before, g, EDGE, 32 - EDGE)]
    part = jnp.concatenate(sides, axis=0).T[:DISPS]
    sides = [part if g == 0 else pltpu.roll(part, TILE - 2 * EDGE * g, 1) for g in range(GROUPS)]
    for target, values in ((wide, parts), (extra, sides)):
        target[GROUPS : GROUPS + DISPS * GROUPS, :] = interleaved(values) * (1.0 / per_group)


def own_row_kernel(
    own, across, limit, indices, gain, head, vol_kernel, raw_out, kernel_out, marks_out,
    gains_out, heads_out, wide, extra, limits, index_rows, gain_held, head_held, kernel, sems,
):
    place = position()
    copies = [
        pltpu.make_async_copy(source, target, sems.at[i])
        for i, (source, target) in enumerate(
            (
                (limit, limits), (indices, index_rows), (gain, gain_held), (head, head_held),
                (vol_kernel, kernel),
            )
        )
    ]
    for copy in copies:
        copy.start()
    tiles = [across[0], own[...], across[across.shape[0] - 1]]
    tiles = [tile.astype(f32) for tile in tiles]
    correlate(
        [tile[:FEAT_CH] for tile in tiles], [tile[FEAT_CH:] for tile in tiles],
        place, 1.0, wide, extra,
    )
    raw_out[...] = jnp.concatenate([wide[...], extra[...]], axis=1).astype(bf16)
    for copy in copies:
        copy.wait()
    marks = [limits[...]] + [index_rows[t] for t in range(ITERS)]
    blank = jnp.zeros((GROUPS - len(marks), TILE), jnp.int32)
    marks_out[...] = jnp.concatenate(marks + [blank], axis=0)
    group_at = lax.broadcasted_iota(jnp.int32, (GROUPS, TILE), 0)
    gains = jnp.zeros((GROUPS, TILE), f32)
    for g in range(GROUPS):
        gains = jnp.where(group_at == g, gain_held[g], gains)
    gains_out[...] = gains
    heads = head_held[...].astype(f32) * feature_scale
    heads_out[...] = jnp.broadcast_to(heads, heads_out.shape).astype(bf16)
    kernel_out[...] = kernel[...]


def volume_kernel(
    gains, odd_own, odd_across, even_own, even_across, marks, marks_across, hidden,
    hidden_across, raw_own, taps_own, out_0, out_1, out_2, out_3, raw, taps, wide, extra, logit, padded, blocks, sems,
):
    place = position()
    band, bands = place[0], place[2]
    is_even = band % 2 == 0
    copies = [
        pltpu.make_async_copy(raw_own, raw, sems.at[0]),
        pltpu.make_async_copy(taps_own, taps, sems.at[1]),
    ]
    for copy in copies:
        copy.start()

    last = odd_across.shape[0] - 1
    odd = [tile.astype(f32) for tile in (odd_across[0], odd_own[...], odd_across[last])]
    even = [tile.astype(f32) for tile in (even_across[0], even_own[...], even_across[last])]
    for b in range(2):
        row = band + 2 * b - 1
        row_ok = ((row >= 0) & (row < bands)).astype(f32)
        tiles = [
            jnp.where(is_even, y, x) if b == 0 else jnp.where(is_even, x, y)
            for x, y in zip(odd, even)
        ]
        correlate(
            [tile[:FEAT_CH] for tile in tiles], [tile[FEAT_CH:] for tile in tiles],
            place, row_ok, wide.at[b], extra.at[b],
        )
    for copy in copies:
        copy.wait()

    lane = lax.broadcasted_iota(jnp.int32, (GROUPS, TILE), 1)
    left_marks = pltpu.roll(marks_across[0], 2 * EDGE, 1)
    levels_of = [marks[...], jnp.where(lane < EDGE, marks_across[last], left_marks)]
    lane8 = lax.broadcasted_iota(jnp.int32, (OUT_SLAB, TILE), 1)
    group_at = lax.broadcasted_iota(jnp.int32, (GROUPS, TILE), 0)
    wanted = [
        [jnp.broadcast_to(rows[t + 1 : t + 2], (GROUPS, TILE)) for t in range(ITERS)]
        for rows in levels_of
    ]
    found = [[jnp.zeros((GROUPS, TILE), f32) for _ in range(ITERS)] for _ in range(2)]
    for q in range(DISPS // BLOCK):
        at = q * OUT_SLAB
        slabs = [
            jnp.concatenate(
                [wide[b, at : at + SLAB, :], extra[b, at : at + SLAB, :]], axis=1
            ).astype(bf16)
            for b in range(2)
        ]
        slabs.insert(1, raw[at : at + SLAB, :])
        product = dot(taps[...], jnp.concatenate(slabs, axis=0))
        halves = [product[:, :TILE], product[:, TILE:]]
        first = [half[:OUT_SLAB] for half in halves]
        middle = [half[OUT_SLAB : 2 * OUT_SLAB] for half in halves]
        after = [half[2 * OUT_SLAB :] for half in halves]
        first_on = pltpu.roll(first[0], 1, 1)
        convs = [
            middle[0]
            + jnp.where(lane8 == 0, pltpu.roll(first[1], TILE - 2 * EDGE + 1, 1), first_on)
            + jnp.where(
                lane8 == TILE - 1,
                pltpu.roll(after[1], TILE - 1, 1),
                pltpu.roll(after[0], TILE - 1, 1),
            ),
            middle[1]
            + jnp.where(lane8 == 0, first_on, pltpu.roll(first[1], 1, 1))
            + jnp.where(
                lane8 == 2 * EDGE - 1,
                pltpu.roll(after[0], 2 * EDGE - 1, 1),
                pltpu.roll(after[1], TILE - 1, 1),
            ),
        ]
        centre = slabs[1].astype(f32)[GROUPS : GROUPS + OUT_SLAB]
        for i in range(2):
            volume = centre[:, i * TILE : (i + 1) * TILE] + jnp.maximum(convs[i], 0.0)
            volume = volume.astype(bf16).astype(f32).reshape(BLOCK, GROUPS, TILE)
            logit[i, q * BLOCK : (q + 1) * BLOCK, :] = jnp.sum(volume * gains[...][None], axis=1)
            for d in range(BLOCK):
                for t in range(ITERS):
                    hit = wanted[i][t] == q * BLOCK + d
                    found[i][t] = found[i][t] + jnp.where(hit, volume[d], 0.0)

    level = lax.broadcasted_iota(jnp.int32, (DISPS, TILE), 0)
    for i in range(2):
        valid = level < levels_of[i][0:1]
        masked = jnp.where(valid, logit[i], floor_logit)
        top = jnp.max(masked, axis=0, keepdims=True)
        weights = jnp.where(valid, jnp.exp(masked - top), 0.0)
        moment = jnp.sum(weights * level.astype(f32), axis=0, keepdims=True)
        start = moment / jnp.sum(weights, axis=0, keepdims=True) / pixel_unit
        high = start.astype(bf16).astype(f32)
        low = (start - high).astype(bf16).astype(f32)
        ends = jnp.where(
            group_at == 0,
            jnp.broadcast_to(high, (GROUPS, TILE)),
            jnp.where(group_at == 1, jnp.broadcast_to(low, (GROUPS, TILE)), 0.0),
        )
        found[i].append(ends)
    has_left, has_right = place[1] > 0, place[1] < place[3] - 1
    is_beside = ((lane < EDGE) & has_right) | ((lane >= EDGE) & (lane < 2 * EDGE) & has_left)
    packed, packed_beside = found[0], [jnp.where(is_beside, x, 0.0) for x in found[1]]

    before = hidden_across[0, TILE - 2 * EDGE :, :].astype(f32)[EDGE:]
    after = hidden_across[last, : 2 * EDGE, :].astype(f32)[:EDGE]
    padded[:EDGE, :] = jnp.where(has_left, before, 0.0)
    padded[EDGE : EDGE + TILE, :] = hidden[...].astype(f32)
    padded[EDGE + TILE :, :] = jnp.where(has_right, after, 0.0)
    for strip in range(QUAD):
        block = [padded[STRIP * strip : STRIP * strip + WINDOW, :]]
        for half in range(2):
            part = jnp.zeros((GROUPS, TILE), f32)
            for i in range(2):
                q, base = 2 * half + i, PITCH * i
                at = lane - base
                moved = pltpu.roll(packed[q], (base + EDGE - STRIP * strip) % TILE, 1)
                if strip == 0:
                    other = pltpu.roll(packed_beside[q], (base - EDGE) % TILE, 1)
                    moved = jnp.where(at < EDGE, other, moved)
                if strip == QUAD - 1:
                    other = pltpu.roll(packed_beside[q], base + WINDOW - EDGE, 1)
                    moved = jnp.where(at >= WINDOW - EDGE, other, moved)
                part = jnp.where((at >= 0) & (at < WINDOW), moved, part)
            block.append(part)
        blocks[strip] = jnp.concatenate(block, axis=0).astype(bf16)
    member = band % QUAD
    for i, out in zip(ORDER, (out_0, out_1, out_2, out_3)):
        out[...] = blocks[strip_at(place, member ^ i)]


def slot_of(member_xor):
    return jnp.where(member_xor == 0, 0, jnp.where(member_xor == 3, 1, member_xor + 1))


def strip_at(place, member):
    return jnp.where(place[1] % 2 == 0, member, QUAD - 1 - member)


def keep(line, target, at, values):
    length = values.shape[0]
    start = EDGE + at
    line[start : start + length, :] = values
    target[at : at + length, 0:HID_CH] = line[start - 1 : start - 1 + length, :].astype(bf16)
    target[at : at + length, HID_CH : 2 * HID_CH] = values.astype(bf16)
    target[at : at + length, 2 * HID_CH :] = line[start + 1 : start + 1 + length, :].astype(bf16)


def around(target, at, length):
    return [target[at + a * WINDOW : at + a * WINDOW + length, :] for a in (-1, 0, 1)]


def weight_kernel(hid_weight, in_weight, out):
    out[: 9 * HID_CH, :] = hid_weight[...]
    out[9 * HID_CH :, :] = in_weight[...]


def refine_kernel(
    own,
    near_b,
    near_a,
    far_d,
    far_c,
    weight,
    heads,
    out_0,
    out_1,
    out_2,
    out_3,
    line,
    looked,
    hidden_at,
    taps,
    reset_taps,
    inputs,
    gate,
    level,
    blocks,
):
    rows, strip = AROUND, STRIP
    place = position()
    band, disp, bands, disps = place
    member, layer = band % QUAD, band // QUAD
    at = strip_at(place, member)
    first = strip * at - EDGE
    first_row = layer * QUAD - REACH

    def block_of(r):
        step, row = (r + 2 * QUAD - REACH) // QUAD - 2, (r + 2 * QUAD - REACH) % QUAD
        slot = slot_of(row ^ member)
        if step == 0:
            return own[slot].astype(f32)
        if abs(step) == 1:
            choice, x, y = (layer % 2 == 0) == (step > 0), near_a, near_b
        else:
            choice, x, y = (layer % 4 < 2) == (step > 0), far_c, far_d
        inside = (first_row + r >= 0) & (first_row + r < bands)
        block = jnp.where(choice, x[slot].astype(f32), y[slot].astype(f32))
        return jnp.where(inside, block, 0.0)

    lane = lax.broadcasted_iota(jnp.int32, (GROUPS, TILE), 1)
    at_sub = lax.broadcasted_iota(jnp.int32, (WINDOW, TILE), 0)
    at_lane = lax.broadcasted_iota(jnp.int32, (WINDOW, TILE), 1)
    spread = jnp.where(at_sub == at_lane % PITCH, 1.0, 0.0).astype(bf16)
    fill = jnp.zeros((PACK, TILE), f32)
    zeros = jnp.zeros((GROUPS, TILE), f32)
    lines = []
    for r in range(rows):
        block = block_of(r)
        packed = block[WINDOW:]
        hidden_at[r * WINDOW : (r + 1) * WINDOW, :] = block[:WINDOW]
        pieces = []
        for b in range(3):
            moved = packed if b == 1 else pltpu.roll(packed, (1 - b) % TILE, 1)
            for q in range(4):
                part = moved[GROUPS * (q // 2) : GROUPS * (q // 2 + 1)]
                pieces.append(jnp.where((lane >= PITCH) == (q % 2 == 1), part, zeros))
        lines.append(jnp.concatenate(pieces + [fill], axis=0).astype(bf16))
    for r in range(0, rows, 2):
        both = dot_nt(spread, jnp.concatenate(lines[r : r + 2], axis=0))
        for i in range(2):
            at = (r + i) * WINDOW
            looked[at : at + WINDOW, :] = both[:, i * HID_CH : (i + 1) * HID_CH]
    sub = lax.broadcasted_iota(jnp.int32, (HID_CH, HID_CH), 0)
    ends = jnp.where((sub == PACK + 24) | (sub == PACK + 25), feature_scale, 0.0).astype(bf16)
    blank = jnp.zeros((EDGE, HID_CH), f32)
    level[:EDGE, :] = blank
    level[EDGE + WINDOW * rows :, :] = blank
    level[EDGE : EDGE + WINDOW * rows, :] = dot(looked[...].astype(bf16), ends)
    line[...] = jnp.zeros_like(line)
    keep(line, taps, 0, hidden_at[...])

    for t in range(ITERS):
        low, high = 1 + 2 * t, rows - 2 - 2 * t
        at, length = (low - 1) * WINDOW, (high - low + 3) * WINDOW
        lane_at = lax.broadcasted_iota(jnp.int32, (length, HID_CH), 1)
        tap, channel = lane_at // PACK, lane_at % PACK
        near = [level[EDGE + at + b : EDGE + at + b + length, :] for b in (-1, 0, 1)]
        value = jnp.where(tap == 0, near[0], jnp.where(tap == 1, near[1], near[2]))
        at_lookup = (channel >= t * GROUPS) & (channel < (t + 1) * GROUPS)
        value = jnp.where(
            (channel == 3 * GROUPS) & (tap < 3),
            value,
            jnp.where(at_lookup, looked[at : at + length, :], 0.0),
        )
        inputs[at : at + length, :] = value.astype(bf16)

        at, length = low * WINDOW, (high - low + 1) * WINDOW
        lhs = around(taps, at, length) + around(inputs, at, length)
        both = dot(jnp.concatenate(lhs, axis=1), weight[:, : 2 * HID_CH])
        gate[at + WINDOW : at + length - WINDOW, :] = (
            0.5 * jnp.tanh(0.5 * both[WINDOW : length - WINDOW, :HID_CH]) + 0.5
        )
        reset = 0.5 * jnp.tanh(0.5 * both[:, HID_CH:]) + 0.5
        keep(line, reset_taps, at, reset * hidden_at[at : at + length, :])

        at, length = at + WINDOW, length - 2 * WINDOW
        lhs = around(reset_taps, at, length) + around(inputs, at, length)
        candidate = jnp.tanh(dot(jnp.concatenate(lhs, axis=1), weight[:, 2 * HID_CH :]))
        hidden = hidden_at[at : at + length, :]
        hidden = hidden + gate[at : at + length, :] * (candidate - hidden)
        pixel = lax.broadcasted_iota(jnp.int32, (length, HID_CH), 0)
        column, row = pixel % WINDOW + first, pixel // WINDOW + (low + 1 + first_row)
        inside = ((column >= 0) | (disp > 0)) & ((column < TILE) | (disp < disps - 1))
        inside = inside & (row >= 0) & (row < bands)
        hidden = jnp.where(inside, hidden, 0.0).astype(bf16)
        level[EDGE + at : EDGE + at + length, :] += dot_nt(hidden, heads[...])
        hidden_at[at : at + length, :] = hidden.astype(f32)
        if t < ITERS - 1:
            keep(line, taps, at, hidden.astype(f32))

    lane = lax.broadcasted_iota(jnp.int32, (strip, HID_CH), 1)
    for r in range(QUAD):
        at = (REACH + r) * WINDOW + EDGE
        hidden = hidden_at[at : at + strip, :]
        value = level[EDGE + at : EDGE + at + strip, :] * (1.0 / feature_scale)
        high = value.astype(bf16).astype(f32)
        middle = (value - high).astype(bf16).astype(f32)
        parts = jnp.where(lane == 0, high, jnp.where(lane == 1, middle, value - high - middle))
        parts = jnp.where(lane < 3, parts, 0.0)
        blocks[r] = jnp.concatenate([hidden, parts], axis=0).astype(bf16)
    for i, out in zip(ORDER, (out_0, out_1, out_2, out_3)):
        out[...] = blocks[member ^ i]


def unpack_kernel(from_0, from_1, from_2, from_3, disparity_out, hidden_out, blocks):
    for i, block in enumerate((from_0, from_1, from_2, from_3)):
        blocks[i] = block[...]
    place = position()
    member = place[0] % QUAD
    slots = [slot_of(strip_at(place, strip) ^ member) for strip in range(QUAD)]
    held = [blocks[slot].astype(f32) for slot in slots]
    hidden_out[0] = jnp.concatenate([block[:STRIP] for block in held], axis=0).astype(bf16)
    parts = jnp.concatenate([block[STRIP:] for block in held], axis=0).T
    disparity_out[...] = parts[0:1] + parts[1:2] + parts[2:3]


def in_hbm(value):
    return pltpu.with_memory_space_constraint(value, pltpu.HBM)


def to_sides(value):
    disps = lax.axis_size("disp")
    right = [(d, d + 1) for d in range(disps - 1)]
    left = [(d + 1, d) for d in range(disps - 1)]
    if disps == 2:
        return lax.ppermute(value, "disp", right + left)[None]
    return jnp.stack([lax.ppermute(value, "disp", right), lax.ppermute(value, "disp", left)])


def in_group(blocks):
    return [blocks[0]] + [
        to_rows(block, lambda band, i=i: band ^ i)
        for i, block in list(zip(ORDER, blocks))[1:]
    ]


def to_layers(value, partner):
    groups = lax.axis_size("band") // QUAD
    if not any(0 <= partner(g) < groups for g in range(groups)):
        return None
    return to_rows(value, lambda band: partner(band // QUAD) * QUAD + band % QUAD)


def to_rows(value, shift):
    bands = lax.axis_size("band")
    return lax.ppermute(
        value, "band", [(i, shift(i)) for i in range(bands) if 0 <= shift(i) < bands]
    )


def odd_pair(i):
    return i ^ 1


def even_pair(i):
    return i - 1 if i % 2 == 0 else i + 1


def local(
    feat_left,
    feat_right,
    limit,
    indices,
    hidden_start,
    vol_kernel,
    group_gain,
    hid_kernel,
    in_kernel,
    head_weight,
):
    bands, disps = lax.axis_size("band"), lax.axis_size("disp")
    vmem = pl.BlockSpec(memory_space=pltpu.VMEM)
    hbm = pl.BlockSpec(memory_space=pltpu.HBM)
    padded = (DISPS + 2) * GROUPS

    feats = jnp.concatenate([feat_left[0], feat_right[0]], axis=0)
    odd_own, even_own = to_rows(feats, odd_pair), to_rows(feats, even_pair)
    across = to_sides(feats)
    raw_own, kernel_held, marks, gains, heads = pl.pallas_call(
        own_row_kernel,
        out_shape=(
            jax.ShapeDtypeStruct((padded, 2 * TILE), bf16),
            jax.ShapeDtypeStruct((27, GROUPS, GROUPS), bf16),
            jax.ShapeDtypeStruct((GROUPS, TILE), jnp.int32),
            jax.ShapeDtypeStruct((GROUPS, TILE), f32),
            jax.ShapeDtypeStruct((HID_CH, HID_CH), bf16),
        ),
        in_specs=[vmem, vmem] + [hbm] * 5,
        out_specs=(vmem,) * 5,
        scratch_shapes=[
            pltpu.VMEM((padded, TILE), f32),
            pltpu.VMEM((padded, TILE), f32),
            pltpu.VMEM((1, TILE), jnp.int32),
            pltpu.VMEM((ITERS, 1, TILE), jnp.int32),
            pltpu.SMEM((GROUPS,), f32),
            pltpu.VMEM((1, HID_CH), bf16),
            pltpu.VMEM((27, GROUPS, GROUPS), bf16),
            pltpu.SemaphoreType.DMA((5,)),
        ],
        compiler_params=pltpu.CompilerParams(vmem_limit_bytes=16 * 2**20),
        cost_estimate=pl.CostEstimate(flops=2 * 10**9, bytes_accessed=4 * 2**20, transcendentals=0),
    )(
        feats, across, in_hbm(limit), in_hbm(indices), in_hbm(group_gain),
        in_hbm(head_weight.reshape(1, HID_CH)), in_hbm(vol_kernel.reshape(27, GROUPS, GROUPS)),
    )
    hidden = hidden_start[0]
    hidden_across = to_sides(hidden)
    odd_own, even_own, raw_own, hidden_across = lax.optimization_barrier(
        (odd_own, even_own, raw_own, hidden_across)
    )
    taps = pl.pallas_call(
        toeplitz_kernel,
        out_shape=jax.ShapeDtypeStruct((3 * OUT_SLAB, 3 * SLAB), bf16),
        in_specs=[vmem],
        out_specs=vmem,
        compiler_params=pltpu.CompilerParams(vmem_limit_bytes=8 * 2**20),
        cost_estimate=pl.CostEstimate(flops=10**9, bytes_accessed=2**20, transcendentals=0),
    )(kernel_held)
    marks_across = to_sides(marks)
    odd_across, even_across = to_sides(odd_own), to_sides(even_own)

    in_weight = jnp.concatenate(
        [in_kernel[:, :, :GROUPS]] * ITERS + [in_kernel[:, :, GROUPS:]], axis=2
    )
    in_weight = jnp.pad(in_weight, ((0, 0), (0, 1), (0, PACK - in_weight.shape[2]), (0, 0)))
    in_weight = in_weight.reshape(3 * HID_CH, 3 * HID_CH)

    blocks = pl.pallas_call(
        volume_kernel,
        out_shape=(jax.ShapeDtypeStruct((BLOCK_ROWS, TILE), bf16),) * QUAD,
        in_specs=[vmem] * 9 + [hbm, hbm],
        out_specs=(vmem,) * QUAD,
        scratch_shapes=[
            pltpu.VMEM((padded, 2 * TILE), bf16),
            pltpu.VMEM((3 * OUT_SLAB, 3 * SLAB), bf16),
            pltpu.VMEM((2, padded, TILE), f32),
            pltpu.VMEM((2, padded, TILE), f32),
            pltpu.VMEM((2, DISPS, TILE), f32),
            pltpu.VMEM((TILE + 2 * EDGE, HID_CH), f32),
            pltpu.VMEM((QUAD, BLOCK_ROWS, TILE), bf16),
            pltpu.SemaphoreType.DMA((2,)),
        ],
        compiler_params=pltpu.CompilerParams(vmem_limit_bytes=24 * 2**20),
        cost_estimate=pl.CostEstimate(
            flops=5 * 10**9, bytes_accessed=16 * 2**20, transcendentals=DISPS * TILE
        ),
    )(
        gains, odd_own, odd_across, even_own, even_across,
        marks, marks_across, hidden, hidden_across, raw_own, taps,
    )

    weight = pl.pallas_call(
        weight_kernel,
        out_shape=jax.ShapeDtypeStruct((12 * HID_CH, 3 * HID_CH), bf16),
        in_specs=[vmem, vmem],
        out_specs=vmem,
        compiler_params=pltpu.CompilerParams(vmem_limit_bytes=8 * 2**20),
        cost_estimate=pl.CostEstimate(flops=10**8, bytes_accessed=2**20, transcendentals=0),
    )(hid_kernel.reshape(9 * HID_CH, 3 * HID_CH), in_weight)
    own, weight = lax.optimization_barrier((jnp.stack(in_group(blocks)), weight))
    around = [
        to_layers(own, lambda g: (g - 1 ^ 1) + 1),
        to_layers(own, lambda g: g ^ 1),
        to_layers(own, lambda g: (g - 2 ^ 2) + 2),
        to_layers(own, lambda g: g ^ 2),
    ]
    if around[2] is None:
        around[2] = around[3]

    pixels = WINDOW * AROUND
    refined = pl.pallas_call(
        refine_kernel,
        out_shape=(jax.ShapeDtypeStruct((2 * STRIP, HID_CH), bf16),) * QUAD,
        in_specs=[vmem] * 7,
        out_specs=(vmem,) * QUAD,
        scratch_shapes=[
            pltpu.VMEM((pixels + 2 * EDGE, HID_CH), f32),
            pltpu.VMEM((pixels, HID_CH), f32),
            pltpu.VMEM((pixels, HID_CH), f32),
            pltpu.VMEM((pixels, 3 * HID_CH), bf16),
            pltpu.VMEM((pixels, 3 * HID_CH), bf16),
            pltpu.VMEM((pixels, HID_CH), bf16),
            pltpu.VMEM((pixels, HID_CH), f32),
            pltpu.VMEM((pixels + 2 * EDGE, HID_CH), f32),
            pltpu.VMEM((QUAD, 2 * STRIP, HID_CH), bf16),
        ],
        compiler_params=pltpu.CompilerParams(vmem_limit_bytes=32 * 2**20),
    )(
        own, *around,
        weight, heads,
    )
    disparity, hidden = pl.pallas_call(
        unpack_kernel,
        out_shape=(
            jax.ShapeDtypeStruct((1, TILE), f32),
            jax.ShapeDtypeStruct((1, TILE, HID_CH), bf16),
        ),
        in_specs=[vmem] * QUAD,
        out_specs=(vmem, vmem),
        scratch_shapes=[pltpu.VMEM((QUAD, 2 * STRIP, HID_CH), bf16)],
        compiler_params=pltpu.CompilerParams(vmem_limit_bytes=4 * 2**20),
    )(*in_group(refined))
    return (disparity, hidden)


def solution(mesh):
    in_specs = (
        P("band", None, "disp"),
        P("band", None, "disp"),
        P("band", "disp"),
        P(None, "band", "disp"),
        P("band", "disp", None),
        P(),
        P(),
        P(),
        P(),
        P(),
    )
    out_specs = (P("band", "disp"), P("band", "disp", None))
    return jax.shard_map(local, mesh=mesh, in_specs=in_specs, out_specs=out_specs, check_vma=False)
```

```python
import jax
import jax.numpy as jnp
from jax import lax
from jax.experimental import pallas as pl
from jax.experimental.pallas import tpu as pltpu
from jax.sharding import PartitionSpec as P

GROUPS = 8
DISPS = 96
FEAT_CH = 96
HID_CH = 128
ITERS = 3
TILE = 128
REACH = 2 * ITERS
EDGE = 8
QUAD = 4
STRIP = TILE // QUAD
WINDOW = STRIP + 2 * EDGE
PACK = 32
PITCH = 64
ORDER = (0, 3, 1, 2)
BLOCK_ROWS = WINDOW + 2 * GROUPS
AROUND = QUAD + 2 * REACH
BLOCK = 8
SLAB = (BLOCK + 2) * GROUPS
OUT_SLAB = BLOCK * GROUPS

pixel_unit = 8.0
feature_scale = 0.25
floor_logit = -1e30

f32 = jnp.float32
bf16 = jnp.bfloat16


def position():
    return (
        lax.axis_index("band"), lax.axis_index("disp"),
        lax.axis_size("band"), lax.axis_size("disp"),
    )


def dot(a, b):
    return jnp.dot(a, b, preferred_element_type=f32)


def dot_nt(a, b):
    return lax.dot_general(a, b, (((1,), (1,)), ((), ())), preferred_element_type=f32)


def copy_all(copies):
    for copy in copies:
        copy.start()
    for copy in copies:
        copy.wait()


def toeplitz(vol_kernel):
    size = 27 * GROUPS
    flat = vol_kernel[...].astype(f32).reshape(size, GROUPS)
    flat = jnp.concatenate([flat, jnp.zeros((size, TILE - GROUPS), f32)], axis=1).T[:GROUPS]
    row = lax.broadcasted_iota(jnp.int32, (9 * GROUPS, size), 0) >> 3
    tap = lax.broadcasted_iota(jnp.int32, (9 * GROUPS, size), 1) >> 3
    tap_a = (tap >= 9).astype(jnp.int32) + (tap >= 18).astype(jnp.int32)
    within = tap - 9 * tap_a
    tap_b = (within >= 3).astype(jnp.int32) + (within >= 6).astype(jnp.int32)
    tap_e = within - 3 * tap_b
    pairs = jnp.where(
        row == 3 * tap_a + tap_e, jnp.concatenate([flat] * 9, axis=0), 0.0
    ).astype(bf16)
    from_row = lax.broadcasted_iota(jnp.int32, (size, 3 * SLAB), 0)
    to = lax.broadcasted_iota(jnp.int32, (size, 3 * SLAB), 1)
    from_tap = from_row >> 3
    from_in = from_tap - 9 * ((from_tap >= 9).astype(jnp.int32) + (from_tap >= 18).astype(jnp.int32))
    from_b = (from_in >= 3).astype(jnp.int32) + (from_in >= 6).astype(jnp.int32)
    to_b = (to >= SLAB).astype(jnp.int32) + (to >= 2 * SLAB).astype(jnp.int32)
    repeat = jnp.where((from_b == to_b) & ((from_row & 7) == (to & 7)), 1.0, 0.0).astype(bf16)
    spread = dot(pairs, repeat)
    to = lax.broadcasted_iota(jnp.int32, (GROUPS, 3 * SLAB), 1)
    to_b = (to >= SLAB).astype(jnp.int32) + (to >= 2 * SLAB).astype(jnp.int32)
    to_d = (to - SLAB * to_b) >> 3
    rows = []
    for e in range(3):
        for d in range(BLOCK):
            value = jnp.zeros((GROUPS, 3 * SLAB), f32)
            for a in range(3):
                at = (3 * a + e) * GROUPS
                value = jnp.where(to_d == d + a, spread[at : at + GROUPS], value)
            rows.append(value)
    return jnp.concatenate(rows, axis=0).astype(bf16)


def interleaved(values):
    stacked = jnp.swapaxes(jnp.stack(values), 0, 1)
    return stacked.reshape(values[0].shape[0] * len(values), values[0].shape[1])


def toeplitz_kernel(vol_kernel, out):
    out[...] = toeplitz(vol_kernel)


def correlate(lefts, rights, place, row_ok, wide, extra):
    has_left = (place[1] > 0).astype(f32)
    has_right = (place[1] < place[3] - 1).astype(f32)
    lane = lax.broadcasted_iota(jnp.int32, (TILE, TILE), 1)
    sub = lax.broadcasted_iota(jnp.int32, (TILE, TILE), 0)
    flip = jnp.where(lane + sub == TILE - 1, 1.0, 0.0).astype(bf16)
    per_group = FEAT_CH // GROUPS
    channel = lax.broadcasted_iota(jnp.int32, (32, FEAT_CH), 1)
    group_masks = [
        (channel >= g * per_group) & (channel < (g + 1) * per_group) for g in range(GROUPS)
    ]
    lane96 = lax.broadcasted_iota(jnp.int32, (FEAT_CH, TILE), 1)
    zero_slab = jnp.zeros((GROUPS, TILE), f32)
    for at in (0, (DISPS + 1) * GROUPS):
        wide[pl.ds(at, GROUPS), :] = zero_slab
        extra[pl.ds(at, GROUPS), :] = zero_slab

    own_t = (lefts[1] * row_ok).T
    side_t = jnp.where(
        lane96 < EDGE,
        lefts[2] * (has_right * row_ok),
        jnp.where(lane96 >= TILE - EDGE, lefts[0] * (has_left * row_ok), 0.0),
    ).T
    sources = jnp.concatenate([rights[2] * has_right, rights[1], rights[0] * has_left], axis=0)
    flipped = dot(sources.astype(bf16), flip)
    reverse = jnp.concatenate(
        [flipped[i * FEAT_CH : (i + 1) * FEAT_CH] for i in range(3)], axis=1
    )
    windows = [
        reverse[:, 2 * TILE - 32 - 32 * k : 3 * TILE - 32 - 32 * k].astype(bf16)
        for k in range(-1, 5)
    ]

    def by_group(rows):
        count = rows.shape[0]
        parts = [jnp.where(m[:count], rows, 0.0) for m in group_masks]
        return jnp.concatenate(parts, axis=0).astype(bf16)

    def shear(product, g, count, first):
        rows = product[count * g : count * g + count]
        return pltpu.roll(rows, TILE - 31 + first, 1, stride=1, stride_axis=0)

    products = [
        dot(by_group(own_t[32 * k : 32 * k + 32]), windows[k + 1]) for k in range(TILE // 32)
    ]
    after = dot(by_group(side_t[:EDGE]), windows[5])
    before = dot(by_group(side_t[TILE - EDGE :]), windows[0])
    parts, sides = [], []
    for g in range(GROUPS):
        part = jnp.concatenate([shear(product, g, 32, 0) for product in products], axis=0)
        parts.append(part.T[:DISPS])
        sides += [shear(after, g, EDGE, 0), shear(before, g, EDGE, 32 - EDGE)]
    part = jnp.concatenate(sides, axis=0).T[:DISPS]
    sides = [part if g == 0 else pltpu.roll(part, TILE - 2 * EDGE * g, 1) for g in range(GROUPS)]
    for target, values in ((wide, parts), (extra, sides)):
        target[GROUPS : GROUPS + DISPS * GROUPS, :] = interleaved(values) * (1.0 / per_group)


def own_row_kernel(
    own, across, limit, indices, gain, head, vol_kernel, raw_out, kernel_out, marks_out,
    gains_out, heads_out, wide, extra, limits, index_rows, gain_held, head_held, kernel, sems,
):
    place = position()
    copies = [
        pltpu.make_async_copy(source, target, sems.at[i])
        for i, (source, target) in enumerate(
            (
                (limit, limits), (indices, index_rows), (gain, gain_held), (head, head_held),
                (vol_kernel, kernel),
            )
        )
    ]
    for copy in copies:
        copy.start()
    tiles = [across[0], own[...], across[across.shape[0] - 1]]
    tiles = [tile.astype(f32) for tile in tiles]
    correlate(
        [tile[:FEAT_CH] for tile in tiles], [tile[FEAT_CH:] for tile in tiles],
        place, 1.0, wide, extra,
    )
    raw_out[...] = jnp.concatenate([wide[...], extra[...]], axis=1).astype(bf16)
    for copy in copies:
        copy.wait()
    marks = [limits[...]] + [index_rows[t] for t in range(ITERS)]
    blank = jnp.zeros((GROUPS - len(marks), TILE), jnp.int32)
    marks_out[...] = jnp.concatenate(marks + [blank], axis=0)
    group_at = lax.broadcasted_iota(jnp.int32, (GROUPS, TILE), 0)
    gains = jnp.zeros((GROUPS, TILE), f32)
    for g in range(GROUPS):
        gains = jnp.where(group_at == g, gain_held[g], gains)
    gains_out[...] = gains
    heads = head_held[...].astype(f32) * feature_scale
    heads_out[...] = jnp.broadcast_to(heads, heads_out.shape).astype(bf16)
    kernel_out[...] = kernel[...]


def volume_kernel(
    gains, odd_own, odd_across, even_own, even_across, marks, marks_across, hidden,
    hidden_across, raw_own, taps_own, out_0, out_1, out_2, out_3, raw, taps, wide, extra, logit, padded, blocks, sems,
):
    place = position()
    band, bands = place[0], place[2]
    is_even = band % 2 == 0
    copies = [
        pltpu.make_async_copy(raw_own, raw, sems.at[0]),
        pltpu.make_async_copy(taps_own, taps, sems.at[1]),
    ]
    for copy in copies:
        copy.start()

    last = odd_across.shape[0] - 1
    odd = [tile.astype(f32) for tile in (odd_across[0], odd_own[...], odd_across[last])]
    even = [tile.astype(f32) for tile in (even_across[0], even_own[...], even_across[last])]
    for b in range(2):
        row = band + 2 * b - 1
        row_ok = ((row >= 0) & (row < bands)).astype(f32)
        tiles = [
            jnp.where(is_even, y, x) if b == 0 else jnp.where(is_even, x, y)
            for x, y in zip(odd, even)
        ]
        correlate(
            [tile[:FEAT_CH] for tile in tiles], [tile[FEAT_CH:] for tile in tiles],
            place, row_ok, wide.at[b], extra.at[b],
        )
    for copy in copies:
        copy.wait()

    lane = lax.broadcasted_iota(jnp.int32, (GROUPS, TILE), 1)
    left_marks = pltpu.roll(marks_across[0], 2 * EDGE, 1)
    levels_of = [marks[...], jnp.where(lane < EDGE, marks_across[last], left_marks)]
    lane8 = lax.broadcasted_iota(jnp.int32, (OUT_SLAB, TILE), 1)
    group_at = lax.broadcasted_iota(jnp.int32, (GROUPS, TILE), 0)
    wanted = [
        [jnp.broadcast_to(rows[t + 1 : t + 2], (GROUPS, TILE)) for t in range(ITERS)]
        for rows in levels_of
    ]
    found = [[jnp.zeros((GROUPS, TILE), f32) for _ in range(ITERS)] for _ in range(2)]
    for q in range(DISPS // BLOCK):
        at = q * OUT_SLAB
        slabs = [
            jnp.concatenate(
                [wide[b, at : at + SLAB, :], extra[b, at : at + SLAB, :]], axis=1
            ).astype(bf16)
            for b in range(2)
        ]
        slabs.insert(1, raw[at : at + SLAB, :])
        product = dot(taps[...], jnp.concatenate(slabs, axis=0))
        halves = [product[:, :TILE], product[:, TILE:]]
        first = [half[:OUT_SLAB] for half in halves]
        middle = [half[OUT_SLAB : 2 * OUT_SLAB] for half in halves]
        after = [half[2 * OUT_SLAB :] for half in halves]
        first_on = pltpu.roll(first[0], 1, 1)
        convs = [
            middle[0]
            + jnp.where(lane8 == 0, pltpu.roll(first[1], TILE - 2 * EDGE + 1, 1), first_on)
            + jnp.where(
                lane8 == TILE - 1,
                pltpu.roll(after[1], TILE - 1, 1),
                pltpu.roll(after[0], TILE - 1, 1),
            ),
            middle[1]
            + jnp.where(lane8 == 0, first_on, pltpu.roll(first[1], 1, 1))
            + jnp.where(
                lane8 == 2 * EDGE - 1,
                pltpu.roll(after[0], 2 * EDGE - 1, 1),
                pltpu.roll(after[1], TILE - 1, 1),
            ),
        ]
        centre = slabs[1].astype(f32)[GROUPS : GROUPS + OUT_SLAB]
        for i in range(2):
            volume = centre[:, i * TILE : (i + 1) * TILE] + jnp.maximum(convs[i], 0.0)
            volume = volume.astype(bf16).astype(f32).reshape(BLOCK, GROUPS, TILE)
            logit[i, q * BLOCK : (q + 1) * BLOCK, :] = jnp.sum(volume * gains[...][None], axis=1)
            for d in range(BLOCK):
                for t in range(ITERS):
                    hit = wanted[i][t] == q * BLOCK + d
                    found[i][t] = found[i][t] + jnp.where(hit, volume[d], 0.0)

    level = lax.broadcasted_iota(jnp.int32, (DISPS, TILE), 0)
    for i in range(2):
        valid = level < levels_of[i][0:1]
        masked = jnp.where(valid, logit[i], floor_logit)
        top = jnp.max(masked, axis=0, keepdims=True)
        weights = jnp.where(valid, jnp.exp(masked - top), 0.0)
        moment = jnp.sum(weights * level.astype(f32), axis=0, keepdims=True)
        start = moment / jnp.sum(weights, axis=0, keepdims=True) / pixel_unit
        high = start.astype(bf16).astype(f32)
        low = (start - high).astype(bf16).astype(f32)
        ends = jnp.where(
            group_at == 0,
            jnp.broadcast_to(high, (GROUPS, TILE)),
            jnp.where(group_at == 1, jnp.broadcast_to(low, (GROUPS, TILE)), 0.0),
        )
        found[i].append(ends)
    has_left, has_right = place[1] > 0, place[1] < place[3] - 1
    is_beside = ((lane < EDGE) & has_right) | ((lane >= EDGE) & (lane < 2 * EDGE) & has_left)
    packed, packed_beside = found[0], [jnp.where(is_beside, x, 0.0) for x in found[1]]

    before = hidden_across[0, TILE - 2 * EDGE :, :].astype(f32)[EDGE:]
    after = hidden_across[last, : 2 * EDGE, :].astype(f32)[:EDGE]
    padded[:EDGE, :] = jnp.where(has_left, before, 0.0)
    padded[EDGE : EDGE + TILE, :] = hidden[...].astype(f32)
    padded[EDGE + TILE :, :] = jnp.where(has_right, after, 0.0)
    for strip in range(QUAD):
        block = [padded[STRIP * strip : STRIP * strip + WINDOW, :]]
        for half in range(2):
            part = jnp.zeros((GROUPS, TILE), f32)
            for i in range(2):
                q, base = 2 * half + i, PITCH * i
                at = lane - base
                moved = pltpu.roll(packed[q], (base + EDGE - STRIP * strip) % TILE, 1)
                if strip == 0:
                    other = pltpu.roll(packed_beside[q], (base - EDGE) % TILE, 1)
                    moved = jnp.where(at < EDGE, other, moved)
                if strip == QUAD - 1:
                    other = pltpu.roll(packed_beside[q], base + WINDOW - EDGE, 1)
                    moved = jnp.where(at >= WINDOW - EDGE, other, moved)
                part = jnp.where((at >= 0) & (at < WINDOW), moved, part)
            block.append(part)
        blocks[strip] = jnp.concatenate(block, axis=0).astype(bf16)
    member = band % QUAD
    for i, out in zip(ORDER, (out_0, out_1, out_2, out_3)):
        out[...] = blocks[strip_at(place, member ^ i)]


def slot_of(member_xor):
    return jnp.where(member_xor == 0, 0, jnp.where(member_xor == 3, 1, member_xor + 1))


def strip_at(place, member):
    return jnp.where(place[1] % 2 == 0, member, QUAD - 1 - member)


def keep(line, target, at, values):
    length = values.shape[0]
    start = EDGE + at
    line[start : start + length, :] = values
    target[at : at + length, 0:HID_CH] = line[start - 1 : start - 1 + length, :].astype(bf16)
    target[at : at + length, HID_CH : 2 * HID_CH] = values.astype(bf16)
    target[at : at + length, 2 * HID_CH :] = line[start + 1 : start + 1 + length, :].astype(bf16)


def around(target, at, length):
    return [target[at + a * WINDOW : at + a * WINDOW + length, :] for a in (-1, 0, 1)]


def chunks(low, high, most):
    count = high - low + 1
    parts = -(-count // most)
    out = []
    for i in range(parts):
        size = count // parts + (1 if i < count % parts else 0)
        out.append((low, size))
        low += size
    return out


def weight_kernel(hid_weight, in_weight, out):
    out[: 9 * HID_CH, :] = hid_weight[...]
    out[9 * HID_CH :, :] = in_weight[...]


def refine_kernel(
    own,
    near_b,
    near_a,
    far_d,
    far_c,
    weight,
    heads,
    out_0,
    out_1,
    out_2,
    out_3,
    line,
    looked,
    hidden_at,
    taps,
    reset_taps,
    inputs,
    gate,
    level,
    blocks,
):
    rows, strip = AROUND, STRIP
    place = position()
    band, disp, bands, disps = place
    member, layer = band % QUAD, band // QUAD
    at = strip_at(place, member)
    first = strip * at - EDGE
    first_row = layer * QUAD - REACH

    def block_of(r):
        step, row = (r + 2 * QUAD - REACH) // QUAD - 2, (r + 2 * QUAD - REACH) % QUAD
        slot = slot_of(row ^ member)
        if step == 0:
            return own[slot].astype(f32)
        if abs(step) == 1:
            choice, x, y = (layer % 2 == 0) == (step > 0), near_a, near_b
        else:
            choice, x, y = (layer % 4 < 2) == (step > 0), far_c, far_d
        inside = (first_row + r >= 0) & (first_row + r < bands)
        block = jnp.where(choice, x[slot].astype(f32), y[slot].astype(f32))
        return jnp.where(inside, block, 0.0)

    lane = lax.broadcasted_iota(jnp.int32, (GROUPS, TILE), 1)
    at_sub = lax.broadcasted_iota(jnp.int32, (WINDOW, TILE), 0)
    at_lane = lax.broadcasted_iota(jnp.int32, (WINDOW, TILE), 1)
    spread = jnp.where(at_sub == at_lane % PITCH, 1.0, 0.0).astype(bf16)
    fill = jnp.zeros((PACK, TILE), f32)
    zeros = jnp.zeros((GROUPS, TILE), f32)
    lines = []
    for r in range(rows):
        block = block_of(r)
        packed = block[WINDOW:]
        hidden_at[r * WINDOW : (r + 1) * WINDOW, :] = block[:WINDOW]
        pieces = []
        for b in range(3):
            moved = packed if b == 1 else pltpu.roll(packed, (1 - b) % TILE, 1)
            for q in range(4):
                part = moved[GROUPS * (q // 2) : GROUPS * (q // 2 + 1)]
                pieces.append(jnp.where((lane >= PITCH) == (q % 2 == 1), part, zeros))
        lines.append(jnp.concatenate(pieces + [fill], axis=0).astype(bf16))
    for r in range(0, rows, 2):
        both = dot_nt(spread, jnp.concatenate(lines[r : r + 2], axis=0))
        for i in range(2):
            at = (r + i) * WINDOW
            looked[at : at + WINDOW, :] = both[:, i * HID_CH : (i + 1) * HID_CH]
    sub = lax.broadcasted_iota(jnp.int32, (HID_CH, HID_CH), 0)
    ends = jnp.where((sub == PACK + 24) | (sub == PACK + 25), feature_scale, 0.0).astype(bf16)
    blank = jnp.zeros((EDGE, HID_CH), f32)
    level[:EDGE, :] = blank
    level[EDGE + WINDOW * rows :, :] = blank
    level[EDGE : EDGE + WINDOW * rows, :] = dot(looked[...].astype(bf16), ends)
    line[...] = jnp.zeros_like(line)
    keep(line, taps, 0, hidden_at[...])

    for t in range(ITERS):
        low, high = 1 + 2 * t, rows - 2 - 2 * t
        at, length = (low - 1) * WINDOW, (high - low + 3) * WINDOW
        lane_at = lax.broadcasted_iota(jnp.int32, (length, HID_CH), 1)
        tap, channel = lane_at // PACK, lane_at % PACK
        near = [level[EDGE + at + b : EDGE + at + b + length, :] for b in (-1, 0, 1)]
        value = jnp.where(tap == 0, near[0], jnp.where(tap == 1, near[1], near[2]))
        at_lookup = (channel >= t * GROUPS) & (channel < (t + 1) * GROUPS)
        value = jnp.where(
            (channel == 3 * GROUPS) & (tap < 3),
            value,
            jnp.where(at_lookup, looked[at : at + length, :], 0.0),
        )
        inputs[at : at + length, :] = value.astype(bf16)

        for r, count in chunks(low, high, 7):
            at, length = r * WINDOW, count * WINDOW
            lhs = around(taps, at, length) + around(inputs, at, length)
            both = dot(jnp.concatenate(lhs, axis=1), weight[:, : 2 * HID_CH])
            skip, until = (WINDOW if r == low else 0), (WINDOW if r + count - 1 == high else 0)
            gate[at + skip : at + length - until, :] = (
                0.5 * jnp.tanh(0.5 * both[skip : length - until, :HID_CH]) + 0.5
            )
            reset = 0.5 * jnp.tanh(0.5 * both[:, HID_CH:]) + 0.5
            keep(line, reset_taps, at, reset * hidden_at[at : at + length, :])

        for r, count in chunks(low + 1, high - 1, 6):
            at, length = r * WINDOW, count * WINDOW
            lhs = around(reset_taps, at, length) + around(inputs, at, length)
            candidate = jnp.tanh(dot(jnp.concatenate(lhs, axis=1), weight[:, 2 * HID_CH :]))
            hidden = hidden_at[at : at + length, :]
            hidden = hidden + gate[at : at + length, :] * (candidate - hidden)
            pixel = lax.broadcasted_iota(jnp.int32, (length, HID_CH), 0)
            column, row = pixel % WINDOW + first, pixel // WINDOW + (r + first_row)
            inside = ((column >= 0) | (disp > 0)) & ((column < TILE) | (disp < disps - 1))
            inside = inside & (row >= 0) & (row < bands)
            hidden = jnp.where(inside, hidden, 0.0).astype(bf16)
            level[EDGE + at : EDGE + at + length, :] += dot_nt(hidden, heads[...])
            hidden_at[at : at + length, :] = hidden.astype(f32)
            if t < ITERS - 1:
                keep(line, taps, at, hidden.astype(f32))

    lane = lax.broadcasted_iota(jnp.int32, (strip, HID_CH), 1)
    for r in range(QUAD):
        at = (REACH + r) * WINDOW + EDGE
        hidden = hidden_at[at : at + strip, :]
        value = level[EDGE + at : EDGE + at + strip, :] * (1.0 / feature_scale)
        high = value.astype(bf16).astype(f32)
        middle = (value - high).astype(bf16).astype(f32)
        parts = jnp.where(lane == 0, high, jnp.where(lane == 1, middle, value - high - middle))
        parts = jnp.where(lane < 3, parts, 0.0)
        blocks[r] = jnp.concatenate([hidden, parts], axis=0).astype(bf16)
    for i, out in zip(ORDER, (out_0, out_1, out_2, out_3)):
        out[...] = blocks[member ^ i]


def unpack_kernel(from_0, from_1, from_2, from_3, disparity_out, hidden_out, blocks):
    for i, block in enumerate((from_0, from_1, from_2, from_3)):
        blocks[i] = block[...]
    place = position()
    member = place[0] % QUAD
    slots = [slot_of(strip_at(place, strip) ^ member) for strip in range(QUAD)]
    held = [blocks[slot].astype(f32) for slot in slots]
    hidden_out[0] = jnp.concatenate([block[:STRIP] for block in held], axis=0).astype(bf16)
    parts = jnp.concatenate([block[STRIP:] for block in held], axis=0).T
    disparity_out[...] = parts[0:1] + parts[1:2] + parts[2:3]


def in_hbm(value):
    return pltpu.with_memory_space_constraint(value, pltpu.HBM)


def to_sides(value):
    disps = lax.axis_size("disp")
    right = [(d, d + 1) for d in range(disps - 1)]
    left = [(d + 1, d) for d in range(disps - 1)]
    if disps == 2:
        return lax.ppermute(value, "disp", right + left)[None]
    return jnp.stack([lax.ppermute(value, "disp", right), lax.ppermute(value, "disp", left)])


def in_group(blocks):
    return [blocks[0]] + [
        to_rows(block, lambda band, i=i: band ^ i)
        for i, block in list(zip(ORDER, blocks))[1:]
    ]


def to_layers(value, partner):
    groups = lax.axis_size("band") // QUAD
    if not any(0 <= partner(g) < groups for g in range(groups)):
        return None
    return to_rows(value, lambda band: partner(band // QUAD) * QUAD + band % QUAD)


def to_rows(value, shift):
    bands = lax.axis_size("band")
    return lax.ppermute(
        value, "band", [(i, shift(i)) for i in range(bands) if 0 <= shift(i) < bands]
    )


def odd_pair(i):
    return i ^ 1


def even_pair(i):
    return i - 1 if i % 2 == 0 else i + 1


def local(
    feat_left,
    feat_right,
    limit,
    indices,
    hidden_start,
    vol_kernel,
    group_gain,
    hid_kernel,
    in_kernel,
    head_weight,
):
    bands, disps = lax.axis_size("band"), lax.axis_size("disp")
    vmem = pl.BlockSpec(memory_space=pltpu.VMEM)
    hbm = pl.BlockSpec(memory_space=pltpu.HBM)
    padded = (DISPS + 2) * GROUPS

    feats = jnp.concatenate([feat_left[0], feat_right[0]], axis=0)
    odd_own, even_own = to_rows(feats, odd_pair), to_rows(feats, even_pair)
    across = to_sides(feats)
    raw_own, kernel_held, marks, gains, heads = pl.pallas_call(
        own_row_kernel,
        out_shape=(
            jax.ShapeDtypeStruct((padded, 2 * TILE), bf16),
            jax.ShapeDtypeStruct((27, GROUPS, GROUPS), bf16),
            jax.ShapeDtypeStruct((GROUPS, TILE), jnp.int32),
            jax.ShapeDtypeStruct((GROUPS, TILE), f32),
            jax.ShapeDtypeStruct((HID_CH, HID_CH), bf16),
        ),
        in_specs=[vmem, vmem] + [hbm] * 5,
        out_specs=(vmem,) * 5,
        scratch_shapes=[
            pltpu.VMEM((padded, TILE), f32),
            pltpu.VMEM((padded, TILE), f32),
            pltpu.VMEM((1, TILE), jnp.int32),
            pltpu.VMEM((ITERS, 1, TILE), jnp.int32),
            pltpu.SMEM((GROUPS,), f32),
            pltpu.VMEM((1, HID_CH), bf16),
            pltpu.VMEM((27, GROUPS, GROUPS), bf16),
            pltpu.SemaphoreType.DMA((5,)),
        ],
        compiler_params=pltpu.CompilerParams(vmem_limit_bytes=16 * 2**20),
        cost_estimate=pl.CostEstimate(flops=2 * 10**9, bytes_accessed=4 * 2**20, transcendentals=0),
    )(
        feats, across, in_hbm(limit), in_hbm(indices), in_hbm(group_gain),
        in_hbm(head_weight.reshape(1, HID_CH)), in_hbm(vol_kernel.reshape(27, GROUPS, GROUPS)),
    )
    hidden = hidden_start[0]
    hidden_across = to_sides(hidden)
    odd_own, even_own, raw_own, hidden_across = lax.optimization_barrier(
        (odd_own, even_own, raw_own, hidden_across)
    )
    taps = pl.pallas_call(
        toeplitz_kernel,
        out_shape=jax.ShapeDtypeStruct((3 * OUT_SLAB, 3 * SLAB), bf16),
        in_specs=[vmem],
        out_specs=vmem,
        compiler_params=pltpu.CompilerParams(vmem_limit_bytes=8 * 2**20),
        cost_estimate=pl.CostEstimate(flops=10**9, bytes_accessed=2**20, transcendentals=0),
    )(kernel_held)
    marks_across = to_sides(marks)
    odd_across, even_across = to_sides(odd_own), to_sides(even_own)

    in_weight = jnp.concatenate(
        [in_kernel[:, :, :GROUPS]] * ITERS + [in_kernel[:, :, GROUPS:]], axis=2
    )
    in_weight = jnp.pad(in_weight, ((0, 0), (0, 1), (0, PACK - in_weight.shape[2]), (0, 0)))
    in_weight = in_weight.reshape(3 * HID_CH, 3 * HID_CH)

    blocks = pl.pallas_call(
        volume_kernel,
        out_shape=(jax.ShapeDtypeStruct((BLOCK_ROWS, TILE), bf16),) * QUAD,
        in_specs=[vmem] * 9 + [hbm, hbm],
        out_specs=(vmem,) * QUAD,
        scratch_shapes=[
            pltpu.VMEM((padded, 2 * TILE), bf16),
            pltpu.VMEM((3 * OUT_SLAB, 3 * SLAB), bf16),
            pltpu.VMEM((2, padded, TILE), f32),
            pltpu.VMEM((2, padded, TILE), f32),
            pltpu.VMEM((2, DISPS, TILE), f32),
            pltpu.VMEM((TILE + 2 * EDGE, HID_CH), f32),
            pltpu.VMEM((QUAD, BLOCK_ROWS, TILE), bf16),
            pltpu.SemaphoreType.DMA((2,)),
        ],
        compiler_params=pltpu.CompilerParams(vmem_limit_bytes=24 * 2**20),
        cost_estimate=pl.CostEstimate(
            flops=5 * 10**9, bytes_accessed=16 * 2**20, transcendentals=DISPS * TILE
        ),
    )(
        gains, odd_own, odd_across, even_own, even_across,
        marks, marks_across, hidden, hidden_across, raw_own, taps,
    )

    weight = pl.pallas_call(
        weight_kernel,
        out_shape=jax.ShapeDtypeStruct((12 * HID_CH, 3 * HID_CH), bf16),
        in_specs=[vmem, vmem],
        out_specs=vmem,
        compiler_params=pltpu.CompilerParams(vmem_limit_bytes=8 * 2**20),
        cost_estimate=pl.CostEstimate(flops=10**8, bytes_accessed=2**20, transcendentals=0),
    )(hid_kernel.reshape(9 * HID_CH, 3 * HID_CH), in_weight)
    own, weight = lax.optimization_barrier((jnp.stack(in_group(blocks)), weight))
    around = [
        to_layers(own, lambda g: (g - 1 ^ 1) + 1),
        to_layers(own, lambda g: g ^ 1),
        to_layers(own, lambda g: (g - 2 ^ 2) + 2),
        to_layers(own, lambda g: g ^ 2),
    ]
    if around[2] is None:
        around[2] = around[3]

    pixels = WINDOW * AROUND
    refined = pl.pallas_call(
        refine_kernel,
        out_shape=(jax.ShapeDtypeStruct((2 * STRIP, HID_CH), bf16),) * QUAD,
        in_specs=[vmem] * 7,
        out_specs=(vmem,) * QUAD,
        scratch_shapes=[
            pltpu.VMEM((pixels + 2 * EDGE, HID_CH), f32),
            pltpu.VMEM((pixels, HID_CH), f32),
            pltpu.VMEM((pixels, HID_CH), f32),
            pltpu.VMEM((pixels, 3 * HID_CH), bf16),
            pltpu.VMEM((pixels, 3 * HID_CH), bf16),
            pltpu.VMEM((pixels, HID_CH), bf16),
            pltpu.VMEM((pixels, HID_CH), f32),
            pltpu.VMEM((pixels + 2 * EDGE, HID_CH), f32),
            pltpu.VMEM((QUAD, 2 * STRIP, HID_CH), bf16),
        ],
        compiler_params=pltpu.CompilerParams(vmem_limit_bytes=32 * 2**20),
    )(
        own, *around,
        weight, heads,
    )
    disparity, hidden = pl.pallas_call(
        unpack_kernel,
        out_shape=(
            jax.ShapeDtypeStruct((1, TILE), f32),
            jax.ShapeDtypeStruct((1, TILE, HID_CH), bf16),
        ),
        in_specs=[vmem] * QUAD,
        out_specs=(vmem, vmem),
        scratch_shapes=[pltpu.VMEM((QUAD, 2 * STRIP, HID_CH), bf16)],
        compiler_params=pltpu.CompilerParams(vmem_limit_bytes=4 * 2**20),
    )(*in_group(refined))
    return (disparity, hidden)


def solution(mesh):
    in_specs = (
        P("band", None, "disp"),
        P("band", None, "disp"),
        P("band", "disp"),
        P(None, "band", "disp"),
        P("band", "disp", None),
        P(),
        P(),
        P(),
        P(),
        P(),
    )
    out_specs = (P("band", "disp"), P("band", "disp", None))
    return jax.shard_map(local, mesh=mesh, in_specs=in_specs, out_specs=out_specs, check_vma=False)
```

```python
import jax
import jax.numpy as jnp
from jax import lax
from jax.experimental import pallas as pl
from jax.experimental.pallas import tpu as pltpu
from jax.sharding import PartitionSpec as P

GROUPS = 8
DISPS = 96
FEAT_CH = 96
HID_CH = 128
ITERS = 3
TILE = 128
REACH = 2 * ITERS
EDGE = 8
QUAD = 4
STRIP = TILE // QUAD
WINDOW = STRIP + 2 * EDGE
PACK = 32
PITCH = 64
ORDER = (0, 3, 1, 2)
BLOCK_ROWS = WINDOW + 2 * GROUPS
AROUND = QUAD + 2 * REACH
BLOCK = 8
SLAB = (BLOCK + 2) * GROUPS
OUT_SLAB = BLOCK * GROUPS

pixel_unit = 8.0
feature_scale = 0.25
floor_logit = -1e30

f32 = jnp.float32
bf16 = jnp.bfloat16


def position():
    return (
        lax.axis_index("band"), lax.axis_index("disp"),
        lax.axis_size("band"), lax.axis_size("disp"),
    )


def dot(a, b):
    return jnp.dot(a, b, preferred_element_type=f32)


def dot_nt(a, b):
    return lax.dot_general(a, b, (((1,), (1,)), ((), ())), preferred_element_type=f32)


def copy_all(copies):
    for copy in copies:
        copy.start()
    for copy in copies:
        copy.wait()


def toeplitz(vol_kernel):
    size = 27 * GROUPS
    flat = vol_kernel[...].astype(f32).reshape(size, GROUPS)
    flat = jnp.concatenate([flat, jnp.zeros((size, TILE - GROUPS), f32)], axis=1).T[:GROUPS]
    row = lax.broadcasted_iota(jnp.int32, (9 * GROUPS, size), 0) >> 3
    tap = lax.broadcasted_iota(jnp.int32, (9 * GROUPS, size), 1) >> 3
    tap_a = (tap >= 9).astype(jnp.int32) + (tap >= 18).astype(jnp.int32)
    within = tap - 9 * tap_a
    tap_b = (within >= 3).astype(jnp.int32) + (within >= 6).astype(jnp.int32)
    tap_e = within - 3 * tap_b
    pairs = jnp.where(
        row == 3 * tap_a + tap_e, jnp.concatenate([flat] * 9, axis=0), 0.0
    ).astype(bf16)
    from_row = lax.broadcasted_iota(jnp.int32, (size, 3 * SLAB), 0)
    to = lax.broadcasted_iota(jnp.int32, (size, 3 * SLAB), 1)
    from_tap = from_row >> 3
    from_in = from_tap - 9 * ((from_tap >= 9).astype(jnp.int32) + (from_tap >= 18).astype(jnp.int32))
    from_b = (from_in >= 3).astype(jnp.int32) + (from_in >= 6).astype(jnp.int32)
    to_b = (to >= SLAB).astype(jnp.int32) + (to >= 2 * SLAB).astype(jnp.int32)
    repeat = jnp.where((from_b == to_b) & ((from_row & 7) == (to & 7)), 1.0, 0.0).astype(bf16)
    spread = dot(pairs, repeat)
    to = lax.broadcasted_iota(jnp.int32, (GROUPS, 3 * SLAB), 1)
    to_b = (to >= SLAB).astype(jnp.int32) + (to >= 2 * SLAB).astype(jnp.int32)
    to_d = (to - SLAB * to_b) >> 3
    rows = []
    for e in range(3):
        for d in range(BLOCK):
            value = jnp.zeros((GROUPS, 3 * SLAB), f32)
            for a in range(3):
                at = (3 * a + e) * GROUPS
                value = jnp.where(to_d == d + a, spread[at : at + GROUPS], value)
            rows.append(value)
    return jnp.concatenate(rows, axis=0).astype(bf16)


def interleaved(values):
    stacked = jnp.swapaxes(jnp.stack(values), 0, 1)
    return stacked.reshape(values[0].shape[0] * len(values), values[0].shape[1])


def toeplitz_kernel(vol_kernel, out):
    out[...] = toeplitz(vol_kernel)


def correlate(lefts, rights, place, row_ok, wide, extra):
    has_left = (place[1] > 0).astype(f32)
    has_right = (place[1] < place[3] - 1).astype(f32)
    lane = lax.broadcasted_iota(jnp.int32, (TILE, TILE), 1)
    sub = lax.broadcasted_iota(jnp.int32, (TILE, TILE), 0)
    flip = jnp.where(lane + sub == TILE - 1, 1.0, 0.0).astype(bf16)
    per_group = FEAT_CH // GROUPS
    channel = lax.broadcasted_iota(jnp.int32, (32, FEAT_CH), 1)
    group_masks = [
        (channel >= g * per_group) & (channel < (g + 1) * per_group) for g in range(GROUPS)
    ]
    lane96 = lax.broadcasted_iota(jnp.int32, (FEAT_CH, TILE), 1)
    zero_slab = jnp.zeros((GROUPS, TILE), f32)
    for at in (0, (DISPS + 1) * GROUPS):
        wide[pl.ds(at, GROUPS), :] = zero_slab
        extra[pl.ds(at, GROUPS), :] = zero_slab

    own_t = (lefts[1] * row_ok).T
    side_t = jnp.where(
        lane96 < EDGE,
        lefts[2] * (has_right * row_ok),
        jnp.where(lane96 >= TILE - EDGE, lefts[0] * (has_left * row_ok), 0.0),
    ).T
    sources = jnp.concatenate([rights[2] * has_right, rights[1], rights[0] * has_left], axis=0)
    flipped = dot(sources.astype(bf16), flip)
    reverse = jnp.concatenate(
        [flipped[i * FEAT_CH : (i + 1) * FEAT_CH] for i in range(3)], axis=1
    )
    windows = [
        reverse[:, 2 * TILE - 32 - 32 * k : 3 * TILE - 32 - 32 * k].astype(bf16)
        for k in range(-1, 5)
    ]

    def by_group(rows):
        count = rows.shape[0]
        parts = [jnp.where(m[:count], rows, 0.0) for m in group_masks]
        return jnp.concatenate(parts, axis=0).astype(bf16)

    def shear(product, g, count, first):
        rows = product[count * g : count * g + count]
        return pltpu.roll(rows, TILE - 31 + first, 1, stride=1, stride_axis=0)

    products = [
        dot(by_group(own_t[32 * k : 32 * k + 32]), windows[k + 1]) for k in range(TILE // 32)
    ]
    after = dot(by_group(side_t[:EDGE]), windows[5])
    before = dot(by_group(side_t[TILE - EDGE :]), windows[0])
    parts, sides = [], []
    for g in range(GROUPS):
        part = jnp.concatenate([shear(product, g, 32, 0) for product in products], axis=0)
        parts.append(part.T[:DISPS])
        sides += [shear(after, g, EDGE, 0), shear(before, g, EDGE, 32 - EDGE)]
    part = jnp.concatenate(sides, axis=0).T[:DISPS]
    sides = [part if g == 0 else pltpu.roll(part, TILE - 2 * EDGE * g, 1) for g in range(GROUPS)]
    for target, values in ((wide, parts), (extra, sides)):
        target[GROUPS : GROUPS + DISPS * GROUPS, :] = interleaved(values) * (1.0 / per_group)


def own_row_kernel(
    own, across, limit, indices, gain, head, vol_kernel, raw_out, kernel_out, marks_out,
    gains_out, heads_out, wide, extra, limits, index_rows, gain_held, head_held, kernel, sems,
):
    place = position()
    copies = [
        pltpu.make_async_copy(source, target, sems.at[i])
        for i, (source, target) in enumerate(
            (
                (limit, limits), (indices, index_rows), (gain, gain_held), (head, head_held),
                (vol_kernel, kernel),
            )
        )
    ]
    for copy in copies:
        copy.start()
    tiles = [across[0], own[...], across[across.shape[0] - 1]]
    tiles = [tile.astype(f32) for tile in tiles]
    correlate(
        [tile[:FEAT_CH] for tile in tiles], [tile[FEAT_CH:] for tile in tiles],
        place, 1.0, wide, extra,
    )
    raw_out[...] = jnp.concatenate([wide[...], extra[...]], axis=1).astype(bf16)
    for copy in copies:
        copy.wait()
    marks = [limits[...]] + [index_rows[t] for t in range(ITERS)]
    blank = jnp.zeros((GROUPS - len(marks), TILE), jnp.int32)
    marks_out[...] = jnp.concatenate(marks + [blank], axis=0)
    group_at = lax.broadcasted_iota(jnp.int32, (GROUPS, TILE), 0)
    gains = jnp.zeros((GROUPS, TILE), f32)
    for g in range(GROUPS):
        gains = jnp.where(group_at == g, gain_held[g], gains)
    gains_out[...] = gains
    heads = head_held[...].astype(f32) * feature_scale
    heads_out[...] = jnp.broadcast_to(heads, heads_out.shape).astype(bf16)
    kernel_out[...] = kernel[...]


def volume_kernel(
    gains, odd_own, odd_across, even_own, even_across, marks, marks_across, hidden,
    hidden_across, raw_own, taps_own, out_0, out_1, out_2, out_3, raw, taps, wide, extra, logit, padded, blocks, sems,
):
    place = position()
    band, bands = place[0], place[2]
    is_even = band % 2 == 0
    copies = [
        pltpu.make_async_copy(raw_own, raw, sems.at[0]),
        pltpu.make_async_copy(taps_own, taps, sems.at[1]),
    ]
    for copy in copies:
        copy.start()

    last = odd_across.shape[0] - 1
    odd = [tile.astype(f32) for tile in (odd_across[0], odd_own[...], odd_across[last])]
    even = [tile.astype(f32) for tile in (even_across[0], even_own[...], even_across[last])]
    for b in range(2):
        row = band + 2 * b - 1
        row_ok = ((row >= 0) & (row < bands)).astype(f32)
        tiles = [
            jnp.where(is_even, y, x) if b == 0 else jnp.where(is_even, x, y)
            for x, y in zip(odd, even)
        ]
        correlate(
            [tile[:FEAT_CH] for tile in tiles], [tile[FEAT_CH:] for tile in tiles],
            place, row_ok, wide.at[b], extra.at[b],
        )
    for copy in copies:
        copy.wait()

    lane = lax.broadcasted_iota(jnp.int32, (GROUPS, TILE), 1)
    left_marks = pltpu.roll(marks_across[0], 2 * EDGE, 1)
    levels_of = [marks[...], jnp.where(lane < EDGE, marks_across[last], left_marks)]
    lane8 = lax.broadcasted_iota(jnp.int32, (OUT_SLAB, TILE), 1)
    group_at = lax.broadcasted_iota(jnp.int32, (GROUPS, TILE), 0)
    wanted = [
        [jnp.broadcast_to(rows[t + 1 : t + 2], (GROUPS, TILE)) for t in range(ITERS)]
        for rows in levels_of
    ]
    found = [[jnp.zeros((GROUPS, TILE), f32) for _ in range(ITERS)] for _ in range(2)]
    for q in range(DISPS // BLOCK):
        at = q * OUT_SLAB
        slabs = [
            jnp.concatenate(
                [wide[b, at : at + SLAB, :], extra[b, at : at + SLAB, :]], axis=1
            ).astype(bf16)
            for b in range(2)
        ]
        slabs.insert(1, raw[at : at + SLAB, :])
        product = dot(taps[...], jnp.concatenate(slabs, axis=0))
        halves = [product[:, :TILE], product[:, TILE:]]
        first = [half[:OUT_SLAB] for half in halves]
        middle = [half[OUT_SLAB : 2 * OUT_SLAB] for half in halves]
        after = [half[2 * OUT_SLAB :] for half in halves]
        first_on = pltpu.roll(first[0], 1, 1)
        convs = [
            middle[0]
            + jnp.where(lane8 == 0, pltpu.roll(first[1], TILE - 2 * EDGE + 1, 1), first_on)
            + jnp.where(
                lane8 == TILE - 1,
                pltpu.roll(after[1], TILE - 1, 1),
                pltpu.roll(after[0], TILE - 1, 1),
            ),
            middle[1]
            + jnp.where(lane8 == 0, first_on, pltpu.roll(first[1], 1, 1))
            + jnp.where(
                lane8 == 2 * EDGE - 1,
                pltpu.roll(after[0], 2 * EDGE - 1, 1),
                pltpu.roll(after[1], TILE - 1, 1),
            ),
        ]
        centre = slabs[1].astype(f32)[GROUPS : GROUPS + OUT_SLAB]
        for i in range(2):
            volume = centre[:, i * TILE : (i + 1) * TILE] + jnp.maximum(convs[i], 0.0)
            volume = volume.astype(bf16).astype(f32).reshape(BLOCK, GROUPS, TILE)
            logit[i, q * BLOCK : (q + 1) * BLOCK, :] = jnp.sum(volume * gains[...][None], axis=1)
            for d in range(BLOCK):
                for t in range(ITERS):
                    hit = wanted[i][t] == q * BLOCK + d
                    found[i][t] = found[i][t] + jnp.where(hit, volume[d], 0.0)

    level = lax.broadcasted_iota(jnp.int32, (DISPS, TILE), 0)
    for i in range(2):
        valid = level < levels_of[i][0:1]
        masked = jnp.where(valid, logit[i], floor_logit)
        top = jnp.max(masked, axis=0, keepdims=True)
        weights = jnp.where(valid, jnp.exp(masked - top), 0.0)
        moment = jnp.sum(weights * level.astype(f32), axis=0, keepdims=True)
        start = moment / jnp.sum(weights, axis=0, keepdims=True) / pixel_unit
        high = start.astype(bf16).astype(f32)
        low = (start - high).astype(bf16).astype(f32)
        ends = jnp.where(
            group_at == 0,
            jnp.broadcast_to(high, (GROUPS, TILE)),
            jnp.where(group_at == 1, jnp.broadcast_to(low, (GROUPS, TILE)), 0.0),
        )
        found[i].append(ends)
    has_left, has_right = place[1] > 0, place[1] < place[3] - 1
    is_beside = ((lane < EDGE) & has_right) | ((lane >= EDGE) & (lane < 2 * EDGE) & has_left)
    packed, packed_beside = found[0], [jnp.where(is_beside, x, 0.0) for x in found[1]]

    before = hidden_across[0, TILE - 2 * EDGE :, :].astype(f32)[EDGE:]
    after = hidden_across[last, : 2 * EDGE, :].astype(f32)[:EDGE]
    padded[:EDGE, :] = jnp.where(has_left, before, 0.0)
    padded[EDGE : EDGE + TILE, :] = hidden[...].astype(f32)
    padded[EDGE + TILE :, :] = jnp.where(has_right, after, 0.0)
    for strip in range(QUAD):
        block = [padded[STRIP * strip : STRIP * strip + WINDOW, :]]
        for half in range(2):
            part = jnp.zeros((GROUPS, TILE), f32)
            for i in range(2):
                q, base = 2 * half + i, PITCH * i
                at = lane - base
                moved = pltpu.roll(packed[q], (base + EDGE - STRIP * strip) % TILE, 1)
                if strip == 0:
                    other = pltpu.roll(packed_beside[q], (base - EDGE) % TILE, 1)
                    moved = jnp.where(at < EDGE, other, moved)
                if strip == QUAD - 1:
                    other = pltpu.roll(packed_beside[q], base + WINDOW - EDGE, 1)
                    moved = jnp.where(at >= WINDOW - EDGE, other, moved)
                part = jnp.where((at >= 0) & (at < WINDOW), moved, part)
            block.append(part)
        blocks[strip] = jnp.concatenate(block, axis=0).astype(bf16)
    member = band % QUAD
    for i, out in zip(ORDER, (out_0, out_1, out_2, out_3)):
        out[...] = blocks[strip_at(place, member ^ i)]


def slot_of(member_xor):
    return jnp.where(member_xor == 0, 0, jnp.where(member_xor == 3, 1, member_xor + 1))


def strip_at(place, member):
    return jnp.where(place[1] % 2 == 0, member, QUAD - 1 - member)


def keep(line, target, at, values):
    length = values.shape[0]
    start = EDGE + at
    line[start : start + length, :] = values
    target[at : at + length, 0:HID_CH] = line[start - 1 : start - 1 + length, :].astype(bf16)
    target[at : at + length, HID_CH : 2 * HID_CH] = values.astype(bf16)
    target[at : at + length, 2 * HID_CH :] = line[start + 1 : start + 1 + length, :].astype(bf16)


def around(target, at, length):
    return [target[at + a * WINDOW : at + a * WINDOW + length, :] for a in (-1, 0, 1)]


def chunks(low, high, most):
    count = high - low + 1
    parts = -(-count // most)
    out = []
    for i in range(parts):
        size = count // parts + (1 if i < count % parts else 0)
        out.append((low, size))
        low += size
    return out


def weight_kernel(hid_weight, in_weight, out):
    out[: 9 * HID_CH, :] = hid_weight[...]
    out[9 * HID_CH :, :] = in_weight[...]


def refine_kernel(
    own,
    near_b,
    near_a,
    far_d,
    far_c,
    weight,
    heads,
    out_0,
    out_1,
    out_2,
    out_3,
    line,
    looked,
    hidden_at,
    taps,
    reset_taps,
    inputs,
    gate,
    level,
    blocks,
):
    rows, strip = AROUND, STRIP
    place = position()
    band, disp, bands, disps = place
    member, layer = band % QUAD, band // QUAD
    at = strip_at(place, member)
    first = strip * at - EDGE
    first_row = layer * QUAD - REACH

    def block_of(r):
        step, row = (r + 2 * QUAD - REACH) // QUAD - 2, (r + 2 * QUAD - REACH) % QUAD
        slot = slot_of(row ^ member)
        if step == 0:
            return own[slot].astype(f32)
        if abs(step) == 1:
            choice, x, y = (layer % 2 == 0) == (step > 0), near_a, near_b
        else:
            choice, x, y = (layer % 4 < 2) == (step > 0), far_c, far_d
        inside = (first_row + r >= 0) & (first_row + r < bands)
        block = jnp.where(choice, x[slot].astype(f32), y[slot].astype(f32))
        return jnp.where(inside, block, 0.0)

    lane = lax.broadcasted_iota(jnp.int32, (GROUPS, TILE), 1)
    at_sub = lax.broadcasted_iota(jnp.int32, (WINDOW, TILE), 0)
    at_lane = lax.broadcasted_iota(jnp.int32, (WINDOW, TILE), 1)
    spread = jnp.where(at_sub == at_lane % PITCH, 1.0, 0.0).astype(bf16)
    fill = jnp.zeros((PACK, TILE), f32)
    zeros = jnp.zeros((GROUPS, TILE), f32)
    lines = []
    for r in range(rows):
        block = block_of(r)
        packed = block[WINDOW:]
        hidden_at[r * WINDOW : (r + 1) * WINDOW, :] = block[:WINDOW]
        pieces = []
        for b in range(3):
            moved = packed if b == 1 else pltpu.roll(packed, (1 - b) % TILE, 1)
            for q in range(4):
                part = moved[GROUPS * (q // 2) : GROUPS * (q // 2 + 1)]
                pieces.append(jnp.where((lane >= PITCH) == (q % 2 == 1), part, zeros))
        lines.append(jnp.concatenate(pieces + [fill], axis=0).astype(bf16))
    for r in range(0, rows, 2):
        both = dot_nt(spread, jnp.concatenate(lines[r : r + 2], axis=0))
        for i in range(2):
            at = (r + i) * WINDOW
            looked[at : at + WINDOW, :] = both[:, i * HID_CH : (i + 1) * HID_CH]
    sub = lax.broadcasted_iota(jnp.int32, (HID_CH, HID_CH), 0)
    ends = jnp.where((sub == PACK + 24) | (sub == PACK + 25), feature_scale, 0.0).astype(bf16)
    blank = jnp.zeros((EDGE, HID_CH), f32)
    level[:EDGE, :] = blank
    level[EDGE + WINDOW * rows :, :] = blank
    level[EDGE : EDGE + WINDOW * rows, :] = dot(looked[...].astype(bf16), ends)
    line[...] = jnp.zeros_like(line)
    keep(line, taps, 0, hidden_at[...])

    for t in range(ITERS):
        low, high = 1 + 2 * t, rows - 2 - 2 * t
        at, length = (low - 1) * WINDOW, (high - low + 3) * WINDOW
        lane_at = lax.broadcasted_iota(jnp.int32, (length, HID_CH), 1)
        tap, channel = lane_at // PACK, lane_at % PACK
        near = [level[EDGE + at + b : EDGE + at + b + length, :] for b in (-1, 0, 1)]
        value = jnp.where(tap == 0, near[0], jnp.where(tap == 1, near[1], near[2]))
        at_lookup = (channel >= t * GROUPS) & (channel < (t + 1) * GROUPS)
        value = jnp.where(
            (channel == 3 * GROUPS) & (tap < 3),
            value,
            jnp.where(at_lookup, looked[at : at + length, :], 0.0),
        )
        inputs[at : at + length, :] = value.astype(bf16)

        for r, count in chunks(low, high, 5):
            at, length = r * WINDOW, count * WINDOW
            lhs = around(taps, at, length) + around(inputs, at, length)
            both = dot(jnp.concatenate(lhs, axis=1), weight[:, : 2 * HID_CH])
            skip, until = (WINDOW if r == low else 0), (WINDOW if r + count - 1 == high else 0)
            gate[at + skip : at + length - until, :] = (
                0.5 * jnp.tanh(0.5 * both[skip : length - until, :HID_CH]) + 0.5
            )
            reset = 0.5 * jnp.tanh(0.5 * both[:, HID_CH:]) + 0.5
            keep(line, reset_taps, at, reset * hidden_at[at : at + length, :])

        for r, count in chunks(low + 1, high - 1, 4):
            at, length = r * WINDOW, count * WINDOW
            lhs = around(reset_taps, at, length) + around(inputs, at, length)
            candidate = jnp.tanh(dot(jnp.concatenate(lhs, axis=1), weight[:, 2 * HID_CH :]))
            hidden = hidden_at[at : at + length, :]
            hidden = hidden + gate[at : at + length, :] * (candidate - hidden)
            pixel = lax.broadcasted_iota(jnp.int32, (length, HID_CH), 0)
            column, row = pixel % WINDOW + first, pixel // WINDOW + (r + first_row)
            inside = ((column >= 0) | (disp > 0)) & ((column < TILE) | (disp < disps - 1))
            inside = inside & (row >= 0) & (row < bands)
            hidden = jnp.where(inside, hidden, 0.0).astype(bf16)
            level[EDGE + at : EDGE + at + length, :] += dot_nt(hidden, heads[...])
            hidden_at[at : at + length, :] = hidden.astype(f32)
            if t < ITERS - 1:
                keep(line, taps, at, hidden.astype(f32))

    lane = lax.broadcasted_iota(jnp.int32, (strip, HID_CH), 1)
    for r in range(QUAD):
        at = (REACH + r) * WINDOW + EDGE
        hidden = hidden_at[at : at + strip, :]
        value = level[EDGE + at : EDGE + at + strip, :] * (1.0 / feature_scale)
        high = value.astype(bf16).astype(f32)
        middle = (value - high).astype(bf16).astype(f32)
        parts = jnp.where(lane == 0, high, jnp.where(lane == 1, middle, value - high - middle))
        parts = jnp.where(lane < 3, parts, 0.0)
        blocks[r] = jnp.concatenate([hidden, parts], axis=0).astype(bf16)
    for i, out in zip(ORDER, (out_0, out_1, out_2, out_3)):
        out[...] = blocks[member ^ i]


def unpack_kernel(from_0, from_1, from_2, from_3, disparity_out, hidden_out, blocks):
    for i, block in enumerate((from_0, from_1, from_2, from_3)):
        blocks[i] = block[...]
    place = position()
    member = place[0] % QUAD
    slots = [slot_of(strip_at(place, strip) ^ member) for strip in range(QUAD)]
    held = [blocks[slot].astype(f32) for slot in slots]
    hidden_out[0] = jnp.concatenate([block[:STRIP] for block in held], axis=0).astype(bf16)
    parts = jnp.concatenate([block[STRIP:] for block in held], axis=0).T
    disparity_out[...] = parts[0:1] + parts[1:2] + parts[2:3]


def in_hbm(value):
    return pltpu.with_memory_space_constraint(value, pltpu.HBM)


def to_sides(value):
    disps = lax.axis_size("disp")
    right = [(d, d + 1) for d in range(disps - 1)]
    left = [(d + 1, d) for d in range(disps - 1)]
    if disps == 2:
        return lax.ppermute(value, "disp", right + left)[None]
    return jnp.stack([lax.ppermute(value, "disp", right), lax.ppermute(value, "disp", left)])


def in_group(blocks):
    return [blocks[0]] + [
        to_rows(block, lambda band, i=i: band ^ i)
        for i, block in list(zip(ORDER, blocks))[1:]
    ]


def to_layers(value, partner):
    groups = lax.axis_size("band") // QUAD
    if not any(0 <= partner(g) < groups for g in range(groups)):
        return None
    return to_rows(value, lambda band: partner(band // QUAD) * QUAD + band % QUAD)


def to_rows(value, shift):
    bands = lax.axis_size("band")
    return lax.ppermute(
        value, "band", [(i, shift(i)) for i in range(bands) if 0 <= shift(i) < bands]
    )


def odd_pair(i):
    return i ^ 1


def even_pair(i):
    return i - 1 if i % 2 == 0 else i + 1


def local(
    feat_left,
    feat_right,
    limit,
    indices,
    hidden_start,
    vol_kernel,
    group_gain,
    hid_kernel,
    in_kernel,
    head_weight,
):
    bands, disps = lax.axis_size("band"), lax.axis_size("disp")
    vmem = pl.BlockSpec(memory_space=pltpu.VMEM)
    hbm = pl.BlockSpec(memory_space=pltpu.HBM)
    padded = (DISPS + 2) * GROUPS

    feats = jnp.concatenate([feat_left[0], feat_right[0]], axis=0)
    odd_own, even_own = to_rows(feats, odd_pair), to_rows(feats, even_pair)
    across = to_sides(feats)
    raw_own, kernel_held, marks, gains, heads = pl.pallas_call(
        own_row_kernel,
        out_shape=(
            jax.ShapeDtypeStruct((padded, 2 * TILE), bf16),
            jax.ShapeDtypeStruct((27, GROUPS, GROUPS), bf16),
            jax.ShapeDtypeStruct((GROUPS, TILE), jnp.int32),
            jax.ShapeDtypeStruct((GROUPS, TILE), f32),
            jax.ShapeDtypeStruct((HID_CH, HID_CH), bf16),
        ),
        in_specs=[vmem, vmem] + [hbm] * 5,
        out_specs=(vmem,) * 5,
        scratch_shapes=[
            pltpu.VMEM((padded, TILE), f32),
            pltpu.VMEM((padded, TILE), f32),
            pltpu.VMEM((1, TILE), jnp.int32),
            pltpu.VMEM((ITERS, 1, TILE), jnp.int32),
            pltpu.SMEM((GROUPS,), f32),
            pltpu.VMEM((1, HID_CH), bf16),
            pltpu.VMEM((27, GROUPS, GROUPS), bf16),
            pltpu.SemaphoreType.DMA((5,)),
        ],
        compiler_params=pltpu.CompilerParams(vmem_limit_bytes=16 * 2**20),
        cost_estimate=pl.CostEstimate(flops=2 * 10**9, bytes_accessed=4 * 2**20, transcendentals=0),
    )(
        feats, across, in_hbm(limit), in_hbm(indices), in_hbm(group_gain),
        in_hbm(head_weight.reshape(1, HID_CH)), in_hbm(vol_kernel.reshape(27, GROUPS, GROUPS)),
    )
    hidden = hidden_start[0]
    hidden_across = to_sides(hidden)
    odd_own, even_own, raw_own, hidden_across = lax.optimization_barrier(
        (odd_own, even_own, raw_own, hidden_across)
    )
    taps = pl.pallas_call(
        toeplitz_kernel,
        out_shape=jax.ShapeDtypeStruct((3 * OUT_SLAB, 3 * SLAB), bf16),
        in_specs=[vmem],
        out_specs=vmem,
        compiler_params=pltpu.CompilerParams(vmem_limit_bytes=8 * 2**20),
        cost_estimate=pl.CostEstimate(flops=10**9, bytes_accessed=2**20, transcendentals=0),
    )(kernel_held)
    marks_across = to_sides(marks)
    odd_across, even_across = to_sides(odd_own), to_sides(even_own)

    in_weight = jnp.concatenate(
        [in_kernel[:, :, :GROUPS]] * ITERS + [in_kernel[:, :, GROUPS:]], axis=2
    )
    in_weight = jnp.pad(in_weight, ((0, 0), (0, 1), (0, PACK - in_weight.shape[2]), (0, 0)))
    in_weight = in_weight.reshape(3 * HID_CH, 3 * HID_CH)

    blocks = pl.pallas_call(
        volume_kernel,
        out_shape=(jax.ShapeDtypeStruct((BLOCK_ROWS, TILE), bf16),) * QUAD,
        in_specs=[vmem] * 9 + [hbm, hbm],
        out_specs=(vmem,) * QUAD,
        scratch_shapes=[
            pltpu.VMEM((padded, 2 * TILE), bf16),
            pltpu.VMEM((3 * OUT_SLAB, 3 * SLAB), bf16),
            pltpu.VMEM((2, padded, TILE), f32),
            pltpu.VMEM((2, padded, TILE), f32),
            pltpu.VMEM((2, DISPS, TILE), f32),
            pltpu.VMEM((TILE + 2 * EDGE, HID_CH), f32),
            pltpu.VMEM((QUAD, BLOCK_ROWS, TILE), bf16),
            pltpu.SemaphoreType.DMA((2,)),
        ],
        compiler_params=pltpu.CompilerParams(vmem_limit_bytes=24 * 2**20),
        cost_estimate=pl.CostEstimate(
            flops=5 * 10**9, bytes_accessed=16 * 2**20, transcendentals=DISPS * TILE
        ),
    )(
        gains, odd_own, odd_across, even_own, even_across,
        marks, marks_across, hidden, hidden_across, raw_own, taps,
    )

    weight = pl.pallas_call(
        weight_kernel,
        out_shape=jax.ShapeDtypeStruct((12 * HID_CH, 3 * HID_CH), bf16),
        in_specs=[vmem, vmem],
        out_specs=vmem,
        compiler_params=pltpu.CompilerParams(vmem_limit_bytes=8 * 2**20),
        cost_estimate=pl.CostEstimate(flops=10**8, bytes_accessed=2**20, transcendentals=0),
    )(hid_kernel.reshape(9 * HID_CH, 3 * HID_CH), in_weight)
    own, weight = lax.optimization_barrier((jnp.stack(in_group(blocks)), weight))
    around = [
        to_layers(own, lambda g: (g - 1 ^ 1) + 1),
        to_layers(own, lambda g: g ^ 1),
        to_layers(own, lambda g: (g - 2 ^ 2) + 2),
        to_layers(own, lambda g: g ^ 2),
    ]
    if around[2] is None:
        around[2] = around[3]

    pixels = WINDOW * AROUND
    refined = pl.pallas_call(
        refine_kernel,
        out_shape=(jax.ShapeDtypeStruct((2 * STRIP, HID_CH), bf16),) * QUAD,
        in_specs=[vmem] * 7,
        out_specs=(vmem,) * QUAD,
        scratch_shapes=[
            pltpu.VMEM((pixels + 2 * EDGE, HID_CH), f32),
            pltpu.VMEM((pixels, HID_CH), f32),
            pltpu.VMEM((pixels, HID_CH), f32),
            pltpu.VMEM((pixels, 3 * HID_CH), bf16),
            pltpu.VMEM((pixels, 3 * HID_CH), bf16),
            pltpu.VMEM((pixels, HID_CH), bf16),
            pltpu.VMEM((pixels, HID_CH), f32),
            pltpu.VMEM((pixels + 2 * EDGE, HID_CH), f32),
            pltpu.VMEM((QUAD, 2 * STRIP, HID_CH), bf16),
        ],
        compiler_params=pltpu.CompilerParams(vmem_limit_bytes=32 * 2**20),
    )(
        own, *around,
        weight, heads,
    )
    disparity, hidden = pl.pallas_call(
        unpack_kernel,
        out_shape=(
            jax.ShapeDtypeStruct((1, TILE), f32),
            jax.ShapeDtypeStruct((1, TILE, HID_CH), bf16),
        ),
        in_specs=[vmem] * QUAD,
        out_specs=(vmem, vmem),
        scratch_shapes=[pltpu.VMEM((QUAD, 2 * STRIP, HID_CH), bf16)],
        compiler_params=pltpu.CompilerParams(vmem_limit_bytes=4 * 2**20),
    )(*in_group(refined))
    return (disparity, hidden)


def solution(mesh):
    in_specs = (
        P("band", None, "disp"),
        P("band", None, "disp"),
        P("band", "disp"),
        P(None, "band", "disp"),
        P("band", "disp", None),
        P(),
        P(),
        P(),
        P(),
        P(),
    )
    out_specs = (P("band", "disp"), P("band", "disp", None))
    return jax.shard_map(local, mesh=mesh, in_specs=in_specs, out_specs=out_specs, check_vma=False)
```
